32 devices in a mesh: items: 8 (over z, x), stream: 4 (over y, core).
Axes of the slice: x: 2, y: 2, z: 4, core: 2. Of those that a mesh axis runs over, the one named last changes fastest.
Arguments:
- tokens: bfloat16 [16384, 768], P(('items', 'stream')), may hold values from -6 to 6
- group_kind: int32 [8], P('items'), may hold values from 0 to 1
- ln1_gain: bfloat16 [768], P(('items', 'stream')), may hold values from 0.099609375 to 1.8984375
- ln1_bias: bfloat16 [768], P(('items', 'stream')), may hold values from -3 to 3
- w_qkv: bfloat16 [768, 2304], P(('items', 'stream')), may hold values from -0.21875 to 0.21875
- q_bias: bfloat16 [768], P(('items', 'stream')), may hold values from -3 to 3
- v_bias: bfloat16 [768], P(('items', 'stream')), may hold values from -3 to 3
- w_out: bfloat16 [768, 768], P(('items', 'stream')), may hold values from -0.625 to 0.625
- out_bias: bfloat16 [768], P(('items', 'stream')), may hold values from -2 to 2
- ln2_gain: bfloat16 [768], P(('items', 'stream')), may hold values from 0.099609375 to 1.8984375
- ln2_bias: bfloat16 [768], P(('items', 'stream')), may hold values from -3 to 3
- w_up: bfloat16 [2, 768, 3072], P(None, ('items', 'stream')), may hold values from -0.21875 to 0.21875
- b_up: bfloat16 [2, 3072], P(None, ('items', 'stream')), may hold values from -3 to 3
- w_down: bfloat16 [2, 3072, 768], P(None, ('items', 'stream')), may hold values from -0.109375 to 0.109375
- b_down: bfloat16 [2, 768], P(None, ('items', 'stream')), may hold values from -2 to 2
- cotangent: bfloat16 [16384, 768], P(('items', 'stream')), may hold values from -6 to 6
Outputs:
- output: bfloat16 [16384, 768], P(('items', 'stream'))
- token_grad: bfloat16 [16384, 768], P(('items', 'stream'))
- grad_ln1_gain: float32 [768], P(('items', 'stream'))
- grad_ln1_bias: float32 [768], P(('items', 'stream'))
- grad_w_qkv: float32 [768, 2304], P(('items', 'stream'))
- grad_q_bias: float32 [768], P(('items', 'stream'))
- grad_v_bias: float32 [768], P(('items', 'stream'))
- grad_w_out: float32 [768, 768], P(('items', 'stream'))
- grad_out_bias: float32 [768], P(('items', 'stream'))
- grad_ln2_gain: float32 [768], P(('items', 'stream'))
- grad_ln2_bias: float32 [768], P(('items', 'stream'))
- grad_w_up: float32 [2, 768, 3072], P(None, ('items', 'stream'))
- grad_b_up: float32 [2, 3072], P(None, ('items', 'stream'))
- grad_w_down: float32 [2, 3072, 768], P(None, ('items', 'stream'))
- grad_b_down: float32 [2, 768], P(None, ('items', 'stream'))
- counts: float32 [2], replicated
The draws below stay inside these ranges and needn't reach their ends.
Inputs may be any that keep to these rules, and one draw needn't show every extreme that they name: `group_kind`: 0 marks a group of 7 items with 197 patch rows, 1 a group of 2 items with 577 patch rows; item and modality of each row follow from it as the steps state.
All inputs are finite; a program needn't handle non-finite values.
Results may differ from the reference program's by a relative error of at most 0.014.
Values may be sent and summed in bfloat16 or wider, within the bound.
A program may use at most 256 MiB of HBM per device.

```python
import jax
import jax.numpy as jnp
from jax import lax

D = 768
HEADS = 12
HEAD_DIM = 64
FF = 3072
ROWS = 512
PATCH_S = 197
PATCH_L = 577
TEXT_LEN = 40
ITEMS_S = 7
ITEMS_L = 2
GROUPS = 8
TOKENS = 16384
N_STREAM = 4


def plant(entries, own_key, least, top_value):
    longest = entries.shape.index(max(entries.shape))
    spots = []
    for shift in (0, 1):
        where = [jax.random.randint(jax.random.fold_in(own_key, axis), (), 0, length) for axis, length in enumerate(entries.shape)]
        where[longest] = (where[longest] + shift) % entries.shape[longest]
        spots.append(tuple(where))
    return entries.at[spots[0]].set(least).at[spots[1]].set(top_value)


def steps_of(stream_key, extent, split, low, top_value):
    factor_of, own = 1.0, jax.random.fold_in(stream_key, 6)
    for axis_at, parts in split:
        steps = jnp.exp(jax.random.uniform(jax.random.fold_in(own, axis_at), (parts,), jnp.float32, low / len(split), top_value / len(split)))
        factor_of = factor_of * jnp.repeat(steps, extent[axis_at] // parts).reshape([-1 if axis == axis_at else 1 for axis in range(len(extent))])
    return factor_of


def gaussian(rng, dims, spread, limit, pieces=(), kind=jnp.bfloat16):
    loudness = steps_of(rng, dims, pieces, -0.22, 0.18) if pieces else 1.0
    values = jax.random.normal(rng, dims, jnp.float32) * spread * loudness
    return jnp.minimum(jnp.maximum(values, -limit), limit).astype(kind)


def setup_inputs(seed: int = 0) -> dict:
    splits = jax.random.split(jax.random.key(seed), 17)
    return {
        "tokens": gaussian(splits[0], (TOKENS, D), 1.0, 6.0, ((0, 32),)),
        "group_kind": plant(jax.random.randint(splits[1], (GROUPS,), 0, 2), jax.random.fold_in(splits[1], 1), 0, 1).astype(jnp.int32),
        "ln1_gain": jnp.clip(1.0 + 0.18 * jax.random.normal(splits[2], (D,), jnp.float32), 0.099609375, 1.8984375).astype(jnp.bfloat16),
        "ln1_bias": gaussian(splits[3], (D,), 0.5, 3.0, ((0, 32),)),
        "w_qkv": gaussian(splits[4], (D, 3 * D), D ** -0.5, 0.21875, ((0, 32),)),
        "q_bias": gaussian(splits[5], (D,), 0.5, 3.0, ((0, 32),)),
        "v_bias": gaussian(splits[6], (D,), 0.5, 3.0, ((0, 32),)),
        "w_out": gaussian(splits[7], (D, D), (D // 8) ** -0.5, 0.625, ((0, 32),)),
        "out_bias": gaussian(splits[8], (D,), 0.3, 2.0, ((0, 32),)),
        "ln2_gain": jnp.clip(1.0 + 0.18 * jax.random.normal(splits[9], (D,), jnp.float32), 0.099609375, 1.8984375).astype(jnp.bfloat16),
        "ln2_bias": gaussian(splits[10], (D,), 0.5, 3.0, ((0, 32),)),
        "w_up": gaussian(splits[11], (2, D, FF), D ** -0.5, 0.21875, ((1, 32),)),
        "b_up": gaussian(splits[12], (2, FF), 0.5, 3.0, ((1, 32),)),
        "w_down": gaussian(splits[13], (2, FF, D), FF ** -0.5, 0.109375, ((1, 32),)),
        "b_down": gaussian(splits[14], (2, D), 0.3, 2.0, ((1, 32),)),
        "cotangent": gaussian(splits[15], (TOKENS, D), 1.0, 6.0, ((0, 32),)),
    }


NORM_EPS = 1e-05
MASKED = -1000000000.0
HIGHEST = lax.Precision.HIGHEST

@jax.custom_vjp
def low(v):
    return lax.optimization_barrier(v.astype(jnp.bfloat16)).astype(jnp.float32)

@jax.custom_vjp
def low_back(v):
    return v

def low_keep(v):
    return (low(v), None)

def low_pass(kept, grad):
    return (grad,)

def back_keep(v):
    return (v, None)

def back_low(kept, grad):
    return (low(grad),)
low.defvjp(low_keep, low_pass)
low_back.defvjp(back_keep, back_low)

def layer_norm(values, gain_row, shift_row):
    row_mean = lax.optimization_barrier(jnp.mean(values, axis=-1, keepdims=True))
    centred = values - row_mean
    variance = lax.optimization_barrier(jnp.mean(centred * centred, axis=-1, keepdims=True))
    return centred * lax.rsqrt(variance + NORM_EPS) * gain_row + shift_row

def layout(group_type, positions, row_count):
    patch_len = jnp.where(group_type == 0, PATCH_S, PATCH_L).astype(jnp.int32)
    members = jnp.where(group_type == 0, ITEMS_S, ITEMS_L).astype(jnp.int32)
    is_patch = positions < 3 * row_count
    patch_item = positions // patch_len
    text_item = jnp.maximum(positions - 3 * row_count, 0) // TEXT_LEN
    member = jnp.where(is_patch, patch_item, text_item)
    member = jnp.where(member < members, member, -1).astype(jnp.int32)
    modality = jnp.where(member < 0, 2, jnp.where(is_patch, 0, 1)).astype(jnp.int32)
    return (member, modality)

def group_attention(group_args):
    queries, keys_all, values_all, member = group_args
    allowed = member[:, None] == member[None, :]
    score_scale = HEAD_DIM ** (-0.5)
    attended = []
    for head_index in range(HEADS):
        columns = slice(head_index * HEAD_DIM, (head_index + 1) * HEAD_DIM)
        raw_scores = jnp.dot(queries[:, columns], keys_all[:, columns].T, precision=HIGHEST)
        scores = jnp.where(allowed, low_back(raw_scores) * score_scale, MASKED)
        row_top = lax.optimization_barrier(jnp.max(scores, axis=1, keepdims=True))
        exponent = jnp.exp(scores - row_top)
        softmax_out = exponent / lax.optimization_barrier(jnp.sum(exponent, axis=1, keepdims=True))
        attended.append(jnp.dot(low(softmax_out), values_all[:, columns], precision=HIGHEST))
    return jnp.concatenate(attended, axis=1)

def reference(tokens, group_kind, ln1_gain, ln1_bias, w_qkv, q_bias, v_bias, w_out, out_bias, ln2_gain, ln2_bias, w_up, b_up, w_down, b_down, cotangent):
    positions = jnp.arange(N_STREAM * ROWS, dtype=jnp.int32)
    members, modalities = jax.vmap(lambda group_type: layout(group_type, positions, ROWS))(group_kind)
    flat_modality = modalities.reshape(-1)
    block_rows = N_STREAM * ROWS

    def forward(values, gain_one, shift_one, qkv_weight, query_shift, value_shift, out_weight, out_shift, gain_two, shift_two, up_all, up_shift, down_all, down_shift):
        normed = low(layer_norm(values, gain_one, shift_one))
        projected = jnp.dot(normed, qkv_weight, precision=HIGHEST)
        queries = low(low_back(projected[:, :D] + query_shift))
        keys_all = low(low_back(projected[:, D:2 * D]))
        values_all = low(low_back(projected[:, 2 * D:] + value_shift))
        mixed = lax.map(jax.checkpoint(group_attention), (queries.reshape(GROUPS, block_rows, D), keys_all.reshape(GROUPS, block_rows, D), values_all.reshape(GROUPS, block_rows, D), members))
        mixed = low(low_back(mixed.reshape(TOKENS, D)))
        residual = values + low_back(jnp.dot(mixed, out_weight, precision=HIGHEST) + out_shift)
        normed_two = low(layer_norm(residual, gain_two, shift_two))
        branch = jnp.zeros((TOKENS, D), jnp.float32)
        for expert in range(2):
            hidden_pre = low_back(jnp.dot(normed_two, up_all[expert], precision=HIGHEST) + up_shift[expert])
            hidden = low(jax.nn.gelu(hidden_pre, approximate=False))
            result = jnp.dot(hidden, down_all[expert], precision=HIGHEST) + down_shift[expert]
            branch = branch + jnp.where(flat_modality[:, None] == expert, result, 0.0)
        return residual + branch
    output, pull = jax.vjp(forward, tokens.astype(jnp.float32), ln1_gain.astype(jnp.float32), ln1_bias.astype(jnp.float32), w_qkv.astype(jnp.float32), q_bias.astype(jnp.float32), v_bias.astype(jnp.float32), w_out.astype(jnp.float32), out_bias.astype(jnp.float32), ln2_gain.astype(jnp.float32), ln2_bias.astype(jnp.float32), w_up.astype(jnp.float32), b_up.astype(jnp.float32), w_down.astype(jnp.float32), b_down.astype(jnp.float32))
    live_rows = (flat_modality < 2).astype(jnp.float32)[:, None]
    gradients = pull(cotangent.astype(jnp.float32) * live_rows)
    counts = jnp.stack([jnp.sum((flat_modality == 0).astype(jnp.float32)), jnp.sum((flat_modality == 1).astype(jnp.float32))])
    factor = lax.rsqrt(counts)
    return (output.astype(jnp.bfloat16), gradients[0].astype(jnp.bfloat16), gradients[1], gradients[2], gradients[3], gradients[4], gradients[5], gradients[6], gradients[7], gradients[8], gradients[9], gradients[10] * factor[:, None, None], gradients[11] * factor[:, None], gradients[12] * factor[:, None, None], gradients[13] * factor[:, None], counts)
```

```python
import functools

import jax
import jax.numpy as jnp
from jax import lax
from jax.experimental import pallas as pl
from jax.experimental.pallas import tpu as pltpu
from jax.sharding import PartitionSpec as P

HEADS = 12
HEAD_DIM = 64
PATCH_S = 197
PATCH_L = 577
TEXT_LEN = 40
ITEMS_S = 7
ITEMS_L = 2


NORM_EPS = 1e-05
MASKED = -1000000000.0


def layer_norm(values, gain_row, shift_row):
    row_mean = jnp.mean(values, axis=-1, keepdims=True)
    centred = values - row_mean
    variance = jnp.mean(centred * centred, axis=-1, keepdims=True)
    return centred * lax.rsqrt(variance + NORM_EPS) * gain_row + shift_row


def gelu_exact(values):
    return jax.nn.gelu(values, approximate=False)


def layout(group_type, positions, row_count):
    patch_len = jnp.where(group_type == 0, PATCH_S, PATCH_L).astype(jnp.int32)
    members = jnp.where(group_type == 0, ITEMS_S, ITEMS_L).astype(jnp.int32)
    is_patch = positions < 3 * row_count
    patch_item = positions // patch_len
    text_item = jnp.maximum(positions - 3 * row_count, 0) // TEXT_LEN
    member = jnp.where(is_patch, patch_item, text_item)
    member = jnp.where(member < members, member, -1)
    modality = jnp.where(member < 0, 2, jnp.where(is_patch, 0, 1)).astype(jnp.int32)
    return (member, modality)


def product(first_op, second_op):
    return jnp.dot(first_op, second_op, preferred_element_type=jnp.float32)


def product_lead(first_op, second_op):
    return lax.dot_general(
        first_op, second_op, (((0,), (0,)), ((), ())), preferred_element_type=jnp.float32
    )


def product_trail(first_op, second_op):
    return lax.dot_general(
        first_op, second_op, (((1,), (1,)), ((), ())), preferred_element_type=jnp.float32
    )


def halves(length):
    return ((0, length // 2), (length // 2, length // 2))


def gather_chunks(model_rows, width, ff_rows, ff):
    rows, down_rows = (0, model_rows), (0, ff_rows)
    chunks = [
        [((0, None), (0, 16), (0, 128), 0, False)]
        + [((1, None), rows, cols, order, False) for order, cols in enumerate(halves(3 * width))],
        [((2, None), rows, cols, order, False) for order, cols in enumerate(halves(width))],
    ]
    for e in range(2):
        chunks.append([((3, e), rows, cols, o, e == 1) for o, cols in enumerate(halves(ff))])
        chunks.append(
            [((4, e), band, (0, width), o, e == 1) for o, band in enumerate(halves(ff_rows))]
        )
    return chunks


def scatter_chunks(model_rows, width, ff_rows, ff):
    rows = (0, model_rows)
    chunks = []
    for e in range(2):
        chunks.append([(0, e, rows, cols, order) for order, cols in enumerate(halves(ff))])
        chunks.append(
            [(1, e, band, (0, width), order) for order, band in enumerate(halves(ff_rows))]
        )
    chunks.append([(2, 0, rows, cols, order) for order, cols in enumerate(halves(width))])
    chunks.append(
        [(3, 0, rows, cols, order) for order, cols in enumerate(halves(3 * width))]
        + [(4, 0, (0, 8), (0, 128), 0)]
    )
    return chunks


MESH = pl.DeviceIdType.MESH
GATHER_ORDERS = (("z", "x", "y"), ("z", "y", "x"), ("y", "x", "z"))
SCATTER_ORDERS = (("y", "x"), ("x", "y"))


def coords():
    items, stream = lax.axis_index("items"), lax.axis_index("stream")
    return dict(z=items // 2, x=items % 2, y=stream // 2, c=stream % 2)


def place(at):
    return (at["z"] * 2 + at["x"], at["y"] * 2 + at["c"])


def moved(at, dim, by, depth):
    return {**at, dim: lax.rem(at[dim] + by, depth if dim == "z" else 2)}


def greet(at, depth):
    peers = [moved(at, "z", k, depth) for k in range(1, depth)]
    peers += [moved(at, d, 1, depth) for d in "xyc"]
    barrier = pltpu.get_barrier_semaphore()
    for peer in peers:
        pl.semaphore_signal(barrier, inc=1, device_id=place(peer), device_id_type=MESH)
    pl.semaphore_wait(barrier, len(peers))


def guard(cond, act):
    if cond is None:
        act()
    else:
        pl.when(cond)(act)


def pipelined(chunks, n_steps, ahead, start, wait):
    count = len(chunks)
    for j in range(min(ahead, count)):
        start(chunks[j], 0)
    for t in range(count + n_steps - 1):
        if t + ahead < count:
            start(chunks[t + ahead], 0)
        for step in range(n_steps - 1, -1, -1):
            j = t - step
            if 0 <= j < count:
                wait(chunks[j], step)
                if step < n_steps - 1:
                    start(chunks[j], step + 1)


def gather_kernel(depth, chunks, entries, n_in, *refs):
    ins, outs = refs[:n_in], refs[n_in : 2 * n_in]
    local_sem, send_sem, recv_sem = refs[2 * n_in :]
    at = coords()
    mine = (at["z"], at["x"], at["y"], at["c"])

    def source(entry):
        k, e = entry
        return ins[k] if e is None else ins[k].at[e]

    def target(entry):
        k, e = entry
        return outs[k] if e is None else outs[k].at[e]

    local = [
        pltpu.make_async_copy(source(entry), target(entry).at[mine], local_sem.at[j])
        for j, entry in enumerate(entries)
    ]
    for copy in local:
        copy.start()
    greet(at, depth)
    for copy in local:
        copy.wait()
    lower, upper = at["y"] == 0, at["y"] == 1
    number = {piece: j for j, piece in enumerate(piece for chunk in chunks for piece in chunk)}

    def stage(piece, step):
        entry, rows, cols, order, text = piece
        dims = GATHER_ORDERS[order] + ("c",)
        dim = dims[step]
        held = tuple(slice(None) if d in dims[:step] else pl.ds(at[d], 1) for d in "zxyc")
        view = target(entry).at[held + (pl.ds(*rows), pl.ds(*cols))]
        sends = recvs = None
        if text and dim == "y":
            sends, recvs = lower, upper
        elif text and "y" in dims[:step]:
            sends = recvs = upper
        found = []
        for k in range(1, depth if dim == "z" else 2):
            sem = {"z": k - 1, "x": depth - 1, "y": depth, "c": depth + 1}[dim]
            found.append(
                pltpu.make_async_remote_copy(
                    src_ref=view,
                    dst_ref=view,
                    send_sem=send_sem.at[number[piece], sem],
                    recv_sem=recv_sem.at[number[piece], sem],
                    device_id=place(moved(at, dim, k, depth)),
                    device_id_type=MESH,
                )
            )
        return found, sends, recvs

    def each(chunk, step, which, call):
        for piece in chunk:
            found = stage(piece, step)

            def act(copies=found[0]):
                for copy in copies:
                    call(copy)

            guard(found[which], act)

    pipelined(
        chunks,
        4,
        2,
        lambda chunk, step: each(chunk, step, 1, lambda copy: copy.start()),
        lambda chunk, step: each(chunk, step, 2, lambda copy: copy.wait_recv()),
    )
    for chunk in chunks:
        for step in range(4):
            each(chunk, step, 1, lambda copy: copy.wait_send())


def gather_all(arrays, lead, chunks, depth):
    n_in = len(arrays)
    entries = []
    out_shape = []
    for k, (array, wide) in enumerate(zip(arrays, lead)):
        entries += [(k, e) for e in range(array.shape[0])] if wide else [(k, None)]
        head = array.shape[:1] if wide else ()
        out_shape.append(
            jax.ShapeDtypeStruct(head + (depth, 2, 2, 2) + array.shape[-2:], array.dtype)
        )
    n_pieces = sum(len(chunk) for chunk in chunks)
    anywhere = pl.BlockSpec(memory_space=pl.ANY)
    return pl.pallas_call(
        functools.partial(gather_kernel, depth, chunks, entries, n_in),
        out_shape=out_shape,
        in_specs=[anywhere] * n_in,
        out_specs=[anywhere] * n_in,
        scratch_shapes=[pltpu.SemaphoreType.DMA((len(entries),))]
        + [pltpu.SemaphoreType.DMA((n_pieces, depth + 2))] * 2,
        compiler_params=pltpu.CompilerParams(
            collective_id=1, has_side_effects=True, vmem_limit_bytes=16 << 20
        ),
    )(*arrays)


def scatter_kernel(depth, kinds, chunks, *refs):
    n = len(kinds)
    ins, factor, outs = refs[:n], refs[n], refs[n + 1 : 2 * n + 1]
    acc, first, second, last = (
        refs[2 * n + 1 + k * n : 2 * n + 1 + (k + 1) * n] for k in range(4)
    )
    send_sem, recv_sem = refs[6 * n + 1 :]
    at = coords()
    z, x, y, c = (at[d] for d in "zxyc")
    greet(at, depth)
    lower, upper = y == 0, y == 1
    text_device = jnp.logical_and(upper, c == 1)
    image_device = jnp.logical_or(lower, c == 0)
    beside_text = jnp.logical_and(upper, c == 0)
    beside_image = jnp.logical_or(lower, c == 1)
    number = {piece: j for j, piece in enumerate(piece for chunk in chunks for piece in chunk)}
    every = slice(None)

    def copies_of(piece, step):
        k, e, rows, cols, order = piece
        box = (pl.ds(*rows), pl.ds(*cols))
        image, text = kinds[k] and e == 0, kinds[k] and e == 1
        dims = ("c",) + SCATTER_ORDERS[order] + ("z",)
        dim = dims[step]
        here = acc[k].at[e]

        def make(src, dst, sem, by=1):
            return pltpu.make_async_remote_copy(
                src_ref=src,
                dst_ref=dst,
                send_sem=send_sem.at[number[piece], sem],
                recv_sem=recv_sem.at[number[piece], sem],
                device_id=place(moved(at, dim, by, depth)),
                device_id_type=MESH,
            )

        sends = recvs = None
        if dim == "c":
            if image:
                sends, recvs = image_device, beside_image
            elif text:
                sends, recvs = text_device, beside_text
            src = ins[k].at[(every, every, every, 1 - c) + box]
            return [(make(src, here.at[(every, every, every) + box], 0), sends, recvs)]
        if dim == "z":
            found = []
            for by in range(1, depth):
                src = here.at[(lax.rem(z + by, depth), x, y) + box]
                found.append((make(src, last[k].at[(e, by - 1) + box], 2 + by, by), None, None))
            return found
        if text and dim == "y":
            sends, recvs = upper, lower
        elif text and step == 1:
            sends = recvs = upper
        if step == 1:
            spot = (every, every, 1 - y) if dim == "y" else (every, 1 - x, every)
            dst = first[k].at[(e, every, every) + box]
        else:
            spot = (every, x, 1 - y) if dim == "y" else (every, 1 - x, y)
            dst = second[k].at[(e, every) + box]
        return [(make(here.at[spot + box], dst, step), sends, recvs)]

    def combine(piece, step):
        k, e, rows, cols, order = piece
        box = (pl.ds(*rows), pl.ds(*cols))
        image, text = kinds[k] and e == 0, kinds[k] and e == 1
        here = acc[k].at[e]

        def over(spots, value_of, keep):
            @pl.loop(0, depth)
            def _(level):
                for index, spot in enumerate(spots):
                    where = (level,) + spot + box
                    value = value_of(level, index, spot)
                    here[where] = value if keep else here[where] + value

        if step == 0:
            spots = [(0, 0), (0, 1), (1, 0), (1, 1)]
            own = lambda level, index, spot: ins[k][(level,) + spot + (c,) + box]
            if image:
                pl.when(lower)(lambda: over(spots, own, False))
                pl.when(beside_text)(lambda: over(spots, own, True))
            elif text:
                pl.when(text_device)(lambda: over(spots, own, True))
            else:
                over(spots, own, False)
        elif step == 1:
            dim = SCATTER_ORDERS[order][0]
            spots = [(0, y), (1, y)] if dim == "y" else [(x, 0), (x, 1)]
            got = lambda level, index, spot: first[k][(e, level, index) + box]
            if text and dim == "y":
                pl.when(lower)(lambda: over(spots, got, True))
            elif text:
                pl.when(upper)(lambda: over(spots, got, False))
            else:
                over(spots, got, False)
        elif step == 2:
            dim = SCATTER_ORDERS[order][1]
            got = lambda level, index, spot: second[k][(e, level) + box]
            if text and dim == "y":
                pl.when(lower)(lambda: over([(x, y)], got, True))
            else:
                over([(x, y)], got, False)
        else:
            total = here[(z, x, y) + box].astype(jnp.float32)
            for by in range(depth - 1):
                total = total + last[k][(e, by) + box].astype(jnp.float32)
            if kinds[k]:
                total = total * factor[0:1, e * 128 : e * 128 + 1]
            outs[k][(e,) + box] = total

    def start(chunk, step):
        for piece in chunk:
            for copy, sends, _ in copies_of(piece, step):
                guard(sends, copy.start)

    def wait(chunk, step):
        for piece in chunk:
            for copy, _, recvs in copies_of(piece, step):
                guard(recvs, copy.wait_recv)
            combine(piece, step)

    pipelined(chunks, 4, 2, start, wait)
    for chunk in chunks:
        for step in range(4):
            for piece in chunk:
                for copy, sends, _ in copies_of(piece, step):
                    guard(sends, copy.wait_send)


def scatter_all(arrays, factor, kinds, chunks, depth, collective):
    n = len(arrays)
    n_pieces = sum(len(chunk) for chunk in chunks)
    inside = pl.BlockSpec(memory_space=pltpu.VMEM)
    shapes = [((2 if kind else 1,), a.shape[4:], a.dtype) for kind, a in zip(kinds, arrays)]
    scratch = []
    for middle in ((depth, 2, 2), (depth, 2), (depth,), (depth - 1,)):
        scratch += [pltpu.VMEM(head + middle + tail, dtype) for head, tail, dtype in shapes]
    return pl.pallas_call(
        functools.partial(scatter_kernel, depth, kinds, chunks),
        out_shape=[jax.ShapeDtypeStruct(head + tail, jnp.float32) for head, tail, _ in shapes],
        in_specs=[inside] * (n + 1),
        out_specs=[inside] * n,
        scratch_shapes=scratch + [pltpu.SemaphoreType.DMA((n_pieces, depth + 2))] * 2,
        compiler_params=pltpu.CompilerParams(
            collective_id=collective, has_side_effects=True, vmem_limit_bytes=60 << 20
        ),
    )(*arrays, factor)


def body(
    near,
    tokens,
    group_kind,
    ln1_gain,
    ln1_bias,
    w_qkv,
    q_bias,
    v_bias,
    w_out,
    out_bias,
    ln2_gain,
    ln2_bias,
    w_up,
    b_up,
    w_down,
    b_down,
    cotangent,
):
    row_count = tokens.shape[0]
    model_width = tokens.shape[1]
    stream_size = lax.axis_size("stream")
    stream_place = lax.axis_index("stream")
    group_type = group_kind[0]
    own_positions = stream_place * row_count + jnp.arange(row_count, dtype=jnp.int32)
    own_member, own_modality = layout(group_type, own_positions, row_count)
    key_member = layout(
        group_type, jnp.arange(stream_size * row_count, dtype=jnp.int32), row_count
    )[0]
    devices = lax.axis_size("items") * stream_size
    totals = None
    expert_pick = jnp.where(stream_place == stream_size - 1, 1, 0).astype(jnp.int32)
    share, ff_share, ff = model_width // devices, w_down.shape[1], w_up.shape[2]
    thin = jnp.concatenate(
        [ln1_gain, ln1_bias, q_bias, v_bias, out_bias, ln2_gain, ln2_bias]
        + [b_up.reshape(-1), b_down.reshape(-1), group_kind.astype(jnp.bfloat16)]
    )
    thin = jnp.pad(thin, (0, 2048 - thin.shape[0])).reshape(16, 128)
    if near:
        depth = lax.axis_size("items") // 2
        thin_all, qkv_weight, out_weight, up_all, down_all = gather_all(
            [thin, w_qkv, w_out, w_up, w_down],
            [False, False, False, True, True],
            gather_chunks(share, model_width, ff_share, ff),
            depth,
        )
        qkv_weight = qkv_weight.reshape(model_width, -1)
        out_weight = out_weight.reshape(model_width, model_width)
        up_all = up_all.reshape(2, model_width, ff)
        down_all = down_all.reshape(2, ff, model_width)
    else:
        both = ("items", "stream")
        thin_all = lax.all_gather(thin, both, axis=0, tiled=True)
        qkv_weight = lax.all_gather(w_qkv, both, axis=0, tiled=True)
        out_weight = lax.all_gather(w_out, both, axis=0, tiled=True)
        up_all = lax.all_gather(w_up, both, axis=1, tiled=True)
        down_all = lax.all_gather(w_down, both, axis=1, tiled=True)
    thin_all = thin_all.reshape(devices, 2048)
    cut = 7 * share
    seven = thin_all[:, :cut].reshape(devices, 7, share).transpose(1, 0, 2).reshape(7, model_width)
    gain_one, shift_one, query_shift, value_shift, out_shift, gain_two, shift_two = seven
    up_shift_all = (
        thin_all[:, cut : cut + 2 * ff_share].reshape(devices, 2, ff_share).transpose(1, 0, 2)
    ).reshape(2, ff)
    cut = cut + 2 * ff_share
    down_shift_all = (
        thin_all[:, cut : cut + 2 * share].reshape(devices, 2, share).transpose(1, 0, 2)
    ).reshape(2, model_width)
    kinds = thin_all[::stream_size, cut + 2 * share].astype(jnp.int32)
    tally = []
    for kind in range(2):
        modality = layout(
            jnp.int32(kind), jnp.arange(stream_size * row_count, dtype=jnp.int32), row_count
        )[1]
        tally.append([jnp.sum((modality == e).astype(jnp.float32)) for e in range(2)])
    totals = jnp.stack(
        [jnp.sum(jnp.where(kinds == 0, tally[0][e], tally[1][e])) for e in range(2)]
    )
    tokens_f = tokens.astype(jnp.float32)
    normed_one, pull_one = jax.vjp(
        layer_norm, tokens_f, gain_one.astype(jnp.float32), shift_one.astype(jnp.float32)
    )
    normed_low = normed_one.astype(jnp.bfloat16)
    projected = product(normed_low, qkv_weight)
    queries = (projected[:, :model_width] + query_shift.astype(jnp.float32)).astype(jnp.bfloat16)
    keys_own = projected[:, model_width : 2 * model_width].astype(jnp.bfloat16)
    values_own = (projected[:, 2 * model_width :] + value_shift.astype(jnp.float32)).astype(
        jnp.bfloat16
    )
    keys_all, values_all = (
        lax.all_gather(keys_own, "stream", axis=0, tiled=True),
        lax.all_gather(values_own, "stream", axis=0, tiled=True),
    )
    allowed = own_member[:, None] == key_member[None, :]
    score_scale = HEAD_DIM ** (-0.5)

    def head_scores(head_index):
        columns = slice(head_index * HEAD_DIM, (head_index + 1) * HEAD_DIM)
        raw_scores = product_trail(queries[:, columns], keys_all[:, columns])
        return jnp.where(allowed, raw_scores * score_scale, MASKED)

    attended = []
    log_totals = []
    for head_index in range(HEADS):
        columns = slice(head_index * HEAD_DIM, (head_index + 1) * HEAD_DIM)
        scores = head_scores(head_index)
        row_top = jnp.max(scores, axis=1, keepdims=True)
        exponent = jnp.exp(scores - row_top)
        row_total = jnp.sum(exponent, axis=1, keepdims=True)
        softmax_low = (exponent / row_total).astype(jnp.bfloat16)
        attended.append(product(softmax_low, values_all[:, columns]))
        log_totals.append(row_top + jnp.log(row_total))
    mixed_low = jnp.concatenate(attended, axis=1).astype(jnp.bfloat16)
    residual = tokens_f + product(mixed_low, out_weight) + out_shift.astype(jnp.float32)
    normed_two, pull_two = jax.vjp(
        layer_norm, residual, gain_two.astype(jnp.float32), shift_two.astype(jnp.float32)
    )
    normed_two_low = normed_two.astype(jnp.bfloat16)
    up_weight = lax.dynamic_index_in_dim(up_all, expert_pick, 0, keepdims=False)
    up_shift = lax.dynamic_index_in_dim(up_shift_all, expert_pick, 0, keepdims=False)
    down_weight = lax.dynamic_index_in_dim(down_all, expert_pick, 0, keepdims=False)
    down_shift = lax.dynamic_index_in_dim(down_shift_all, expert_pick, 0, keepdims=False)
    hidden_pre = product(normed_two_low, up_weight) + up_shift.astype(jnp.float32)
    hidden, pull_gelu = jax.vjp(gelu_exact, hidden_pre)
    hidden_low = hidden.astype(jnp.bfloat16)
    branch = product(hidden_low, down_weight) + down_shift.astype(jnp.float32)
    expert_mask = (own_modality == expert_pick).astype(jnp.float32)[:, None]
    output = (residual + branch * expert_mask).astype(jnp.bfloat16)
    live_rows = (own_modality < 2).astype(jnp.float32)[:, None]
    out_grad = cotangent.astype(jnp.float32) * live_rows
    branch_grad = (out_grad * expert_mask).astype(jnp.bfloat16)
    grad_down = product_lead(hidden_low, branch_grad)
    grad_down_shift = jnp.sum(branch_grad.astype(jnp.float32), axis=0)
    hidden_grad = product_trail(branch_grad, down_weight)
    pre_grad = pull_gelu(hidden_grad)[0].astype(jnp.bfloat16)
    grad_up = product_lead(normed_two_low, pre_grad)
    grad_up_shift = jnp.sum(pre_grad.astype(jnp.float32), axis=0)
    norm_two_grad = product_trail(pre_grad, up_weight)
    residual_part, grad_gain_two, grad_shift_two = pull_two(norm_two_grad)
    residual_grad = out_grad + residual_part
    residual_low = residual_grad.astype(jnp.bfloat16)
    grad_out_weight = product_lead(mixed_low, residual_low)
    grad_out_shift = jnp.sum(residual_low.astype(jnp.float32), axis=0)
    mixed_grad = product_trail(residual_low, out_weight).astype(jnp.bfloat16)
    query_parts = []
    key_parts = []
    value_parts = []
    centres = []
    for head_index in range(HEADS):
        columns = slice(head_index * HEAD_DIM, (head_index + 1) * HEAD_DIM)
        softmax_out = jnp.exp(head_scores(head_index) - log_totals[head_index])
        mixed_part = mixed_grad[:, columns]
        prob_grad = product_trail(mixed_part, values_all[:, columns])
        centre = jnp.sum(softmax_out * prob_grad, axis=1, keepdims=True)
        centres.append(centre)
        score_grad = (softmax_out * (prob_grad - centre) * score_scale).astype(jnp.bfloat16)
        query_parts.append(product(score_grad, keys_all[:, columns]))
        key_parts.append(product_lead(score_grad, queries[:, columns]))
        value_parts.append(product_lead(softmax_out.astype(jnp.bfloat16), mixed_part))
    key_terms = jnp.concatenate(key_parts, axis=1)
    value_terms = jnp.concatenate(value_parts, axis=1)
    key_grad, value_grad = (
        lax.psum_scatter(key_terms, "stream", scatter_dimension=0, tiled=True),
        lax.psum_scatter(value_terms, "stream", scatter_dimension=0, tiled=True),
    )
    qkv_grad = jnp.concatenate(
        [
            jnp.concatenate(query_parts, axis=1).astype(jnp.bfloat16),
            key_grad.astype(jnp.bfloat16),
            value_grad.astype(jnp.bfloat16),
        ],
        axis=1,
    )
    grad_qkv = product_lead(normed_low, qkv_grad)
    grad_query_shift = jnp.sum(qkv_grad[:, :model_width].astype(jnp.float32), axis=0)
    grad_value_shift = jnp.sum(qkv_grad[:, 2 * model_width :].astype(jnp.float32), axis=0)
    norm_one_grad = product_trail(qkv_grad, qkv_weight)
    token_part, grad_gain_one, grad_shift_one = pull_one(norm_one_grad)
    token_grad = (residual_grad + token_part).astype(jnp.bfloat16)
    factor = lax.rsqrt(totals)
    pick = (jnp.arange(2, dtype=jnp.int32) == expert_pick).astype(jnp.float32)[:, None] * factor[:, None]

    def dealt(vector):
        return vector.reshape(devices, -1)

    thin_grad = jnp.concatenate(
        [dealt(v) for v in (grad_gain_one, grad_shift_one, grad_query_shift, grad_value_shift)]
        + [dealt(v) for v in (grad_out_shift, grad_gain_two, grad_shift_two)]
        + [(pick * grad_up_shift[None]).reshape(2, devices, ff_share).transpose(1, 0, 2).reshape(devices, -1)]
        + [(pick * grad_down_shift[None]).reshape(2, devices, share).transpose(1, 0, 2).reshape(devices, -1)],
        axis=1,
    )
    thin_grad = jnp.pad(thin_grad, ((0, 0), (0, 1024 - thin_grad.shape[1])))
    if near:
        box = (depth, 2, 2, 2)
        low = jnp.bfloat16
        up_sum, down_sum, out_sum, qkv_sum, thin_sum = scatter_all(
            [
                grad_up.astype(low).reshape(box + (share, ff)),
                grad_down.astype(low).reshape(box + (ff_share, model_width)),
                grad_out_weight.astype(low).reshape(box + (share, model_width)),
                grad_qkv.astype(low).reshape(box + (share, 3 * model_width)),
                thin_grad.reshape(box + (8, 128)),
            ],
            jnp.broadcast_to(jnp.repeat(factor, 128)[None], (8, 256)),
            (True, True, False, False, False),
            scatter_chunks(share, model_width, ff_share, ff),
            depth,
            2,
        )
        out_sum, qkv_sum = out_sum[0], qkv_sum[0]
    else:
        both = ("items", "stream")
        scatter = functools.partial(
            lax.psum_scatter, axis_name=both, scatter_dimension=0, tiled=True
        )
        wide = functools.partial(lax.psum_scatter, axis_name=both, scatter_dimension=1, tiled=True)
        up_sum = wide(pick[:, :, None] * grad_up[None])
        down_sum = wide(pick[:, :, None] * grad_down[None])
        out_sum, qkv_sum, thin_sum = scatter(grad_out_weight), scatter(grad_qkv), scatter(thin_grad)
    thin_sum = thin_sum.reshape(-1)
    seven = [thin_sum[k * share : (k + 1) * share] for k in range(7)]
    cut = 7 * share
    up_shift_sum = thin_sum[cut : cut + 2 * ff_share].reshape(2, ff_share)
    cut = cut + 2 * ff_share
    down_shift_sum = thin_sum[cut : cut + 2 * share].reshape(2, share)
    return (
        output,
        token_grad,
        seven[0],
        seven[1],
        qkv_sum,
        seven[2],
        seven[3],
        out_sum,
        seven[4],
        seven[5],
        seven[6],
        up_sum,
        up_shift_sum,
        down_sum,
        down_shift_sum,
        totals,
    )


def solution(mesh):
    placed = (
        P(("items", "stream"), None),
        P("items"),
        P(("items", "stream")),
        P(("items", "stream")),
        P(("items", "stream"), None),
        P(("items", "stream")),
        P(("items", "stream")),
        P(("items", "stream"), None),
        P(("items", "stream")),
        P(("items", "stream")),
        P(("items", "stream")),
        P(None, ("items", "stream"), None),
        P(None, ("items", "stream")),
        P(None, ("items", "stream"), None),
        P(None, ("items", "stream")),
        P(("items", "stream"), None),
    )
    near = mesh.shape["items"] == 8 and mesh.shape["stream"] == 4
    return jax.shard_map(
        functools.partial(body, near),
        mesh=mesh,
        in_specs=placed,
        out_specs=(
            P(("items", "stream"), None),
            P(("items", "stream"), None),
            P(("items", "stream")),
            P(("items", "stream")),
            P(("items", "stream"), None),
            P(("items", "stream")),
            P(("items", "stream")),
            P(("items", "stream"), None),
            P(("items", "stream")),
            P(("items", "stream")),
            P(("items", "stream")),
            P(None, ("items", "stream"), None),
            P(None, ("items", "stream")),
            P(None, ("items", "stream"), None),
            P(None, ("items", "stream")),
            P(),
        ),
        check_vma=False,
    )
```

```python
import functools

import jax
import jax.numpy as jnp
from jax import lax
from jax.experimental import pallas as pl
from jax.experimental.pallas import tpu as pltpu
from jax.sharding import PartitionSpec as P

HEADS = 12
HEAD_DIM = 64
PATCH_S = 197
PATCH_L = 577
TEXT_LEN = 40
ITEMS_S = 7
ITEMS_L = 2


NORM_EPS = 1e-05
MASKED = -1000000000.0
KV_HOOKS = ((0, 3), (4, 3))
SCATTER_HOOKS = ((0, 0), (3, 0))


def layer_norm(values, gain_row, shift_row):
    row_mean = jnp.mean(values, axis=-1, keepdims=True)
    centred = values - row_mean
    variance = jnp.mean(centred * centred, axis=-1, keepdims=True)
    return centred * lax.rsqrt(variance + NORM_EPS) * gain_row + shift_row


def gelu_exact(values):
    return jax.nn.gelu(values, approximate=False)


def layout(group_type, positions, row_count):
    patch_len = jnp.where(group_type == 0, PATCH_S, PATCH_L).astype(jnp.int32)
    members = jnp.where(group_type == 0, ITEMS_S, ITEMS_L).astype(jnp.int32)
    is_patch = positions < 3 * row_count
    patch_item = positions // patch_len
    text_item = jnp.maximum(positions - 3 * row_count, 0) // TEXT_LEN
    member = jnp.where(is_patch, patch_item, text_item)
    member = jnp.where(member < members, member, -1)
    modality = jnp.where(member < 0, 2, jnp.where(is_patch, 0, 1)).astype(jnp.int32)
    return (member, modality)


def product(first_op, second_op):
    return jnp.dot(first_op, second_op, preferred_element_type=jnp.float32)


def product_lead(first_op, second_op):
    return lax.dot_general(
        first_op, second_op, (((0,), (0,)), ((), ())), preferred_element_type=jnp.float32
    )


def product_trail(first_op, second_op):
    return lax.dot_general(
        first_op, second_op, (((1,), (1,)), ((), ())), preferred_element_type=jnp.float32
    )


def halves(length):
    return ((0, length // 2), (length // 2, length // 2))


def gather_chunks(share, width, ff_share, ff):
    rows = (0, share)
    chunks = [
        [((0, None), (0, THIN_ROWS), (0, 128), 0, False)]
        + [((1, None), rows, cols, order, False) for order, cols in enumerate(halves(3 * width))],
        [((2, None), rows, cols, order, False) for order, cols in enumerate(halves(width))],
    ]
    for e in range(2):
        chunks.append([((3, e), rows, cols, o, e == 1) for o, cols in enumerate(halves(ff))])
        chunks.append(
            [((4, e), band, (0, width), o, e == 1) for o, band in enumerate(halves(ff_share))]
        )
    return chunks


def scatter_chunks(share, width, ff_share, ff):
    rows = (0, share)
    chunks = [[(2, 0, rows, cols, order) for order, cols in enumerate(halves(width))]]
    for e in range(2):
        chunks.append([(0, e, rows, cols, order) for order, cols in enumerate(halves(ff))])
        chunks.append(
            [(1, e, band, (0, width), order) for order, band in enumerate(halves(ff_share))]
        )
    chunks.append([])
    chunks.append(
        [(3, 0, rows, cols, order) for order, cols in enumerate(halves(3 * width))]
        + [(4, 0, (0, THIN_ROWS), (0, 128), 0)]
    )
    return chunks


MESH = pl.DeviceIdType.MESH
GATHER_ORDERS = (("z", "x", "y"), ("z", "y", "x"), ("y", "x", "z"))
SCATTER_ORDERS = (("y", "x"), ("x", "y"))
EVERY = slice(None)
THIN_ROWS = 16


def coords():
    items, stream = lax.axis_index("items"), lax.axis_index("stream")
    return dict(z=items // 2, x=items % 2, y=stream // 2, c=stream % 2)


def place(at):
    return (at["z"] * 2 + at["x"], at["y"] * 2 + at["c"])


def moved(at, dim, by, depth):
    return {**at, dim: lax.rem(at[dim] + by, depth if dim == "z" else 2)}


def greet(at, depth):
    peers = [moved(at, "z", k, depth) for k in range(1, depth)]
    peers += [moved(at, d, 1, depth) for d in "xyc"]
    barrier = pltpu.get_barrier_semaphore()
    for peer in peers:
        pl.semaphore_signal(barrier, inc=1, device_id=place(peer), device_id_type=MESH)
    pl.semaphore_wait(barrier, len(peers))


def guard(cond, act):
    if cond is None:
        act()
    else:
        pl.when(cond)(act)


def remote(src, dst, sems, index, device):
    return pltpu.make_async_remote_copy(
        src_ref=src,
        dst_ref=dst,
        send_sem=sems[0].at[index],
        recv_sem=sems[1].at[index],
        device_id=place(device),
        device_id_type=MESH,
    )


def pipelined(chunks, n_steps, ahead, start, wait, hooks):
    count = len(chunks)
    for j in range(min(ahead, count)):
        start(chunks[j], 0)
    for t in range(count + n_steps - 1):
        if t + ahead < count:
            start(chunks[t + ahead], 0)
        for step in range(n_steps - 1, -1, -1):
            j = t - step
            if 0 <= j < count:
                wait(chunks[j], step)
                if step < n_steps - 1:
                    start(chunks[j], step + 1)
                if (j, step) in hooks:
                    hooks[(j, step)]()


def spots_of(depth):
    return [(a, b, c, d) for a in range(depth) for b in range(2) for c in range(2) for d in range(2)]


def columns_over(share, width):
    column = lax.broadcasted_iota(jnp.int32, (1, width), 1).astype(jnp.float32)
    owner = jnp.floor((column + 0.5) * (1.0 / share))
    return owner, column - owner * share


def spread(thin, share, width):
    owner, lane = columns_over(share, width)
    picks = lax.broadcasted_iota(jnp.int32, (128, width), 0).astype(jnp.float32) == lane
    wide = jnp.dot(thin, picks.astype(jnp.bfloat16), preferred_element_type=jnp.float32)
    total = jnp.zeros((THIN_ROWS, width), jnp.float32)
    for device in range(thin.shape[0] // THIN_ROWS):
        part = wide[device * THIN_ROWS : (device + 1) * THIN_ROWS]
        total = total + jnp.where(owner == device, part, 0.0)
    return total


def dealt(rows, share, devices):
    width = rows.shape[1]
    owner, lane = columns_over(share, width)
    picks = lax.broadcasted_iota(jnp.int32, (128, width), 0).astype(jnp.float32) == lane
    tall = jnp.concatenate(
        [jnp.where(owner == device, rows, 0.0) for device in range(devices)], axis=0
    )
    return lax.dot_general(
        tall,
        picks.astype(jnp.float32),
        (((1,), (1,)), ((), ())),
        precision=lax.Precision.HIGHEST,
        preferred_element_type=jnp.float32,
    )


def gather_kernel(depth, chunks, entries, kv_hooks, *refs):
    n_in = 5
    ins, tokens = refs[:n_in], refs[n_in]
    thin_out, out_all, up_all, down_all, qkv_weight, normed, queries, vectors, kv = refs[n_in + 1 : n_in + 10]
    thin_all, qkv_all, kv_own = refs[n_in + 10 : n_in + 13]
    local_sem, *sems = refs[n_in + 13 : n_in + 16]
    kv_sems = refs[n_in + 16 : n_in + 18]
    keep_sem = refs[n_in + 18]
    outs = (thin_all, qkv_all, out_all, up_all, down_all)
    rows, width = tokens.shape
    devices = depth * 8
    share = width // devices
    at = coords()
    mine = (at["z"], at["x"], at["y"], at["c"])
    slot = at["y"] * 2 + at["c"]

    def source(entry):
        k, e = entry
        return ins[k] if e is None else ins[k].at[e]

    def target(entry):
        k, e = entry
        return outs[k] if e is None else outs[k].at[e]

    local = [
        pltpu.make_async_copy(source(entry), target(entry).at[mine], local_sem.at[j])
        for j, entry in enumerate(entries)
    ]
    for copy in local:
        copy.start()
    greet(at, depth)
    for copy in local:
        copy.wait()
    lower, upper = at["y"] == 0, at["y"] == 1
    number = {piece: j for j, piece in enumerate(piece for chunk in chunks for piece in chunk)}

    def stage(piece, step):
        entry, band, cols, order, text = piece
        dims = GATHER_ORDERS[order] + ("c",)
        dim = dims[step]
        held = tuple(EVERY if d in dims[:step] else pl.ds(at[d], 1) for d in "zxyc")
        view = target(entry).at[held + (pl.ds(*band), pl.ds(*cols))]
        sends = recvs = None
        if text and dim == "y":
            sends, recvs = lower, upper
        elif text and "y" in dims[:step]:
            sends = recvs = upper
        found = []
        for k in range(1, depth if dim == "z" else 2):
            sem = {"z": k - 1, "x": depth - 1, "y": depth, "c": depth + 1}[dim]
            found.append(remote(view, view, sems, (number[piece], sem), moved(at, dim, k, depth)))
        return found, sends, recvs

    def each(chunk, step, which, call):
        for piece in chunk:
            found = stage(piece, step)

            def act(copies=found[0]):
                for copy in copies:
                    call(copy)

            guard(found[which], act)

    beside, across = moved(at, "c", 1, depth), moved(at, "y", 1, depth)
    other = across["y"] * 2 + across["c"]
    to_across = remote(kv_own, kv.at[slot], kv_sems, 0, across)
    to_beside = remote(kv_own, kv.at[slot], kv_sems, 1, beside)
    onward = remote(kv.at[other], kv.at[other], kv_sems, 2, beside)
    keep = [
        pltpu.make_async_copy(kv_own, kv.at[slot], keep_sem.at[0]),
        pltpu.make_async_copy(thin_all, thin_out, keep_sem.at[1]),
    ]

    def project():
        spots = spots_of(depth)
        for j, spot in enumerate(spots):
            qkv_weight[j * share : (j + 1) * share, :] = qkv_all[spot]
        thin = jnp.concatenate([thin_all[spot] for spot in spots], axis=0)
        vectors[...] = spread(thin, share, width)

        @pl.loop(0, rows // 128)
        def _(j):
            block = pl.ds(pl.multiple_of(j * 128, 128), 128)
            value = tokens[block, :].astype(jnp.float32)
            centred = value - jnp.mean(value, axis=-1, keepdims=True)
            scale = lax.rsqrt(jnp.mean(centred * centred, axis=-1, keepdims=True) + NORM_EPS)
            normed[block, :] = (centred * scale * vectors[0:1, :] + vectors[1:2, :]).astype(
                jnp.bfloat16
            )

        step = width // 2
        for part in range(3):

            @pl.loop(0, 2)
            def _(j, part=part):
                cols = pl.ds(pl.multiple_of(j * step, 128), step)
                value = jnp.dot(
                    normed[...],
                    qkv_weight[:, pl.ds(pl.multiple_of(part * width + j * step, 128), step)],
                    preferred_element_type=jnp.float32,
                )
                if part == 0:
                    queries[:, cols] = (value + vectors[2:3, cols]).astype(jnp.bfloat16)
                elif part == 1:
                    kv_own[:, cols] = value.astype(jnp.bfloat16)
                else:
                    kv_own[:, pl.ds(pl.multiple_of(width + j * step, 128), step)] = (
                        value + vectors[3:4, cols]
                    ).astype(jnp.bfloat16)

        to_across.start()
        to_beside.start()
        for copy in keep:
            copy.start()

    def pass_on():
        to_across.wait_recv()
        onward.start()

    pipelined(
        chunks,
        4,
        2,
        lambda chunk, step: each(chunk, step, 1, lambda copy: copy.start()),
        lambda chunk, step: each(chunk, step, 2, lambda copy: copy.wait_recv()),
        {kv_hooks[0]: project, kv_hooks[1]: pass_on},
    )
    to_beside.wait_recv()
    onward.wait_recv()
    for copy in (to_across, to_beside, onward):
        copy.wait_send()
    for copy in keep:
        copy.wait()
    for chunk in chunks:
        for step in range(4):
            each(chunk, step, 1, lambda copy: copy.wait_send())


def gather_all(thin, w_qkv, w_out, w_up, w_down, tokens, depth):
    rows, width = tokens.shape
    share, ff_share, ff = w_qkv.shape[0], w_down.shape[1], w_up.shape[2]
    entries = [(0, None), (1, None), (2, None), (3, 0), (3, 1), (4, 0), (4, 1)]
    chunks = gather_chunks(share, width, ff_share, ff)
    n_pieces = sum(len(chunk) for chunk in chunks)
    anywhere = pl.BlockSpec(memory_space=pl.ANY)
    inside = pl.BlockSpec(memory_space=pltpu.VMEM)
    low = jnp.bfloat16
    box = (depth, 2, 2, 2)
    return pl.pallas_call(
        functools.partial(gather_kernel, depth, chunks, entries, KV_HOOKS),
        out_shape=[
            jax.ShapeDtypeStruct(box + thin.shape, low),
            jax.ShapeDtypeStruct(box + (share, width), low),
            jax.ShapeDtypeStruct((2,) + box + (share, ff), low),
            jax.ShapeDtypeStruct((2,) + box + (ff_share, width), low),
            jax.ShapeDtypeStruct((width, 3 * width), low),
            jax.ShapeDtypeStruct((rows, width), low),
            jax.ShapeDtypeStruct((rows, width), low),
            jax.ShapeDtypeStruct((THIN_ROWS, width), jnp.float32),
            jax.ShapeDtypeStruct((4, rows, 2 * width), low),
        ],
        in_specs=[anywhere] * 5 + [inside],
        out_specs=[anywhere] * 4 + [inside] * 4 + [anywhere],
        scratch_shapes=[
            pltpu.VMEM(box + thin.shape, low),
            pltpu.VMEM(box + (share, 3 * width), low),
            pltpu.VMEM((rows, 2 * width), low),
            pltpu.SemaphoreType.DMA((len(entries),)),
            pltpu.SemaphoreType.DMA((n_pieces, depth + 2)),
            pltpu.SemaphoreType.DMA((n_pieces, depth + 2)),
            pltpu.SemaphoreType.DMA((3,)),
            pltpu.SemaphoreType.DMA((3,)),
            pltpu.SemaphoreType.DMA((2,)),
        ],
        compiler_params=pltpu.CompilerParams(
            collective_id=1, has_side_effects=True, vmem_limit_bytes=40 << 20
        ),
    )(thin, w_qkv, w_out, w_up, w_down, tokens)


def scatter_kernel(depth, kinds, chunks, hook_at, n_thin, *refs):
    n = len(kinds)
    n_far = 3
    it = iter(refs)
    take = lambda count: [next(it) for _ in range(count)]
    far = take(n_far)
    factor, thin_in, dq, dkv, normed, weight, tokens, residual_grad, vectors = take(9)
    outs = take(n)
    (token_grad,) = take(1)
    acc, first, second, last = take(n), take(n), take(n), take(n)
    own_half = take(n_far)
    qkv_terms, thin_terms, kv_sum, kv_got, kv_mine, qkv_grad, flipped = take(7)
    sems = take(2)
    local_sem = next(it)
    kv_sems = take(2)
    rows, width = tokens.shape
    devices = depth * 8
    share = width // devices
    at = coords()
    z, x, y, c = (at[d] for d in "zxyc")
    ins = far + [qkv_terms, thin_terms]
    halves_in = [
        pltpu.make_async_copy(far[k].at[EVERY, EVERY, EVERY, c], own_half[k], local_sem.at[k])
        for k in range(n_far)
    ] + [
        pltpu.make_async_copy(dkv.at[EVERY, c], kv_mine, local_sem.at[n_far]),
    ]
    for copy in halves_in:
        copy.start()
    greet(at, depth)
    beside, across = moved(at, "c", 1, depth), moved(at, "y", 1, depth)
    kv_beside = remote(dkv.at[EVERY, 1 - c], kv_sum, kv_sems, 0, beside)
    kv_across = remote(kv_sum.at[1 - y], kv_got, kv_sems, 1, across)
    kv_beside.start()
    lower, upper = y == 0, y == 1
    text_device = jnp.logical_and(upper, c == 1)
    image_device = jnp.logical_or(lower, c == 0)
    beside_text = jnp.logical_and(upper, c == 0)
    beside_image = jnp.logical_or(lower, c == 1)
    number = {piece: j for j, piece in enumerate(piece for chunk in chunks for piece in chunk)}

    def copies_of(piece, step):
        k, e, band, cols, order = piece
        box = (pl.ds(*band), pl.ds(*cols))
        image, text = kinds[k] and e == 0, kinds[k] and e == 1
        dim = (("c",) + SCATTER_ORDERS[order] + ("z",))[step]
        here = acc[k].at[e]

        def make(src, dst, sem, by=1):
            return remote(src, dst, sems, (number[piece], sem), moved(at, dim, by, depth))

        sends = recvs = None
        if dim == "c":
            if image:
                sends, recvs = image_device, beside_image
            elif text:
                sends, recvs = text_device, beside_text
            src = ins[k].at[(EVERY, EVERY, EVERY, 1 - c) + box]
            return [(make(src, here.at[(EVERY, EVERY, EVERY) + box], 0), sends, recvs)]
        if dim == "z":
            found = []
            for by in range(1, depth):
                src = here.at[(lax.rem(z + by, depth), x, y) + box]
                found.append((make(src, last[k].at[(e, by - 1) + box], 2 + by, by), None, None))
            return found
        if text and dim == "y":
            sends, recvs = upper, lower
        elif text and step == 1:
            sends = recvs = upper
        if step == 1:
            spot = (EVERY, EVERY, 1 - y) if dim == "y" else (EVERY, 1 - x, EVERY)
            dst = first[k].at[(e, EVERY, EVERY) + box]
        else:
            spot = (EVERY, x, 1 - y) if dim == "y" else (EVERY, 1 - x, y)
            dst = second[k].at[(e, EVERY) + box]
        return [(make(here.at[spot + box], dst, step), sends, recvs)]

    def combine(piece, step):
        k, e, band, cols, order = piece
        box = (pl.ds(*band), pl.ds(*cols))
        image, text = kinds[k] and e == 0, kinds[k] and e == 1
        here = acc[k].at[e]

        def over(spots, value_of, keep):
            @pl.loop(0, depth)
            def _(level):
                for index, spot in enumerate(spots):
                    where = (level,) + spot + box
                    value = value_of(level, index, spot)
                    here[where] = value if keep else here[where] + value

        if step == 0:
            spots = [(0, 0), (0, 1), (1, 0), (1, 1)]

            def own(level, index, spot):
                if k < n_far:
                    return own_half[k][(level,) + spot + box]
                return ins[k][(level,) + spot + (c,) + box]

            if image:
                pl.when(lower)(lambda: over(spots, own, False))
                pl.when(beside_text)(lambda: over(spots, own, True))
            elif text:
                pl.when(text_device)(lambda: over(spots, own, True))
            else:
                over(spots, own, False)
        elif step == 1:
            dim = SCATTER_ORDERS[order][0]
            spots = [(0, y), (1, y)] if dim == "y" else [(x, 0), (x, 1)]
            got = lambda level, index, spot: first[k][(e, level, index) + box]
            if text and dim == "y":
                pl.when(lower)(lambda: over(spots, got, True))
            elif text:
                pl.when(upper)(lambda: over(spots, got, False))
            else:
                over(spots, got, False)
        elif step == 2:
            dim = SCATTER_ORDERS[order][1]
            got = lambda level, index, spot: second[k][(e, level) + box]
            if text and dim == "y":
                pl.when(lower)(lambda: over([(x, y)], got, True))
            else:
                over([(x, y)], got, False)
        else:
            total = here[(z, x, y) + box].astype(jnp.float32)
            for by in range(depth - 1):
                total = total + last[k][(e, by) + box].astype(jnp.float32)
            if kinds[k]:
                total = total * factor[0:1, e * 128 : e * 128 + 1]
            outs[k][(e,) + box] = total

    def start(chunk, step):
        for piece in chunk:
            for copy, sends, _ in copies_of(piece, step):
                guard(sends, copy.start)

    def wait(chunk, step):
        for piece in chunk:
            for copy, _, recvs in copies_of(piece, step):
                guard(recvs, copy.wait_recv)
            combine(piece, step)

    def halve():
        kv_beside.wait_recv()

        @pl.loop(0, rows // 64)
        def _(j):
            block = pl.ds(pl.multiple_of(j * 64, 64), 64)
            for level in range(2):
                kv_sum[level, block, :] = kv_sum[level, block, :] + kv_mine[level, block, :]

        kv_across.start()

    def project_back():
        kv_across.wait_recv()
        sums = [jnp.zeros((8, width), jnp.float32) for _ in range(4)]
        qkv_grad[:, :width] = dq[...]
        thin_terms[...] = thin_in[...]

        def fold(value):
            return jnp.sum(value.reshape(-1, 8, width), axis=0)

        def join(j, carry):
            block = pl.ds(pl.multiple_of(j * 64, 64), 64)
            total = (
                kv_sum[y, block, :].astype(jnp.float32) + kv_got[block, :].astype(jnp.float32)
            ).astype(jnp.bfloat16)
            qkv_grad[block, width:] = total
            return (
                carry[0] + fold(dq[block, :].astype(jnp.float32)),
                carry[1] + fold(total[:, width:].astype(jnp.float32)),
            )

        sums[2], sums[3] = lax.fori_loop(0, rows // 64, join, (sums[2], sums[3]))
        flipped[...] = normed[...].T
        step = width // 2
        spots = spots_of(depth)

        @pl.loop(0, 6)
        def _(j):
            cols = pl.ds(pl.multiple_of(j * step, 128), step)
            value = jnp.dot(
                flipped[...], qkv_grad[:, cols], preferred_element_type=jnp.float32
            ).astype(jnp.bfloat16)
            for index, spot in enumerate(spots):
                qkv_terms[spot + (EVERY, cols)] = value[index * share : (index + 1) * share]

        def back(j, carry):
            block = pl.ds(pl.multiple_of(j * 128, 128), 128)
            value = tokens[block, :].astype(jnp.float32)
            centred = value - jnp.mean(value, axis=-1, keepdims=True)
            scale = lax.rsqrt(jnp.mean(centred * centred, axis=-1, keepdims=True) + NORM_EPS)
            unit = centred * scale
            grad = product_trail(qkv_grad[block, :], weight[...])
            lifted = grad * vectors[0:1, :]
            inner = jnp.mean(lifted * unit, axis=-1, keepdims=True)
            part = scale * (lifted - jnp.mean(lifted, axis=-1, keepdims=True) - unit * inner)
            token_grad[block, :] = (residual_grad[block, :] + part).astype(jnp.bfloat16)
            return carry[0] + fold(grad * unit), carry[1] + fold(grad)

        sums[0], sums[1] = lax.fori_loop(0, rows // 128, back, (sums[0], sums[1]))
        lines = [jnp.sum(value, axis=0, keepdims=True) for value in sums]
        stacked = jnp.concatenate(lines + [jnp.zeros((4, width), jnp.float32)], axis=0)
        flat = dealt(stacked, share, devices)
        for index, spot in enumerate(spots):
            thin_terms[spot + (slice(0, 8),)] += flat[index * 8 : (index + 1) * 8]

    for copy in halves_in:
        copy.wait()
    pipelined(chunks, 4, 2, start, wait, {hook_at[0]: halve, hook_at[1]: project_back})
    for copy in (kv_beside, kv_across):
        copy.wait_send()
    for chunk in chunks:
        for step in range(4):
            for piece in chunk:
                for copy, sends, _ in copies_of(piece, step):
                    guard(sends, copy.wait_send)


def scatter_all(up, down, out, factor, thin, dq, dkv, normed, weight, tokens, residual_grad, vectors, depth):
    rows, width = tokens.shape
    far = [up, down, out]
    kinds = (True, True, False, False, False)
    share, ff_share, ff = up.shape[4], down.shape[4], up.shape[5]
    chunks = scatter_chunks(share, width, ff_share, ff)
    n_pieces = sum(len(chunk) for chunk in chunks)
    anywhere, inside = pl.BlockSpec(memory_space=pl.ANY), pl.BlockSpec(memory_space=pltpu.VMEM)
    low, box = jnp.bfloat16, (depth, 2, 2, 2)
    tails = [a.shape[4:] for a in far] + [(share, 3 * width), thin.shape[4:]]
    dtypes = [low] * 4 + [jnp.float32]
    shapes = [((2 if kind else 1,), tail, dtype) for kind, tail, dtype in zip(kinds, tails, dtypes)]
    scratch = []
    for middle in ((depth, 2, 2), (depth, 2), (depth,), (depth - 1,)):
        scratch += [pltpu.VMEM(head + middle + tail, dtype) for head, tail, dtype in shapes]
    scratch += [pltpu.VMEM((depth, 2, 2) + a.shape[4:], low) for a in far]
    scratch += [
        pltpu.VMEM(box + (share, 3 * width), low),
        pltpu.VMEM(thin.shape, jnp.float32),
        pltpu.VMEM((2, rows, 2 * width), low),
        pltpu.VMEM((rows, 2 * width), low),
        pltpu.VMEM((2, rows, 2 * width), low),
        pltpu.VMEM((rows, 3 * width), low),
        pltpu.VMEM((width, rows), low),
        pltpu.SemaphoreType.DMA((n_pieces, depth + 2)),
        pltpu.SemaphoreType.DMA((n_pieces, depth + 2)),
        pltpu.SemaphoreType.DMA((4,)),
        pltpu.SemaphoreType.DMA((2,)),
        pltpu.SemaphoreType.DMA((2,)),
    ]
    return pl.pallas_call(
        functools.partial(scatter_kernel, depth, kinds, chunks, SCATTER_HOOKS, thin.shape[4]),
        out_shape=[jax.ShapeDtypeStruct(head + tail, jnp.float32) for head, tail, _ in shapes]
        + [jax.ShapeDtypeStruct((rows, width), low)],
        in_specs=[anywhere] * 3 + [inside] * 3 + [anywhere] + [inside] * 5,
        out_specs=[inside] * 6,
        scratch_shapes=scratch,
        compiler_params=pltpu.CompilerParams(
            collective_id=2, has_side_effects=True, vmem_limit_bytes=63 << 20
        ),
    )(up, down, out, factor, thin, dq, dkv.reshape(2, 2, rows, 2 * width), normed, weight, tokens, residual_grad, vectors)


TQ, TK = 256, 128
BATCH, BATCH_BACK = 12, 12
PAIR = 2 * HEAD_DIM


def trail(first_op, second_op):
    return lax.dot_general(
        first_op, second_op, (((1,), (1,)), ((), ())), preferred_element_type=jnp.float32
    )


def span(kind, start, length, image_rows):
    patch_len = jnp.where(kind == 0, PATCH_S, PATCH_L)
    members = jnp.where(kind == 0, ITEMS_S, ITEMS_L)
    image = start < image_rows
    unit = jnp.where(image, patch_len, TEXT_LEN)
    begin = jnp.where(image, start, start - image_rows)
    return lax.div(begin, unit), lax.div(begin + length - 1, unit), members


def meets(kind, first, second, image_rows):
    low_a, high_a, members = span(kind, *first, image_rows)
    low_b, high_b, _ = span(kind, *second, image_rows)
    low = jnp.maximum(low_a, low_b)
    high = jnp.minimum(jnp.minimum(high_a, high_b), members - 1)
    return low <= high, jnp.logical_and(high_a >= members, high_b >= members)


def half_of(pair, which):
    lanes = lax.broadcasted_iota(jnp.int32, pair.shape, 1)
    return jnp.where((lanes < HEAD_DIM) == (which == 0), pair, jnp.zeros_like(pair))


def upper_of(pair, which):
    keep = pair[which * HEAD_DIM : (which + 1) * HEAD_DIM]
    parts = [keep, jnp.zeros_like(keep)]
    return jnp.concatenate(parts if which == 0 else parts[::-1], axis=0)


def attend_kernel(meta, q_ref, kv_ref, kmem_ref, qmem_ref, mixed_ref, ot_ref, lse_ref, vt, qs, top, total):
    kind, stream = meta[0], meta[1]
    rows, width = q_ref.shape
    heads = width // HEAD_DIM
    everyone = kv_ref.shape[0]
    image_rows = everyone - rows
    for pair in range(heads // 2):
        columns = slice(pair * PAIR, (pair + 1) * PAIR)
        value = (q_ref[:, columns] * jnp.bfloat16(HEAD_DIM ** (-0.5))).T
        for which in range(2):
            qs[2 * pair + which] = upper_of(value, which)

    @pl.loop(0, everyone // TK)
    def _(kt):
        keys = pl.ds(pl.multiple_of(kt * TK, TK), TK)
        vt[:, keys] = kv_ref[keys, width:].T

    for qt in range(rows // TQ):
        here = slice(qt * TQ, (qt + 1) * TQ)
        top[...] = jnp.full(top.shape, -1e30, jnp.float32)
        total[...] = jnp.zeros(total.shape, jnp.float32)
        ot_ref[:, here] = jnp.zeros((width, TQ), jnp.float32)

        @pl.loop(0, everyone // TK)
        def _(kt):
            shared, loose = meets(
                kind, (stream * rows + qt * TQ, TQ), (kt * TK, TK), image_rows
            )

            @pl.when(jnp.logical_or(shared, loose))
            def _():
                keys = pl.ds(pl.multiple_of(kt * TK, TK), TK)
                allowed = kmem_ref[keys, :] == qmem_ref[:, here]
                for base in range(0, heads, BATCH):
                    group = range(base, base + BATCH)
                    scores, parts, fades = [], [], []
                    for head in group:
                        pair = slice(head // 2 * PAIR, (head // 2 + 1) * PAIR)
                        raw = jnp.dot(
                            kv_ref[keys, pair], qs[head, :, here], preferred_element_type=jnp.float32
                        )
                        scores.append(jnp.where(allowed, raw, MASKED))
                    for head, score in zip(group, scores):
                        line = slice(head, head + 1)
                        old = top[line]
                        new = jnp.maximum(old, jnp.max(score, axis=0, keepdims=True))
                        top[line] = new
                        fade = jnp.exp(old - new)
                        part = jnp.exp(score - new)
                        total[line] = total[line] * fade + jnp.sum(part, axis=0, keepdims=True)
                        parts.append(part.astype(jnp.bfloat16))
                        fades.append(fade)
                    for head, part, fade in zip(group, parts, fades):
                        own = slice(head * HEAD_DIM, (head + 1) * HEAD_DIM)
                        ot_ref[own, here] = ot_ref[own, here] * fade + jnp.dot(
                            vt[own, keys], part, preferred_element_type=jnp.float32
                        )

        for head in range(heads):
            own = slice(head * HEAD_DIM, (head + 1) * HEAD_DIM)
            line = slice(head, head + 1)
            ot_ref[own, here] = ot_ref[own, here] / total[line]
        lse_ref[:, here] = top[...] + jnp.log(total[...])
        mixed_ref[here, :] = ot_ref[:, here].T.astype(jnp.bfloat16)


def attend(meta, queries, kv, key_member, own_member):
    rows, width = queries.shape
    heads = width // HEAD_DIM
    inside = pl.BlockSpec(memory_space=pltpu.VMEM)
    lines = -(-heads // 8) * 8
    return pl.pallas_call(
        attend_kernel,
        out_shape=(
            jax.ShapeDtypeStruct((rows, width), jnp.bfloat16),
            jax.ShapeDtypeStruct((width, rows), jnp.float32),
            jax.ShapeDtypeStruct((lines, rows), jnp.float32),
        ),
        in_specs=[pl.BlockSpec(memory_space=pltpu.SMEM)] + [inside] * 4,
        out_specs=(inside,) * 3,
        scratch_shapes=[
            pltpu.VMEM((width, kv.shape[0]), jnp.bfloat16),
            pltpu.VMEM((heads, PAIR, rows), jnp.bfloat16),
            pltpu.VMEM((lines, TQ), jnp.float32),
            pltpu.VMEM((lines, TQ), jnp.float32),
        ],
        compiler_params=pltpu.CompilerParams(vmem_limit_bytes=56 << 20),
    )(meta, queries, kv, key_member, own_member)


def attend_back_kernel(
    meta, q_ref, kv_ref, kmem_ref, qmem_ref, mg_ref, ot_ref, lse_ref, dq_ref, dkv_ref,
    kt_ref, qs, gs, qst, gst, dqt, delta, dk, dv,
):
    kind, stream = meta[0], meta[1]
    rows, width = q_ref.shape
    heads = width // HEAD_DIM
    everyone = kv_ref.shape[0]
    image_rows = everyone - rows
    for pair in range(heads // 2):
        columns = slice(pair * PAIR, (pair + 1) * PAIR)
        value = q_ref[:, columns] * jnp.bfloat16(HEAD_DIM ** (-0.5))
        grad = mg_ref[:, columns]
        for which in range(2):
            qs[2 * pair + which] = half_of(value, which)
            gs[2 * pair + which] = half_of(grad, which)
            qst[2 * pair + which] = upper_of(value.T, which)
            gst[2 * pair + which] = upper_of(grad.T, which)
        product = ot_ref[columns, :] * grad.astype(jnp.float32).T
        for which in range(2):
            line = 2 * pair + which
            delta[line : line + 1] = jnp.sum(
                product[which * HEAD_DIM : (which + 1) * HEAD_DIM], axis=0, keepdims=True
            )

    @pl.loop(0, everyone // TK)
    def _(kt):
        keys = pl.ds(pl.multiple_of(kt * TK, TK), TK)
        kt_ref[:, keys] = kv_ref[keys, :width].T
        dk[keys, :] = jnp.zeros((TK, width), jnp.float32)
        dv[keys, :] = jnp.zeros((TK, width), jnp.float32)

    for qt in range(rows // TQ):
        here = slice(qt * TQ, (qt + 1) * TQ)
        dqt[...] = jnp.zeros(dqt.shape, jnp.float32)

        @pl.loop(0, everyone // TK)
        def _(kt):
            shared, _ = meets(kind, (stream * rows + qt * TQ, TQ), (kt * TK, TK), image_rows)

            @pl.when(shared)
            def _():
                keys = pl.ds(pl.multiple_of(kt * TK, TK), TK)
                allowed = kmem_ref[keys, :] == qmem_ref[:, here]
                for base in range(0, heads, BATCH_BACK):
                    group = range(base, base + BATCH_BACK)
                    scores, prob_grads, probs_low, score_low = [], [], [], []
                    for head in group:
                        begin = head // 2 * PAIR
                        scores.append(
                            jnp.dot(
                                kv_ref[keys, begin : begin + PAIR],
                                qst[head, :, here],
                                preferred_element_type=jnp.float32,
                            )
                        )
                        prob_grads.append(
                            jnp.dot(
                                kv_ref[keys, width + begin : width + begin + PAIR],
                                gst[head, :, here],
                                preferred_element_type=jnp.float32,
                            )
                        )
                    for head, score, prob_grad in zip(group, scores, prob_grads):
                        line = slice(head, head + 1)
                        probs = jnp.exp(jnp.where(allowed, score - lse_ref[line, here], MASKED))
                        probs_low.append(probs.astype(jnp.bfloat16))
                        score_low.append(
                            (probs * (prob_grad - delta[line, here])).astype(jnp.bfloat16)
                        )
                    for j, head in enumerate(group):
                        own = slice(head * HEAD_DIM, (head + 1) * HEAD_DIM)
                        dqt[own, :] += jnp.dot(
                            kt_ref[own, keys], score_low[j], preferred_element_type=jnp.float32
                        )
                    for j in range(0, BATCH_BACK, 2):
                        head = base + j
                        columns = slice(head * HEAD_DIM, head * HEAD_DIM + PAIR)
                        dk[keys, columns] += jnp.dot(
                            score_low[j], qs[head, here, :], preferred_element_type=jnp.float32
                        ) + jnp.dot(
                            score_low[j + 1], qs[head + 1, here, :], preferred_element_type=jnp.float32
                        )
                        dv[keys, columns] += jnp.dot(
                            probs_low[j], gs[head, here, :], preferred_element_type=jnp.float32
                        ) + jnp.dot(
                            probs_low[j + 1], gs[head + 1, here, :], preferred_element_type=jnp.float32
                        )

        dq_ref[here, :] = (dqt[...].T * HEAD_DIM ** (-0.5)).astype(jnp.bfloat16)

    @pl.loop(0, everyone // TK)
    def _(kt):
        keys = pl.ds(pl.multiple_of(kt * TK, TK), TK)
        dkv_ref[keys, :width] = dk[keys, :].astype(jnp.bfloat16)
        dkv_ref[keys, width:] = dv[keys, :].astype(jnp.bfloat16)


def attend_back(meta, queries, kv, key_member, own_member, mixed_grad, mixed_t, log_total):
    rows, width = queries.shape
    heads = width // HEAD_DIM
    inside = pl.BlockSpec(memory_space=pltpu.VMEM)
    lines = -(-heads // 8) * 8
    everyone = kv.shape[0]
    return pl.pallas_call(
        attend_back_kernel,
        out_shape=(
            jax.ShapeDtypeStruct((rows, width), jnp.bfloat16),
            jax.ShapeDtypeStruct((everyone, 2 * width), jnp.bfloat16),
        ),
        in_specs=[pl.BlockSpec(memory_space=pltpu.SMEM)] + [inside] * 7,
        out_specs=(inside,) * 2,
        scratch_shapes=[
            pltpu.VMEM((width, everyone), jnp.bfloat16),
            pltpu.VMEM((heads, rows, PAIR), jnp.bfloat16),
            pltpu.VMEM((heads, rows, PAIR), jnp.bfloat16),
            pltpu.VMEM((heads, PAIR, rows), jnp.bfloat16),
            pltpu.VMEM((heads, PAIR, rows), jnp.bfloat16),
            pltpu.VMEM((width, TQ), jnp.float32),
            pltpu.VMEM((lines, rows), jnp.float32),
            pltpu.VMEM((everyone, width), jnp.float32),
            pltpu.VMEM((everyone, width), jnp.float32),
        ],
        compiler_params=pltpu.CompilerParams(vmem_limit_bytes=58 << 20),
    )(meta, queries, kv, key_member, own_member, mixed_grad, mixed_t, log_total)


def padded(values):
    return jnp.pad(values, ((0, 0), (0, 128 - values.shape[1])))


def body(
    near,
    tokens,
    group_kind,
    ln1_gain,
    ln1_bias,
    w_qkv,
    q_bias,
    v_bias,
    w_out,
    out_bias,
    ln2_gain,
    ln2_bias,
    w_up,
    b_up,
    w_down,
    b_down,
    cotangent,
):
    row_count, model_width = tokens.shape
    stream_size = lax.axis_size("stream")
    stream_place = lax.axis_index("stream")
    devices = lax.axis_size("items") * stream_size
    group_type = group_kind[0]
    own_positions = stream_place * row_count + jnp.arange(row_count, dtype=jnp.int32)
    own_member, own_modality = layout(group_type, own_positions, row_count)
    key_member = layout(
        group_type, jnp.arange(stream_size * row_count, dtype=jnp.int32), row_count
    )[0]
    expert_pick = jnp.where(stream_place == stream_size - 1, 1, 0).astype(jnp.int32)
    share, ff_share, ff = model_width // devices, w_down.shape[1], w_up.shape[2]
    both = ("items", "stream")
    low = jnp.bfloat16
    thin = jnp.stack([ln1_gain, ln1_bias, q_bias, v_bias, out_bias, ln2_gain, ln2_bias])
    thin = jnp.concatenate(
        [padded(thin), padded(b_up), padded(b_down), padded(group_kind.astype(low)[:, None])]
    )
    thin = jnp.pad(thin, ((0, THIN_ROWS - thin.shape[0]), (0, 0)))
    tokens_f = tokens.astype(jnp.float32)
    if near:
        depth = lax.axis_size("items") // 2
        thin_all, out_weight, up_all, down_all, qkv_weight, normed_low, queries, vectors, kv = (
            gather_all(thin, w_qkv, w_out, w_up, w_down, tokens, depth)
        )
        thin_all = thin_all.reshape(devices, THIN_ROWS, 128)
        out_weight = out_weight.reshape(model_width, model_width)
        up_all = up_all.reshape(2, model_width, ff)
        down_all = down_all.reshape(2, ff, model_width)
        kv = kv.reshape(stream_size * row_count, 2 * model_width)
    else:
        thin_all = lax.all_gather(thin, both, axis=0)
        qkv_weight = lax.all_gather(w_qkv, both, axis=0, tiled=True)
        out_weight = lax.all_gather(w_out, both, axis=0, tiled=True)
        up_all = lax.all_gather(w_up, both, axis=1, tiled=True)
        down_all = lax.all_gather(w_down, both, axis=1, tiled=True)
        vectors = (
            thin_all[:, :, :share].transpose(1, 0, 2).reshape(THIN_ROWS, -1).astype(jnp.float32)
        )
        normed_low = layer_norm(tokens_f, vectors[0], vectors[1]).astype(low)
        shifts = jnp.concatenate([vectors[2], jnp.zeros_like(vectors[2]), vectors[3]])
        projected = (product(normed_low, qkv_weight) + shifts).astype(low)
        queries = projected[:, :model_width]
        kv = lax.all_gather(projected[:, model_width:], "stream", axis=0, tiled=True)
    out_shift, gain_two, shift_two = vectors[4], vectors[5], vectors[6]
    down_shift = jnp.where(expert_pick == 0, vectors[9], vectors[10])
    up_shift_all = thin_all[:, 7:9, :ff_share].transpose(1, 0, 2).reshape(2, ff)
    kinds = vectors[11, :: stream_size * share].astype(jnp.int32)
    tally = []
    for kind in range(2):
        modality = layout(
            jnp.int32(kind), jnp.arange(stream_size * row_count, dtype=jnp.int32), row_count
        )[1]
        tally.append([jnp.sum((modality == e).astype(jnp.float32)) for e in range(2)])
    totals = jnp.stack(
        [jnp.sum(jnp.where(kinds == 0, tally[0][e], tally[1][e])) for e in range(2)]
    )
    meta = jnp.stack([group_type, stream_place.astype(jnp.int32)])
    own_row = own_member[None]
    key_column = key_member[:, None]
    mixed_low, mixed_t, log_total = attend(meta, queries, kv, key_column, own_row)
    residual = tokens_f + product(mixed_low, out_weight) + out_shift
    normed_two, pull_two = jax.vjp(layer_norm, residual, gain_two, shift_two)
    normed_two_low = normed_two.astype(low)
    up_weight = lax.dynamic_index_in_dim(up_all, expert_pick, 0, keepdims=False)
    up_shift = lax.dynamic_index_in_dim(up_shift_all, expert_pick, 0, keepdims=False)
    down_weight = lax.dynamic_index_in_dim(down_all, expert_pick, 0, keepdims=False)
    hidden_pre = product(normed_two_low, up_weight) + up_shift.astype(jnp.float32)
    hidden, pull_gelu = jax.vjp(gelu_exact, hidden_pre)
    hidden_low = hidden.astype(low)
    branch = product(hidden_low, down_weight) + down_shift
    expert_mask = (own_modality == expert_pick).astype(jnp.float32)[:, None]
    output = (residual + branch * expert_mask).astype(low)
    live_rows = (own_modality < 2).astype(jnp.float32)[:, None]
    out_grad = cotangent.astype(jnp.float32) * live_rows
    branch_grad = (out_grad * expert_mask).astype(low)
    grad_down = product_lead(hidden_low, branch_grad)
    grad_down_shift = jnp.sum(branch_grad.astype(jnp.float32), axis=0)
    hidden_grad = product_trail(branch_grad, down_weight)
    pre_grad = pull_gelu(hidden_grad)[0].astype(low)
    grad_up = product_lead(normed_two_low, pre_grad)
    grad_up_shift = jnp.sum(pre_grad.astype(jnp.float32), axis=0)
    norm_two_grad = product_trail(pre_grad, up_weight)
    residual_part, grad_gain_two, grad_shift_two = pull_two(norm_two_grad)
    residual_grad = out_grad + residual_part
    residual_low = residual_grad.astype(low)
    grad_out_weight = product_lead(mixed_low, residual_low)
    grad_out_shift = jnp.sum(residual_low.astype(jnp.float32), axis=0)
    mixed_grad = product_trail(residual_low, out_weight).astype(low)
    query_grad, kv_terms = attend_back(
        meta, queries, kv, key_column, own_row, mixed_grad, mixed_t, log_total
    )
    factor = lax.rsqrt(totals)
    pick = (jnp.arange(2, dtype=jnp.int32) == expert_pick).astype(jnp.float32) * factor

    def lanes(values):
        values = values.reshape(values.shape[0], devices, -1).transpose(1, 0, 2)
        return jnp.pad(values, ((0, 0), (0, 0), (0, 128 - values.shape[2])))

    def thin_of(rows):
        thin_terms = jnp.concatenate(
            [
                lanes(jnp.stack(rows)),
                lanes(pick[:, None] * grad_up_shift[None]),
                lanes(pick[:, None] * grad_down_shift[None]),
            ],
            axis=1,
        )
        return jnp.pad(thin_terms, ((0, 0), (0, THIN_ROWS - thin_terms.shape[1]), (0, 0)))

    late = [grad_out_shift, grad_gain_two, grad_shift_two]
    if near:
        box = (depth, 2, 2, 2)
        up_sum, down_sum, out_sum, qkv_sum, thin_sum, token_grad = scatter_all(
            grad_up.astype(low).reshape(box + (share, ff)),
            grad_down.astype(low).reshape(box + (ff_share, model_width)),
            grad_out_weight.astype(low).reshape(box + (share, model_width)),
            jnp.broadcast_to(jnp.repeat(factor, 128)[None], (8, 256)),
            thin_of([jnp.zeros_like(grad_out_shift)] * 4 + late).reshape(box + (THIN_ROWS, 128)),
            query_grad,
            kv_terms,
            normed_low,
            qkv_weight,
            tokens,
            residual_grad,
            vectors,
            depth,
        )
        out_sum, qkv_sum, thin_sum = out_sum[0], qkv_sum[0], thin_sum[0]
    else:
        scatter = functools.partial(
            lax.psum_scatter, axis_name=both, scatter_dimension=0, tiled=True
        )
        wide = functools.partial(lax.psum_scatter, axis_name=both, scatter_dimension=1, tiled=True)
        kv_grad = lax.psum_scatter(
            kv_terms.astype(jnp.float32), "stream", scatter_dimension=0, tiled=True
        )
        qkv_grad = jnp.concatenate([query_grad, kv_grad.astype(low)], axis=1)
        grad_qkv = product_lead(normed_low, qkv_grad)
        early = [
            jnp.sum(qkv_grad[:, :model_width].astype(jnp.float32), axis=0),
            jnp.sum(qkv_grad[:, 2 * model_width :].astype(jnp.float32), axis=0),
        ]
        norm_one_grad = product_trail(qkv_grad, qkv_weight)
        token_part, *grads_one = jax.vjp(layer_norm, tokens_f, vectors[0], vectors[1])[1](
            norm_one_grad
        )
        token_grad = (residual_grad + token_part).astype(low)
        up_sum = wide(pick[:, None, None] * grad_up[None])
        down_sum = wide(pick[:, None, None] * grad_down[None])
        out_sum, qkv_sum = scatter(grad_out_weight), scatter(grad_qkv)
        thin_sum = scatter(thin_of(grads_one + early + late))[0]
    small = [thin_sum[k, :share] for k in range(7)]
    return (
        output,
        token_grad,
        small[0],
        small[1],
        qkv_sum,
        small[2],
        small[3],
        out_sum,
        small[4],
        small[5],
        small[6],
        up_sum,
        thin_sum[7:9, :ff_share],
        down_sum,
        thin_sum[9:11, :share],
        totals,
    )


def solution(mesh):
    placed = (
        P(("items", "stream"), None),
        P("items"),
        P(("items", "stream")),
        P(("items", "stream")),
        P(("items", "stream"), None),
        P(("items", "stream")),
        P(("items", "stream")),
        P(("items", "stream"), None),
        P(("items", "stream")),
        P(("items", "stream")),
        P(("items", "stream")),
        P(None, ("items", "stream"), None),
        P(None, ("items", "stream")),
        P(None, ("items", "stream"), None),
        P(None, ("items", "stream")),
        P(("items", "stream"), None),
    )
    near = mesh.shape["items"] == 8 and mesh.shape["stream"] == 4
    return jax.shard_map(
        functools.partial(body, near),
        mesh=mesh,
        in_specs=placed,
        out_specs=(
            P(("items", "stream"), None),
            P(("items", "stream"), None),
            P(("items", "stream")),
            P(("items", "stream")),
            P(("items", "stream"), None),
            P(("items", "stream")),
            P(("items", "stream")),
            P(("items", "stream"), None),
            P(("items", "stream")),
            P(("items", "stream")),
            P(("items", "stream")),
            P(None, ("items", "stream"), None),
            P(None, ("items", "stream")),
            P(None, ("items", "stream"), None),
            P(None, ("items", "stream")),
            P(),
        ),
        check_vma=False,
    )
```

```python
import functools

import jax
import jax.numpy as jnp
from jax import lax
from jax.experimental import pallas as pl
from jax.experimental.pallas import tpu as pltpu
from jax.sharding import PartitionSpec as P

HEADS = 12
HEAD_DIM = 64
PATCH_S = 197
PATCH_L = 577
TEXT_LEN = 40
ITEMS_S = 7
ITEMS_L = 2


NORM_EPS = 1e-05
MASKED = -1000000000.0


def layer_norm(values, gain_row, shift_row):
    row_mean = jnp.mean(values, axis=-1, keepdims=True)
    centred = values - row_mean
    variance = jnp.mean(centred * centred, axis=-1, keepdims=True)
    return centred * lax.rsqrt(variance + NORM_EPS) * gain_row + shift_row


def gelu_exact(values):
    return jax.nn.gelu(values, approximate=False)


def layout(group_type, positions, row_count):
    patch_len = jnp.where(group_type == 0, PATCH_S, PATCH_L).astype(jnp.int32)
    members = jnp.where(group_type == 0, ITEMS_S, ITEMS_L).astype(jnp.int32)
    is_patch = positions < 3 * row_count
    patch_item = positions // patch_len
    text_item = jnp.maximum(positions - 3 * row_count, 0) // TEXT_LEN
    member = jnp.where(is_patch, patch_item, text_item)
    member = jnp.where(member < members, member, -1)
    modality = jnp.where(member < 0, 2, jnp.where(is_patch, 0, 1)).astype(jnp.int32)
    return (member, modality)


def product(first_op, second_op):
    return jnp.dot(first_op, second_op, preferred_element_type=jnp.float32)


def product_lead(first_op, second_op):
    return lax.dot_general(
        first_op, second_op, (((0,), (0,)), ((), ())), preferred_element_type=jnp.float32
    )


def product_trail(first_op, second_op):
    return lax.dot_general(
        first_op, second_op, (((1,), (1,)), ((), ())), preferred_element_type=jnp.float32
    )


def halves(length):
    return ((0, length // 2), (length // 2, length // 2))


def divided(length, unit, *shares):
    found, begin = [], 0
    for share in shares:
        found.append((begin, share * unit))
        begin += share * unit
    assert begin == length
    return found


def gather_chunks(share, width, ff_share, ff):
    rows = (0, share)
    near_cols = divided(3 * width, 128, 7, 7, 4)
    out_cols = divided(width, 128, 2, 3, 1)
    up_cols = divided(ff, 128, 6, 13, 5)
    down_rows = divided(ff_share, 16, 2, 3, 1)
    chunks = [
        [((0, None), (0, THIN_ROWS), (0, 128), 0, False)]
        + [((1, None), rows, cols, order, False) for order, cols in enumerate(near_cols)],
        [((2, None), rows, cols, order, False) for order, cols in enumerate(out_cols)],
    ]
    for e in range(2):
        chunks.append([((3, e), rows, cols, order, e == 1) for order, cols in enumerate(up_cols)])
        chunks.append(
            [((4, e), band, (0, width), order, e == 1) for order, band in enumerate(down_rows)]
        )
    return chunks


def scatter_chunks(share, width, ff_share, ff):
    rows = (0, share)
    near_cols = divided(3 * width, 128, 7, 7, 4)
    out_cols = divided(width, 128, 2, 3, 1)
    up_cols = divided(ff, 128, 6, 13, 5)
    down_rows = divided(ff_share, 16, 2, 3, 1)
    chunks = [[(2, 0, rows, cols, order) for order, cols in enumerate(out_cols)]]
    for e in range(2):
        chunks.append([(0, e, rows, cols, order) for order, cols in enumerate(up_cols)])
        chunks.append(
            [(1, e, band, (0, width), order) for order, band in enumerate(down_rows)]
        )
    chunks.append([])
    chunks.append(
        [(3, 0, rows, cols, order) for order, cols in enumerate(near_cols)]
        + [(4, 0, (0, THIN_ROWS), (0, 128), 0)]
    )
    cuts = (
        (0, up_cols[2][0]),
        (down_rows[2][0], 0),
        (0, out_cols[2][0]),
        (0, near_cols[2][0]),
        (0, 0),
    )
    return chunks, cuts


TQ, TK = 256, 128
PAIR = 2 * HEAD_DIM


def trail(first_op, second_op):
    return lax.dot_general(
        first_op, second_op, (((1,), (1,)), ((), ())), preferred_element_type=jnp.float32
    )


def span(kind, start, length, image_rows):
    patch_len, members = ((PATCH_S, ITEMS_S), (PATCH_L, ITEMS_L))[kind]
    image = start < image_rows
    low = jnp.where(image, lax.div(start, patch_len), lax.div(start - image_rows, TEXT_LEN))
    high = jnp.where(
        image,
        lax.div(start + length - 1, patch_len),
        lax.div(start + length - 1 - image_rows, TEXT_LEN),
    )
    return low, high, members


def meets(first, second, image_rows, loose):
    found = False
    for kind in range(2):
        low_a, high_a, members = span(kind, *first, image_rows)
        low_b, high_b, _ = span(kind, *second, image_rows)
        low = jnp.maximum(low_a, low_b)
        high = jnp.minimum(jnp.minimum(high_a, high_b), members - 1)
        found = jnp.logical_or(found, low <= high)
        if loose:
            both = jnp.logical_and(high_a >= members, high_b >= members)
            found = jnp.logical_or(found, both)
    return found


def member_of(kind, position, image_rows):
    patch_len = PATCH_S + kind * float(PATCH_L - PATCH_S)
    members = ITEMS_S + kind * float(ITEMS_L - ITEMS_S)
    patch = jnp.floor((position + 0.5) / patch_len)
    text = jnp.floor((position - image_rows + 0.5) * (1.0 / TEXT_LEN))
    member = jnp.where(position < image_rows, patch, text)
    return jnp.where(member < members, member, -1.0)


def same_item(kind, stream, rows, qt, kt, image_rows):
    keys = lax.broadcasted_iota(jnp.int32, (TK, 1), 0) + kt * TK
    own = lax.broadcasted_iota(jnp.int32, (1, TQ), 1) + (stream * rows + qt * TQ)
    key_member = member_of(kind, keys.astype(jnp.float32), image_rows)
    return key_member == member_of(kind, own.astype(jnp.float32), image_rows)


def half_of(pair, which):
    lanes = lax.broadcasted_iota(jnp.int32, pair.shape, 1)
    return jnp.where((lanes < HEAD_DIM) == (which == 0), pair, jnp.zeros_like(pair))


def upper_of(pair, which):
    keep = pair[which * HEAD_DIM : (which + 1) * HEAD_DIM]
    parts = [keep, jnp.zeros_like(keep)]
    return jnp.concatenate(parts if which == 0 else parts[::-1], axis=0)


def scale_queries(q_ref, scaled):
    for pair in range(q_ref.shape[1] // PAIR):
        columns = slice(pair * PAIR, (pair + 1) * PAIR)
        value = (q_ref[:, columns] * jnp.bfloat16(HEAD_DIM ** (-0.5))).T
        for which in range(2):
            scaled[2 * pair + which] = upper_of(value, which)


def flip_columns(kv_ref, begin, flipped):
    width = flipped.shape[0]

    @pl.loop(0, flipped.shape[1] // TK)
    def _(kt):
        keys = pl.ds(pl.multiple_of(kt * TK, TK), TK)
        flipped[:, keys] = kv_ref[keys, begin : begin + width].T


def attend_part(qt, begin, end, kind_ref, stream, kv_ref, values_t, scaled, mixed_ref, mixed_t, log_total, top, total):
    width, everyone = values_t.shape
    rows = mixed_ref.shape[0]
    heads = width // HEAD_DIM
    image_rows = everyone - rows
    here = slice(qt * TQ, (qt + 1) * TQ)
    if begin == 0:
        top[...] = jnp.full(top.shape, -1e30, jnp.float32)
        total[...] = jnp.zeros(total.shape, jnp.float32)
        mixed_t[:, here] = jnp.zeros((width, TQ), jnp.float32)

    @pl.loop(begin, end)
    def _(kt):
        needed = meets((stream * rows + qt * TQ, TQ), (kt * TK, TK), image_rows, True)

        @pl.when(needed)
        def _():
            keys = pl.ds(pl.multiple_of(kt * TK, TK), TK)
            allowed = same_item(kind_ref[0:1, 0:1], stream, rows, qt, kt, image_rows)
            scores, parts, fades = [], [], []
            for head in range(heads):
                pair = slice(head // 2 * PAIR, (head // 2 + 1) * PAIR)
                raw = jnp.dot(
                    kv_ref[keys, pair], scaled[head, :, here], preferred_element_type=jnp.float32
                )
                scores.append(jnp.where(allowed, raw, MASKED))
            for head, score in enumerate(scores):
                line = slice(head, head + 1)
                old = top[line]
                new = jnp.maximum(old, jnp.max(score, axis=0, keepdims=True))
                top[line] = new
                fade = jnp.exp(old - new)
                part = jnp.exp(score - new)
                total[line] = total[line] * fade + jnp.sum(part, axis=0, keepdims=True)
                parts.append(part.astype(jnp.bfloat16))
                fades.append(fade)
            for head in range(heads):
                own = slice(head * HEAD_DIM, (head + 1) * HEAD_DIM)
                mixed_t[own, here] = mixed_t[own, here] * fades[head] + jnp.dot(
                    values_t[own, keys], parts[head], preferred_element_type=jnp.float32
                )

    if end == everyone // TK:
        for head in range(heads):
            own = slice(head * HEAD_DIM, (head + 1) * HEAD_DIM)
            mixed_t[own, here] = mixed_t[own, here] / total[head : head + 1]
        log_total[:, here] = top[...] + jnp.log(total[...])
        mixed_ref[here, :] = mixed_t[:, here].T.astype(jnp.bfloat16)


def attend_kernel(kind, place_ref, q_ref, kv_ref, mixed_ref, mixed_t, log_total, values_t, scaled, top, total):
    scale_queries(q_ref, scaled)
    flip_columns(kv_ref, q_ref.shape[1], values_t)
    for qt in range(q_ref.shape[0] // TQ):
        attend_part(
            qt, 0, kv_ref.shape[0] // TK, kind, place_ref[0], kv_ref, values_t, scaled, mixed_ref,
            mixed_t, log_total, top, total,
        )


def attend(kind, place_at, queries, kv):
    rows, width = queries.shape
    heads = width // HEAD_DIM
    inside = pl.BlockSpec(memory_space=pltpu.VMEM)
    lines = -(-heads // 8) * 8
    return pl.pallas_call(
        attend_kernel,
        out_shape=(
            jax.ShapeDtypeStruct((rows, width), jnp.bfloat16),
            jax.ShapeDtypeStruct((width, rows), jnp.float32),
            jax.ShapeDtypeStruct((lines, rows), jnp.float32),
        ),
        in_specs=[inside, pl.BlockSpec(memory_space=pltpu.SMEM)] + [inside] * 2,
        out_specs=(inside,) * 3,
        scratch_shapes=[
            pltpu.VMEM((width, kv.shape[0]), jnp.bfloat16),
            pltpu.VMEM((heads, PAIR, rows), jnp.bfloat16),
            pltpu.VMEM((lines, TQ), jnp.float32),
            pltpu.VMEM((lines, TQ), jnp.float32),
        ],
        compiler_params=pltpu.CompilerParams(vmem_limit_bytes=56 << 20),
    )(kind, place_at, queries, kv)


def back_group(
    group, kind, stream, log_total, keys_ref, values_ref, q_ref, g_ref, mixed_t, dq_ref,
    keys_t, scaled, grads, scaled_t, grads_t, dq_t, centre, dk, dv,
):
    everyone, width = keys_ref.shape
    rows = q_ref.shape[0]
    heads = width // HEAD_DIM
    image_rows = everyone - rows
    for pair in range(heads // 2):
        columns = slice(pair * PAIR, (pair + 1) * PAIR)
        value = q_ref[:, columns] * jnp.bfloat16(HEAD_DIM ** (-0.5))
        grad = g_ref[:, columns]
        value_t, grad_t = value.T, grad.T
        product = mixed_t[columns, :] * grad_t.astype(jnp.float32)
        for which in range(2):
            head = 2 * pair + which
            scaled[head] = half_of(value, which)
            grads[head] = half_of(grad, which)
            scaled_t[head] = upper_of(value_t, which)
            grads_t[head] = upper_of(grad_t, which)
            centre[head : head + 1] = jnp.sum(
                product[which * HEAD_DIM : (which + 1) * HEAD_DIM], axis=0, keepdims=True
            )
    flip_columns(keys_ref, 0, keys_t)

    @pl.loop(0, everyone // TK)
    def _(kt):
        keys = pl.ds(pl.multiple_of(kt * TK, TK), TK)
        dk[keys, :] = jnp.zeros((TK, width), jnp.float32)
        dv[keys, :] = jnp.zeros((TK, width), jnp.float32)

    for qt in range(rows // TQ):
        here = slice(qt * TQ, (qt + 1) * TQ)
        dq_t[...] = jnp.zeros(dq_t.shape, jnp.float32)

        @pl.loop(0, everyone // TK)
        def _(kt, qt=qt, here=here):
            needed = meets((stream * rows + qt * TQ, TQ), (kt * TK, TK), image_rows, False)

            @pl.when(needed)
            def _():
                keys = pl.ds(pl.multiple_of(kt * TK, TK), TK)
                allowed = same_item(kind[0:1, 0:1], stream, rows, qt, kt, image_rows)
                scores, prob_grads, probs_low, score_low = [], [], [], []
                for head in range(heads):
                    pair = slice(head // 2 * PAIR, (head // 2 + 1) * PAIR)
                    scores.append(
                        jnp.dot(
                            keys_ref[keys, pair],
                            scaled_t[head, :, here],
                            preferred_element_type=jnp.float32,
                        )
                    )
                    prob_grads.append(
                        jnp.dot(
                            values_ref[keys, pair],
                            grads_t[head, :, here],
                            preferred_element_type=jnp.float32,
                        )
                    )
                for head in range(heads):
                    line = slice(group * heads + head, group * heads + head + 1)
                    shifted = scores[head] - log_total[line, here]
                    probs = jnp.exp(jnp.where(allowed, shifted, MASKED))
                    probs_low.append(probs.astype(jnp.bfloat16))
                    inner = prob_grads[head] - centre[head : head + 1, here]
                    score_low.append((probs * inner).astype(jnp.bfloat16))
                for head in range(heads):
                    own = slice(head * HEAD_DIM, (head + 1) * HEAD_DIM)
                    dq_t[own, :] += jnp.dot(
                        keys_t[own, keys], score_low[head], preferred_element_type=jnp.float32
                    )
                for head in range(0, heads, 2):
                    columns = slice(head * HEAD_DIM, head * HEAD_DIM + PAIR)
                    for terms, left, right in ((dk, score_low, scaled), (dv, probs_low, grads)):
                        terms[keys, columns] += jnp.dot(
                            left[head], right[head, here, :], preferred_element_type=jnp.float32
                        ) + jnp.dot(
                            left[head + 1],
                            right[head + 1, here, :],
                            preferred_element_type=jnp.float32,
                        )

        dq_ref[here, :] = (dq_t[...].T * HEAD_DIM ** (-0.5)).astype(jnp.bfloat16)


def attend_back_kernel(
    kind, place_ref, q_ref, kv_ref, g_ref, mixed_t, log_total, dq_ref, dkv_ref, *work
):
    width = q_ref.shape[1]
    back_group(
        0, kind, place_ref[0], log_total, kv_ref.at[:, pl.ds(0, width)],
        kv_ref.at[:, pl.ds(width, width)], q_ref, g_ref, mixed_t, dq_ref, *work,
    )
    dk, dv = work[-2:]

    @pl.loop(0, kv_ref.shape[0] // TK)
    def _(kt):
        keys = pl.ds(pl.multiple_of(kt * TK, TK), TK)
        dkv_ref[keys, :width] = dk[keys, :].astype(jnp.bfloat16)
        dkv_ref[keys, width:] = dv[keys, :].astype(jnp.bfloat16)


def attend_back(kind, place_at, queries, kv, mixed_grad, mixed_t, log_total):
    rows, width = queries.shape
    heads = width // HEAD_DIM
    inside = pl.BlockSpec(memory_space=pltpu.VMEM)
    lines = -(-heads // 8) * 8
    everyone = kv.shape[0]
    return pl.pallas_call(
        attend_back_kernel,
        out_shape=(
            jax.ShapeDtypeStruct((rows, width), jnp.bfloat16),
            jax.ShapeDtypeStruct((everyone, 2 * width), jnp.bfloat16),
        ),
        in_specs=[inside, pl.BlockSpec(memory_space=pltpu.SMEM)] + [inside] * 5,
        out_specs=(inside,) * 2,
        scratch_shapes=[
            pltpu.VMEM((width, everyone), jnp.bfloat16),
            pltpu.VMEM((heads, rows, PAIR), jnp.bfloat16),
            pltpu.VMEM((heads, rows, PAIR), jnp.bfloat16),
            pltpu.VMEM((heads, PAIR, rows), jnp.bfloat16),
            pltpu.VMEM((heads, PAIR, rows), jnp.bfloat16),
            pltpu.VMEM((width, TQ), jnp.float32),
            pltpu.VMEM((lines, rows), jnp.float32),
            pltpu.VMEM((everyone, width), jnp.float32),
            pltpu.VMEM((everyone, width), jnp.float32),
        ],
        compiler_params=pltpu.CompilerParams(vmem_limit_bytes=58 << 20),
    )(kind, place_at, queries, kv, mixed_grad, mixed_t, log_total)


MESH = pl.DeviceIdType.MESH
GATHER_ORDERS = (("z", "x", "y"), ("z", "y", "x"), ("y", "x", "z"))
SCATTER_ORDERS = (("y", "x", "z"), ("x", "y", "z"), ("z", "x", "y"))
EVERY = slice(None)
THIN_ROWS = 16


def coords():
    items, stream = lax.axis_index("items"), lax.axis_index("stream")
    return dict(z=items // 2, x=items % 2, y=stream // 2, c=stream % 2)


def place(at):
    return (at["z"] * 2 + at["x"], at["y"] * 2 + at["c"])


def moved(at, dim, by, depth):
    return {**at, dim: lax.rem(at[dim] + by, depth if dim == "z" else 2)}


def greet(at, depth):
    peers = [moved(at, "z", k, depth) for k in range(1, depth)]
    peers += [moved(at, d, 1, depth) for d in "xyc"]
    barrier = pltpu.get_barrier_semaphore()
    for peer in peers:
        pl.semaphore_signal(barrier, inc=1, device_id=place(peer), device_id_type=MESH)
    pl.semaphore_wait(barrier, len(peers))


def guard(cond, act):
    if cond is None:
        act()
    else:
        pl.when(cond)(act)


def remote(src, dst, sems, index, device):
    return pltpu.make_async_remote_copy(
        src_ref=src,
        dst_ref=dst,
        send_sem=sems[0].at[index],
        recv_sem=sems[1].at[index],
        device_id=place(device),
        device_id_type=MESH,
    )


def pipelined(chunks, n_steps, ahead, start, wait, hooks, before):
    count = len(chunks)
    for j in range(min(ahead, count)):
        start(chunks[j], 0)
    for t in range(count + n_steps - 1):
        if t in before:
            before[t]()
        if t + ahead < count:
            start(chunks[t + ahead], 0)
        for step in range(n_steps):
            j = t - step
            if 0 <= j < count:
                wait(chunks[j], step)
                if step < n_steps - 1:
                    start(chunks[j], step + 1)
                if (j, step) in hooks:
                    hooks[(j, step)]()


def spots_of(depth):
    return [(a, b, c, d) for a in range(depth) for b in range(2) for c in range(2) for d in range(2)]


def columns_over(share, width):
    column = lax.broadcasted_iota(jnp.int32, (1, width), 1).astype(jnp.float32)
    owner = jnp.floor((column + 0.5) * (1.0 / share))
    return owner, column - owner * share


def spread(thin, share, width):
    owner, lane = columns_over(share, width)
    picks = lax.broadcasted_iota(jnp.int32, (128, width), 0).astype(jnp.float32) == lane
    wide = jnp.dot(thin, picks.astype(jnp.bfloat16), preferred_element_type=jnp.float32)
    total = jnp.zeros((THIN_ROWS, width), jnp.float32)
    for device in range(thin.shape[0] // THIN_ROWS):
        part = wide[device * THIN_ROWS : (device + 1) * THIN_ROWS]
        total = total + jnp.where(owner == device, part, 0.0)
    return total


def dealt(rows, share, devices):
    width = rows.shape[1]
    owner, lane = columns_over(share, width)
    picks = lax.broadcasted_iota(jnp.int32, (128, width), 0).astype(jnp.float32) == lane
    tall = jnp.concatenate(
        [jnp.where(owner == device, rows, 0.0) for device in range(devices)], axis=0
    )
    return lax.dot_general(
        tall,
        picks.astype(jnp.float32),
        (((1,), (1,)), ((), ())),
        precision=lax.Precision.HIGHEST,
        preferred_element_type=jnp.float32,
    )


def gather_kernel(depth, chunks, entries, *refs):
    it = iter(refs)
    take = lambda count: [next(it) for _ in range(count)]
    ins = take(5)
    tokens, kind = take(2)
    thin_out, out_all, up_all, down_all = take(4)
    qkv_weight, normed, queries, vectors, kv_out, mixed, mixed_t, log_total = take(8)
    thin_all, qkv_all, kv, values_t, scaled, top, total = take(7)
    local_sem = next(it)
    sems, kv_sems = take(2), take(2)
    keep_sem = next(it)
    outs = (thin_all, qkv_all, out_all, up_all, down_all)
    rows, width = tokens.shape
    devices = depth * 8
    share = width // devices
    at = coords()
    mine = (at["z"], at["x"], at["y"], at["c"])
    slot = at["y"] * 2 + at["c"]

    def source(entry):
        k, e = entry
        return ins[k] if e is None else ins[k].at[e]

    def target(entry):
        k, e = entry
        return outs[k] if e is None else outs[k].at[e]

    local = [
        pltpu.make_async_copy(source(entry), target(entry).at[mine], local_sem.at[j])
        for j, entry in enumerate(entries)
    ]
    for copy in local:
        copy.start()
    greet(at, depth)
    for copy in local:
        copy.wait()
    lower, upper = at["y"] == 0, at["y"] == 1
    number = {piece: j for j, piece in enumerate(piece for chunk in chunks for piece in chunk)}

    def stage(piece, step):
        entry, band, cols, order, text = piece
        dims = GATHER_ORDERS[order] + ("c",)
        dim = dims[step]
        held = tuple(EVERY if d in dims[:step] else pl.ds(at[d], 1) for d in "zxyc")
        view = target(entry).at[held + (pl.ds(*band), pl.ds(*cols))]
        sends = recvs = None
        if text and dim == "y":
            sends, recvs = lower, upper
        elif text and "y" in dims[:step]:
            sends = recvs = upper
        found = []
        for k in range(1, depth if dim == "z" else 2):
            sem = {"z": k - 1, "x": depth - 1, "y": depth, "c": depth + 1}[dim]
            found.append(remote(view, view, sems, (number[piece], sem), moved(at, dim, k, depth)))
        return found, sends, recvs

    def each(chunk, step, which, call):
        for piece in chunk:
            found = stage(piece, step)

            def act(copies=found[0]):
                for copy in copies:
                    call(copy)

            guard(found[which], act)

    beside, across = moved(at, "c", 1, depth), moved(at, "y", 1, depth)
    other = across["y"] * 2 + across["c"]
    own_slot = pl.ds(pl.multiple_of(slot * rows, rows), rows)
    other_slot = pl.ds(pl.multiple_of(other * rows, rows), rows)
    to_across = remote(kv.at[own_slot], kv.at[own_slot], kv_sems, 0, across)
    to_beside = remote(kv.at[own_slot], kv.at[own_slot], kv_sems, 1, beside)
    onward = remote(kv.at[other_slot], kv.at[other_slot], kv_sems, 2, beside)
    keep_thin = pltpu.make_async_copy(thin_all, thin_out, keep_sem.at[0])
    keep_kv = pltpu.make_async_copy(kv, kv_out, keep_sem.at[1])

    def project():
        spots = spots_of(depth)
        for j, spot in enumerate(spots):
            qkv_weight[j * share : (j + 1) * share, :] = qkv_all[spot]
        thin = jnp.concatenate([thin_all[spot] for spot in spots], axis=0)
        vectors[...] = spread(thin, share, width)

        @pl.loop(0, rows // 128)
        def _(j):
            block = pl.ds(pl.multiple_of(j * 128, 128), 128)
            value = tokens[block, :].astype(jnp.float32)
            centred = value - jnp.mean(value, axis=-1, keepdims=True)
            scale = lax.rsqrt(jnp.mean(centred * centred, axis=-1, keepdims=True) + NORM_EPS)
            normed[block, :] = (centred * scale * vectors[0:1, :] + vectors[1:2, :]).astype(
                jnp.bfloat16
            )

        step = width // 2
        for part in (1, 2, 0):

            @pl.loop(0, 2)
            def _(j, part=part):
                cols = pl.ds(pl.multiple_of(j * step, 128), step)
                value = jnp.dot(
                    normed[...],
                    qkv_weight[:, pl.ds(pl.multiple_of(part * width + j * step, 128), step)],
                    preferred_element_type=jnp.float32,
                )
                if part == 0:
                    queries[:, cols] = (value + vectors[2:3, cols]).astype(jnp.bfloat16)
                elif part == 1:
                    kv[own_slot, cols] = value.astype(jnp.bfloat16)
                else:
                    kv[own_slot, pl.ds(pl.multiple_of(width + j * step, 128), step)] = (
                        value + vectors[3:4, cols]
                    ).astype(jnp.bfloat16)

            if part == 2:
                to_across.start()
                to_beside.start()
                keep_thin.start()
        scale_queries(queries, scaled)

    def pass_on():
        to_across.wait_recv()
        onward.start()

    def attend_first():
        to_beside.wait_recv()
        onward.wait_recv()
        keep_kv.start()
        flip_columns(kv, width, values_t)

    parts = (kind, slot, kv, values_t, scaled, mixed, mixed_t, log_total, top, total)

    def attention(qt, begin, end):
        def act():
            if qt == 0 and begin == 0:
                attend_first()
            attend_part(qt, begin, end, *parts)

        return act

    everyone = kv.shape[0] // TK
    pipelined(
        chunks,
        4,
        2,
        lambda chunk, step: each(chunk, step, 1, lambda copy: copy.start()),
        lambda chunk, step: each(chunk, step, 2, lambda copy: copy.wait_recv()),
        {
            (0, 3): project,
            (2, 3): pass_on,
            (3, 3): attention(0, 0, everyone),
            (4, 3): attention(1, 0, everyone // 2),
        },
        {},
    )
    attention(1, everyone // 2, everyone)()
    for copy in (to_beside, to_across, onward):
        copy.wait_send()
    keep_thin.wait()
    keep_kv.wait()
    for chunk in chunks:
        for step in range(4):
            each(chunk, step, 1, lambda copy: copy.wait_send())


def gather_all(thin, w_qkv, w_out, w_up, w_down, tokens, kind, depth):
    rows, width = tokens.shape
    share, ff_share, ff = w_qkv.shape[0], w_down.shape[1], w_up.shape[2]
    entries = [(0, None), (1, None), (2, None), (3, 0), (3, 1), (4, 0), (4, 1)]
    chunks = gather_chunks(share, width, ff_share, ff)
    n_pieces = sum(len(chunk) for chunk in chunks)
    anywhere = pl.BlockSpec(memory_space=pl.ANY)
    inside = pl.BlockSpec(memory_space=pltpu.VMEM)
    low = jnp.bfloat16
    box = (depth, 2, 2, 2)
    heads, lines = width // HEAD_DIM, -(-(width // HEAD_DIM) // 8) * 8
    return pl.pallas_call(
        functools.partial(gather_kernel, depth, chunks, entries),
        out_shape=[
            jax.ShapeDtypeStruct(box + thin.shape, low),
            jax.ShapeDtypeStruct(box + (share, width), low),
            jax.ShapeDtypeStruct((2,) + box + (share, ff), low),
            jax.ShapeDtypeStruct((2,) + box + (ff_share, width), low),
            jax.ShapeDtypeStruct((width, 3 * width), low),
            jax.ShapeDtypeStruct((rows, width), low),
            jax.ShapeDtypeStruct((rows, width), low),
            jax.ShapeDtypeStruct((THIN_ROWS, width), jnp.float32),
            jax.ShapeDtypeStruct((4 * rows, 2 * width), low),
            jax.ShapeDtypeStruct((rows, width), low),
            jax.ShapeDtypeStruct((width, rows), jnp.float32),
            jax.ShapeDtypeStruct((lines, rows), jnp.float32),
        ],
        in_specs=[anywhere] * 5 + [inside] * 2,
        out_specs=[anywhere] * 4 + [inside] * 4 + [anywhere] + [inside] * 3,
        scratch_shapes=[
            pltpu.VMEM(box + thin.shape, low),
            pltpu.VMEM(box + (share, 3 * width), low),
            pltpu.VMEM((4 * rows, 2 * width), low),
            pltpu.VMEM((width, 4 * rows), low),
            pltpu.VMEM((heads, PAIR, rows), low),
            pltpu.VMEM((lines, TQ), jnp.float32),
            pltpu.VMEM((lines, TQ), jnp.float32),
            pltpu.SemaphoreType.DMA((len(entries),)),
            pltpu.SemaphoreType.DMA((n_pieces, depth + 2)),
            pltpu.SemaphoreType.DMA((n_pieces, depth + 2)),
            pltpu.SemaphoreType.DMA((3,)),
            pltpu.SemaphoreType.DMA((3,)),
            pltpu.SemaphoreType.DMA((2,)),
        ],
        compiler_params=pltpu.CompilerParams(
            collective_id=1, has_side_effects=True, vmem_limit_bytes=48 << 20
        ),
    )(thin, w_qkv, w_out, w_up, w_down, tokens, kind)


def scatter_kernel(depth, kinds, chunks, cuts, *refs):
    n, n_far = len(kinds), 3
    it = iter(refs)
    take = lambda count: [next(it) for _ in range(count)]
    far = take(n_far)
    factor, thin_in, vectors, kind, log_total = take(5)
    queries, kv, mixed_grad, mixed_t, normed, weight, tokens, residual_grad = take(8)
    outs = take(n)
    token_grad, kv_away = take(2)
    acc, first, second, last = take(n), take(n), take(n), take(n)
    z_first, z_second, z_last = take(n), take(n), take(n)
    own_half = take(n_far)
    qkv_terms, thin_terms, kv_sum, kv_got, kv_mine, dq = take(6)
    sems = take(2)
    local_sem, away_sem = take(2)
    kv_sems = take(2)
    rows, width = residual_grad.shape
    devices = depth * 8
    share = width // devices
    at = coords()
    z, x, y, c = (at[d] for d in "zxyc")
    ins = far + [qkv_terms, thin_terms]
    local = [
        pltpu.make_async_copy(far[k].at[EVERY, EVERY, EVERY, c], own_half[k], local_sem.at[k])
        for k in range(n_far)
    ]
    for copy in local:
        copy.start()
    greet(at, depth)
    for copy in local:
        copy.wait()
    beside, across = moved(at, "c", 1, depth), moved(at, "y", 1, depth)
    kv_beside = remote(kv_away, kv_sum, kv_sems, 0, beside)
    kv_across = remote(kv_sum.at[1 - y], kv_got, kv_sems, 1, across)
    lower, upper = y == 0, y == 1
    text_device = jnp.logical_and(upper, c == 1)
    image_device = jnp.logical_or(lower, c == 0)
    beside_text = jnp.logical_and(upper, c == 0)
    beside_image = jnp.logical_or(lower, c == 1)
    number = {piece: j for j, piece in enumerate(piece for chunk in chunks for piece in chunk)}

    def boxes(piece):
        k, e, band, cols, order = piece
        cut = cuts[k] if order == 2 else (0, 0)
        return (
            (pl.ds(*band), pl.ds(*cols)),
            (pl.ds(band[0] - cut[0], band[1]), pl.ds(cols[0] - cut[1], cols[1])),
        )

    def copies_of(piece, step):
        k, e, band, cols, order = piece
        box, inner = boxes(piece)
        image, text = kinds[k] and e == 0, kinds[k] and e == 1
        dims = ("c",) + SCATTER_ORDERS[order]
        dim = dims[step]
        here = acc[k].at[e]

        def make(src, dst, sem, by=1):
            return remote(src, dst, sems, (number[piece], sem), moved(at, dim, by, depth))

        sends = recvs = None
        if dim == "c":
            if image:
                sends, recvs = image_device, beside_image
            elif text:
                sends, recvs = text_device, beside_text
            src = ins[k].at[(EVERY, EVERY, EVERY, 1 - c) + box]
            return [(make(src, here.at[(EVERY, EVERY, EVERY) + box], 0), sends, recvs)]
        if text and dim == "y":
            sends, recvs = upper, lower
        elif text and "y" not in dims[:step]:
            sends = recvs = upper
        if dim == "z":
            found = []
            for by in range(1, depth):
                to = lax.rem(z + by, depth)
                if order == 2:
                    src = here.at[(to, EVERY, EVERY) + box]
                    dst = z_first[k].at[(e, by - 1, EVERY, EVERY) + inner]
                else:
                    src = here.at[(to, x, y) + box]
                    dst = last[k].at[(e, by - 1) + inner]
                found.append((make(src, dst, 2 + by, by), sends, recvs))
            return found
        if order == 2 and dim == "x":
            src, dst = here.at[(z, 1 - x, EVERY) + box], z_second[k].at[(e, EVERY) + inner]
            return [(make(src, dst, 1), sends, recvs)]
        if order == 2:
            src, dst = here.at[(z, x, 1 - y) + box], z_last[k].at[(e,) + inner]
            return [(make(src, dst, 2), sends, recvs)]
        if step == 1:
            spot = (EVERY, EVERY, 1 - y) if dim == "y" else (EVERY, 1 - x, EVERY)
            dst = first[k].at[(e, EVERY, EVERY) + inner]
        else:
            spot = (EVERY, x, 1 - y) if dim == "y" else (EVERY, 1 - x, y)
            dst = second[k].at[(e, EVERY) + inner]
        return [(make(here.at[spot + box], dst, step), sends, recvs)]

    def combine(piece, step):
        k, e, band, cols, order = piece
        box, inner = boxes(piece)
        image, text = kinds[k] and e == 0, kinds[k] and e == 1
        dims = ("c",) + SCATTER_ORDERS[order]
        dim = dims[step]
        here = acc[k].at[e]

        def over(spots, value_of, keep):
            @pl.loop(0, depth)
            def _(level):
                for index, spot in enumerate(spots):
                    where = (level,) + spot + box
                    value = value_of(level, index, spot)
                    here[where] = value if keep else here[where] + value

        def wide(value):
            return value.astype(jnp.float32)

        if step == 0:
            spots = [(0, 0), (0, 1), (1, 0), (1, 1)]

            def own(level, index, spot):
                if k < n_far:
                    return own_half[k][(level,) + spot + box]
                return ins[k][(level,) + spot + (c,) + box]

            if image:
                pl.when(lower)(lambda: over(spots, own, False))
                pl.when(beside_text)(lambda: over(spots, own, True))
            elif text:
                pl.when(text_device)(lambda: over(spots, own, True))
            else:
                over(spots, own, False)
        elif step == 3:

            def finish(total):
                if kinds[k]:
                    total = total * factor[0:1, e * 128 : e * 128 + 1]
                outs[k][(e,) + box] = total

            def own():
                return wide(here[(z, x, y) + box])

            if order == 2:
                got = lambda: wide(z_last[k][(e,) + inner])
                if text:
                    pl.when(lower)(lambda: finish(got()))
                    pl.when(upper)(lambda: finish(own()))
                else:
                    finish(own() + got())
            else:
                total = own()
                for by in range(depth - 1):
                    total = total + wide(last[k][(e, by) + inner])
                finish(total)
        elif order == 2:

            def act():
                if step == 1:
                    for spot in [(0, 0), (0, 1), (1, 0), (1, 1)]:
                        where = (z,) + spot + box
                        total = wide(here[where])
                        for by in range(depth - 1):
                            total = total + wide(z_first[k][(e, by) + spot + inner])
                        here[where] = total.astype(here.dtype)
                else:
                    for other in range(2):
                        where = (z, x, other) + box
                        here[where] = here[where] + z_second[k][(e, other) + inner]

            guard(upper if text else None, act)
        elif step == 1:
            spots = [(0, y), (1, y)] if dim == "y" else [(x, 0), (x, 1)]
            got = lambda level, index, spot: first[k][(e, level, index) + inner]
            if text and dim == "y":
                pl.when(lower)(lambda: over(spots, got, True))
            elif text:
                pl.when(upper)(lambda: over(spots, got, False))
            else:
                over(spots, got, False)
        else:
            got = lambda level, index, spot: second[k][(e, level) + inner]
            if text and dim == "y":
                pl.when(lower)(lambda: over([(x, y)], got, True))
            else:
                over([(x, y)], got, False)

    def start(chunk, step):
        for piece in chunk:
            for copy, sends, _ in copies_of(piece, step):
                guard(sends, copy.start)

    def wait(chunk, step):
        for piece in chunk:
            for copy, _, recvs in copies_of(piece, step):
                guard(recvs, copy.wait_recv)
            combine(piece, step)

    def halve():
        kv_beside.wait_recv()

        @pl.loop(0, rows // 64)
        def _(j):
            block = pl.ds(pl.multiple_of(j * 64, 64), 64)
            for level in range(2):
                kv_sum[level, block, :] = kv_sum[level, block, :] + kv_mine[level, block, :]

        kv_across.start()

    def project_back(qkv_grad, flipped, normed_in, weight_in, tokens_in, residual_in, token_out):
        pairs = [(normed, normed_in), (weight, weight_in), (tokens, tokens_in), (residual_grad, residual_in)]
        loads = [pltpu.make_async_copy(src, dst, away_sem.at[j]) for j, (src, dst) in enumerate(pairs)]
        for copy in loads:
            copy.start()
        for copy in loads:
            copy.wait()
        flipped[...] = normed_in[...].T
        qkv_grad[:, :width] = dq[...]
        thin_terms[...] = thin_in[...]
        kv_across.wait_recv()

        def fold(value):
            return jnp.sum(value.reshape(-1, 8, width), axis=0)

        zero = jnp.zeros((8, width), jnp.float32)

        def join(j, carry):
            block = pl.ds(pl.multiple_of(j * 64, 64), 64)
            total = (
                kv_sum[y, block, :].astype(jnp.float32) + kv_got[block, :].astype(jnp.float32)
            ).astype(jnp.bfloat16)
            qkv_grad[block, width:] = total
            return (
                carry[0] + fold(dq[block, :].astype(jnp.float32)),
                carry[1] + fold(total[:, width:].astype(jnp.float32)),
            )

        sum_q, sum_v = lax.fori_loop(0, rows // 64, join, (zero, zero))
        step = width // 2
        spots = spots_of(depth)

        @pl.loop(0, 6)
        def _(j):
            cols = pl.ds(pl.multiple_of(j * step, 128), step)
            value = jnp.dot(
                flipped[...], qkv_grad[:, cols], preferred_element_type=jnp.float32
            ).astype(jnp.bfloat16)
            for index, spot in enumerate(spots):
                qkv_terms[spot + (EVERY, cols)] = value[index * share : (index + 1) * share]

        def back(j, carry):
            block = pl.ds(pl.multiple_of(j * 128, 128), 128)
            value = tokens_in[block, :].astype(jnp.float32)
            centred = value - jnp.mean(value, axis=-1, keepdims=True)
            scale = lax.rsqrt(jnp.mean(centred * centred, axis=-1, keepdims=True) + NORM_EPS)
            unit = centred * scale
            grad = product_trail(qkv_grad[block, :], weight_in[...])
            lifted = grad * vectors[0:1, :]
            inner = jnp.mean(lifted * unit, axis=-1, keepdims=True)
            part = scale * (lifted - jnp.mean(lifted, axis=-1, keepdims=True) - unit * inner)
            token_out[block, :] = (residual_in[block, :] + part).astype(jnp.bfloat16)
            return carry[0] + fold(grad * unit), carry[1] + fold(grad)

        sum_gain, sum_shift = lax.fori_loop(0, rows // 128, back, (zero, zero))
        store = pltpu.make_async_copy(token_out, token_grad, away_sem.at[0])
        store.start()
        lines = [jnp.sum(value, axis=0, keepdims=True) for value in (sum_gain, sum_shift, sum_q, sum_v)]
        stacked = jnp.concatenate(lines + [jnp.zeros((4, width), jnp.float32)], axis=0)
        flat = dealt(stacked, share, devices)
        for index, spot in enumerate(spots):
            thin_terms[spot + (slice(0, 8),)] += flat[index * 8 : (index + 1) * 8]
        store.wait()

    def project_scope():
        low = jnp.bfloat16
        pl.run_scoped(
            project_back,
            pltpu.VMEM((rows, 3 * width), low),
            pltpu.VMEM((width, rows), low),
            pltpu.VMEM((rows, width), low),
            pltpu.VMEM((width, 3 * width), low),
            pltpu.VMEM((rows, width), low),
            pltpu.VMEM((rows, width), jnp.float32),
            pltpu.VMEM((rows, width), low),
        )

    group_width = width // 2
    stream = y * 2 + c

    def attention(group):
        cols = pl.ds(group * group_width, group_width)
        value_cols = pl.ds(width + group * group_width, group_width)

        def act(keys, values, q_in, g_in, mixed_in, *work):
            pairs = [
                (kv.at[:, cols], keys),
                (kv.at[:, value_cols], values),
                (queries.at[:, cols], q_in),
                (mixed_grad.at[:, cols], g_in),
                (mixed_t.at[cols, :], mixed_in),
            ]
            loads = [pltpu.make_async_copy(src, dst, away_sem.at[j]) for j, (src, dst) in enumerate(pairs)]
            for copy in loads:
                copy.start()
            for copy in loads:
                copy.wait()
            back_group(
                group, kind, stream, log_total, keys, values, q_in, g_in, mixed_in,
                dq.at[:, cols], *work,
            )
            dk, dv = work[-2:]
            for part, (terms, rest, begin) in enumerate(((dk, keys, cols), (dv, values, value_cols))):
                for level in range(2):
                    mine = (level * 2 + c) * rows
                    away = (level * 2 + 1 - c) * rows

                    @pl.loop(0, rows // 128)
                    def _(j, level=level, mine=mine, away=away, terms=terms, rest=rest, begin=begin):
                        to = pl.ds(pl.multiple_of(j * 128, 128), 128)
                        kept = pl.ds(pl.multiple_of(mine + j * 128, 128), 128)
                        sent = pl.ds(pl.multiple_of(away + j * 128, 128), 128)
                        kv_mine[level, to, begin] = terms[kept, :].astype(jnp.bfloat16)
                        rest[sent, :] = terms[sent, :].astype(jnp.bfloat16)

            stores = []
            for part, (rest, begin) in enumerate(((keys, cols), (values, value_cols))):
                for level in range(2):
                    sent = pl.ds(pl.multiple_of((level * 2 + 1 - c) * rows, rows), rows)
                    stores.append(
                        pltpu.make_async_copy(
                            rest.at[sent], kv_away.at[level, :, begin], away_sem.at[part * 2 + level]
                        )
                    )
            for copy in stores:
                copy.start()
            for copy in stores:
                copy.wait()
            if group == 1:
                kv_beside.start()

        def scope():
            low = jnp.bfloat16
            heads = group_width // HEAD_DIM
            everyone = 4 * rows
            pl.run_scoped(
                act,
                pltpu.VMEM((everyone, group_width), low),
                pltpu.VMEM((everyone, group_width), low),
                pltpu.VMEM((rows, group_width), low),
                pltpu.VMEM((rows, group_width), low),
                pltpu.VMEM((group_width, rows), jnp.float32),
                pltpu.VMEM((group_width, everyone), low),
                pltpu.VMEM((heads, rows, PAIR), low),
                pltpu.VMEM((heads, rows, PAIR), low),
                pltpu.VMEM((heads, PAIR, rows), low),
                pltpu.VMEM((heads, PAIR, rows), low),
                pltpu.VMEM((group_width, TQ), jnp.float32),
                pltpu.VMEM((8, rows), jnp.float32),
                pltpu.VMEM((everyone, group_width), jnp.float32),
                pltpu.VMEM((everyone, group_width), jnp.float32),
            )

        return scope

    before = {0: attention(0), 1: attention(1), 3: halve, 4: project_scope}
    pipelined(chunks, 4, 2, start, wait, {}, before)
    for copy in (kv_beside, kv_across):
        copy.wait_send()
    for chunk in chunks:
        for step in range(4):
            for piece in chunk:
                for copy, sends, _ in copies_of(piece, step):
                    guard(sends, copy.wait_send)


def scatter_all(
    up, down, out, factor, thin, vectors, kind, log_total,
    queries, kv, mixed_grad, mixed_t, normed, weight, tokens, residual_grad, depth,
):
    rows, width = tokens.shape
    far = [up, down, out]
    kinds = (True, True, False, False, False)
    share, ff_share, ff = up.shape[4], down.shape[4], up.shape[5]
    chunks, cuts = scatter_chunks(share, width, ff_share, ff)
    n_pieces = sum(len(chunk) for chunk in chunks)
    anywhere, inside = pl.BlockSpec(memory_space=pl.ANY), pl.BlockSpec(memory_space=pltpu.VMEM)
    low, box = jnp.bfloat16, (depth, 2, 2, 2)
    tails = [a.shape[4:] for a in far] + [(share, 3 * width), thin.shape[4:]]
    dtypes = [low] * 4 + [jnp.float32]
    experts = [2 if kind else 1 for kind in kinds]
    scratch = [
        pltpu.VMEM((e, depth, 2, 2) + tail, dtype) for e, tail, dtype in zip(experts, tails, dtypes)
    ]
    plain, turned = [], []
    for tail, cut in zip(tails, cuts):
        plain.append((cut[0] or tail[0], cut[1] or tail[1]))
        turned.append((tail[0] - cut[0], tail[1] - cut[1]) if any(cut) else (8, 128))
    for middle in ((depth, 2), (depth,), (depth - 1,)):
        scratch += [pltpu.VMEM((e,) + middle + t, d) for e, t, d in zip(experts, plain, dtypes)]
    for middle in ((depth - 1, 2, 2), (2,), ()):
        scratch += [pltpu.VMEM((e,) + middle + t, d) for e, t, d in zip(experts, turned, dtypes)]
    scratch += [pltpu.VMEM((depth, 2, 2) + a.shape[4:], low) for a in far]
    scratch += [
        pltpu.VMEM(box + (share, 3 * width), low),
        pltpu.VMEM(thin.shape, jnp.float32),
        pltpu.VMEM((2, rows, 2 * width), low),
        pltpu.VMEM((rows, 2 * width), low),
        pltpu.VMEM((2, rows, 2 * width), low),
        pltpu.VMEM((rows, width), low),
        pltpu.SemaphoreType.DMA((n_pieces, depth + 2)),
        pltpu.SemaphoreType.DMA((n_pieces, depth + 2)),
        pltpu.SemaphoreType.DMA((3,)),
        pltpu.SemaphoreType.DMA((5,)),
        pltpu.SemaphoreType.DMA((2,)),
        pltpu.SemaphoreType.DMA((2,)),
    ]
    return pl.pallas_call(
        functools.partial(scatter_kernel, depth, kinds, chunks, cuts),
        out_shape=[
            jax.ShapeDtypeStruct((e,) + tail, jnp.float32) for e, tail in zip(experts, tails)
        ]
        + [jax.ShapeDtypeStruct((rows, width), low), jax.ShapeDtypeStruct((2, rows, 2 * width), low)],
        in_specs=[anywhere] * 3 + [inside] * 5 + [anywhere] * 8,
        out_specs=[inside] * 5 + [anywhere] * 2,
        scratch_shapes=scratch,
        compiler_params=pltpu.CompilerParams(
            collective_id=2, has_side_effects=True, vmem_limit_bytes=61 << 20
        ),
    )(
        up, down, out, factor, thin, vectors, kind, log_total,
        queries, kv, mixed_grad, mixed_t, normed, weight, tokens, residual_grad,
    )[:6]


def padded(values):
    return jnp.pad(values, ((0, 0), (0, 128 - values.shape[1])))


def body(
    near,
    tokens,
    group_kind,
    ln1_gain,
    ln1_bias,
    w_qkv,
    q_bias,
    v_bias,
    w_out,
    out_bias,
    ln2_gain,
    ln2_bias,
    w_up,
    b_up,
    w_down,
    b_down,
    cotangent,
):
    row_count, model_width = tokens.shape
    stream_size = lax.axis_size("stream")
    stream_place = lax.axis_index("stream")
    devices = lax.axis_size("items") * stream_size
    group_type = group_kind[0]
    own_positions = stream_place * row_count + jnp.arange(row_count, dtype=jnp.int32)
    own_modality = layout(group_type, own_positions, row_count)[1]
    expert_pick = jnp.where(stream_place == stream_size - 1, 1, 0).astype(jnp.int32)
    share, ff_share, ff = model_width // devices, w_down.shape[1], w_up.shape[2]
    both = ("items", "stream")
    low = jnp.bfloat16
    thin = jnp.stack([ln1_gain, ln1_bias, q_bias, v_bias, out_bias, ln2_gain, ln2_bias])
    thin = jnp.concatenate(
        [padded(thin), padded(b_up), padded(b_down), padded(group_kind.astype(low)[:, None])]
    )
    thin = jnp.pad(thin, ((0, THIN_ROWS - thin.shape[0]), (0, 0)))
    tokens_f = tokens.astype(jnp.float32)
    kind_wide = jnp.broadcast_to(group_type.astype(jnp.float32), (8, 128))
    place_at = stream_place.astype(jnp.int32)[None]
    if near:
        depth = lax.axis_size("items") // 2
        (
            thin_all,
            out_weight,
            up_all,
            down_all,
            qkv_weight,
            normed_low,
            queries,
            vectors,
            kv,
            mixed_low,
            mixed_t,
            log_total,
        ) = gather_all(thin, w_qkv, w_out, w_up, w_down, tokens, kind_wide, depth)
        thin_all = thin_all.reshape(devices, THIN_ROWS, 128)
        out_weight = out_weight.reshape(model_width, model_width)
        up_all = up_all.reshape(2, model_width, ff)
        down_all = down_all.reshape(2, ff, model_width)
    else:
        thin_all = lax.all_gather(thin, both, axis=0)
        qkv_weight = lax.all_gather(w_qkv, both, axis=0, tiled=True)
        out_weight = lax.all_gather(w_out, both, axis=0, tiled=True)
        up_all = lax.all_gather(w_up, both, axis=1, tiled=True)
        down_all = lax.all_gather(w_down, both, axis=1, tiled=True)
        vectors = (
            thin_all[:, :, :share].transpose(1, 0, 2).reshape(THIN_ROWS, -1).astype(jnp.float32)
        )
        normed_low = layer_norm(tokens_f, vectors[0], vectors[1]).astype(low)
        shifts = jnp.concatenate([vectors[2], jnp.zeros_like(vectors[2]), vectors[3]])
        projected = (product(normed_low, qkv_weight) + shifts).astype(low)
        queries = projected[:, :model_width]
        kv = lax.all_gather(projected[:, model_width:], "stream", axis=0, tiled=True)
        mixed_low, mixed_t, log_total = attend(kind_wide, place_at, queries, kv)
    out_shift, gain_two, shift_two = vectors[4], vectors[5], vectors[6]
    down_shift = jnp.where(expert_pick == 0, vectors[9], vectors[10])
    up_shift_all = thin_all[:, 7:9, :ff_share].transpose(1, 0, 2).reshape(2, ff)
    kinds = vectors[11, :: stream_size * share].astype(jnp.int32)
    tally = []
    for kind in range(2):
        modality = layout(
            jnp.int32(kind), jnp.arange(stream_size * row_count, dtype=jnp.int32), row_count
        )[1]
        tally.append([jnp.sum((modality == e).astype(jnp.float32)) for e in range(2)])
    totals = jnp.stack(
        [jnp.sum(jnp.where(kinds == 0, tally[0][e], tally[1][e])) for e in range(2)]
    )
    residual = tokens_f + product(mixed_low, out_weight) + out_shift
    normed_two, pull_two = jax.vjp(layer_norm, residual, gain_two, shift_two)
    normed_two_low = normed_two.astype(low)
    up_weight = lax.dynamic_index_in_dim(up_all, expert_pick, 0, keepdims=False)
    up_shift = lax.dynamic_index_in_dim(up_shift_all, expert_pick, 0, keepdims=False)
    down_weight = lax.dynamic_index_in_dim(down_all, expert_pick, 0, keepdims=False)
    hidden_pre = product(normed_two_low, up_weight) + up_shift.astype(jnp.float32)
    hidden, pull_gelu = jax.vjp(gelu_exact, hidden_pre)
    hidden_low = hidden.astype(low)
    branch = product(hidden_low, down_weight) + down_shift
    expert_mask = (own_modality == expert_pick).astype(jnp.float32)[:, None]
    output = (residual + branch * expert_mask).astype(low)
    live_rows = (own_modality < 2).astype(jnp.float32)[:, None]
    out_grad = cotangent.astype(jnp.float32) * live_rows
    branch_grad = (out_grad * expert_mask).astype(low)
    grad_down = product_lead(hidden_low, branch_grad)
    grad_down_shift = jnp.sum(branch_grad.astype(jnp.float32), axis=0)
    hidden_grad = product_trail(branch_grad, down_weight)
    pre_grad = pull_gelu(hidden_grad)[0].astype(low)
    grad_up = product_lead(normed_two_low, pre_grad)
    grad_up_shift = jnp.sum(pre_grad.astype(jnp.float32), axis=0)
    norm_two_grad = product_trail(pre_grad, up_weight)
    residual_part, grad_gain_two, grad_shift_two = pull_two(norm_two_grad)
    residual_grad = out_grad + residual_part
    residual_low = residual_grad.astype(low)
    grad_out_weight = product_lead(mixed_low, residual_low)
    grad_out_shift = jnp.sum(residual_low.astype(jnp.float32), axis=0)
    mixed_grad = product_trail(residual_low, out_weight).astype(low)
    factor = lax.rsqrt(totals)
    pick = (jnp.arange(2, dtype=jnp.int32) == expert_pick).astype(jnp.float32) * factor

    def lanes(values):
        values = values.reshape(values.shape[0], devices, -1).transpose(1, 0, 2)
        return jnp.pad(values, ((0, 0), (0, 0), (0, 128 - values.shape[2])))

    def thin_of(rows):
        thin_terms = jnp.concatenate(
            [
                lanes(jnp.stack(rows)),
                lanes(pick[:, None] * grad_up_shift[None]),
                lanes(pick[:, None] * grad_down_shift[None]),
            ],
            axis=1,
        )
        return jnp.pad(thin_terms, ((0, 0), (0, THIN_ROWS - thin_terms.shape[1]), (0, 0)))

    late = [grad_out_shift, grad_gain_two, grad_shift_two]
    if near:
        box = (depth, 2, 2, 2)
        up_sum, down_sum, out_sum, qkv_sum, thin_sum, token_grad = scatter_all(
            grad_up.astype(low).reshape(box + (share, ff)),
            grad_down.astype(low).reshape(box + (ff_share, model_width)),
            grad_out_weight.astype(low).reshape(box + (share, model_width)),
            jnp.broadcast_to(jnp.repeat(factor, 128)[None], (8, 256)),
            thin_of([jnp.zeros_like(grad_out_shift)] * 4 + late).reshape(box + (THIN_ROWS, 128)),
            vectors,
            kind_wide,
            log_total,
            queries,
            kv,
            mixed_grad,
            mixed_t,
            normed_low,
            qkv_weight,
            tokens,
            residual_grad,
            depth,
        )
        out_sum, qkv_sum, thin_sum = out_sum[0], qkv_sum[0], thin_sum[0]
    else:
        scatter = functools.partial(
            lax.psum_scatter, axis_name=both, scatter_dimension=0, tiled=True
        )
        wide = functools.partial(lax.psum_scatter, axis_name=both, scatter_dimension=1, tiled=True)
        query_grad, kv_terms = attend_back(
            kind_wide, place_at, queries, kv, mixed_grad, mixed_t, log_total
        )
        kv_grad = lax.psum_scatter(
            kv_terms.astype(jnp.float32), "stream", scatter_dimension=0, tiled=True
        )
        qkv_grad = jnp.concatenate([query_grad, kv_grad.astype(low)], axis=1)
        grad_qkv = product_lead(normed_low, qkv_grad)
        early = [
            jnp.sum(qkv_grad[:, :model_width].astype(jnp.float32), axis=0),
            jnp.sum(qkv_grad[:, 2 * model_width :].astype(jnp.float32), axis=0),
        ]
        norm_one_grad = product_trail(qkv_grad, qkv_weight)
        token_part, *grads_one = jax.vjp(layer_norm, tokens_f, vectors[0], vectors[1])[1](
            norm_one_grad
        )
        token_grad = (residual_grad + token_part).astype(low)
        up_sum = wide(pick[:, None, None] * grad_up[None])
        down_sum = wide(pick[:, None, None] * grad_down[None])
        out_sum, qkv_sum = scatter(grad_out_weight), scatter(grad_qkv)
        thin_sum = scatter(thin_of(grads_one + early + late))[0]
    small = [thin_sum[k, :share] for k in range(7)]
    return (
        output,
        token_grad,
        small[0],
        small[1],
        qkv_sum,
        small[2],
        small[3],
        out_sum,
        small[4],
        small[5],
        small[6],
        up_sum,
        thin_sum[7:9, :ff_share],
        down_sum,
        thin_sum[9:11, :share],
        totals,
    )


def solution(mesh):
    placed = (
        P(("items", "stream"), None),
        P("items"),
        P(("items", "stream")),
        P(("items", "stream")),
        P(("items", "stream"), None),
        P(("items", "stream")),
        P(("items", "stream")),
        P(("items", "stream"), None),
        P(("items", "stream")),
        P(("items", "stream")),
        P(("items", "stream")),
        P(None, ("items", "stream"), None),
        P(None, ("items", "stream")),
        P(None, ("items", "stream"), None),
        P(None, ("items", "stream")),
        P(("items", "stream"), None),
    )
    near = mesh.shape["items"] == 8 and mesh.shape["stream"] == 4
    return jax.shard_map(
        functools.partial(body, near),
        mesh=mesh,
        in_specs=placed,
        out_specs=(
            P(("items", "stream"), None),
            P(("items", "stream"), None),
            P(("items", "stream")),
            P(("items", "stream")),
            P(("items", "stream"), None),
            P(("items", "stream")),
            P(("items", "stream")),
            P(("items", "stream"), None),
            P(("items", "stream")),
            P(("items", "stream")),
            P(("items", "stream")),
            P(None, ("items", "stream"), None),
            P(None, ("items", "stream")),
            P(None, ("items", "stream"), None),
            P(None, ("items", "stream")),
            P(),
        ),
        check_vma=False,
    )
```

```python
import functools

import jax
import jax.numpy as jnp
from jax import lax
from jax.experimental import pallas as pl
from jax.experimental.pallas import tpu as pltpu
from jax.sharding import PartitionSpec as P

HEADS = 12
HEAD_DIM = 64
PATCH_S = 197
PATCH_L = 577
TEXT_LEN = 40
ITEMS_S = 7
ITEMS_L = 2


NORM_EPS = 1e-05
MASKED = -1000000000.0


def layer_norm(values, gain_row, shift_row):
    row_mean = jnp.mean(values, axis=-1, keepdims=True)
    centred = values - row_mean
    variance = jnp.mean(centred * centred, axis=-1, keepdims=True)
    return centred * lax.rsqrt(variance + NORM_EPS) * gain_row + shift_row


def gelu_exact(values):
    return jax.nn.gelu(values, approximate=False)


def layout(group_type, positions, row_count):
    patch_len = jnp.where(group_type == 0, PATCH_S, PATCH_L).astype(jnp.int32)
    members = jnp.where(group_type == 0, ITEMS_S, ITEMS_L).astype(jnp.int32)
    is_patch = positions < 3 * row_count
    patch_item = positions // patch_len
    text_item = jnp.maximum(positions - 3 * row_count, 0) // TEXT_LEN
    member = jnp.where(is_patch, patch_item, text_item)
    member = jnp.where(member < members, member, -1)
    modality = jnp.where(member < 0, 2, jnp.where(is_patch, 0, 1)).astype(jnp.int32)
    return (member, modality)


def product(first_op, second_op):
    return jnp.dot(first_op, second_op, preferred_element_type=jnp.float32)


def product_lead(first_op, second_op):
    return lax.dot_general(
        first_op, second_op, (((0,), (0,)), ((), ())), preferred_element_type=jnp.float32
    )


def product_trail(first_op, second_op):
    return lax.dot_general(
        first_op, second_op, (((1,), (1,)), ((), ())), preferred_element_type=jnp.float32
    )


def halves(length):
    return ((0, length // 2), (length // 2, length // 2))


def divided(length, unit, *shares):
    found, begin = [], 0
    for share in shares:
        found.append((begin, share * unit))
        begin += share * unit
    assert begin == length
    return found


def gather_chunks(share, width, ff_share, ff):
    rows = (0, share)
    near_cols = divided(3 * width, 128, 9, 9)
    out_cols = divided(width, 128, 3, 3)
    up_cols = divided(ff, 128, 4, 14, 6)
    down_rows = divided(ff_share, 16, 1, 3, 2)
    chunks = [
        [((0, None), (0, THIN_ROWS), (0, 128), 0, False)]
        + [((1, None), rows, cols, order, False) for order, cols in enumerate(near_cols)],
        [((2, None), rows, cols, order, False) for order, cols in enumerate(out_cols)],
    ]
    for e in (1, 0):
        chunks.append([((3, e), rows, cols, order, e == 1) for order, cols in enumerate(up_cols)])
        chunks.append(
            [((4, e), band, (0, width), order, e == 1) for order, band in enumerate(down_rows)]
        )
    return chunks


def scatter_chunks(share, width, ff_share, ff):
    rows = (0, share)
    near_cols = divided(3 * width, 128, 7, 7, 4)
    out_cols = divided(width, 128, 2, 3, 1)
    up_cols = divided(ff, 128, 4, 14, 6)
    down_rows = divided(ff_share, 16, 1, 3, 2)
    chunks = [[(2, 0, rows, cols, order) for order, cols in enumerate(out_cols)]]
    for e in (1, 0):
        chunks.append([(0, e, rows, cols, order) for order, cols in enumerate(up_cols)])
        chunks.append(
            [(1, e, band, (0, width), order) for order, band in enumerate(down_rows)]
        )
    chunks += [[], [], [], []]
    chunks.append(
        [(3, 0, rows, cols, order) for order, cols in enumerate(near_cols)]
        + [(4, 0, (0, THIN_ROWS), (0, 128), 0)]
    )
    cuts = (
        (0, up_cols[2][0]),
        (down_rows[2][0], 0),
        (0, out_cols[2][0]),
        (0, near_cols[2][0]),
        (0, 0),
    )
    return chunks, cuts


TQ, TK = 256, 128
PAIR = 2 * HEAD_DIM


def trail(first_op, second_op):
    return lax.dot_general(
        first_op, second_op, (((1,), (1,)), ((), ())), preferred_element_type=jnp.float32
    )


def span(kind, start, length, image_rows):
    patch_len, members = ((PATCH_S, ITEMS_S), (PATCH_L, ITEMS_L))[kind]
    image = start < image_rows
    low = jnp.where(image, lax.div(start, patch_len), lax.div(start - image_rows, TEXT_LEN))
    high = jnp.where(
        image,
        lax.div(start + length - 1, patch_len),
        lax.div(start + length - 1 - image_rows, TEXT_LEN),
    )
    return low, high, members


def meets(first, second, image_rows, loose):
    found = False
    for kind in range(2):
        low_a, high_a, members = span(kind, *first, image_rows)
        low_b, high_b, _ = span(kind, *second, image_rows)
        low = jnp.maximum(low_a, low_b)
        high = jnp.minimum(jnp.minimum(high_a, high_b), members - 1)
        found = jnp.logical_or(found, low <= high)
        if loose:
            both = jnp.logical_and(high_a >= members, high_b >= members)
            found = jnp.logical_or(found, both)
    return found


def member_of(kind, position, image_rows):
    patch_len = PATCH_S + kind * float(PATCH_L - PATCH_S)
    members = ITEMS_S + kind * float(ITEMS_L - ITEMS_S)
    patch = jnp.floor((position + 0.5) / patch_len)
    text = jnp.floor((position - image_rows + 0.5) * (1.0 / TEXT_LEN))
    member = jnp.where(position < image_rows, patch, text)
    return jnp.where(member < members, member, -1.0)


def same_item(kind, stream, rows, qt, kt, image_rows):
    keys = lax.broadcasted_iota(jnp.int32, (TK, 1), 0) + kt * TK
    own = lax.broadcasted_iota(jnp.int32, (1, TQ), 1) + (stream * rows + qt * TQ)
    key_member = member_of(kind, keys.astype(jnp.float32), image_rows)
    return key_member == member_of(kind, own.astype(jnp.float32), image_rows)


def half_of(pair, which):
    lanes = lax.broadcasted_iota(jnp.int32, pair.shape, 1)
    return jnp.where((lanes < HEAD_DIM) == (which == 0), pair, jnp.zeros_like(pair))


def upper_of(pair, which):
    keep = pair[which * HEAD_DIM : (which + 1) * HEAD_DIM]
    parts = [keep, jnp.zeros_like(keep)]
    return jnp.concatenate(parts if which == 0 else parts[::-1], axis=0)


def scale_queries(q_ref, scaled):
    for pair in range(q_ref.shape[1] // PAIR):
        columns = slice(pair * PAIR, (pair + 1) * PAIR)
        value = (q_ref[:, columns] * jnp.bfloat16(HEAD_DIM ** (-0.5))).T
        for which in range(2):
            scaled[2 * pair + which] = upper_of(value, which)


def flip_columns(kv_ref, begin, flipped):
    width = flipped.shape[0]

    @pl.loop(0, flipped.shape[1] // TK)
    def _(kt):
        keys = pl.ds(pl.multiple_of(kt * TK, TK), TK)
        flipped[:, keys] = kv_ref[keys, begin : begin + width].T


def attend_part(qt, begin, end, kind_ref, stream, kv_ref, values_t, scaled, mixed_ref, mixed_t, log_total, top, total):
    width, everyone = values_t.shape
    rows = mixed_ref.shape[0]
    heads = width // HEAD_DIM
    image_rows = everyone - rows
    here = slice(qt * TQ, (qt + 1) * TQ)
    if begin == 0:
        top[...] = jnp.full(top.shape, -1e30, jnp.float32)
        total[...] = jnp.zeros(total.shape, jnp.float32)
        mixed_t[:, here] = jnp.zeros((width, TQ), jnp.float32)

    @pl.loop(begin, end)
    def _(kt):
        needed = meets((stream * rows + qt * TQ, TQ), (kt * TK, TK), image_rows, True)

        @pl.when(needed)
        def _():
            keys = pl.ds(pl.multiple_of(kt * TK, TK), TK)
            allowed = same_item(kind_ref[0:1, 0:1], stream, rows, qt, kt, image_rows)
            scores, parts, fades = [], [], []
            for head in range(heads):
                pair = slice(head // 2 * PAIR, (head // 2 + 1) * PAIR)
                raw = jnp.dot(
                    kv_ref[keys, pair], scaled[head, :, here], preferred_element_type=jnp.float32
                )
                scores.append(jnp.where(allowed, raw, MASKED))
            for head, score in enumerate(scores):
                line = slice(head, head + 1)
                old = top[line]
                new = jnp.maximum(old, jnp.max(score, axis=0, keepdims=True))
                top[line] = new
                fade = jnp.exp(old - new)
                part = jnp.exp(score - new)
                total[line] = total[line] * fade + jnp.sum(part, axis=0, keepdims=True)
                parts.append(part.astype(jnp.bfloat16))
                fades.append(fade)
            for head in range(heads):
                own = slice(head * HEAD_DIM, (head + 1) * HEAD_DIM)
                mixed_t[own, here] = mixed_t[own, here] * fades[head] + jnp.dot(
                    values_t[own, keys], parts[head], preferred_element_type=jnp.float32
                )

    if end == everyone // TK:
        for head in range(heads):
            own = slice(head * HEAD_DIM, (head + 1) * HEAD_DIM)
            mixed_t[own, here] = mixed_t[own, here] / total[head : head + 1]
        log_total[:, here] = top[...] + jnp.log(total[...])
        mixed_ref[here, :] = mixed_t[:, here].T.astype(jnp.bfloat16)


def attend_kernel(kind, place_ref, q_ref, kv_ref, mixed_ref, mixed_t, log_total, values_t, scaled, top, total):
    scale_queries(q_ref, scaled)
    flip_columns(kv_ref, q_ref.shape[1], values_t)
    for qt in range(q_ref.shape[0] // TQ):
        attend_part(
            qt, 0, kv_ref.shape[0] // TK, kind, place_ref[0], kv_ref, values_t, scaled, mixed_ref,
            mixed_t, log_total, top, total,
        )


def attend(kind, place_at, queries, kv):
    rows, width = queries.shape
    heads = width // HEAD_DIM
    inside = pl.BlockSpec(memory_space=pltpu.VMEM)
    lines = -(-heads // 8) * 8
    return pl.pallas_call(
        attend_kernel,
        out_shape=(
            jax.ShapeDtypeStruct((rows, width), jnp.bfloat16),
            jax.ShapeDtypeStruct((width, rows), jnp.float32),
            jax.ShapeDtypeStruct((lines, rows), jnp.float32),
        ),
        in_specs=[inside, pl.BlockSpec(memory_space=pltpu.SMEM)] + [inside] * 2,
        out_specs=(inside,) * 3,
        scratch_shapes=[
            pltpu.VMEM((width, kv.shape[0]), jnp.bfloat16),
            pltpu.VMEM((heads, PAIR, rows), jnp.bfloat16),
            pltpu.VMEM((lines, TQ), jnp.float32),
            pltpu.VMEM((lines, TQ), jnp.float32),
        ],
        compiler_params=pltpu.CompilerParams(vmem_limit_bytes=56 << 20),
    )(kind, place_at, queries, kv)


def back_group(
    group, kind, stream, log_total, keys_ref, values_ref, q_ref, g_ref, mixed_t, dq_ref, between,
    keys_t, scaled, grads, scaled_t, grads_t, dq_t, centre, dk, dv,
):
    everyone, width = keys_ref.shape
    rows = q_ref.shape[0]
    heads = width // HEAD_DIM
    image_rows = everyone - rows
    for pair in range(heads // 2):
        columns = slice(pair * PAIR, (pair + 1) * PAIR)
        value = q_ref[:, columns] * jnp.bfloat16(HEAD_DIM ** (-0.5))
        grad = g_ref[:, columns]
        value_t, grad_t = value.T, grad.T
        product = mixed_t[columns, :] * grad_t.astype(jnp.float32)
        for which in range(2):
            head = 2 * pair + which
            scaled[head] = half_of(value, which)
            grads[head] = half_of(grad, which)
            scaled_t[head] = upper_of(value_t, which)
            grads_t[head] = upper_of(grad_t, which)
            centre[head : head + 1] = jnp.sum(
                product[which * HEAD_DIM : (which + 1) * HEAD_DIM], axis=0, keepdims=True
            )
    flip_columns(keys_ref, 0, keys_t)

    @pl.loop(0, everyone // TK)
    def _(kt):
        keys = pl.ds(pl.multiple_of(kt * TK, TK), TK)
        dk[keys, :] = jnp.zeros((TK, width), jnp.float32)
        dv[keys, :] = jnp.zeros((TK, width), jnp.float32)

    for qt in range(rows // TQ):
        here = slice(qt * TQ, (qt + 1) * TQ)
        if qt:
            between()
        dq_t[...] = jnp.zeros(dq_t.shape, jnp.float32)

        @pl.loop(0, everyone // TK)
        def _(kt, qt=qt, here=here):
            needed = meets((stream * rows + qt * TQ, TQ), (kt * TK, TK), image_rows, False)

            @pl.when(needed)
            def _():
                keys = pl.ds(pl.multiple_of(kt * TK, TK), TK)
                allowed = same_item(kind[0:1, 0:1], stream, rows, qt, kt, image_rows)
                scores, prob_grads, probs_low, score_low = [], [], [], []
                for head in range(heads):
                    pair = slice(head // 2 * PAIR, (head // 2 + 1) * PAIR)
                    scores.append(
                        jnp.dot(
                            keys_ref[keys, pair],
                            scaled_t[head, :, here],
                            preferred_element_type=jnp.float32,
                        )
                    )
                    prob_grads.append(
                        jnp.dot(
                            values_ref[keys, pair],
                            grads_t[head, :, here],
                            preferred_element_type=jnp.float32,
                        )
                    )
                for head in range(heads):
                    line = slice(group * heads + head, group * heads + head + 1)
                    shifted = scores[head] - log_total[line, here]
                    probs = jnp.exp(jnp.where(allowed, shifted, MASKED))
                    probs_low.append(probs.astype(jnp.bfloat16))
                    inner = prob_grads[head] - centre[head : head + 1, here]
                    score_low.append((probs * inner).astype(jnp.bfloat16))
                for head in range(heads):
                    own = slice(head * HEAD_DIM, (head + 1) * HEAD_DIM)
                    dq_t[own, :] += jnp.dot(
                        keys_t[own, keys], score_low[head], preferred_element_type=jnp.float32
                    )
                for head in range(0, heads, 2):
                    columns = slice(head * HEAD_DIM, head * HEAD_DIM + PAIR)
                    for terms, left, right in ((dk, score_low, scaled), (dv, probs_low, grads)):
                        terms[keys, columns] += jnp.dot(
                            left[head], right[head, here, :], preferred_element_type=jnp.float32
                        ) + jnp.dot(
                            left[head + 1],
                            right[head + 1, here, :],
                            preferred_element_type=jnp.float32,
                        )

        dq_ref[here, :] = (dq_t[...].T * HEAD_DIM ** (-0.5)).astype(jnp.bfloat16)


def attend_back_kernel(
    kind, place_ref, q_ref, kv_ref, g_ref, mixed_t, log_total, dq_ref, dkv_ref, *work
):
    width = q_ref.shape[1]
    back_group(
        0, kind, place_ref[0], log_total, kv_ref.at[:, pl.ds(0, width)],
        kv_ref.at[:, pl.ds(width, width)], q_ref, g_ref, mixed_t, dq_ref, lambda: None,
        *work,
    )
    dk, dv = work[-2:]

    @pl.loop(0, kv_ref.shape[0] // TK)
    def _(kt):
        keys = pl.ds(pl.multiple_of(kt * TK, TK), TK)
        dkv_ref[keys, :width] = dk[keys, :].astype(jnp.bfloat16)
        dkv_ref[keys, width:] = dv[keys, :].astype(jnp.bfloat16)


def attend_back(kind, place_at, queries, kv, mixed_grad, mixed_t, log_total):
    rows, width = queries.shape
    heads = width // HEAD_DIM
    inside = pl.BlockSpec(memory_space=pltpu.VMEM)
    lines = -(-heads // 8) * 8
    everyone = kv.shape[0]
    return pl.pallas_call(
        attend_back_kernel,
        out_shape=(
            jax.ShapeDtypeStruct((rows, width), jnp.bfloat16),
            jax.ShapeDtypeStruct((everyone, 2 * width), jnp.bfloat16),
        ),
        in_specs=[inside, pl.BlockSpec(memory_space=pltpu.SMEM)] + [inside] * 5,
        out_specs=(inside,) * 2,
        scratch_shapes=[
            pltpu.VMEM((width, everyone), jnp.bfloat16),
            pltpu.VMEM((heads, rows, PAIR), jnp.bfloat16),
            pltpu.VMEM((heads, rows, PAIR), jnp.bfloat16),
            pltpu.VMEM((heads, PAIR, rows), jnp.bfloat16),
            pltpu.VMEM((heads, PAIR, rows), jnp.bfloat16),
            pltpu.VMEM((width, TQ), jnp.float32),
            pltpu.VMEM((lines, rows), jnp.float32),
            pltpu.VMEM((everyone, width), jnp.float32),
            pltpu.VMEM((everyone, width), jnp.float32),
        ],
        compiler_params=pltpu.CompilerParams(vmem_limit_bytes=58 << 20),
    )(kind, place_at, queries, kv, mixed_grad, mixed_t, log_total)

def feed_kernel(
    pick, place_ref, kind, vectors, up_shift, tokens, mixed, out_weight, cotangent, up, down,
    output, residual_grad, grad_out, mixed_grad, grad_up, grad_down, small, up_shift_sum,
    residual, normed, normed_t, grad, branch, back,
):
    step = pl.program_id(0)
    rows, width = tokens.shape
    image_rows = (lax.axis_size("stream") - 1) * rows
    tall = 128

    def blocks(act):
        @pl.loop(0, rows // tall)
        def _(j):
            act(pl.ds(pl.multiple_of(j * tall, tall), tall))

    def unit_of(value):
        centred = value - jnp.mean(value, axis=-1, keepdims=True)
        scale = lax.rsqrt(jnp.mean(centred * centred, axis=-1, keepdims=True) + NORM_EPS)
        return centred * scale, scale

    def live(j_start):
        position = lax.broadcasted_iota(jnp.int32, (tall, 1), 0) + (place_ref[0] * rows + j_start)
        return member_of(kind[0:1, 0:1], position.astype(jnp.float32), image_rows) >= 0.0

    @pl.when(step == 0)
    def _():
        @pl.loop(0, rows // tall)
        def _(j):
            block = pl.ds(pl.multiple_of(j * tall, tall), tall)
            value = (
                tokens[block, :].astype(jnp.float32)
                + jnp.dot(mixed[block, :], out_weight[...], preferred_element_type=jnp.float32)
                + vectors[4:5, :]
            )
            residual[block, :] = value
            unit, _ = unit_of(value)
            normed[block, :] = (unit * vectors[5:6, :] + vectors[6:7, :]).astype(jnp.bfloat16)
            given = cotangent[block, :]
            grad[block, :] = jnp.where(live(j * tall), given, jnp.zeros_like(given))

        normed_t[...] = normed[...].T
        branch[...] = jnp.zeros(branch.shape, jnp.float32)
        back[...] = jnp.zeros(back.shape, jnp.float32)

    before = (
        jnp.dot(normed[...], up[0], preferred_element_type=jnp.float32) + up_shift[0].astype(jnp.float32)
    )
    hidden_grad = product_trail(grad[...], down[0])
    half = 0.5 + 0.5 * lax.erf(before * 0.5**0.5)
    hidden = (before * half).astype(jnp.bfloat16)
    slope = half + before * (jnp.exp(-0.5 * before * before) * 0.3989422804014327)
    before_grad = hidden_grad * slope
    low_grad = before_grad.astype(jnp.bfloat16)
    up_shift_sum[...] = jnp.broadcast_to(
        jnp.sum(low_grad.astype(jnp.float32), axis=0, keepdims=True), up_shift_sum.shape
    )
    branch[...] += jnp.dot(hidden, down[0], preferred_element_type=jnp.float32)
    back[...] += product_trail(low_grad, up[0])
    grad_up[...] = jnp.dot(normed_t[...], low_grad, preferred_element_type=jnp.float32).astype(
        jnp.bfloat16
    )
    grad_down[...] = jnp.dot(hidden.T, grad[...], preferred_element_type=jnp.float32).astype(
        jnp.bfloat16
    )

    @pl.when(step == pl.num_programs(0) - 1)
    def _():
        down_shift = jnp.where(pick[0] == 0, vectors[9:10, :], vectors[10:11, :])

        def fold(value):
            return jnp.sum(value.reshape(-1, 8, width), axis=0)

        def finish(j, carry):
            block = pl.ds(pl.multiple_of(j * tall, tall), tall)
            value = residual[block, :]
            kept = live(j * tall)
            output[block, :] = (
                value + jnp.where(kept, branch[block, :] + down_shift, 0.0)
            ).astype(jnp.bfloat16)
            unit, scale = unit_of(value)
            given = back[block, :]
            lifted = given * vectors[5:6, :]
            inner = jnp.mean(lifted * unit, axis=-1, keepdims=True)
            own = grad[block, :].astype(jnp.float32)
            total = own + scale * (
                lifted - jnp.mean(lifted, axis=-1, keepdims=True) - unit * inner
            )
            residual_grad[block, :] = total
            total_low = total.astype(jnp.bfloat16)
            normed[block, :] = total_low
            mixed_grad[block, :] = product_trail(total_low, out_weight[...]).astype(jnp.bfloat16)
            terms = (total_low.astype(jnp.float32), given * unit, given, own)
            return tuple(held + fold(term) for held, term in zip(carry, terms))

        zero = jnp.zeros((8, width), jnp.float32)
        sums = lax.fori_loop(0, rows // tall, finish, (zero,) * 4)
        lines = [jnp.sum(value, axis=0, keepdims=True) for value in sums]
        small[...] = jnp.concatenate(lines + [jnp.zeros((4, width), jnp.float32)], axis=0)
        grad_out[...] = jnp.dot(
            mixed[...].T, normed[...], preferred_element_type=jnp.float32
        ).astype(jnp.bfloat16)


def feed(pick, place_at, kind, vectors, up_shift, tokens, mixed, out_weight, cotangent, up, down):
    rows, width = tokens.shape
    ff = up.shape[2]
    band = 512
    low, wide = jnp.bfloat16, jnp.float32

    def whole(array):
        return pl.BlockSpec(array.shape, lambda i, pick, place_at: (0,) * array.ndim)

    fixed = [
        jax.ShapeDtypeStruct((rows, width), low),
        jax.ShapeDtypeStruct((rows, width), wide),
        jax.ShapeDtypeStruct((width, width), low),
        jax.ShapeDtypeStruct((rows, width), low),
    ]
    last = jax.ShapeDtypeStruct((8, width), wide)
    return pl.pallas_call(
        feed_kernel,
        out_shape=fixed
        + [
            jax.ShapeDtypeStruct((width, ff), low),
            jax.ShapeDtypeStruct((ff, width), low),
            last,
            jax.ShapeDtypeStruct((8, ff), wide),
        ],
        grid_spec=pltpu.PrefetchScalarGridSpec(
            num_scalar_prefetch=2,
            grid=(ff // band,),
            in_specs=[
                whole(kind),
                whole(vectors),
                pl.BlockSpec((1, 1, band), lambda i, pick, place_at: (pick[0], 0, i)),
                whole(tokens),
                whole(mixed),
                whole(out_weight),
                whole(cotangent),
                pl.BlockSpec((1, width, band), lambda i, pick, place_at: (pick[0], 0, i)),
                pl.BlockSpec((1, band, width), lambda i, pick, place_at: (pick[0], i, 0)),
            ],
            out_specs=[whole(array) for array in fixed]
            + [
                pl.BlockSpec((width, band), lambda i, pick, place_at: (0, i)),
                pl.BlockSpec((band, width), lambda i, pick, place_at: (i, 0)),
                whole(last),
                pl.BlockSpec((8, band), lambda i, pick, place_at: (0, i)),
            ],
            scratch_shapes=[
                pltpu.VMEM((rows, width), wide),
                pltpu.VMEM((rows, width), low),
                pltpu.VMEM((width, rows), low),
                pltpu.VMEM((rows, width), low),
                pltpu.VMEM((rows, width), wide),
                pltpu.VMEM((rows, width), wide),
            ],
        ),
        compiler_params=pltpu.CompilerParams(vmem_limit_bytes=56 << 20),
    )(pick, place_at, kind, vectors, up_shift, tokens, mixed, out_weight, cotangent, up, down)


MESH = pl.DeviceIdType.MESH
GATHER_ORDERS = (("z", "f", "x", "y"), ("z", "f", "y", "x"), ("y", "x", "z", "f"))
SCATTER_ORDERS = (("y", "x", "a", "z"), ("x", "y", "a", "z"), ("a", "z", "x", "y"))
STEPS = 5
EVERY = slice(None)
THIN_ROWS = 16


def coords():
    items, stream = lax.axis_index("items"), lax.axis_index("stream")
    return dict(z=items // 2, x=items % 2, y=stream // 2, c=stream % 2)


def place(at):
    return (at["z"] * 2 + at["x"], at["y"] * 2 + at["c"])


def moved(at, dim, by, depth):
    return {**at, dim: lax.rem(at[dim] + by, depth if dim == "z" else 2)}


def greet(at, depth):
    peers = [moved(at, "z", k, depth) for k in range(1, depth)]
    peers += [moved(at, d, 1, depth) for d in "xyc"]
    barrier = pltpu.get_barrier_semaphore()
    for peer in peers:
        pl.semaphore_signal(barrier, inc=1, device_id=place(peer), device_id_type=MESH)
    pl.semaphore_wait(barrier, len(peers))


def guard(cond, act):
    if cond is None:
        act()
    else:
        pl.when(cond)(act)


def remote(src, dst, sems, index, device):
    return pltpu.make_async_remote_copy(
        src_ref=src,
        dst_ref=dst,
        send_sem=sems[0].at[index],
        recv_sem=sems[1].at[index],
        device_id=place(device),
        device_id_type=MESH,
    )


def both_of(first, second):
    if first is None or second is None:
        return second if first is None else first
    return jnp.logical_and(first, second)


class Pipeline:
    def __init__(self, chunks, ahead, start, wait):
        self.chunks, self.ahead, self.start, self.wait = chunks, ahead, start, wait
        self.ticks = 0
        for chunk in chunks[:ahead]:
            start(chunk, 0)

    def tick(self, times=1):
        count = len(self.chunks)
        for t in range(self.ticks, min(self.ticks + times, count + STEPS - 1)):
            if t + self.ahead < count:
                self.start(self.chunks[t + self.ahead], 0)
            for step in range(STEPS):
                if 0 <= t - step < count:
                    self.wait(self.chunks[t - step], step)
                    if step < STEPS - 1:
                        self.start(self.chunks[t - step], step + 1)
        self.ticks += times


def spots_of(depth):
    return [(a, b, c, d) for a in range(depth) for b in range(2) for c in range(2) for d in range(2)]


def columns_over(share, width):
    column = lax.broadcasted_iota(jnp.int32, (1, width), 1).astype(jnp.float32)
    owner = jnp.floor((column + 0.5) * (1.0 / share))
    return owner, column - owner * share


def spread(thin, share, width):
    owner, lane = columns_over(share, width)
    picks = lax.broadcasted_iota(jnp.int32, (128, width), 0).astype(jnp.float32) == lane
    wide = jnp.dot(thin, picks.astype(jnp.bfloat16), preferred_element_type=jnp.float32)
    total = jnp.zeros((THIN_ROWS, width), jnp.float32)
    for device in range(thin.shape[0] // THIN_ROWS):
        part = wide[device * THIN_ROWS : (device + 1) * THIN_ROWS]
        total = total + jnp.where(owner == device, part, 0.0)
    return total


def dealt(rows, share, devices):
    width = rows.shape[1]
    owner, lane = columns_over(share, width)
    picks = lax.broadcasted_iota(jnp.int32, (128, width), 0).astype(jnp.float32) == lane
    tall = jnp.concatenate(
        [jnp.where(owner == device, rows, 0.0) for device in range(devices)], axis=0
    )
    return lax.dot_general(
        tall,
        picks.astype(jnp.float32),
        (((1,), (1,)), ((), ())),
        precision=lax.Precision.HIGHEST,
        preferred_element_type=jnp.float32,
    )


def gather_kernel(depth, chunks, entries, *refs):
    it = iter(refs)
    take = lambda count: [next(it) for _ in range(count)]
    ins = take(5)
    tokens, kind = take(2)
    thin_out, out_all, up_all, down_all = take(4)
    qkv_weight, normed, queries, vectors, kv_out, mixed, mixed_t, log_total = take(8)
    thin_all, qkv_all, kv, values_t, scaled, top, total = take(7)
    local_sem = next(it)
    sems, kv_sems = take(2), take(2)
    keep_sem = next(it)
    outs = (thin_all, qkv_all, out_all, up_all, down_all)
    rows, width = tokens.shape
    devices = depth * 8
    share = width // devices
    at = coords()
    mine = (at["z"], at["x"], at["y"], at["c"])
    slot = at["y"] * 2 + at["c"]

    def source(entry):
        k, e = entry
        return ins[k] if e is None else ins[k].at[e]

    def target(entry):
        k, e = entry
        return outs[k] if e is None else outs[k].at[e]

    local = [
        pltpu.make_async_copy(source(entry), target(entry).at[mine], local_sem.at[j])
        for j, entry in enumerate(entries)
    ]
    for copy in local:
        copy.start()
    greet(at, depth)
    for copy in local:
        copy.wait()
    lower, upper = at["y"] == 0, at["y"] == 1
    number = {piece: j for j, piece in enumerate(piece for chunk in chunks for piece in chunk)}

    z = at["z"]

    def stage(piece, step):
        entry, band, cols, order, text = piece
        dims = GATHER_ORDERS[order] + ("c",)
        dim = dims[step]
        box = (pl.ds(*band), pl.ds(*cols))
        live = upper if text and "y" in dims[:step] else None

        def held(level):
            spot = {d: EVERY if d in dims[:step] else pl.ds(at[d], 1) for d in "zxyc"}
            if level is not None:
                spot["z"] = pl.ds(level, 1)
            return target(entry).at[tuple(spot[d] for d in "zxyc") + box]

        if dim == "f":
            up_view, down_view = held(0), held(depth - 1)
            up = remote(up_view, up_view, sems, (number[piece], depth + 2), {**at, "z": z + 1})
            down = remote(down_view, down_view, sems, (number[piece], depth + 2), {**at, "z": z - 1})
            return [
                (up, both_of(live, z == depth - 2), both_of(live, z == depth - 1)),
                (down, both_of(live, z == 1), both_of(live, z == 0)),
            ]
        view = held(None)
        if dim == "z":
            found = []
            for k in range(1, depth):
                to, source_level = lax.rem(z + k, depth), lax.rem(z + depth - k, depth)
                copy = remote(view, view, sems, (number[piece], k - 1), {**at, "z": to})
                sends = both_of(live, jnp.abs(to - z) != depth - 1)
                found.append((copy, sends, both_of(live, jnp.abs(source_level - z) != depth - 1)))
            return found
        sem = {"x": depth - 1, "y": depth, "c": depth + 1}[dim]
        copy = remote(view, view, sems, (number[piece], sem), moved(at, dim, 1, depth))
        if text and dim == "y":
            return [(copy, lower, upper)]
        return [(copy, live, live)]

    def each(chunk, step, which, call):
        for piece in chunk:
            for found in stage(piece, step):
                guard(found[which], functools.partial(call, found[0]))

    beside, across = moved(at, "c", 1, depth), moved(at, "y", 1, depth)
    other = across["y"] * 2 + across["c"]
    own_slot = pl.ds(pl.multiple_of(slot * rows, rows), rows)
    other_slot = pl.ds(pl.multiple_of(other * rows, rows), rows)
    to_across = remote(kv.at[own_slot], kv.at[own_slot], kv_sems, 0, across)
    to_beside = remote(kv.at[own_slot], kv.at[own_slot], kv_sems, 1, beside)
    onward = remote(kv.at[other_slot], kv.at[other_slot], kv_sems, 2, beside)
    keep_thin = pltpu.make_async_copy(thin_all, thin_out, keep_sem.at[0])
    keep_kv = pltpu.make_async_copy(kv, kv_out, keep_sem.at[1])

    def project():
        spots = spots_of(depth)
        for j, spot in enumerate(spots):
            qkv_weight[j * share : (j + 1) * share, :] = qkv_all[spot]
        thin = jnp.concatenate([thin_all[spot] for spot in spots], axis=0)
        vectors[...] = spread(thin, share, width)

        @pl.loop(0, rows // 128)
        def _(j):
            block = pl.ds(pl.multiple_of(j * 128, 128), 128)
            value = tokens[block, :].astype(jnp.float32)
            centred = value - jnp.mean(value, axis=-1, keepdims=True)
            scale = lax.rsqrt(jnp.mean(centred * centred, axis=-1, keepdims=True) + NORM_EPS)
            normed[block, :] = (centred * scale * vectors[0:1, :] + vectors[1:2, :]).astype(
                jnp.bfloat16
            )

        step = width // 2
        for part in (1, 2, 0):

            @pl.loop(0, 2)
            def _(j, part=part):
                cols = pl.ds(pl.multiple_of(j * step, 128), step)
                value = jnp.dot(
                    normed[...],
                    qkv_weight[:, pl.ds(pl.multiple_of(part * width + j * step, 128), step)],
                    preferred_element_type=jnp.float32,
                )
                if part == 0:
                    queries[:, cols] = (value + vectors[2:3, cols]).astype(jnp.bfloat16)
                elif part == 1:
                    kv[own_slot, cols] = value.astype(jnp.bfloat16)
                else:
                    kv[own_slot, pl.ds(pl.multiple_of(width + j * step, 128), step)] = (
                        value + vectors[3:4, cols]
                    ).astype(jnp.bfloat16)

            if part == 2:
                to_across.start()
                to_beside.start()
                keep_thin.start()
        scale_queries(queries, scaled)

    def pass_on():
        to_across.wait_recv()
        onward.start()

    def attend_first():
        to_beside.wait_recv()
        onward.wait_recv()
        keep_kv.start()
        flip_columns(kv, width, values_t)

    parts = (kind, slot, kv, values_t, scaled, mixed, mixed_t, log_total, top, total)

    def attention(qt, begin, end):
        def act():
            if qt == 0 and begin == 0:
                attend_first()
            attend_part(qt, begin, end, *parts)

        return act

    everyone = kv.shape[0] // TK
    flow = Pipeline(
        chunks,
        2,
        lambda chunk, step: each(chunk, step, 1, lambda copy: copy.start()),
        lambda chunk, step: each(chunk, step, 2, lambda copy: copy.wait_recv()),
    )
    flow.tick(5)
    project()
    flow.tick()
    pass_on()
    flow.tick()
    attention(0, 0, everyone // 2)()
    flow.tick()
    attention(0, everyone // 2, everyone)()
    flow.tick()
    attention(1, 0, everyone // 2)()
    flow.tick()
    attention(1, everyone // 2, everyone)()
    flow.tick(STEPS + len(chunks))
    for copy in (to_beside, to_across, onward):
        copy.wait_send()
    keep_thin.wait()
    keep_kv.wait()
    for chunk in chunks:
        for step in range(STEPS):
            each(chunk, step, 1, lambda copy: copy.wait_send())


def gather_all(thin, w_qkv, w_out, w_up, w_down, tokens, kind, depth):
    rows, width = tokens.shape
    share, ff_share, ff = w_qkv.shape[0], w_down.shape[1], w_up.shape[2]
    entries = [(0, None), (1, None), (2, None), (3, 0), (3, 1), (4, 0), (4, 1)]
    chunks = gather_chunks(share, width, ff_share, ff)
    n_pieces = sum(len(chunk) for chunk in chunks)
    anywhere = pl.BlockSpec(memory_space=pl.ANY)
    inside = pl.BlockSpec(memory_space=pltpu.VMEM)
    low = jnp.bfloat16
    box = (depth, 2, 2, 2)
    heads, lines = width // HEAD_DIM, -(-(width // HEAD_DIM) // 8) * 8
    return pl.pallas_call(
        functools.partial(gather_kernel, depth, chunks, entries),
        out_shape=[
            jax.ShapeDtypeStruct(box + thin.shape, low),
            jax.ShapeDtypeStruct(box + (share, width), low),
            jax.ShapeDtypeStruct((2,) + box + (share, ff), low),
            jax.ShapeDtypeStruct((2,) + box + (ff_share, width), low),
            jax.ShapeDtypeStruct((width, 3 * width), low),
            jax.ShapeDtypeStruct((rows, width), low),
            jax.ShapeDtypeStruct((rows, width), low),
            jax.ShapeDtypeStruct((THIN_ROWS, width), jnp.float32),
            jax.ShapeDtypeStruct((4 * rows, 2 * width), low),
            jax.ShapeDtypeStruct((rows, width), low),
            jax.ShapeDtypeStruct((width, rows), jnp.float32),
            jax.ShapeDtypeStruct((lines, rows), jnp.float32),
        ],
        in_specs=[anywhere] * 5 + [inside] * 2,
        out_specs=[anywhere] * 4 + [inside] * 4 + [anywhere] + [inside] * 3,
        scratch_shapes=[
            pltpu.VMEM(box + thin.shape, low),
            pltpu.VMEM(box + (share, 3 * width), low),
            pltpu.VMEM((4 * rows, 2 * width), low),
            pltpu.VMEM((width, 4 * rows), low),
            pltpu.VMEM((heads, PAIR, rows), low),
            pltpu.VMEM((lines, TQ), jnp.float32),
            pltpu.VMEM((lines, TQ), jnp.float32),
            pltpu.SemaphoreType.DMA((len(entries),)),
            pltpu.SemaphoreType.DMA((n_pieces, depth + 3)),
            pltpu.SemaphoreType.DMA((n_pieces, depth + 3)),
            pltpu.SemaphoreType.DMA((3,)),
            pltpu.SemaphoreType.DMA((3,)),
            pltpu.SemaphoreType.DMA((2,)),
        ],
        compiler_params=pltpu.CompilerParams(
            collective_id=1, has_side_effects=True, vmem_limit_bytes=48 << 20
        ),
    )(thin, w_qkv, w_out, w_up, w_down, tokens, kind)


def scatter_kernel(depth, kinds, chunks, cuts, *refs):
    n, n_far = len(kinds), 3
    it = iter(refs)
    take = lambda count: [next(it) for _ in range(count)]
    far = take(n_far)
    factor, small, up_shift_sum, vectors, kind, log_total = take(6)
    queries, kv, mixed_grad, mixed_t, normed, weight, tokens, residual_grad = take(8)
    outs = take(n)
    token_grad, kv_away = take(2)
    acc, first, second, last = take(n), take(n), take(n), take(n)
    relay, z_relay, z_first, z_second, z_last = (take(n) for _ in range(5))
    own_half = take(n_far)
    qkv_terms, thin_terms, kv_sum, kv_got, kv_mine, dq = take(6)
    sems = take(2)
    local_sem, away_sem = take(2)
    kv_sems = take(2)
    rows, width = residual_grad.shape
    devices = depth * 8
    share = width // devices
    at = coords()
    z, x, y, c = (at[d] for d in "zxyc")
    ins = far + [qkv_terms, thin_terms]
    local = [
        pltpu.make_async_copy(far[k].at[EVERY, EVERY, EVERY, c], own_half[k], local_sem.at[k])
        for k in range(n_far)
    ]
    for copy in local:
        copy.start()
    greet(at, depth)
    for copy in local:
        copy.wait()
    beside, across = moved(at, "c", 1, depth), moved(at, "y", 1, depth)
    kv_beside = remote(kv_away, kv_sum, kv_sems, 0, beside)
    kv_across = remote(kv_sum.at[1 - y], kv_got, kv_sems, 1, across)
    lower, upper = y == 0, y == 1
    text_device = jnp.logical_and(upper, c == 1)
    image_device = jnp.logical_or(lower, c == 0)
    beside_text = jnp.logical_and(upper, c == 0)
    beside_image = jnp.logical_or(lower, c == 1)
    number = {piece: j for j, piece in enumerate(piece for chunk in chunks for piece in chunk)}

    sources = (
        (z == 0, range(2, depth)),
        (jnp.logical_and(z > 0, z < depth - 1), range(1, depth)),
        (z == depth - 1, range(1, depth - 1)),
    )

    def boxes(piece):
        k, e, band, cols, order = piece
        cut = cuts[k] if order == 2 else (0, 0)
        return (
            (pl.ds(*band), pl.ds(*cols)),
            (pl.ds(band[0] - cut[0], band[1]), pl.ds(cols[0] - cut[1], cols[1])),
        )

    def copies_of(piece, step):
        k, e, band, cols, order = piece
        box, inner = boxes(piece)
        image, text = kinds[k] and e == 0, kinds[k] and e == 1
        dims = ("c",) + SCATTER_ORDERS[order]
        dim = dims[step]
        here = acc[k].at[e]

        def make(src, dst, sem, by=1):
            return remote(src, dst, sems, (number[piece], sem), moved(at, dim, by, depth))

        sends = recvs = None
        if dim == "c":
            if image:
                sends, recvs = image_device, beside_image
            elif text:
                sends, recvs = text_device, beside_text
            src = ins[k].at[(EVERY, EVERY, EVERY, 1 - c) + box]
            return [(make(src, here.at[(EVERY, EVERY, EVERY) + box], 0), sends, recvs)]
        if text and dim == "y":
            sends, recvs = upper, lower
        elif text and "y" not in dims[:step]:
            sends = recvs = upper
        where = (EVERY, EVERY) if order == 2 else (x, y)
        if dim == "a":
            src = here.at[(depth - 1 - z,) + where + box]
            dst = z_relay[k].at[(e, EVERY, EVERY) + inner] if order == 2 else relay[k].at[(e,) + inner]
            to = {**at, "z": jnp.where(z == 0, 1, depth - 2)}
            copy = remote(src, dst, sems, (number[piece], depth + 2), to)
            ends = jnp.logical_or(z == 0, z == depth - 1)
            middle = jnp.logical_and(z > 0, z < depth - 1)
            return [(copy, both_of(sends, ends), both_of(recvs, middle))]
        if dim == "z":
            found = []
            for by in range(1, depth):
                to, source_level = lax.rem(z + by, depth), lax.rem(z + depth - by, depth)
                src = here.at[(to,) + where + box]
                if order == 2:
                    dst = z_first[k].at[(e, by - 1, EVERY, EVERY) + inner]
                else:
                    dst = last[k].at[(e, by - 1) + inner]
                found.append(
                    (
                        make(src, dst, 2 + by, by),
                        both_of(sends, jnp.abs(to - z) != depth - 1),
                        both_of(recvs, jnp.abs(source_level - z) != depth - 1),
                    )
                )
            return found
        if order == 2 and dim == "x":
            src, dst = here.at[(z, 1 - x, EVERY) + box], z_second[k].at[(e, EVERY) + inner]
            return [(make(src, dst, 1), sends, recvs)]
        if order == 2:
            src, dst = here.at[(z, x, 1 - y) + box], z_last[k].at[(e,) + inner]
            return [(make(src, dst, 2), sends, recvs)]
        if step == 1:
            spot = (EVERY, EVERY, 1 - y) if dim == "y" else (EVERY, 1 - x, EVERY)
            dst = first[k].at[(e, EVERY, EVERY) + inner]
        else:
            spot = (EVERY, x, 1 - y) if dim == "y" else (EVERY, 1 - x, y)
            dst = second[k].at[(e, EVERY) + inner]
        return [(make(here.at[spot + box], dst, step), sends, recvs)]

    def combine(piece, step):
        k, e, band, cols, order = piece
        box, inner = boxes(piece)
        image, text = kinds[k] and e == 0, kinds[k] and e == 1
        dims = ("c",) + SCATTER_ORDERS[order]
        dim = dims[step]
        here = acc[k].at[e]

        def over(spots, value_of, keep):
            @pl.loop(0, depth)
            def _(level):
                for index, spot in enumerate(spots):
                    where = (level,) + spot + box
                    value = value_of(level, index, spot)
                    here[where] = value if keep else here[where] + value

        def wide(value):
            return value.astype(jnp.float32)

        if step == 0:
            spots = [(0, 0), (0, 1), (1, 0), (1, 1)]

            def own(level, index, spot):
                if k < n_far:
                    return own_half[k][(level,) + spot + box]
                return ins[k][(level,) + spot + (c,) + box]

            if image:
                pl.when(lower)(lambda: over(spots, own, False))
                pl.when(beside_text)(lambda: over(spots, own, True))
            elif text:
                pl.when(text_device)(lambda: over(spots, own, True))
            else:
                over(spots, own, False)
        elif dim == "a":
            dest = jnp.where(z == 1, depth - 1, 0)

            def act():
                if order == 2:
                    for spot in [(0, 0), (0, 1), (1, 0), (1, 1)]:
                        where = (dest,) + spot + box
                        here[where] = here[where] + z_relay[k][(e,) + spot + inner]
                else:
                    where = (dest, x, y) + box
                    here[where] = here[where] + relay[k][(e,) + inner]

            middle = jnp.logical_and(z > 0, z < depth - 1)
            guard(both_of(upper if text and order == 2 else None, middle), act)
        elif step == STEPS - 1:

            def finish(total):
                if kinds[k]:
                    total = total * factor[0:1, e * 128 : e * 128 + 1]
                outs[k][(e,) + box] = total

            def own():
                return wide(here[(z, x, y) + box])

            if order == 2:
                got = lambda: wide(z_last[k][(e,) + inner])
                if text:
                    pl.when(lower)(lambda: finish(got()))
                    pl.when(upper)(lambda: finish(own()))
                else:
                    finish(own() + got())
            else:
                for cond, bys in sources:

                    @pl.when(cond)
                    def _(bys=bys):
                        total = own()
                        for by in bys:
                            total = total + wide(last[k][(e, by - 1) + inner])
                        finish(total)
        elif dim == "z":
            for cond, bys in sources:

                def act(bys=bys):
                    for spot in [(0, 0), (0, 1), (1, 0), (1, 1)]:
                        where = (z,) + spot + box
                        total = wide(here[where])
                        for by in bys:
                            total = total + wide(z_first[k][(e, by - 1) + spot + inner])
                        here[where] = total.astype(here.dtype)

                guard(both_of(upper if text else None, cond), act)
        elif order == 2:

            def act():
                for other in range(2):
                    where = (z, x, other) + box
                    here[where] = here[where] + z_second[k][(e, other) + inner]

            guard(upper if text else None, act)
        elif step == 1:
            spots = [(0, y), (1, y)] if dim == "y" else [(x, 0), (x, 1)]
            got = lambda level, index, spot: first[k][(e, level, index) + inner]
            if text and dim == "y":
                pl.when(lower)(lambda: over(spots, got, True))
            elif text:
                pl.when(upper)(lambda: over(spots, got, False))
            else:
                over(spots, got, False)
        else:
            got = lambda level, index, spot: second[k][(e, level) + inner]
            if text and dim == "y":
                pl.when(lower)(lambda: over([(x, y)], got, True))
            else:
                over([(x, y)], got, False)

    def start(chunk, step):
        for piece in chunk:
            for copy, sends, _ in copies_of(piece, step):
                guard(sends, copy.start)

    def wait(chunk, step):
        for piece in chunk:
            for copy, _, recvs in copies_of(piece, step):
                guard(recvs, copy.wait_recv)
            combine(piece, step)

    def halve():
        kv_beside.wait_recv()

        @pl.loop(0, rows // 64)
        def _(j):
            block = pl.ds(pl.multiple_of(j * 64, 64), 64)
            for level in range(2):
                kv_sum[level, block, :] = kv_sum[level, block, :] + kv_mine[level, block, :]

        kv_across.start()

    def project_back(qkv_grad, flipped, normed_in, weight_in, tokens_in, residual_in, token_out):
        pairs = [(normed, normed_in), (weight, weight_in), (tokens, tokens_in), (residual_grad, residual_in)]
        loads = [pltpu.make_async_copy(src, dst, away_sem.at[j]) for j, (src, dst) in enumerate(pairs)]
        for copy in loads:
            copy.start()
        for copy in loads:
            copy.wait()
        flipped[...] = normed_in[...].T
        qkv_grad[:, :width] = dq[...]
        kv_across.wait_recv()

        def fold(value):
            return jnp.sum(value.reshape(-1, 8, width), axis=0)

        zero = jnp.zeros((8, width), jnp.float32)

        def join(j, carry):
            block = pl.ds(pl.multiple_of(j * 64, 64), 64)
            total = (
                kv_sum[y, block, :].astype(jnp.float32) + kv_got[block, :].astype(jnp.float32)
            ).astype(jnp.bfloat16)
            qkv_grad[block, width:] = total
            return (
                carry[0] + fold(dq[block, :].astype(jnp.float32)),
                carry[1] + fold(total[:, width:].astype(jnp.float32)),
            )

        sum_q, sum_v = lax.fori_loop(0, rows // 64, join, (zero, zero))
        step = width // 2
        spots = spots_of(depth)

        @pl.loop(0, 6)
        def _(j):
            cols = pl.ds(pl.multiple_of(j * step, 128), step)
            value = jnp.dot(
                flipped[...], qkv_grad[:, cols], preferred_element_type=jnp.float32
            ).astype(jnp.bfloat16)
            for index, spot in enumerate(spots):
                qkv_terms[spot + (EVERY, cols)] = value[index * share : (index + 1) * share]

        def back(j, carry):
            block = pl.ds(pl.multiple_of(j * 128, 128), 128)
            value = tokens_in[block, :].astype(jnp.float32)
            centred = value - jnp.mean(value, axis=-1, keepdims=True)
            scale = lax.rsqrt(jnp.mean(centred * centred, axis=-1, keepdims=True) + NORM_EPS)
            unit = centred * scale
            grad = product_trail(qkv_grad[block, :], weight_in[...])
            lifted = grad * vectors[0:1, :]
            inner = jnp.mean(lifted * unit, axis=-1, keepdims=True)
            part = scale * (lifted - jnp.mean(lifted, axis=-1, keepdims=True) - unit * inner)
            token_out[block, :] = (residual_in[block, :] + part).astype(jnp.bfloat16)
            return carry[0] + fold(grad * unit), carry[1] + fold(grad)

        sum_gain, sum_shift = lax.fori_loop(0, rows // 128, back, (zero, zero))
        store = pltpu.make_async_copy(token_out, token_grad, away_sem.at[0])
        store.start()
        lines = [jnp.sum(value, axis=0, keepdims=True) for value in (sum_gain, sum_shift, sum_q, sum_v)]
        def stack(parts):
            count = sum(part.shape[0] for part in parts)
            return jnp.concatenate(parts + [jnp.zeros((8 - count, parts[0].shape[1]), jnp.float32)])

        scales = [
            jnp.where(text_device == (e == 1), factor[0:1, e * 128 : e * 128 + 1], 0.0)
            for e in range(2)
        ]
        down_part = [small[3:4, :] * scale for scale in scales]
        up_part = [up_shift_sum[0:1, :] * scale for scale in scales]
        ff = up_shift_sum.shape[1]
        head = dealt(stack(lines + [small[0:3, :]]), share, devices)
        tail = dealt(stack(down_part), share, devices) + dealt(
            stack([jnp.zeros((2, ff), jnp.float32)] + up_part), ff // devices, devices
        )
        for index, spot in enumerate(spots):
            rows_of = slice(index * 8, (index + 1) * 8)
            thin_terms[spot] = jnp.concatenate([head[rows_of], tail[rows_of]], axis=0)
        store.wait()

    def project_scope():
        low = jnp.bfloat16
        pl.run_scoped(
            project_back,
            pltpu.VMEM((rows, 3 * width), low),
            pltpu.VMEM((width, rows), low),
            pltpu.VMEM((rows, width), low),
            pltpu.VMEM((width, 3 * width), low),
            pltpu.VMEM((rows, width), low),
            pltpu.VMEM((rows, width), jnp.float32),
            pltpu.VMEM((rows, width), low),
        )

    group_width = width // 2
    stream = y * 2 + c

    def attention(group):
        cols = pl.ds(group * group_width, group_width)
        value_cols = pl.ds(width + group * group_width, group_width)

        def act(keys, values, q_in, g_in, mixed_in, *work):
            pairs = [
                (kv.at[:, cols], keys),
                (kv.at[:, value_cols], values),
                (queries.at[:, cols], q_in),
                (mixed_grad.at[:, cols], g_in),
                (mixed_t.at[cols, :], mixed_in),
            ]
            loads = [pltpu.make_async_copy(src, dst, away_sem.at[j]) for j, (src, dst) in enumerate(pairs)]
            for copy in loads:
                copy.start()
            for copy in loads:
                copy.wait()
            back_group(
                group, kind, stream, log_total, keys, values, q_in, g_in, mixed_in,
                dq.at[:, cols], flow.tick, *work,
            )
            dk, dv = work[-2:]
            for part, (terms, rest, begin) in enumerate(((dk, keys, cols), (dv, values, value_cols))):
                for level in range(2):
                    mine = (level * 2 + c) * rows
                    away = (level * 2 + 1 - c) * rows

                    @pl.loop(0, rows // 128)
                    def _(j, level=level, mine=mine, away=away, terms=terms, rest=rest, begin=begin):
                        to = pl.ds(pl.multiple_of(j * 128, 128), 128)
                        kept = pl.ds(pl.multiple_of(mine + j * 128, 128), 128)
                        sent = pl.ds(pl.multiple_of(away + j * 128, 128), 128)
                        kv_mine[level, to, begin] = terms[kept, :].astype(jnp.bfloat16)
                        rest[sent, :] = terms[sent, :].astype(jnp.bfloat16)

            stores = []
            for part, (rest, begin) in enumerate(((keys, cols), (values, value_cols))):
                for level in range(2):
                    sent = pl.ds(pl.multiple_of((level * 2 + 1 - c) * rows, rows), rows)
                    stores.append(
                        pltpu.make_async_copy(
                            rest.at[sent], kv_away.at[level, :, begin], away_sem.at[part * 2 + level]
                        )
                    )
            for copy in stores:
                copy.start()
            for copy in stores:
                copy.wait()
            if group == 1:
                kv_beside.start()

        def scope():
            low = jnp.bfloat16
            heads = group_width // HEAD_DIM
            everyone = 4 * rows
            pl.run_scoped(
                act,
                pltpu.VMEM((everyone, group_width), low),
                pltpu.VMEM((everyone, group_width), low),
                pltpu.VMEM((rows, group_width), low),
                pltpu.VMEM((rows, group_width), low),
                pltpu.VMEM((group_width, rows), jnp.float32),
                pltpu.VMEM((group_width, everyone), low),
                pltpu.VMEM((heads, rows, PAIR), low),
                pltpu.VMEM((heads, rows, PAIR), low),
                pltpu.VMEM((heads, PAIR, rows), low),
                pltpu.VMEM((heads, PAIR, rows), low),
                pltpu.VMEM((group_width, TQ), jnp.float32),
                pltpu.VMEM((8, rows), jnp.float32),
                pltpu.VMEM((everyone, group_width), jnp.float32),
                pltpu.VMEM((everyone, group_width), jnp.float32),
            )

        return scope

    flow = Pipeline(chunks, 2, start, wait)
    flow.tick(2)
    attention(0)()
    flow.tick()
    attention(1)()
    flow.tick()
    halve()
    flow.tick()
    project_scope()
    flow.tick(STEPS + len(chunks))
    for copy in (kv_beside, kv_across):
        copy.wait_send()
    for chunk in chunks:
        for step in range(STEPS):
            for piece in chunk:
                for copy, sends, _ in copies_of(piece, step):
                    guard(sends, copy.wait_send)


def scatter_all(
    up, down, out, factor, small, up_shift_sum, vectors, kind, log_total,
    queries, kv, mixed_grad, mixed_t, normed, weight, tokens, residual_grad, depth,
):
    rows, width = tokens.shape
    far = [up, down, out]
    kinds = (True, True, False, False, False)
    share, ff_share, ff = up.shape[4], down.shape[4], up.shape[5]
    chunks, cuts = scatter_chunks(share, width, ff_share, ff)
    n_pieces = sum(len(chunk) for chunk in chunks)
    anywhere, inside = pl.BlockSpec(memory_space=pl.ANY), pl.BlockSpec(memory_space=pltpu.VMEM)
    low, box = jnp.bfloat16, (depth, 2, 2, 2)
    tails = [a.shape[4:] for a in far] + [(share, 3 * width), (THIN_ROWS, 128)]
    dtypes = [low] * 4 + [jnp.float32]
    experts = [2 if kind else 1 for kind in kinds]
    scratch = [
        pltpu.VMEM((e, depth, 2, 2) + tail, dtype) for e, tail, dtype in zip(experts, tails, dtypes)
    ]
    plain, turned = [], []
    for tail, cut in zip(tails, cuts):
        plain.append((cut[0] or tail[0], cut[1] or tail[1]))
        turned.append((tail[0] - cut[0], tail[1] - cut[1]) if any(cut) else (8, 128))
    for middle in ((depth, 2), (depth,), (depth - 1,)):
        scratch += [pltpu.VMEM((e,) + middle + t, d) for e, t, d in zip(experts, plain, dtypes)]
    scratch += [pltpu.VMEM((e,) + t, d) for e, t, d in zip(experts, plain, dtypes)]
    for middle in ((2, 2), (depth - 1, 2, 2), (2,), ()):
        scratch += [pltpu.VMEM((e,) + middle + t, d) for e, t, d in zip(experts, turned, dtypes)]
    scratch += [pltpu.VMEM((depth, 2, 2) + a.shape[4:], low) for a in far]
    scratch += [
        pltpu.VMEM(box + (share, 3 * width), low),
        pltpu.VMEM(box + (THIN_ROWS, 128), jnp.float32),
        pltpu.VMEM((2, rows, 2 * width), low),
        pltpu.VMEM((rows, 2 * width), low),
        pltpu.VMEM((2, rows, 2 * width), low),
        pltpu.VMEM((rows, width), low),
        pltpu.SemaphoreType.DMA((n_pieces, depth + 3)),
        pltpu.SemaphoreType.DMA((n_pieces, depth + 3)),
        pltpu.SemaphoreType.DMA((3,)),
        pltpu.SemaphoreType.DMA((5,)),
        pltpu.SemaphoreType.DMA((2,)),
        pltpu.SemaphoreType.DMA((2,)),
    ]
    return pl.pallas_call(
        functools.partial(scatter_kernel, depth, kinds, chunks, cuts),
        out_shape=[
            jax.ShapeDtypeStruct((e,) + tail, jnp.float32) for e, tail in zip(experts, tails)
        ]
        + [jax.ShapeDtypeStruct((rows, width), low), jax.ShapeDtypeStruct((2, rows, 2 * width), low)],
        in_specs=[anywhere] * 3 + [inside] * 6 + [anywhere] * 8,
        out_specs=[inside] * 5 + [anywhere] * 2,
        scratch_shapes=scratch,
        compiler_params=pltpu.CompilerParams(
            collective_id=2, has_side_effects=True, vmem_limit_bytes=61 << 20
        ),
    )(
        up, down, out, factor, small, up_shift_sum, vectors, kind, log_total,
        queries, kv, mixed_grad, mixed_t, normed, weight, tokens, residual_grad,
    )[:6]


def padded(values):
    return jnp.pad(values, ((0, 0), (0, 128 - values.shape[1])))


def body(
    near,
    tokens,
    group_kind,
    ln1_gain,
    ln1_bias,
    w_qkv,
    q_bias,
    v_bias,
    w_out,
    out_bias,
    ln2_gain,
    ln2_bias,
    w_up,
    b_up,
    w_down,
    b_down,
    cotangent,
):
    row_count, model_width = tokens.shape
    stream_size = lax.axis_size("stream")
    stream_place = lax.axis_index("stream")
    devices = lax.axis_size("items") * stream_size
    group_type = group_kind[0]
    expert_pick = jnp.where(stream_place == stream_size - 1, 1, 0).astype(jnp.int32)
    share, ff_share, ff = model_width // devices, w_down.shape[1], w_up.shape[2]
    both = ("items", "stream")
    low = jnp.bfloat16
    thin = jnp.stack([ln1_gain, ln1_bias, q_bias, v_bias, out_bias, ln2_gain, ln2_bias])
    thin = jnp.concatenate(
        [padded(thin), padded(b_up), padded(b_down), padded(group_kind.astype(low)[:, None])]
    )
    thin = jnp.pad(thin, ((0, THIN_ROWS - thin.shape[0]), (0, 0)))
    tokens_f = tokens.astype(jnp.float32)
    kind_wide = jnp.broadcast_to(group_type.astype(jnp.float32), (8, 128))
    place_at = stream_place.astype(jnp.int32)[None]
    if near:
        depth = lax.axis_size("items") // 2
        (
            thin_all,
            out_weight,
            up_all,
            down_all,
            qkv_weight,
            normed_low,
            queries,
            vectors,
            kv,
            mixed_low,
            mixed_t,
            log_total,
        ) = gather_all(thin, w_qkv, w_out, w_up, w_down, tokens, kind_wide, depth)
        thin_all = thin_all.reshape(devices, THIN_ROWS, 128)
        out_weight = out_weight.reshape(model_width, model_width)
        up_all = up_all.reshape(2, model_width, ff)
        down_all = down_all.reshape(2, ff, model_width)
    else:
        thin_all = lax.all_gather(thin, both, axis=0)
        qkv_weight = lax.all_gather(w_qkv, both, axis=0, tiled=True)
        out_weight = lax.all_gather(w_out, both, axis=0, tiled=True)
        up_all = lax.all_gather(w_up, both, axis=1, tiled=True)
        down_all = lax.all_gather(w_down, both, axis=1, tiled=True)
        vectors = (
            thin_all[:, :, :share].transpose(1, 0, 2).reshape(THIN_ROWS, -1).astype(jnp.float32)
        )
        normed_low = layer_norm(tokens_f, vectors[0], vectors[1]).astype(low)
        shifts = jnp.concatenate([vectors[2], jnp.zeros_like(vectors[2]), vectors[3]])
        projected = (product(normed_low, qkv_weight) + shifts).astype(low)
        queries = projected[:, :model_width]
        kv = lax.all_gather(projected[:, model_width:], "stream", axis=0, tiled=True)
        mixed_low, mixed_t, log_total = attend(kind_wide, place_at, queries, kv)
    up_shift_all = thin_all[:, 7:9, :ff_share].transpose(1, 0, 2).reshape(2, ff)
    kinds = vectors[11, :: stream_size * share].astype(jnp.int32)
    tally = []
    for kind in range(2):
        modality = layout(
            jnp.int32(kind), jnp.arange(stream_size * row_count, dtype=jnp.int32), row_count
        )[1]
        tally.append([jnp.sum((modality == e).astype(jnp.float32)) for e in range(2)])
    totals = jnp.stack(
        [jnp.sum(jnp.where(kinds == 0, tally[0][e], tally[1][e])) for e in range(2)]
    )
    (
        output,
        residual_grad,
        grad_out_weight,
        mixed_grad,
        grad_up,
        grad_down,
        small,
        grad_up_shift,
    ) = feed(
        expert_pick[None],
        place_at,
        kind_wide,
        vectors,
        up_shift_all[:, None],
        tokens,
        mixed_low,
        out_weight,
        cotangent,
        up_all,
        down_all,
    )
    factor = lax.rsqrt(totals)
    if near:
        box = (depth, 2, 2, 2)
        up_sum, down_sum, out_sum, qkv_sum, thin_sum, token_grad = scatter_all(
            grad_up.reshape(box + (share, ff)),
            grad_down.reshape(box + (ff_share, model_width)),
            grad_out_weight.reshape(box + (share, model_width)),
            jnp.broadcast_to(jnp.repeat(factor, 128)[None], (8, 256)),
            small,
            grad_up_shift,
            vectors,
            kind_wide,
            log_total,
            queries,
            kv,
            mixed_grad,
            mixed_t,
            normed_low,
            qkv_weight,
            tokens,
            residual_grad,
            depth,
        )
        out_sum, qkv_sum, thin_sum = out_sum[0], qkv_sum[0], thin_sum[0]
    else:
        pick = (jnp.arange(2, dtype=jnp.int32) == expert_pick).astype(jnp.float32) * factor

        def lanes(values):
            values = values.reshape(values.shape[0], devices, -1).transpose(1, 0, 2)
            return jnp.pad(values, ((0, 0), (0, 0), (0, 128 - values.shape[2])))

        scatter = functools.partial(
            lax.psum_scatter, axis_name=both, scatter_dimension=0, tiled=True
        )
        wide = functools.partial(lax.psum_scatter, axis_name=both, scatter_dimension=1, tiled=True)
        query_grad, kv_terms = attend_back(
            kind_wide, place_at, queries, kv, mixed_grad, mixed_t, log_total
        )
        kv_grad = lax.psum_scatter(
            kv_terms.astype(jnp.float32), "stream", scatter_dimension=0, tiled=True
        )
        qkv_grad = jnp.concatenate([query_grad, kv_grad.astype(low)], axis=1)
        grad_qkv = product_lead(normed_low, qkv_grad)
        early = [
            jnp.sum(qkv_grad[:, :model_width].astype(jnp.float32), axis=0),
            jnp.sum(qkv_grad[:, 2 * model_width :].astype(jnp.float32), axis=0),
        ]
        norm_one_grad = product_trail(qkv_grad, qkv_weight)
        token_part, *grads_one = jax.vjp(layer_norm, tokens_f, vectors[0], vectors[1])[1](
            norm_one_grad
        )
        token_grad = (residual_grad + token_part).astype(low)
        up_sum = wide(pick[:, None, None] * grad_up.astype(jnp.float32)[None])
        down_sum = wide(pick[:, None, None] * grad_down.astype(jnp.float32)[None])
        out_sum, qkv_sum = scatter(grad_out_weight.astype(jnp.float32)), scatter(grad_qkv)
        thin_terms = [
            lanes(jnp.stack(grads_one + early + [small[0], small[1], small[2]])),
            jnp.zeros((devices, 1, 128), jnp.float32),
            lanes(pick[:, None] * small[3][None]),
            lanes(pick[:, None] * grad_up_shift[0][None]),
            jnp.zeros((devices, THIN_ROWS - 12, 128), jnp.float32),
        ]
        thin_sum = scatter(jnp.concatenate(thin_terms, axis=1))[0]
    lines = [thin_sum[k, :share] for k in range(7)]
    return (
        output,
        token_grad,
        lines[0],
        lines[1],
        qkv_sum,
        lines[2],
        lines[3],
        out_sum,
        lines[4],
        lines[5],
        lines[6],
        up_sum,
        thin_sum[10:12, :ff_share],
        down_sum,
        thin_sum[8:10, :share],
        totals,
    )


def solution(mesh):
    placed = (
        P(("items", "stream"), None),
        P("items"),
        P(("items", "stream")),
        P(("items", "stream")),
        P(("items", "stream"), None),
        P(("items", "stream")),
        P(("items", "stream")),
        P(("items", "stream"), None),
        P(("items", "stream")),
        P(("items", "stream")),
        P(("items", "stream")),
        P(None, ("items", "stream"), None),
        P(None, ("items", "stream")),
        P(None, ("items", "stream"), None),
        P(None, ("items", "stream")),
        P(("items", "stream"), None),
    )
    near = mesh.shape["items"] == 8 and mesh.shape["stream"] == 4
    return jax.shard_map(
        functools.partial(body, near),
        mesh=mesh,
        in_specs=placed,
        out_specs=(
            P(("items", "stream"), None),
            P(("items", "stream"), None),
            P(("items", "stream")),
            P(("items", "stream")),
            P(("items", "stream"), None),
            P(("items", "stream")),
            P(("items", "stream")),
            P(("items", "stream"), None),
            P(("items", "stream")),
            P(("items", "stream")),
            P(("items", "stream")),
            P(None, ("items", "stream"), None),
            P(None, ("items", "stream")),
            P(None, ("items", "stream"), None),
            P(None, ("items", "stream")),
            P(),
        ),
        check_vma=False,
    )
```

```python
import functools

import jax
import jax.numpy as jnp
from jax import lax
from jax.experimental import pallas as pl
from jax.experimental.pallas import tpu as pltpu
from jax.sharding import PartitionSpec as P

HEADS = 12
HEAD_DIM = 64
PATCH_S = 197
PATCH_L = 577
TEXT_LEN = 40
ITEMS_S = 7
ITEMS_L = 2


NORM_EPS = 1e-05
MASKED = -1000000000.0


def layer_norm(values, gain_row, shift_row):
    row_mean = jnp.mean(values, axis=-1, keepdims=True)
    centred = values - row_mean
    variance = jnp.mean(centred * centred, axis=-1, keepdims=True)
    return centred * lax.rsqrt(variance + NORM_EPS) * gain_row + shift_row


def gelu_exact(values):
    return jax.nn.gelu(values, approximate=False)


def layout(group_type, positions, row_count):
    patch_len = jnp.where(group_type == 0, PATCH_S, PATCH_L).astype(jnp.int32)
    members = jnp.where(group_type == 0, ITEMS_S, ITEMS_L).astype(jnp.int32)
    is_patch = positions < 3 * row_count
    patch_item = positions // patch_len
    text_item = jnp.maximum(positions - 3 * row_count, 0) // TEXT_LEN
    member = jnp.where(is_patch, patch_item, text_item)
    member = jnp.where(member < members, member, -1)
    modality = jnp.where(member < 0, 2, jnp.where(is_patch, 0, 1)).astype(jnp.int32)
    return (member, modality)


def product(first_op, second_op):
    return jnp.dot(first_op, second_op, preferred_element_type=jnp.float32)


def product_lead(first_op, second_op):
    return lax.dot_general(
        first_op, second_op, (((0,), (0,)), ((), ())), preferred_element_type=jnp.float32
    )


def product_trail(first_op, second_op):
    return lax.dot_general(
        first_op, second_op, (((1,), (1,)), ((), ())), preferred_element_type=jnp.float32
    )


def halves(length):
    return ((0, length // 2), (length // 2, length // 2))


def divided(length, unit, *shares):
    found, begin = [], 0
    for share in shares:
        found.append((begin, share * unit))
        begin += share * unit
    assert begin == length
    return found


def gather_chunks(share, width, ff_share, ff):
    rows = (0, share)
    near_cols = divided(3 * width, 128, 9, 9)
    out_cols = divided(width, 128, 3, 3)
    up_cols = divided(ff, 128, 4, 14, 6)
    down_rows = divided(ff_share, 16, 1, 3, 2)
    chunks = [
        [((0, None), (0, THIN_ROWS), (0, 128), 0, False)]
        + [((1, None), rows, cols, order, False) for order, cols in enumerate(near_cols)],
        [((2, None), rows, cols, order, False) for order, cols in enumerate(out_cols)],
    ]
    def up_chunk(e, parts):
        return [((3, e), rows, cols, order, e == 1) for order, cols in enumerate(parts) if cols[1]]

    def down_chunk(e, parts):
        return [((4, e), band, (0, width), order, e == 1) for order, band in enumerate(parts)]

    chunks += [up_chunk(1, up_cols), down_chunk(1, down_rows), down_chunk(0, down_rows)]
    unit, begin = 128, 0
    for shares in ((2, 7, 3), (1, 5, 2), (1, 2, 1)):
        parts = []
        for blocks in shares:
            parts.append((begin * unit, blocks * unit))
            begin += blocks
        chunks.append(up_chunk(0, parts))
    return chunks


def scatter_chunks(share, width, ff_share, ff):
    rows = (0, share)
    near_cols = divided(3 * width, 128, 7, 7, 4)
    out_cols = divided(width, 128, 2, 3, 1)
    up_cols = divided(ff, 128, 4, 14, 6)
    down_rows = divided(ff_share, 16, 1, 3, 2)
    chunks = [[(2, 0, rows, cols, order) for order, cols in enumerate(out_cols)]]
    for e in (1, 0):
        chunks.append([(0, e, rows, cols, order) for order, cols in enumerate(up_cols)])
        chunks.append(
            [(1, e, band, (0, width), order) for order, band in enumerate(down_rows)]
        )
    chunks += [[], []]
    chunks.append(
        [(3, 0, rows, cols, order) for order, cols in enumerate(near_cols)]
        + [(4, 0, (0, THIN_ROWS), (0, 128), 0)]
    )
    cuts = (
        (0, up_cols[2][0]),
        (down_rows[2][0], 0),
        (0, out_cols[2][0]),
        (0, near_cols[2][0]),
        (0, 0),
    )
    return chunks, cuts


TQ, TK = 256, 128
PAIR = 2 * HEAD_DIM


def trail(first_op, second_op):
    return lax.dot_general(
        first_op, second_op, (((1,), (1,)), ((), ())), preferred_element_type=jnp.float32
    )


def span(kind, start, length, image_rows):
    patch_len, members = ((PATCH_S, ITEMS_S), (PATCH_L, ITEMS_L))[kind]
    image = start < image_rows
    low = jnp.where(image, lax.div(start, patch_len), lax.div(start - image_rows, TEXT_LEN))
    high = jnp.where(
        image,
        lax.div(start + length - 1, patch_len),
        lax.div(start + length - 1 - image_rows, TEXT_LEN),
    )
    return low, high, members


def meets(first, second, image_rows, loose):
    found = False
    for kind in range(2):
        low_a, high_a, members = span(kind, *first, image_rows)
        low_b, high_b, _ = span(kind, *second, image_rows)
        low = jnp.maximum(low_a, low_b)
        high = jnp.minimum(jnp.minimum(high_a, high_b), members - 1)
        found = jnp.logical_or(found, low <= high)
        if loose:
            both = jnp.logical_and(high_a >= members, high_b >= members)
            found = jnp.logical_or(found, both)
    return found


def member_of(kind, position, image_rows):
    patch_len = PATCH_S + kind * float(PATCH_L - PATCH_S)
    members = ITEMS_S + kind * float(ITEMS_L - ITEMS_S)
    patch = jnp.floor((position + 0.5) / patch_len)
    text = jnp.floor((position - image_rows + 0.5) * (1.0 / TEXT_LEN))
    member = jnp.where(position < image_rows, patch, text)
    return jnp.where(member < members, member, -1.0)


def same_item(kind, stream, rows, qt, kt, image_rows):
    keys = lax.broadcasted_iota(jnp.int32, (TK, 1), 0) + kt * TK
    own = lax.broadcasted_iota(jnp.int32, (1, TQ), 1) + (stream * rows + qt * TQ)
    key_member = member_of(kind, keys.astype(jnp.float32), image_rows)
    return key_member == member_of(kind, own.astype(jnp.float32), image_rows)


def half_of(pair, which):
    lanes = lax.broadcasted_iota(jnp.int32, pair.shape, 1)
    return jnp.where((lanes < HEAD_DIM) == (which == 0), pair, jnp.zeros_like(pair))


def upper_of(pair, which):
    keep = pair[which * HEAD_DIM : (which + 1) * HEAD_DIM]
    parts = [keep, jnp.zeros_like(keep)]
    return jnp.concatenate(parts if which == 0 else parts[::-1], axis=0)


def scale_queries(q_ref, scaled):
    for pair in range(q_ref.shape[1] // PAIR):
        columns = slice(pair * PAIR, (pair + 1) * PAIR)
        value = (q_ref[:, columns] * jnp.bfloat16(HEAD_DIM ** (-0.5))).T
        for which in range(2):
            scaled[2 * pair + which] = upper_of(value, which)


def flip_columns(kv_ref, begin, flipped):
    width = flipped.shape[0]

    @pl.loop(0, flipped.shape[1] // TK)
    def _(kt):
        keys = pl.ds(pl.multiple_of(kt * TK, TK), TK)
        flipped[:, keys] = kv_ref[keys, begin : begin + width].T


def attend_part(qt, begin, end, kind_ref, stream, kv_ref, values_t, scaled, mixed_ref, mixed_t, log_total, top, total):
    width, everyone = values_t.shape
    rows = mixed_ref.shape[0]
    heads = width // HEAD_DIM
    image_rows = everyone - rows
    here = slice(qt * TQ, (qt + 1) * TQ)
    if begin == 0:
        top[...] = jnp.full(top.shape, -1e30, jnp.float32)
        total[...] = jnp.zeros(total.shape, jnp.float32)
        mixed_t[:, here] = jnp.zeros((width, TQ), jnp.float32)

    @pl.loop(begin, end)
    def _(kt):
        needed = meets((stream * rows + qt * TQ, TQ), (kt * TK, TK), image_rows, True)

        @pl.when(needed)
        def _():
            keys = pl.ds(pl.multiple_of(kt * TK, TK), TK)
            allowed = same_item(kind_ref[0:1, 0:1], stream, rows, qt, kt, image_rows)
            scores, parts, fades = [], [], []
            for head in range(heads):
                pair = slice(head // 2 * PAIR, (head // 2 + 1) * PAIR)
                raw = jnp.dot(
                    kv_ref[keys, pair], scaled[head, :, here], preferred_element_type=jnp.float32
                )
                scores.append(jnp.where(allowed, raw, MASKED))
            for head, score in enumerate(scores):
                line = slice(head, head + 1)
                old = top[line]
                new = jnp.maximum(old, jnp.max(score, axis=0, keepdims=True))
                top[line] = new
                fade = jnp.exp(old - new)
                part = jnp.exp(score - new)
                total[line] = total[line] * fade + jnp.sum(part, axis=0, keepdims=True)
                parts.append(part.astype(jnp.bfloat16))
                fades.append(fade)
            for head in range(heads):
                own = slice(head * HEAD_DIM, (head + 1) * HEAD_DIM)
                mixed_t[own, here] = mixed_t[own, here] * fades[head] + jnp.dot(
                    values_t[own, keys], parts[head], preferred_element_type=jnp.float32
                )

    if end == everyone // TK:
        for head in range(heads):
            own = slice(head * HEAD_DIM, (head + 1) * HEAD_DIM)
            mixed_t[own, here] = mixed_t[own, here] / total[head : head + 1]
        log_total[:, here] = top[...] + jnp.log(total[...])
        mixed_ref[here, :] = mixed_t[:, here].T.astype(jnp.bfloat16)


def attend_kernel(kind, place_ref, q_ref, kv_ref, mixed_ref, mixed_t, log_total, values_t, scaled, top, total):
    scale_queries(q_ref, scaled)
    flip_columns(kv_ref, q_ref.shape[1], values_t)
    for qt in range(q_ref.shape[0] // TQ):
        attend_part(
            qt, 0, kv_ref.shape[0] // TK, kind, place_ref[0], kv_ref, values_t, scaled, mixed_ref,
            mixed_t, log_total, top, total,
        )


def attend(kind, place_at, queries, kv):
    rows, width = queries.shape
    heads = width // HEAD_DIM
    inside = pl.BlockSpec(memory_space=pltpu.VMEM)
    lines = -(-heads // 8) * 8
    return pl.pallas_call(
        attend_kernel,
        out_shape=(
            jax.ShapeDtypeStruct((rows, width), jnp.bfloat16),
            jax.ShapeDtypeStruct((width, rows), jnp.float32),
            jax.ShapeDtypeStruct((lines, rows), jnp.float32),
        ),
        in_specs=[inside, pl.BlockSpec(memory_space=pltpu.SMEM)] + [inside] * 2,
        out_specs=(inside,) * 3,
        scratch_shapes=[
            pltpu.VMEM((width, kv.shape[0]), jnp.bfloat16),
            pltpu.VMEM((heads, PAIR, rows), jnp.bfloat16),
            pltpu.VMEM((lines, TQ), jnp.float32),
            pltpu.VMEM((lines, TQ), jnp.float32),
        ],
        compiler_params=pltpu.CompilerParams(vmem_limit_bytes=56 << 20),
    )(kind, place_at, queries, kv)


def back_group(
    group, kind, stream, log_total, keys_ref, values_ref, q_ref, g_ref, mixed_t, dq_ref, between,
    keys_t, scaled, grads, scaled_t, grads_t, dq_t, centre, dk, dv,
):
    everyone, width = keys_ref.shape
    rows = q_ref.shape[0]
    heads = width // HEAD_DIM
    image_rows = everyone - rows
    for pair in range(heads // 2):
        columns = slice(pair * PAIR, (pair + 1) * PAIR)
        value = q_ref[:, columns] * jnp.bfloat16(HEAD_DIM ** (-0.5))
        grad = g_ref[:, columns]
        value_t, grad_t = value.T, grad.T
        product = mixed_t[columns, :] * grad_t.astype(jnp.float32)
        for which in range(2):
            head = 2 * pair + which
            scaled[head] = half_of(value, which)
            grads[head] = half_of(grad, which)
            scaled_t[head] = upper_of(value_t, which)
            grads_t[head] = upper_of(grad_t, which)
            centre[head : head + 1] = jnp.sum(
                product[which * HEAD_DIM : (which + 1) * HEAD_DIM], axis=0, keepdims=True
            )
    flip_columns(keys_ref, 0, keys_t)

    @pl.loop(0, everyone // TK)
    def _(kt):
        keys = pl.ds(pl.multiple_of(kt * TK, TK), TK)
        dk[keys, :] = jnp.zeros((TK, width), jnp.float32)
        dv[keys, :] = jnp.zeros((TK, width), jnp.float32)

    for qt in range(rows // TQ):
        here = slice(qt * TQ, (qt + 1) * TQ)
        if qt:
            between()
        dq_t[...] = jnp.zeros(dq_t.shape, jnp.float32)

        @pl.loop(0, everyone // TK)
        def _(kt, qt=qt, here=here):
            needed = meets((stream * rows + qt * TQ, TQ), (kt * TK, TK), image_rows, False)

            @pl.when(needed)
            def _():
                keys = pl.ds(pl.multiple_of(kt * TK, TK), TK)
                allowed = same_item(kind[0:1, 0:1], stream, rows, qt, kt, image_rows)
                scores, prob_grads, probs_low, score_low = [], [], [], []
                for head in range(heads):
                    pair = slice(head // 2 * PAIR, (head // 2 + 1) * PAIR)
                    scores.append(
                        jnp.dot(
                            keys_ref[keys, pair],
                            scaled_t[head, :, here],
                            preferred_element_type=jnp.float32,
                        )
                    )
                    prob_grads.append(
                        jnp.dot(
                            values_ref[keys, pair],
                            grads_t[head, :, here],
                            preferred_element_type=jnp.float32,
                        )
                    )
                for head in range(heads):
                    line = slice(group * heads + head, group * heads + head + 1)
                    shifted = scores[head] - log_total[line, here]
                    probs = jnp.exp(jnp.where(allowed, shifted, MASKED))
                    probs_low.append(probs.astype(jnp.bfloat16))
                    inner = prob_grads[head] - centre[head : head + 1, here]
                    score_low.append((probs * inner).astype(jnp.bfloat16))
                for head in range(heads):
                    own = slice(head * HEAD_DIM, (head + 1) * HEAD_DIM)
                    dq_t[own, :] += jnp.dot(
                        keys_t[own, keys], score_low[head], preferred_element_type=jnp.float32
                    )
                for head in range(0, heads, 2):
                    columns = slice(head * HEAD_DIM, head * HEAD_DIM + PAIR)
                    for terms, left, right in ((dk, score_low, scaled), (dv, probs_low, grads)):
                        terms[keys, columns] += jnp.dot(
                            left[head], right[head, here, :], preferred_element_type=jnp.float32
                        ) + jnp.dot(
                            left[head + 1],
                            right[head + 1, here, :],
                            preferred_element_type=jnp.float32,
                        )

        dq_ref[here, :] = (dq_t[...].T * HEAD_DIM ** (-0.5)).astype(jnp.bfloat16)


def attend_back_kernel(
    kind, place_ref, q_ref, kv_ref, g_ref, mixed_t, log_total, dq_ref, dkv_ref, *work
):
    width = q_ref.shape[1]
    back_group(
        0, kind, place_ref[0], log_total, kv_ref.at[:, pl.ds(0, width)],
        kv_ref.at[:, pl.ds(width, width)], q_ref, g_ref, mixed_t, dq_ref, lambda: None,
        *work,
    )
    dk, dv = work[-2:]

    @pl.loop(0, kv_ref.shape[0] // TK)
    def _(kt):
        keys = pl.ds(pl.multiple_of(kt * TK, TK), TK)
        dkv_ref[keys, :width] = dk[keys, :].astype(jnp.bfloat16)
        dkv_ref[keys, width:] = dv[keys, :].astype(jnp.bfloat16)


def attend_back(kind, place_at, queries, kv, mixed_grad, mixed_t, log_total):
    rows, width = queries.shape
    heads = width // HEAD_DIM
    inside = pl.BlockSpec(memory_space=pltpu.VMEM)
    lines = -(-heads // 8) * 8
    everyone = kv.shape[0]
    return pl.pallas_call(
        attend_back_kernel,
        out_shape=(
            jax.ShapeDtypeStruct((rows, width), jnp.bfloat16),
            jax.ShapeDtypeStruct((everyone, 2 * width), jnp.bfloat16),
        ),
        in_specs=[inside, pl.BlockSpec(memory_space=pltpu.SMEM)] + [inside] * 5,
        out_specs=(inside,) * 2,
        scratch_shapes=[
            pltpu.VMEM((width, everyone), jnp.bfloat16),
            pltpu.VMEM((heads, rows, PAIR), jnp.bfloat16),
            pltpu.VMEM((heads, rows, PAIR), jnp.bfloat16),
            pltpu.VMEM((heads, PAIR, rows), jnp.bfloat16),
            pltpu.VMEM((heads, PAIR, rows), jnp.bfloat16),
            pltpu.VMEM((width, TQ), jnp.float32),
            pltpu.VMEM((lines, rows), jnp.float32),
            pltpu.VMEM((everyone, width), jnp.float32),
            pltpu.VMEM((everyone, width), jnp.float32),
        ],
        compiler_params=pltpu.CompilerParams(vmem_limit_bytes=58 << 20),
    )(kind, place_at, queries, kv, mixed_grad, mixed_t, log_total)

def feed_kernel(
    pick, place_ref, kind, vectors, up_shift, tokens, mixed, out_weight, cotangent, up, down,
    output, residual_grad, grad_out, mixed_grad, grad_up, grad_down, small, up_shift_sum,
    residual, normed, normed_t, grad, branch, back,
):
    step = pl.program_id(0)
    rows, width = tokens.shape
    image_rows = (lax.axis_size("stream") - 1) * rows
    tall = 128

    def blocks(act):
        @pl.loop(0, rows // tall)
        def _(j):
            act(pl.ds(pl.multiple_of(j * tall, tall), tall))

    def unit_of(value):
        centred = value - jnp.mean(value, axis=-1, keepdims=True)
        scale = lax.rsqrt(jnp.mean(centred * centred, axis=-1, keepdims=True) + NORM_EPS)
        return centred * scale, scale

    def live(j_start):
        position = lax.broadcasted_iota(jnp.int32, (tall, 1), 0) + (place_ref[0] * rows + j_start)
        return member_of(kind[0:1, 0:1], position.astype(jnp.float32), image_rows) >= 0.0

    @pl.when(step == 0)
    def _():
        @pl.loop(0, rows // tall)
        def _(j):
            block = pl.ds(pl.multiple_of(j * tall, tall), tall)
            value = (
                tokens[block, :].astype(jnp.float32)
                + jnp.dot(mixed[block, :], out_weight[...], preferred_element_type=jnp.float32)
                + vectors[4:5, :]
            )
            residual[block, :] = value
            unit, _ = unit_of(value)
            normed[block, :] = (unit * vectors[5:6, :] + vectors[6:7, :]).astype(jnp.bfloat16)
            given = cotangent[block, :]
            grad[block, :] = jnp.where(live(j * tall), given, jnp.zeros_like(given))

        normed_t[...] = normed[...].T
        branch[...] = jnp.zeros(branch.shape, jnp.float32)
        back[...] = jnp.zeros(back.shape, jnp.float32)

    before = (
        jnp.dot(normed[...], up[0], preferred_element_type=jnp.float32) + up_shift[0].astype(jnp.float32)
    )
    hidden_grad = product_trail(grad[...], down[0])
    half = 0.5 + 0.5 * lax.erf(before * 0.5**0.5)
    hidden = (before * half).astype(jnp.bfloat16)
    slope = half + before * (jnp.exp(-0.5 * before * before) * 0.3989422804014327)
    before_grad = hidden_grad * slope
    low_grad = before_grad.astype(jnp.bfloat16)
    up_shift_sum[...] = jnp.broadcast_to(
        jnp.sum(low_grad.astype(jnp.float32), axis=0, keepdims=True), up_shift_sum.shape
    )
    branch[...] += jnp.dot(hidden, down[0], preferred_element_type=jnp.float32)
    back[...] += product_trail(low_grad, up[0])
    grad_up[...] = jnp.dot(normed_t[...], low_grad, preferred_element_type=jnp.float32).astype(
        jnp.bfloat16
    )
    grad_down[...] = jnp.dot(hidden.T, grad[...], preferred_element_type=jnp.float32).astype(
        jnp.bfloat16
    )

    @pl.when(step == pl.num_programs(0) - 1)
    def _():
        down_shift = jnp.where(pick[0] == 0, vectors[9:10, :], vectors[10:11, :])

        def fold(value):
            return jnp.sum(value.reshape(-1, 8, width), axis=0)

        def finish(j, carry):
            block = pl.ds(pl.multiple_of(j * tall, tall), tall)
            value = residual[block, :]
            kept = live(j * tall)
            output[block, :] = (
                value + jnp.where(kept, branch[block, :] + down_shift, 0.0)
            ).astype(jnp.bfloat16)
            unit, scale = unit_of(value)
            given = back[block, :]
            lifted = given * vectors[5:6, :]
            inner = jnp.mean(lifted * unit, axis=-1, keepdims=True)
            own = grad[block, :].astype(jnp.float32)
            total = own + scale * (
                lifted - jnp.mean(lifted, axis=-1, keepdims=True) - unit * inner
            )
            residual_grad[block, :] = total
            total_low = total.astype(jnp.bfloat16)
            normed[block, :] = total_low
            mixed_grad[block, :] = product_trail(total_low, out_weight[...]).astype(jnp.bfloat16)
            terms = (total_low.astype(jnp.float32), given * unit, given, own)
            return tuple(held + fold(term) for held, term in zip(carry, terms))

        zero = jnp.zeros((8, width), jnp.float32)
        sums = lax.fori_loop(0, rows // tall, finish, (zero,) * 4)
        lines = [jnp.sum(value, axis=0, keepdims=True) for value in sums]
        small[...] = jnp.concatenate(lines + [jnp.zeros((4, width), jnp.float32)], axis=0)
        grad_out[...] = jnp.dot(
            mixed[...].T, normed[...], preferred_element_type=jnp.float32
        ).astype(jnp.bfloat16)


def feed(pick, place_at, kind, vectors, up_shift, tokens, mixed, out_weight, cotangent, up, down):
    rows, width = tokens.shape
    ff = up.shape[2]
    band = 512
    low, wide = jnp.bfloat16, jnp.float32

    def whole(array):
        return pl.BlockSpec(array.shape, lambda i, pick, place_at: (0,) * array.ndim)

    fixed = [
        jax.ShapeDtypeStruct((rows, width), low),
        jax.ShapeDtypeStruct((rows, width), wide),
        jax.ShapeDtypeStruct((width, width), low),
        jax.ShapeDtypeStruct((rows, width), low),
    ]
    last = jax.ShapeDtypeStruct((8, width), wide)
    return pl.pallas_call(
        feed_kernel,
        out_shape=fixed
        + [
            jax.ShapeDtypeStruct((width, ff), low),
            jax.ShapeDtypeStruct((ff, width), low),
            last,
            jax.ShapeDtypeStruct((8, ff), wide),
        ],
        grid_spec=pltpu.PrefetchScalarGridSpec(
            num_scalar_prefetch=2,
            grid=(ff // band,),
            in_specs=[
                whole(kind),
                whole(vectors),
                pl.BlockSpec((1, 1, band), lambda i, pick, place_at: (pick[0], 0, i)),
                whole(tokens),
                whole(mixed),
                whole(out_weight),
                whole(cotangent),
                pl.BlockSpec((1, width, band), lambda i, pick, place_at: (pick[0], 0, i)),
                pl.BlockSpec((1, band, width), lambda i, pick, place_at: (pick[0], i, 0)),
            ],
            out_specs=[whole(array) for array in fixed]
            + [
                pl.BlockSpec((width, band), lambda i, pick, place_at: (0, i)),
                pl.BlockSpec((band, width), lambda i, pick, place_at: (i, 0)),
                whole(last),
                pl.BlockSpec((8, band), lambda i, pick, place_at: (0, i)),
            ],
            scratch_shapes=[
                pltpu.VMEM((rows, width), wide),
                pltpu.VMEM((rows, width), low),
                pltpu.VMEM((width, rows), low),
                pltpu.VMEM((rows, width), low),
                pltpu.VMEM((rows, width), wide),
                pltpu.VMEM((rows, width), wide),
            ],
        ),
        compiler_params=pltpu.CompilerParams(vmem_limit_bytes=62 << 20),
    )(pick, place_at, kind, vectors, up_shift, tokens, mixed, out_weight, cotangent, up, down)


MESH = pl.DeviceIdType.MESH
GATHER_ORDERS = (("z", "f", "x", "y"), ("z", "f", "y", "x"), ("y", "x", "z", "f"))
SCATTER_ORDERS = (("y", "x", "a", "z"), ("x", "y", "a", "z"), ("a", "z", "x", "y"))
STEPS = 5
EVERY = slice(None)
THIN_ROWS = 16


def coords():
    items, stream = lax.axis_index("items"), lax.axis_index("stream")
    return dict(z=items // 2, x=items % 2, y=stream // 2, c=stream % 2)


def place(at):
    return (at["z"] * 2 + at["x"], at["y"] * 2 + at["c"])


def moved(at, dim, by, depth):
    return {**at, dim: lax.rem(at[dim] + by, depth if dim == "z" else 2)}


def greet(at, depth):
    peers = [moved(at, "z", k, depth) for k in range(1, depth)]
    peers += [moved(at, d, 1, depth) for d in "xyc"]
    barrier = pltpu.get_barrier_semaphore()
    for peer in peers:
        pl.semaphore_signal(barrier, inc=1, device_id=place(peer), device_id_type=MESH)
    pl.semaphore_wait(barrier, len(peers))


def guard(cond, act):
    if cond is None:
        act()
    else:
        pl.when(cond)(act)


def remote(src, dst, sems, index, device):
    return pltpu.make_async_remote_copy(
        src_ref=src,
        dst_ref=dst,
        send_sem=sems[0].at[index],
        recv_sem=sems[1].at[index],
        device_id=place(device),
        device_id_type=MESH,
    )


def both_of(first, second):
    if first is None or second is None:
        return second if first is None else first
    return jnp.logical_and(first, second)


class Pipeline:
    def __init__(self, chunks, ahead, start, wait):
        self.chunks, self.ahead, self.start, self.wait = chunks, ahead, start, wait
        self.ticks = 0
        for chunk in chunks[:ahead]:
            start(chunk, 0)

    def tick(self, times=1):
        count = len(self.chunks)
        for t in range(self.ticks, min(self.ticks + times, count + STEPS - 1)):
            if t + self.ahead < count:
                self.start(self.chunks[t + self.ahead], 0)
            for step in range(STEPS):
                if 0 <= t - step < count:
                    self.wait(self.chunks[t - step], step)
                    if step < STEPS - 1:
                        self.start(self.chunks[t - step], step + 1)
        self.ticks += times


def spots_of(depth):
    return [(a, b, c, d) for a in range(depth) for b in range(2) for c in range(2) for d in range(2)]


def columns_over(share, width):
    column = lax.broadcasted_iota(jnp.int32, (1, width), 1).astype(jnp.float32)
    owner = jnp.floor((column + 0.5) * (1.0 / share))
    return owner, column - owner * share


def spread(thin, share, width):
    owner, lane = columns_over(share, width)
    picks = lax.broadcasted_iota(jnp.int32, (128, width), 0).astype(jnp.float32) == lane
    wide = jnp.dot(thin, picks.astype(jnp.bfloat16), preferred_element_type=jnp.float32)
    total = jnp.zeros((THIN_ROWS, width), jnp.float32)
    for device in range(thin.shape[0] // THIN_ROWS):
        part = wide[device * THIN_ROWS : (device + 1) * THIN_ROWS]
        total = total + jnp.where(owner == device, part, 0.0)
    return total


def dealt(rows, share, devices):
    width = rows.shape[1]
    owner, lane = columns_over(share, width)
    picks = lax.broadcasted_iota(jnp.int32, (128, width), 0).astype(jnp.float32) == lane
    tall = jnp.concatenate(
        [jnp.where(owner == device, rows, 0.0) for device in range(devices)], axis=0
    )
    return lax.dot_general(
        tall,
        picks.astype(jnp.float32),
        (((1,), (1,)), ((), ())),
        precision=lax.Precision.HIGHEST,
        preferred_element_type=jnp.float32,
    )


def gather_kernel(depth, chunks, entries, *refs):
    it = iter(refs)
    take = lambda count: [next(it) for _ in range(count)]
    ins = take(5)
    tokens, kind = take(2)
    thin_out, out_all, up_all, down_all = take(4)
    weight_out, normed_out, queries_out, vectors, kv_out, mixed, mixed_t_out, log_total = take(8)
    thin_all, qkv_all, kv, values_t, scaled, top, total = take(7)
    qkv_weight, normed, queries, mixed_t = take(4)
    local_sem = next(it)
    sems, kv_sems = take(2), take(2)
    keep_sem = next(it)
    outs = (thin_all, qkv_all, out_all, up_all, down_all)
    rows, width = tokens.shape
    devices = depth * 8
    share = width // devices
    at = coords()
    mine = (at["z"], at["x"], at["y"], at["c"])
    slot = at["y"] * 2 + at["c"]

    def source(entry):
        k, e = entry
        return ins[k] if e is None else ins[k].at[e]

    def target(entry):
        k, e = entry
        return outs[k] if e is None else outs[k].at[e]

    local = [
        pltpu.make_async_copy(source(entry), target(entry).at[mine], local_sem.at[j])
        for j, entry in enumerate(entries)
    ]
    for copy in local:
        copy.start()
    greet(at, depth)
    for copy in local:
        copy.wait()
    lower, upper = at["y"] == 0, at["y"] == 1
    number = {piece: j for j, piece in enumerate(piece for chunk in chunks for piece in chunk)}

    z = at["z"]

    def stage(piece, step):
        entry, band, cols, order, text = piece
        dims = GATHER_ORDERS[order] + ("c",)
        dim = dims[step]
        box = (pl.ds(*band), pl.ds(*cols))
        live = upper if text and "y" in dims[:step] else None

        def held(level):
            spot = {d: EVERY if d in dims[:step] else pl.ds(at[d], 1) for d in "zxyc"}
            if level is not None:
                spot["z"] = pl.ds(level, 1)
            return target(entry).at[tuple(spot[d] for d in "zxyc") + box]

        if dim == "f":
            up_view, down_view = held(0), held(depth - 1)
            up = remote(up_view, up_view, sems, (number[piece], depth + 2), {**at, "z": z + 1})
            down = remote(down_view, down_view, sems, (number[piece], depth + 2), {**at, "z": z - 1})
            return [
                (up, both_of(live, z == depth - 2), both_of(live, z == depth - 1)),
                (down, both_of(live, z == 1), both_of(live, z == 0)),
            ]
        view = held(None)
        if dim == "z":
            found = []
            for k in range(1, depth):
                to, source_level = lax.rem(z + k, depth), lax.rem(z + depth - k, depth)
                copy = remote(view, view, sems, (number[piece], k - 1), {**at, "z": to})
                sends = both_of(live, jnp.abs(to - z) != depth - 1)
                found.append((copy, sends, both_of(live, jnp.abs(source_level - z) != depth - 1)))
            return found
        sem = {"x": depth - 1, "y": depth, "c": depth + 1}[dim]
        copy = remote(view, view, sems, (number[piece], sem), moved(at, dim, 1, depth))
        if text and dim == "y":
            return [(copy, lower, upper)]
        return [(copy, live, live)]

    def each(chunk, step, which, call):
        for piece in chunk:
            for found in stage(piece, step):
                guard(found[which], functools.partial(call, found[0]))

    beside, across = moved(at, "c", 1, depth), moved(at, "y", 1, depth)
    other = across["y"] * 2 + across["c"]
    own_slot = pl.ds(pl.multiple_of(slot * rows, rows), rows)
    other_slot = pl.ds(pl.multiple_of(other * rows, rows), rows)
    to_across = remote(kv.at[own_slot], kv.at[own_slot], kv_sems, 0, across)
    to_beside = remote(kv.at[own_slot], kv.at[own_slot], kv_sems, 1, beside)
    onward = remote(kv.at[other_slot], kv.at[other_slot], kv_sems, 2, beside)
    keep_kv = pltpu.make_async_copy(kv, kv_out, keep_sem.at[0])
    keep_mixed = pltpu.make_async_copy(mixed_t, mixed_t_out, keep_sem.at[1])
    keep_early = [
        pltpu.make_async_copy(src, dst, keep_sem.at[2 + j])
        for j, (src, dst) in enumerate(
            [(thin_all, thin_out), (qkv_weight, weight_out), (normed, normed_out), (queries, queries_out)]
        )
    ]

    def project():
        spots = spots_of(depth)
        for j, spot in enumerate(spots):
            qkv_weight[j * share : (j + 1) * share, :] = qkv_all[spot]
        thin = jnp.concatenate([thin_all[spot] for spot in spots], axis=0)
        vectors[...] = spread(thin, share, width)

        @pl.loop(0, rows // 128)
        def _(j):
            block = pl.ds(pl.multiple_of(j * 128, 128), 128)
            value = tokens[block, :].astype(jnp.float32)
            centred = value - jnp.mean(value, axis=-1, keepdims=True)
            scale = lax.rsqrt(jnp.mean(centred * centred, axis=-1, keepdims=True) + NORM_EPS)
            normed[block, :] = (centred * scale * vectors[0:1, :] + vectors[1:2, :]).astype(
                jnp.bfloat16
            )

        step = width // 2
        for part in (1, 2, 0):

            @pl.loop(0, 2)
            def _(j, part=part):
                cols = pl.ds(pl.multiple_of(j * step, 128), step)
                value = jnp.dot(
                    normed[...],
                    qkv_weight[:, pl.ds(pl.multiple_of(part * width + j * step, 128), step)],
                    preferred_element_type=jnp.float32,
                )
                if part == 0:
                    queries[:, cols] = (value + vectors[2:3, cols]).astype(jnp.bfloat16)
                elif part == 1:
                    kv[own_slot, cols] = value.astype(jnp.bfloat16)
                else:
                    kv[own_slot, pl.ds(pl.multiple_of(width + j * step, 128), step)] = (
                        value + vectors[3:4, cols]
                    ).astype(jnp.bfloat16)

            if part == 2:
                to_across.start()
                to_beside.start()
        for copy in keep_early:
            copy.start()
        scale_queries(queries, scaled)

    def pass_on():
        to_across.wait_recv()
        onward.start()

    def attend_first():
        to_beside.wait_recv()
        onward.wait_recv()
        keep_kv.start()
        flip_columns(kv, width, values_t)

    parts = (kind, slot, kv, values_t, scaled, mixed, mixed_t, log_total, top, total)

    def attention(qt, begin, end):
        def act():
            if qt == 0 and begin == 0:
                attend_first()
            attend_part(qt, begin, end, *parts)

        return act

    everyone = kv.shape[0] // TK
    flow = Pipeline(
        chunks,
        2,
        lambda chunk, step: each(chunk, step, 1, lambda copy: copy.start()),
        lambda chunk, step: each(chunk, step, 2, lambda copy: copy.wait_recv()),
    )
    flow.tick(5)
    project()
    flow.tick()
    pass_on()
    flow.tick()
    attention(0, 0, everyone // 2)()
    flow.tick()
    attention(0, everyone // 2, everyone)()
    flow.tick()
    attention(1, 0, everyone // 2)()
    flow.tick()
    attention(1, everyone // 2, everyone)()
    flow.tick(STEPS + len(chunks))
    for copy in (to_beside, to_across, onward):
        copy.wait_send()
    keep_mixed.start()
    for copy in keep_early + [keep_kv, keep_mixed]:
        copy.wait()
    for chunk in chunks:
        for step in range(STEPS):
            each(chunk, step, 1, lambda copy: copy.wait_send())


def gather_all(thin, w_qkv, w_out, w_up, w_down, tokens, kind, depth):
    rows, width = tokens.shape
    share, ff_share, ff = w_qkv.shape[0], w_down.shape[1], w_up.shape[2]
    entries = [(0, None), (1, None), (2, None), (3, 0), (3, 1), (4, 0), (4, 1)]
    chunks = gather_chunks(share, width, ff_share, ff)
    n_pieces = sum(len(chunk) for chunk in chunks)
    anywhere = pl.BlockSpec(memory_space=pl.ANY)
    inside = pl.BlockSpec(memory_space=pltpu.VMEM)
    low = jnp.bfloat16
    box = (depth, 2, 2, 2)
    heads, lines = width // HEAD_DIM, -(-(width // HEAD_DIM) // 8) * 8
    return pl.pallas_call(
        functools.partial(gather_kernel, depth, chunks, entries),
        out_shape=[
            jax.ShapeDtypeStruct(box + thin.shape, low),
            jax.ShapeDtypeStruct(box + (share, width), low),
            jax.ShapeDtypeStruct((2,) + box + (share, ff), low),
            jax.ShapeDtypeStruct((2,) + box + (ff_share, width), low),
            jax.ShapeDtypeStruct((width, 3 * width), low),
            jax.ShapeDtypeStruct((rows, width), low),
            jax.ShapeDtypeStruct((rows, width), low),
            jax.ShapeDtypeStruct((THIN_ROWS, width), jnp.float32),
            jax.ShapeDtypeStruct((4 * rows, 2 * width), low),
            jax.ShapeDtypeStruct((rows, width), low),
            jax.ShapeDtypeStruct((width, rows), jnp.float32),
            jax.ShapeDtypeStruct((lines, rows), jnp.float32),
        ],
        in_specs=[inside] * 7,
        out_specs=[anywhere] * 7 + [inside, anywhere, inside, anywhere, inside],
        scratch_shapes=[
            pltpu.VMEM(box + thin.shape, low),
            pltpu.VMEM(box + (share, 3 * width), low),
            pltpu.VMEM((4 * rows, 2 * width), low),
            pltpu.VMEM((width, 4 * rows), low),
            pltpu.VMEM((heads, PAIR, rows), low),
            pltpu.VMEM((lines, TQ), jnp.float32),
            pltpu.VMEM((lines, TQ), jnp.float32),
            pltpu.VMEM((width, 3 * width), low),
            pltpu.VMEM((rows, width), low),
            pltpu.VMEM((rows, width), low),
            pltpu.VMEM((width, rows), jnp.float32),
            pltpu.SemaphoreType.DMA((len(entries),)),
            pltpu.SemaphoreType.DMA((n_pieces, depth + 3)),
            pltpu.SemaphoreType.DMA((n_pieces, depth + 3)),
            pltpu.SemaphoreType.DMA((3,)),
            pltpu.SemaphoreType.DMA((3,)),
            pltpu.SemaphoreType.DMA((6,)),
        ],
        compiler_params=pltpu.CompilerParams(
            collective_id=1, has_side_effects=True, vmem_limit_bytes=62 << 20
        ),
    )(thin, w_qkv, w_out, w_up, w_down, tokens, kind)


def rows_of_kind(kind, rows):
    patch_len, members = ((PATCH_S, ITEMS_S), (PATCH_L, ITEMS_L))[kind]
    return float(min(patch_len * members, 3 * rows)), float(min(TEXT_LEN * members, rows))


def scatter_kernel(depth, kinds, chunks, cuts, *refs):
    n, n_far = len(kinds), 3
    it = iter(refs)
    take = lambda count: [next(it) for _ in range(count)]
    far = take(n_far)
    small, up_shift_sum, vectors, kind, log_total = take(5)
    queries, kv, mixed_grad, mixed_t, normed, weight, tokens, residual_grad = take(8)
    outs = take(n)
    token_grad, kv_away = take(2)
    acc, first, second, last = take(n), take(n), take(n), take(n)
    relay, z_relay, z_first, z_second, z_last = (take(n) for _ in range(5))
    own_half = take(n_far)
    qkv_terms, thin_terms, kv_sum, kv_got, kv_mine, dq = take(6)
    sems = take(2)
    local_sem, away_sem = take(2)
    kv_sems = take(2)
    rows, width = residual_grad.shape
    devices = depth * 8
    share = width // devices
    at = coords()
    z, x, y, c = (at[d] for d in "zxyc")
    ins = far + [qkv_terms, thin_terms]
    groups = devices // 4
    lane = lax.broadcasted_iota(jnp.int32, (1, width), 1)
    marks = functools.reduce(
        jnp.logical_or, [lane == group * (width // groups) for group in range(groups)]
    )
    second_kind = jnp.sum(jnp.where(marks, vectors[11:12, :], 0.0), axis=1, keepdims=True)
    counts = [
        first_count * (groups - second_kind) + second_count * second_kind
        for first_count, second_count in zip(*(rows_of_kind(kind_of, rows) for kind_of in range(2)))
    ]
    factors = [lax.rsqrt(count) for count in counts]
    local = [
        pltpu.make_async_copy(far[k].at[EVERY, EVERY, EVERY, c], own_half[k], local_sem.at[k])
        for k in range(n_far)
    ]
    for copy in local:
        copy.start()
    greet(at, depth)
    for copy in local:
        copy.wait()
    beside, across = moved(at, "c", 1, depth), moved(at, "y", 1, depth)
    kv_beside = remote(kv_away, kv_sum, kv_sems, 0, beside)
    kv_across = remote(kv_sum.at[1 - y], kv_got, kv_sems, 1, across)
    lower, upper = y == 0, y == 1
    text_device = jnp.logical_and(upper, c == 1)
    image_device = jnp.logical_or(lower, c == 0)
    beside_text = jnp.logical_and(upper, c == 0)
    beside_image = jnp.logical_or(lower, c == 1)
    number = {piece: j for j, piece in enumerate(piece for chunk in chunks for piece in chunk)}

    sources = (
        (z == 0, range(2, depth)),
        (jnp.logical_and(z > 0, z < depth - 1), range(1, depth)),
        (z == depth - 1, range(1, depth - 1)),
    )

    def boxes(piece):
        k, e, band, cols, order = piece
        cut = cuts[k] if order == 2 else (0, 0)
        return (
            (pl.ds(*band), pl.ds(*cols)),
            (pl.ds(band[0] - cut[0], band[1]), pl.ds(cols[0] - cut[1], cols[1])),
        )

    def copies_of(piece, step):
        k, e, band, cols, order = piece
        box, inner = boxes(piece)
        image, text = kinds[k] and e == 0, kinds[k] and e == 1
        dims = ("c",) + SCATTER_ORDERS[order]
        dim = dims[step]
        here = acc[k].at[e]

        def make(src, dst, sem, by=1):
            return remote(src, dst, sems, (number[piece], sem), moved(at, dim, by, depth))

        sends = recvs = None
        if dim == "c":
            if image:
                sends, recvs = image_device, beside_image
            elif text:
                sends, recvs = text_device, beside_text
            src = ins[k].at[(EVERY, EVERY, EVERY, 1 - c) + box]
            return [(make(src, here.at[(EVERY, EVERY, EVERY) + box], 0), sends, recvs)]
        if text and dim == "y":
            sends, recvs = upper, lower
        elif text and "y" not in dims[:step]:
            sends = recvs = upper
        where = (EVERY, EVERY) if order == 2 else (x, y)
        if dim == "a":
            src = here.at[(depth - 1 - z,) + where + box]
            dst = z_relay[k].at[(e, EVERY, EVERY) + inner] if order == 2 else relay[k].at[(e,) + inner]
            to = {**at, "z": jnp.where(z == 0, 1, depth - 2)}
            copy = remote(src, dst, sems, (number[piece], depth + 2), to)
            ends = jnp.logical_or(z == 0, z == depth - 1)
            middle = jnp.logical_and(z > 0, z < depth - 1)
            return [(copy, both_of(sends, ends), both_of(recvs, middle))]
        if dim == "z":
            found = []
            for by in range(1, depth):
                to, source_level = lax.rem(z + by, depth), lax.rem(z + depth - by, depth)
                src = here.at[(to,) + where + box]
                if order == 2:
                    dst = z_first[k].at[(e, by - 1, EVERY, EVERY) + inner]
                else:
                    dst = last[k].at[(e, by - 1) + inner]
                found.append(
                    (
                        make(src, dst, 2 + by, by),
                        both_of(sends, jnp.abs(to - z) != depth - 1),
                        both_of(recvs, jnp.abs(source_level - z) != depth - 1),
                    )
                )
            return found
        if order == 2 and dim == "x":
            src, dst = here.at[(z, 1 - x, EVERY) + box], z_second[k].at[(e, EVERY) + inner]
            return [(make(src, dst, 1), sends, recvs)]
        if order == 2:
            src, dst = here.at[(z, x, 1 - y) + box], z_last[k].at[(e,) + inner]
            return [(make(src, dst, 2), sends, recvs)]
        if step == 1:
            spot = (EVERY, EVERY, 1 - y) if dim == "y" else (EVERY, 1 - x, EVERY)
            dst = first[k].at[(e, EVERY, EVERY) + inner]
        else:
            spot = (EVERY, x, 1 - y) if dim == "y" else (EVERY, 1 - x, y)
            dst = second[k].at[(e, EVERY) + inner]
        return [(make(here.at[spot + box], dst, step), sends, recvs)]

    def combine(piece, step):
        k, e, band, cols, order = piece
        box, inner = boxes(piece)
        image, text = kinds[k] and e == 0, kinds[k] and e == 1
        dims = ("c",) + SCATTER_ORDERS[order]
        dim = dims[step]
        here = acc[k].at[e]

        def over(spots, value_of, keep):
            @pl.loop(0, depth)
            def _(level):
                for index, spot in enumerate(spots):
                    where = (level,) + spot + box
                    value = value_of(level, index, spot)
                    here[where] = value if keep else here[where] + value

        def wide(value):
            return value.astype(jnp.float32)

        if step == 0:
            spots = [(0, 0), (0, 1), (1, 0), (1, 1)]

            def own(level, index, spot):
                if k < n_far:
                    return own_half[k][(level,) + spot + box]
                return ins[k][(level,) + spot + (c,) + box]

            if image:
                pl.when(lower)(lambda: over(spots, own, False))
                pl.when(beside_text)(lambda: over(spots, own, True))
            elif text:
                pl.when(text_device)(lambda: over(spots, own, True))
            else:
                over(spots, own, False)
        elif dim == "a":
            dest = jnp.where(z == 1, depth - 1, 0)

            def act():
                if order == 2:
                    for spot in [(0, 0), (0, 1), (1, 0), (1, 1)]:
                        where = (dest,) + spot + box
                        here[where] = here[where] + z_relay[k][(e,) + spot + inner]
                else:
                    where = (dest, x, y) + box
                    here[where] = here[where] + relay[k][(e,) + inner]

            middle = jnp.logical_and(z > 0, z < depth - 1)
            guard(both_of(upper if text and order == 2 else None, middle), act)
        elif step == STEPS - 1:

            def finish(total):
                if kinds[k]:
                    total = total * factors[e]
                outs[k][(e,) + box] = total

            def own():
                return wide(here[(z, x, y) + box])

            if order == 2:
                got = lambda: wide(z_last[k][(e,) + inner])
                if text:
                    pl.when(lower)(lambda: finish(got()))
                    pl.when(upper)(lambda: finish(own()))
                else:
                    finish(own() + got())
            else:
                for cond, bys in sources:

                    @pl.when(cond)
                    def _(bys=bys):
                        total = own()
                        for by in bys:
                            total = total + wide(last[k][(e, by - 1) + inner])
                        finish(total)
        elif dim == "z":
            for cond, bys in sources:

                def act(bys=bys):
                    for spot in [(0, 0), (0, 1), (1, 0), (1, 1)]:
                        where = (z,) + spot + box
                        total = wide(here[where])
                        for by in bys:
                            total = total + wide(z_first[k][(e, by - 1) + spot + inner])
                        here[where] = total.astype(here.dtype)

                guard(both_of(upper if text else None, cond), act)
        elif order == 2:

            def act():
                for other in range(2):
                    where = (z, x, other) + box
                    here[where] = here[where] + z_second[k][(e, other) + inner]

            guard(upper if text else None, act)
        elif step == 1:
            spots = [(0, y), (1, y)] if dim == "y" else [(x, 0), (x, 1)]
            got = lambda level, index, spot: first[k][(e, level, index) + inner]
            if text and dim == "y":
                pl.when(lower)(lambda: over(spots, got, True))
            elif text:
                pl.when(upper)(lambda: over(spots, got, False))
            else:
                over(spots, got, False)
        else:
            got = lambda level, index, spot: second[k][(e, level) + inner]
            if text and dim == "y":
                pl.when(lower)(lambda: over([(x, y)], got, True))
            else:
                over([(x, y)], got, False)

    def start(chunk, step):
        for piece in chunk:
            for copy, sends, _ in copies_of(piece, step):
                guard(sends, copy.start)

    def wait(chunk, step):
        for piece in chunk:
            for copy, _, recvs in copies_of(piece, step):
                guard(recvs, copy.wait_recv)
            combine(piece, step)

    def halve():
        kv_beside.wait_recv()

        @pl.loop(0, rows // 64)
        def _(j):
            block = pl.ds(pl.multiple_of(j * 64, 64), 64)
            for level in range(2):
                kv_sum[level, block, :] = kv_sum[level, block, :] + kv_mine[level, block, :]

        kv_across.start()

    def project_back(qkv_grad, flipped, normed_in, weight_in, tokens_in, residual_in, token_out):
        pairs = [(normed, normed_in), (weight, weight_in), (tokens, tokens_in), (residual_grad, residual_in)]
        loads = [pltpu.make_async_copy(src, dst, away_sem.at[j]) for j, (src, dst) in enumerate(pairs)]
        for copy in loads:
            copy.start()
        for copy in loads:
            copy.wait()
        flipped[...] = normed_in[...].T
        qkv_grad[:, :width] = dq[...]
        kv_across.wait_recv()

        def fold(value):
            return jnp.sum(value.reshape(-1, 8, width), axis=0)

        zero = jnp.zeros((8, width), jnp.float32)

        def join(j, carry):
            block = pl.ds(pl.multiple_of(j * 64, 64), 64)
            total = (
                kv_sum[y, block, :].astype(jnp.float32) + kv_got[block, :].astype(jnp.float32)
            ).astype(jnp.bfloat16)
            qkv_grad[block, width:] = total
            return (
                carry[0] + fold(dq[block, :].astype(jnp.float32)),
                carry[1] + fold(total[:, width:].astype(jnp.float32)),
            )

        sum_q, sum_v = lax.fori_loop(0, rows // 64, join, (zero, zero))
        step = width // 2
        spots = spots_of(depth)

        @pl.loop(0, 6)
        def _(j):
            cols = pl.ds(pl.multiple_of(j * step, 128), step)
            value = jnp.dot(
                flipped[...], qkv_grad[:, cols], preferred_element_type=jnp.float32
            ).astype(jnp.bfloat16)
            for index, spot in enumerate(spots):
                qkv_terms[spot + (EVERY, cols)] = value[index * share : (index + 1) * share]

        def back(j, carry):
            block = pl.ds(pl.multiple_of(j * 128, 128), 128)
            value = tokens_in[block, :].astype(jnp.float32)
            centred = value - jnp.mean(value, axis=-1, keepdims=True)
            scale = lax.rsqrt(jnp.mean(centred * centred, axis=-1, keepdims=True) + NORM_EPS)
            unit = centred * scale
            grad = product_trail(qkv_grad[block, :], weight_in[...])
            lifted = grad * vectors[0:1, :]
            inner = jnp.mean(lifted * unit, axis=-1, keepdims=True)
            part = scale * (lifted - jnp.mean(lifted, axis=-1, keepdims=True) - unit * inner)
            token_out[block, :] = (residual_in[block, :] + part).astype(jnp.bfloat16)
            return carry[0] + fold(grad * unit), carry[1] + fold(grad)

        sum_gain, sum_shift = lax.fori_loop(0, rows // 128, back, (zero, zero))
        store = pltpu.make_async_copy(token_out, token_grad, away_sem.at[0])
        store.start()
        lines = [jnp.sum(value, axis=0, keepdims=True) for value in (sum_gain, sum_shift, sum_q, sum_v)]
        def stack(parts):
            count = sum(part.shape[0] for part in parts)
            return jnp.concatenate(parts + [jnp.zeros((8 - count, parts[0].shape[1]), jnp.float32)])

        scales = [
            jnp.where(text_device == (e == 1), factors[e], 0.0)
            for e in range(2)
        ]
        down_part = [small[3:4, :] * scale for scale in scales]
        up_part = [up_shift_sum[0:1, :] * scale for scale in scales]
        ff = up_shift_sum.shape[1]
        head = dealt(stack(lines + [small[0:3, :]]), share, devices)
        tail = dealt(stack(down_part), share, devices) + dealt(
            stack([jnp.zeros((2, ff), jnp.float32)] + up_part), ff // devices, devices
        )
        for index, spot in enumerate(spots):
            rows_of = slice(index * 8, (index + 1) * 8)
            thin_terms[spot] = jnp.concatenate([head[rows_of], tail[rows_of]], axis=0)
        store.wait()

    def project_scope():
        low = jnp.bfloat16
        pl.run_scoped(
            project_back,
            pltpu.VMEM((rows, 3 * width), low),
            pltpu.VMEM((width, rows), low),
            pltpu.VMEM((rows, width), low),
            pltpu.VMEM((width, 3 * width), low),
            pltpu.VMEM((rows, width), low),
            pltpu.VMEM((rows, width), jnp.float32),
            pltpu.VMEM((rows, width), low),
        )

    group_width = width // 2
    stream = y * 2 + c

    def attention(group):
        cols = pl.ds(group * group_width, group_width)
        value_cols = pl.ds(width + group * group_width, group_width)

        def act(keys, values, q_in, g_in, mixed_in, *work):
            pairs = [
                (kv.at[:, cols], keys),
                (kv.at[:, value_cols], values),
                (queries.at[:, cols], q_in),
                (mixed_grad.at[:, cols], g_in),
                (mixed_t.at[cols, :], mixed_in),
            ]
            loads = [pltpu.make_async_copy(src, dst, away_sem.at[j]) for j, (src, dst) in enumerate(pairs)]
            for copy in loads:
                copy.start()
            for copy in loads:
                copy.wait()
            back_group(
                group, kind, stream, log_total, keys, values, q_in, g_in, mixed_in,
                dq.at[:, cols], flow.tick, *work,
            )
            dk, dv = work[-2:]
            for part, (terms, rest, begin) in enumerate(((dk, keys, cols), (dv, values, value_cols))):
                for level in range(2):
                    mine = (level * 2 + c) * rows
                    away = (level * 2 + 1 - c) * rows

                    @pl.loop(0, rows // 128)
                    def _(j, level=level, mine=mine, away=away, terms=terms, rest=rest, begin=begin):
                        to = pl.ds(pl.multiple_of(j * 128, 128), 128)
                        kept = pl.ds(pl.multiple_of(mine + j * 128, 128), 128)
                        sent = pl.ds(pl.multiple_of(away + j * 128, 128), 128)
                        kv_mine[level, to, begin] = terms[kept, :].astype(jnp.bfloat16)
                        rest[sent, :] = terms[sent, :].astype(jnp.bfloat16)

            stores = []
            for part, (rest, begin) in enumerate(((keys, cols), (values, value_cols))):
                for level in range(2):
                    sent = pl.ds(pl.multiple_of((level * 2 + 1 - c) * rows, rows), rows)
                    stores.append(
                        pltpu.make_async_copy(
                            rest.at[sent], kv_away.at[level, :, begin], away_sem.at[part * 2 + level]
                        )
                    )
            for copy in stores:
                copy.start()
            for copy in stores:
                copy.wait()
            if group == 1:
                kv_beside.start()

        def scope():
            low = jnp.bfloat16
            heads = group_width // HEAD_DIM
            everyone = 4 * rows
            pl.run_scoped(
                act,
                pltpu.VMEM((everyone, group_width), low),
                pltpu.VMEM((everyone, group_width), low),
                pltpu.VMEM((rows, group_width), low),
                pltpu.VMEM((rows, group_width), low),
                pltpu.VMEM((group_width, rows), jnp.float32),
                pltpu.VMEM((group_width, everyone), low),
                pltpu.VMEM((heads, rows, PAIR), low),
                pltpu.VMEM((heads, rows, PAIR), low),
                pltpu.VMEM((heads, PAIR, rows), low),
                pltpu.VMEM((heads, PAIR, rows), low),
                pltpu.VMEM((group_width, TQ), jnp.float32),
                pltpu.VMEM((8, rows), jnp.float32),
                pltpu.VMEM((everyone, group_width), jnp.float32),
                pltpu.VMEM((everyone, group_width), jnp.float32),
            )

        return scope

    flow = Pipeline(chunks, 2, start, wait)
    attention(0)()
    flow.tick()
    attention(1)()
    flow.tick()
    halve()
    flow.tick()
    project_scope()
    flow.tick(STEPS + len(chunks))
    lane = lax.broadcasted_iota(jnp.int32, (1, 128), 1)
    outs[4][0, THIN_ROWS - 1 : THIN_ROWS, :] = jnp.where(
        lane == 0, counts[0], jnp.where(lane == 1, counts[1], 0.0)
    )
    for copy in (kv_beside, kv_across):
        copy.wait_send()
    for chunk in chunks:
        for step in range(STEPS):
            for piece in chunk:
                for copy, sends, _ in copies_of(piece, step):
                    guard(sends, copy.wait_send)


def scatter_all(
    up, down, out, small, up_shift_sum, vectors, kind, log_total,
    queries, kv, mixed_grad, mixed_t, normed, weight, tokens, residual_grad, depth,
):
    rows, width = tokens.shape
    far = [up, down, out]
    kinds = (True, True, False, False, False)
    share, ff_share, ff = up.shape[4], down.shape[4], up.shape[5]
    chunks, cuts = scatter_chunks(share, width, ff_share, ff)
    n_pieces = sum(len(chunk) for chunk in chunks)
    anywhere, inside = pl.BlockSpec(memory_space=pl.ANY), pl.BlockSpec(memory_space=pltpu.VMEM)
    low, box = jnp.bfloat16, (depth, 2, 2, 2)
    tails = [a.shape[4:] for a in far] + [(share, 3 * width), (THIN_ROWS, 128)]
    dtypes = [low] * 4 + [jnp.float32]
    experts = [2 if kind else 1 for kind in kinds]
    scratch = [
        pltpu.VMEM((e, depth, 2, 2) + tail, dtype) for e, tail, dtype in zip(experts, tails, dtypes)
    ]
    plain, turned = [], []
    for tail, cut in zip(tails, cuts):
        plain.append((cut[0] or tail[0], cut[1] or tail[1]))
        turned.append((tail[0] - cut[0], tail[1] - cut[1]) if any(cut) else (8, 128))
    for middle in ((depth, 2), (depth,), (depth - 1,)):
        scratch += [pltpu.VMEM((e,) + middle + t, d) for e, t, d in zip(experts, plain, dtypes)]
    scratch += [pltpu.VMEM((e,) + t, d) for e, t, d in zip(experts, plain, dtypes)]
    for middle in ((2, 2), (depth - 1, 2, 2), (2,), ()):
        scratch += [pltpu.VMEM((e,) + middle + t, d) for e, t, d in zip(experts, turned, dtypes)]
    scratch += [pltpu.VMEM((depth, 2, 2) + a.shape[4:], low) for a in far]
    scratch += [
        pltpu.VMEM(box + (share, 3 * width), low),
        pltpu.VMEM(box + (THIN_ROWS, 128), jnp.float32),
        pltpu.VMEM((2, rows, 2 * width), low),
        pltpu.VMEM((rows, 2 * width), low),
        pltpu.VMEM((2, rows, 2 * width), low),
        pltpu.VMEM((rows, width), low),
        pltpu.SemaphoreType.DMA((n_pieces, depth + 3)),
        pltpu.SemaphoreType.DMA((n_pieces, depth + 3)),
        pltpu.SemaphoreType.DMA((3,)),
        pltpu.SemaphoreType.DMA((5,)),
        pltpu.SemaphoreType.DMA((2,)),
        pltpu.SemaphoreType.DMA((2,)),
    ]
    return pl.pallas_call(
        functools.partial(scatter_kernel, depth, kinds, chunks, cuts),
        out_shape=[
            jax.ShapeDtypeStruct((e,) + tail, jnp.float32) for e, tail in zip(experts, tails)
        ]
        + [jax.ShapeDtypeStruct((rows, width), low), jax.ShapeDtypeStruct((2, rows, 2 * width), low)],
        in_specs=[anywhere] * 3 + [inside] * 5 + [anywhere] * 8,
        out_specs=[inside] * 5 + [anywhere] * 2,
        scratch_shapes=scratch,
        compiler_params=pltpu.CompilerParams(
            collective_id=2, has_side_effects=True, vmem_limit_bytes=61 << 20
        ),
    )(
        up, down, out, small, up_shift_sum, vectors, kind, log_total,
        queries, kv, mixed_grad, mixed_t, normed, weight, tokens, residual_grad,
    )[:6]


def publish_kernel(*refs):
    count = len(refs) // 2
    for src, dst in zip(refs[:count], refs[count:]):
        dst[...] = src[...]


def publish(arrays):
    inside = pl.BlockSpec(memory_space=pltpu.VMEM)
    return pl.pallas_call(
        publish_kernel,
        out_shape=[jax.ShapeDtypeStruct(array.shape, array.dtype) for array in arrays],
        in_specs=[inside] * len(arrays),
        out_specs=[inside] * len(arrays),
        compiler_params=pltpu.CompilerParams(vmem_limit_bytes=32 << 20),
    )(*arrays)


def padded(values):
    return jnp.pad(values, ((0, 0), (0, 128 - values.shape[1])))


def body(
    near,
    tokens,
    group_kind,
    ln1_gain,
    ln1_bias,
    w_qkv,
    q_bias,
    v_bias,
    w_out,
    out_bias,
    ln2_gain,
    ln2_bias,
    w_up,
    b_up,
    w_down,
    b_down,
    cotangent,
):
    row_count, model_width = tokens.shape
    stream_size = lax.axis_size("stream")
    stream_place = lax.axis_index("stream")
    devices = lax.axis_size("items") * stream_size
    group_type = group_kind[0]
    expert_pick = jnp.where(stream_place == stream_size - 1, 1, 0).astype(jnp.int32)
    share, ff_share, ff = model_width // devices, w_down.shape[1], w_up.shape[2]
    both = ("items", "stream")
    low = jnp.bfloat16
    thin = jnp.stack([ln1_gain, ln1_bias, q_bias, v_bias, out_bias, ln2_gain, ln2_bias])
    thin = jnp.concatenate(
        [padded(thin), padded(b_up), padded(b_down), padded(group_kind.astype(low)[:, None])]
    )
    thin = jnp.pad(thin, ((0, THIN_ROWS - thin.shape[0]), (0, 0)))
    tokens_f = tokens.astype(jnp.float32)
    kind_wide = jnp.broadcast_to(group_type.astype(jnp.float32), (8, 128))
    place_at = stream_place.astype(jnp.int32)[None]
    if near:
        depth = lax.axis_size("items") // 2
        (
            thin_all,
            out_weight,
            up_all,
            down_all,
            qkv_weight,
            normed_low,
            queries,
            vectors,
            kv,
            mixed_low,
            mixed_t,
            log_total,
        ) = gather_all(thin, w_qkv, w_out, w_up, w_down, tokens, kind_wide, depth)
        thin_all = thin_all.reshape(devices, THIN_ROWS, 128)
        out_weight = out_weight.reshape(model_width, model_width)
        up_all = up_all.reshape(2, model_width, ff)
        down_all = down_all.reshape(2, ff, model_width)
    else:
        thin_all = lax.all_gather(thin, both, axis=0)
        qkv_weight = lax.all_gather(w_qkv, both, axis=0, tiled=True)
        out_weight = lax.all_gather(w_out, both, axis=0, tiled=True)
        up_all = lax.all_gather(w_up, both, axis=1, tiled=True)
        down_all = lax.all_gather(w_down, both, axis=1, tiled=True)
        vectors = (
            thin_all[:, :, :share].transpose(1, 0, 2).reshape(THIN_ROWS, -1).astype(jnp.float32)
        )
        normed_low = layer_norm(tokens_f, vectors[0], vectors[1]).astype(low)
        shifts = jnp.concatenate([vectors[2], jnp.zeros_like(vectors[2]), vectors[3]])
        projected = (product(normed_low, qkv_weight) + shifts).astype(low)
        queries = projected[:, :model_width]
        kv = lax.all_gather(projected[:, model_width:], "stream", axis=0, tiled=True)
        mixed_low, mixed_t, log_total = attend(kind_wide, place_at, queries, kv)
    up_shift_all = thin_all[:, 7:9, :ff_share].transpose(1, 0, 2).reshape(2, ff)
    (
        output,
        residual_grad,
        grad_out_weight,
        mixed_grad,
        grad_up,
        grad_down,
        small,
        grad_up_shift,
    ) = feed(
        expert_pick[None],
        place_at,
        kind_wide,
        vectors,
        up_shift_all[:, None],
        tokens,
        mixed_low,
        out_weight,
        cotangent,
        up_all,
        down_all,
    )
    if near:
        box = (depth, 2, 2, 2)
        up_sum, down_sum, out_sum, qkv_sum, thin_sum, token_grad = scatter_all(
            grad_up.reshape(box + (share, ff)),
            grad_down.reshape(box + (ff_share, model_width)),
            grad_out_weight.reshape(box + (share, model_width)),
            small,
            grad_up_shift,
            vectors,
            kind_wide,
            log_total,
            queries,
            kv,
            mixed_grad,
            mixed_t,
            normed_low,
            qkv_weight,
            tokens,
            residual_grad,
            depth,
        )
        thin_sum = thin_sum[0]
        totals = thin_sum[THIN_ROWS - 1, :2]
        up_sum, down_sum, out_sum, qkv_sum, token_grad = publish(
            [up_sum, down_sum, out_sum[0], qkv_sum[0], token_grad]
        )
    else:
        kinds = vectors[11, :: stream_size * share].astype(jnp.int32)
        tally = []
        for kind in range(2):
            modality = layout(
                jnp.int32(kind), jnp.arange(stream_size * row_count, dtype=jnp.int32), row_count
            )[1]
            tally.append([jnp.sum((modality == e).astype(jnp.float32)) for e in range(2)])
        totals = jnp.stack(
            [jnp.sum(jnp.where(kinds == 0, tally[0][e], tally[1][e])) for e in range(2)]
        )
        factor = lax.rsqrt(totals)
        pick = (jnp.arange(2, dtype=jnp.int32) == expert_pick).astype(jnp.float32) * factor

        def lanes(values):
            values = values.reshape(values.shape[0], devices, -1).transpose(1, 0, 2)
            return jnp.pad(values, ((0, 0), (0, 0), (0, 128 - values.shape[2])))

        scatter = functools.partial(
            lax.psum_scatter, axis_name=both, scatter_dimension=0, tiled=True
        )
        wide = functools.partial(lax.psum_scatter, axis_name=both, scatter_dimension=1, tiled=True)
        query_grad, kv_terms = attend_back(
            kind_wide, place_at, queries, kv, mixed_grad, mixed_t, log_total
        )
        kv_grad = lax.psum_scatter(
            kv_terms.astype(jnp.float32), "stream", scatter_dimension=0, tiled=True
        )
        qkv_grad = jnp.concatenate([query_grad, kv_grad.astype(low)], axis=1)
        grad_qkv = product_lead(normed_low, qkv_grad)
        early = [
            jnp.sum(qkv_grad[:, :model_width].astype(jnp.float32), axis=0),
            jnp.sum(qkv_grad[:, 2 * model_width :].astype(jnp.float32), axis=0),
        ]
        norm_one_grad = product_trail(qkv_grad, qkv_weight)
        token_part, *grads_one = jax.vjp(layer_norm, tokens_f, vectors[0], vectors[1])[1](
            norm_one_grad
        )
        token_grad = (residual_grad + token_part).astype(low)
        up_sum = wide(pick[:, None, None] * grad_up.astype(jnp.float32)[None])
        down_sum = wide(pick[:, None, None] * grad_down.astype(jnp.float32)[None])
        out_sum, qkv_sum = scatter(grad_out_weight.astype(jnp.float32)), scatter(grad_qkv)
        thin_terms = [
            lanes(jnp.stack(grads_one + early + [small[0], small[1], small[2]])),
            jnp.zeros((devices, 1, 128), jnp.float32),
            lanes(pick[:, None] * small[3][None]),
            lanes(pick[:, None] * grad_up_shift[0][None]),
            jnp.zeros((devices, THIN_ROWS - 12, 128), jnp.float32),
        ]
        thin_sum = scatter(jnp.concatenate(thin_terms, axis=1))[0]
    lines = [thin_sum[k, :share] for k in range(7)]
    return (
        output,
        token_grad,
        lines[0],
        lines[1],
        qkv_sum,
        lines[2],
        lines[3],
        out_sum,
        lines[4],
        lines[5],
        lines[6],
        up_sum,
        thin_sum[10:12, :ff_share],
        down_sum,
        thin_sum[8:10, :share],
        totals,
    )


def solution(mesh):
    placed = (
        P(("items", "stream"), None),
        P("items"),
        P(("items", "stream")),
        P(("items", "stream")),
        P(("items", "stream"), None),
        P(("items", "stream")),
        P(("items", "stream")),
        P(("items", "stream"), None),
        P(("items", "stream")),
        P(("items", "stream")),
        P(("items", "stream")),
        P(None, ("items", "stream"), None),
        P(None, ("items", "stream")),
        P(None, ("items", "stream"), None),
        P(None, ("items", "stream")),
        P(("items", "stream"), None),
    )
    near = mesh.shape["items"] == 8 and mesh.shape["stream"] == 4
    return jax.shard_map(
        functools.partial(body, near),
        mesh=mesh,
        in_specs=placed,
        out_specs=(
            P(("items", "stream"), None),
            P(("items", "stream"), None),
            P(("items", "stream")),
            P(("items", "stream")),
            P(("items", "stream"), None),
            P(("items", "stream")),
            P(("items", "stream")),
            P(("items", "stream"), None),
            P(("items", "stream")),
            P(("items", "stream")),
            P(("items", "stream")),
            P(None, ("items", "stream"), None),
            P(None, ("items", "stream")),
            P(None, ("items", "stream"), None),
            P(None, ("items", "stream")),
            P(),
        ),
        check_vma=False,
    )
```

```python
import functools

import jax
import jax.numpy as jnp
from jax import lax
from jax.experimental import pallas as pl
from jax.experimental.pallas import tpu as pltpu
from jax.sharding import PartitionSpec as P

HEADS = 12
HEAD_DIM = 64
PATCH_S = 197
PATCH_L = 577
TEXT_LEN = 40
ITEMS_S = 7
ITEMS_L = 2


NORM_EPS = 1e-05
MASKED = -1000000000.0


def layer_norm(values, gain_row, shift_row):
    row_mean = jnp.mean(values, axis=-1, keepdims=True)
    centred = values - row_mean
    variance = jnp.mean(centred * centred, axis=-1, keepdims=True)
    return centred * lax.rsqrt(variance + NORM_EPS) * gain_row + shift_row


def gelu_exact(values):
    return jax.nn.gelu(values, approximate=False)


def layout(group_type, positions, row_count):
    patch_len = jnp.where(group_type == 0, PATCH_S, PATCH_L).astype(jnp.int32)
    members = jnp.where(group_type == 0, ITEMS_S, ITEMS_L).astype(jnp.int32)
    is_patch = positions < 3 * row_count
    patch_item = positions // patch_len
    text_item = jnp.maximum(positions - 3 * row_count, 0) // TEXT_LEN
    member = jnp.where(is_patch, patch_item, text_item)
    member = jnp.where(member < members, member, -1)
    modality = jnp.where(member < 0, 2, jnp.where(is_patch, 0, 1)).astype(jnp.int32)
    return (member, modality)


def product(first_op, second_op):
    return jnp.dot(first_op, second_op, preferred_element_type=jnp.float32)


def product_lead(first_op, second_op):
    return lax.dot_general(
        first_op, second_op, (((0,), (0,)), ((), ())), preferred_element_type=jnp.float32
    )


def product_trail(first_op, second_op):
    return lax.dot_general(
        first_op, second_op, (((1,), (1,)), ((), ())), preferred_element_type=jnp.float32
    )


def halves(length):
    return ((0, length // 2), (length // 2, length // 2))


def divided(length, unit, *shares):
    found, begin = [], 0
    for share in shares:
        found.append((begin, share * unit))
        begin += share * unit
    assert begin == length
    return found


def gather_chunks(share, width, ff_share, ff):
    rows = (0, share)
    near_cols = divided(3 * width, 128, 9, 9)
    out_cols = divided(width, 128, 3, 3)
    up_cols = divided(ff, 128, 4, 14, 6)
    down_rows = divided(ff_share, 16, 1, 3, 2)
    chunks = [
        [((0, None), (0, THIN_ROWS), (0, 128), 0, False)]
        + [((1, None), rows, cols, order, False) for order, cols in enumerate(near_cols)],
        [((2, None), rows, cols, order, False) for order, cols in enumerate(out_cols)],
    ]
    def up_chunk(e, parts):
        return [((3, e), rows, cols, order, e == 1) for order, cols in enumerate(parts) if cols[1]]

    def down_chunk(e, parts):
        return [((4, e), band, (0, width), order, e == 1) for order, band in enumerate(parts)]

    chunks += [up_chunk(1, up_cols), down_chunk(1, down_rows), down_chunk(0, down_rows)]
    unit, begin = 128, 0
    for shares in ((2, 7, 3), (1, 5, 2), (1, 2, 1)):
        parts = []
        for blocks in shares:
            parts.append((begin * unit, blocks * unit))
            begin += blocks
        chunks.append(up_chunk(0, parts))
    return chunks


def scatter_chunks(share, width, ff_share, ff):
    rows = (0, share)
    near_cols = divided(3 * width, 128, 7, 7, 4)
    out_cols = divided(width, 128, 2, 3, 1)
    up_cols = divided(ff, 128, 4, 14, 6)
    down_rows = divided(ff_share, 16, 1, 3, 2)
    chunks = [[(2, 0, rows, cols, order) for order, cols in enumerate(out_cols)]]
    for e in (1, 0):
        chunks.append([(0, e, rows, cols, order) for order, cols in enumerate(up_cols)])
        chunks.append(
            [(1, e, band, (0, width), order) for order, band in enumerate(down_rows)]
        )
    chunks.append([])
    chunks.append(
        [(3, 0, rows, cols, order) for order, cols in enumerate(near_cols)]
    )
    chunks.append([(4, 0, (0, THIN_ROWS), (0, 128), 0)])
    cuts = (
        (0, up_cols[2][0]),
        (down_rows[2][0], 0),
        (0, out_cols[2][0]),
        (0, near_cols[2][0]),
        (0, 0),
    )
    return chunks, cuts


TQ, TK = 256, 128
PAIR = 2 * HEAD_DIM


def trail(first_op, second_op):
    return lax.dot_general(
        first_op, second_op, (((1,), (1,)), ((), ())), preferred_element_type=jnp.float32
    )


def span(kind, start, length, image_rows):
    patch_len, members = ((PATCH_S, ITEMS_S), (PATCH_L, ITEMS_L))[kind]
    image = start < image_rows
    low = jnp.where(image, lax.div(start, patch_len), lax.div(start - image_rows, TEXT_LEN))
    high = jnp.where(
        image,
        lax.div(start + length - 1, patch_len),
        lax.div(start + length - 1 - image_rows, TEXT_LEN),
    )
    return low, high, members


def meets(first, second, image_rows, loose):
    found = False
    for kind in range(2):
        low_a, high_a, members = span(kind, *first, image_rows)
        low_b, high_b, _ = span(kind, *second, image_rows)
        low = jnp.maximum(low_a, low_b)
        high = jnp.minimum(jnp.minimum(high_a, high_b), members - 1)
        found = jnp.logical_or(found, low <= high)
        if loose:
            both = jnp.logical_and(high_a >= members, high_b >= members)
            found = jnp.logical_or(found, both)
    return found


def member_of(kind, position, image_rows):
    patch_len = PATCH_S + kind * float(PATCH_L - PATCH_S)
    members = ITEMS_S + kind * float(ITEMS_L - ITEMS_S)
    patch = jnp.floor((position + 0.5) / patch_len)
    text = jnp.floor((position - image_rows + 0.5) * (1.0 / TEXT_LEN))
    member = jnp.where(position < image_rows, patch, text)
    return jnp.where(member < members, member, -1.0)


def same_item(kind, stream, rows, qt, kt, image_rows):
    keys = lax.broadcasted_iota(jnp.int32, (TK, 1), 0) + kt * TK
    own = lax.broadcasted_iota(jnp.int32, (1, TQ), 1) + (stream * rows + qt * TQ)
    key_member = member_of(kind, keys.astype(jnp.float32), image_rows)
    return key_member == member_of(kind, own.astype(jnp.float32), image_rows)


def half_of(pair, which):
    lanes = lax.broadcasted_iota(jnp.int32, pair.shape, 1)
    return jnp.where((lanes < HEAD_DIM) == (which == 0), pair, jnp.zeros_like(pair))


def upper_of(pair, which):
    keep = pair[which * HEAD_DIM : (which + 1) * HEAD_DIM]
    parts = [keep, jnp.zeros_like(keep)]
    return jnp.concatenate(parts if which == 0 else parts[::-1], axis=0)


def scale_queries(q_ref, scaled):
    for pair in range(q_ref.shape[1] // PAIR):
        columns = slice(pair * PAIR, (pair + 1) * PAIR)
        value = (q_ref[:, columns] * jnp.bfloat16(HEAD_DIM ** (-0.5))).T
        for which in range(2):
            scaled[2 * pair + which] = upper_of(value, which)


def flip_columns(kv_ref, begin, flipped):
    width = flipped.shape[0]

    @pl.loop(0, flipped.shape[1] // TK)
    def _(kt):
        keys = pl.ds(pl.multiple_of(kt * TK, TK), TK)
        flipped[:, keys] = kv_ref[keys, begin : begin + width].T


def attend_part(qt, begin, end, kind_ref, stream, kv_ref, values_t, scaled, mixed_ref, mixed_t, log_total, top, total):
    width, everyone = values_t.shape
    rows = mixed_ref.shape[0]
    heads = width // HEAD_DIM
    image_rows = everyone - rows
    here = slice(qt * TQ, (qt + 1) * TQ)
    if begin == 0:
        top[...] = jnp.full(top.shape, -1e30, jnp.float32)
        total[...] = jnp.zeros(total.shape, jnp.float32)
        mixed_t[:, here] = jnp.zeros((width, TQ), jnp.float32)

    @pl.loop(begin, end)
    def _(kt):
        needed = meets((stream * rows + qt * TQ, TQ), (kt * TK, TK), image_rows, True)

        @pl.when(needed)
        def _():
            keys = pl.ds(pl.multiple_of(kt * TK, TK), TK)
            allowed = same_item(kind_ref[0:1, 0:1], stream, rows, qt, kt, image_rows)
            scores, parts, fades = [], [], []
            for head in range(heads):
                pair = slice(head // 2 * PAIR, (head // 2 + 1) * PAIR)
                raw = jnp.dot(
                    kv_ref[keys, pair], scaled[head, :, here], preferred_element_type=jnp.float32
                )
                scores.append(jnp.where(allowed, raw, MASKED))
            for head, score in enumerate(scores):
                line = slice(head, head + 1)
                old = top[line]
                new = jnp.maximum(old, jnp.max(score, axis=0, keepdims=True))
                top[line] = new
                fade = jnp.exp(old - new)
                part = jnp.exp(score - new)
                total[line] = total[line] * fade + jnp.sum(part, axis=0, keepdims=True)
                parts.append(part.astype(jnp.bfloat16))
                fades.append(fade)
            for head in range(heads):
                own = slice(head * HEAD_DIM, (head + 1) * HEAD_DIM)
                mixed_t[own, here] = mixed_t[own, here] * fades[head] + jnp.dot(
                    values_t[own, keys], parts[head], preferred_element_type=jnp.float32
                )

    if end == everyone // TK:
        for head in range(heads):
            own = slice(head * HEAD_DIM, (head + 1) * HEAD_DIM)
            mixed_t[own, here] = mixed_t[own, here] / total[head : head + 1]
        log_total[:, here] = top[...] + jnp.log(total[...])
        mixed_ref[here, :] = mixed_t[:, here].T.astype(jnp.bfloat16)


def attend_kernel(kind, place_ref, q_ref, kv_ref, mixed_ref, mixed_t, log_total, values_t, scaled, top, total):
    scale_queries(q_ref, scaled)
    flip_columns(kv_ref, q_ref.shape[1], values_t)
    for qt in range(q_ref.shape[0] // TQ):
        attend_part(
            qt, 0, kv_ref.shape[0] // TK, kind, place_ref[0], kv_ref, values_t, scaled, mixed_ref,
            mixed_t, log_total, top, total,
        )


def attend(kind, place_at, queries, kv):
    rows, width = queries.shape
    heads = width // HEAD_DIM
    inside = pl.BlockSpec(memory_space=pltpu.VMEM)
    lines = -(-heads // 8) * 8
    return pl.pallas_call(
        attend_kernel,
        out_shape=(
            jax.ShapeDtypeStruct((rows, width), jnp.bfloat16),
            jax.ShapeDtypeStruct((width, rows), jnp.float32),
            jax.ShapeDtypeStruct((lines, rows), jnp.float32),
        ),
        in_specs=[inside, pl.BlockSpec(memory_space=pltpu.SMEM)] + [inside] * 2,
        out_specs=(inside,) * 3,
        scratch_shapes=[
            pltpu.VMEM((width, kv.shape[0]), jnp.bfloat16),
            pltpu.VMEM((heads, PAIR, rows), jnp.bfloat16),
            pltpu.VMEM((lines, TQ), jnp.float32),
            pltpu.VMEM((lines, TQ), jnp.float32),
        ],
        compiler_params=pltpu.CompilerParams(vmem_limit_bytes=56 << 20),
    )(kind, place_at, queries, kv)


def back_group(
    group, kind, stream, log_total, keys_ref, values_ref, q_ref, g_ref, mixed_t, dq_ref, between,
    keys_t, scaled, grads, scaled_t, grads_t, dq_t, centre, dk, dv,
):
    everyone, width = keys_ref.shape
    rows = q_ref.shape[0]
    heads = width // HEAD_DIM
    image_rows = everyone - rows
    for pair in range(heads // 2):
        columns = slice(pair * PAIR, (pair + 1) * PAIR)
        value = q_ref[:, columns] * jnp.bfloat16(HEAD_DIM ** (-0.5))
        grad = g_ref[:, columns]
        value_t, grad_t = value.T, grad.T
        product = mixed_t[columns, :] * grad_t.astype(jnp.float32)
        for which in range(2):
            head = 2 * pair + which
            scaled[head] = half_of(value, which)
            grads[head] = half_of(grad, which)
            scaled_t[head] = upper_of(value_t, which)
            grads_t[head] = upper_of(grad_t, which)
            centre[head : head + 1] = jnp.sum(
                product[which * HEAD_DIM : (which + 1) * HEAD_DIM], axis=0, keepdims=True
            )
    flip_columns(keys_ref, 0, keys_t)

    @pl.loop(0, everyone // TK)
    def _(kt):
        keys = pl.ds(pl.multiple_of(kt * TK, TK), TK)
        dk[keys, :] = jnp.zeros((TK, width), jnp.float32)
        dv[keys, :] = jnp.zeros((TK, width), jnp.float32)

    for qt in range(rows // TQ):
        here = slice(qt * TQ, (qt + 1) * TQ)
        if qt:
            between()
        dq_t[...] = jnp.zeros(dq_t.shape, jnp.float32)

        @pl.loop(0, everyone // TK)
        def _(kt, qt=qt, here=here):
            needed = meets((stream * rows + qt * TQ, TQ), (kt * TK, TK), image_rows, False)

            @pl.when(needed)
            def _():
                keys = pl.ds(pl.multiple_of(kt * TK, TK), TK)
                allowed = same_item(kind[0:1, 0:1], stream, rows, qt, kt, image_rows)
                scores, prob_grads, probs_low, score_low = [], [], [], []
                for head in range(heads):
                    pair = slice(head // 2 * PAIR, (head // 2 + 1) * PAIR)
                    scores.append(
                        jnp.dot(
                            keys_ref[keys, pair],
                            scaled_t[head, :, here],
                            preferred_element_type=jnp.float32,
                        )
                    )
                    prob_grads.append(
                        jnp.dot(
                            values_ref[keys, pair],
                            grads_t[head, :, here],
                            preferred_element_type=jnp.float32,
                        )
                    )
                for head in range(heads):
                    line = slice(group * heads + head, group * heads + head + 1)
                    shifted = scores[head] - log_total[line, here]
                    probs = jnp.exp(jnp.where(allowed, shifted, MASKED))
                    probs_low.append(probs.astype(jnp.bfloat16))
                    inner = prob_grads[head] - centre[head : head + 1, here]
                    score_low.append((probs * inner).astype(jnp.bfloat16))
                for head in range(heads):
                    own = slice(head * HEAD_DIM, (head + 1) * HEAD_DIM)
                    dq_t[own, :] += jnp.dot(
                        keys_t[own, keys], score_low[head], preferred_element_type=jnp.float32
                    )
                for head in range(0, heads, 2):
                    columns = slice(head * HEAD_DIM, head * HEAD_DIM + PAIR)
                    for terms, left, right in ((dk, score_low, scaled), (dv, probs_low, grads)):
                        terms[keys, columns] += jnp.dot(
                            left[head], right[head, here, :], preferred_element_type=jnp.float32
                        ) + jnp.dot(
                            left[head + 1],
                            right[head + 1, here, :],
                            preferred_element_type=jnp.float32,
                        )

        dq_ref[here, :] = (dq_t[...].T * HEAD_DIM ** (-0.5)).astype(jnp.bfloat16)


def attend_back_kernel(
    kind, place_ref, q_ref, kv_ref, g_ref, mixed_t, log_total, dq_ref, dkv_ref, *work
):
    width = q_ref.shape[1]
    back_group(
        0, kind, place_ref[0], log_total, kv_ref.at[:, pl.ds(0, width)],
        kv_ref.at[:, pl.ds(width, width)], q_ref, g_ref, mixed_t, dq_ref, lambda: None,
        *work,
    )
    dk, dv = work[-2:]

    @pl.loop(0, kv_ref.shape[0] // TK)
    def _(kt):
        keys = pl.ds(pl.multiple_of(kt * TK, TK), TK)
        dkv_ref[keys, :width] = dk[keys, :].astype(jnp.bfloat16)
        dkv_ref[keys, width:] = dv[keys, :].astype(jnp.bfloat16)


def attend_back(kind, place_at, queries, kv, mixed_grad, mixed_t, log_total):
    rows, width = queries.shape
    heads = width // HEAD_DIM
    inside = pl.BlockSpec(memory_space=pltpu.VMEM)
    lines = -(-heads // 8) * 8
    everyone = kv.shape[0]
    return pl.pallas_call(
        attend_back_kernel,
        out_shape=(
            jax.ShapeDtypeStruct((rows, width), jnp.bfloat16),
            jax.ShapeDtypeStruct((everyone, 2 * width), jnp.bfloat16),
        ),
        in_specs=[inside, pl.BlockSpec(memory_space=pltpu.SMEM)] + [inside] * 5,
        out_specs=(inside,) * 2,
        scratch_shapes=[
            pltpu.VMEM((width, everyone), jnp.bfloat16),
            pltpu.VMEM((heads, rows, PAIR), jnp.bfloat16),
            pltpu.VMEM((heads, rows, PAIR), jnp.bfloat16),
            pltpu.VMEM((heads, PAIR, rows), jnp.bfloat16),
            pltpu.VMEM((heads, PAIR, rows), jnp.bfloat16),
            pltpu.VMEM((width, TQ), jnp.float32),
            pltpu.VMEM((lines, rows), jnp.float32),
            pltpu.VMEM((everyone, width), jnp.float32),
            pltpu.VMEM((everyone, width), jnp.float32),
        ],
        compiler_params=pltpu.CompilerParams(vmem_limit_bytes=58 << 20),
    )(kind, place_at, queries, kv, mixed_grad, mixed_t, log_total)

def feed_kernel(
    pick, place_ref, kind, vectors, up_shift, tokens, mixed, out_weight, cotangent, up, down,
    output, residual_grad, grad_out, mixed_grad, grad_up, grad_down, small, up_shift_sum,
    residual, normed, normed_t, grad, branch, back,
):
    step = pl.program_id(0)
    rows, width = tokens.shape
    image_rows = (lax.axis_size("stream") - 1) * rows
    tall = 128

    def blocks(act):
        @pl.loop(0, rows // tall)
        def _(j):
            act(pl.ds(pl.multiple_of(j * tall, tall), tall))

    def unit_of(value):
        centred = value - jnp.mean(value, axis=-1, keepdims=True)
        scale = lax.rsqrt(jnp.mean(centred * centred, axis=-1, keepdims=True) + NORM_EPS)
        return centred * scale, scale

    def live(j_start):
        position = lax.broadcasted_iota(jnp.int32, (tall, 1), 0) + (place_ref[0] * rows + j_start)
        return member_of(kind[0:1, 0:1], position.astype(jnp.float32), image_rows) >= 0.0

    @pl.when(step == 0)
    def _():
        @pl.loop(0, rows // tall)
        def _(j):
            block = pl.ds(pl.multiple_of(j * tall, tall), tall)
            value = (
                tokens[block, :].astype(jnp.float32)
                + jnp.dot(mixed[block, :], out_weight[...], preferred_element_type=jnp.float32)
                + vectors[4:5, :]
            )
            residual[block, :] = value
            unit, _ = unit_of(value)
            normed[block, :] = (unit * vectors[5:6, :] + vectors[6:7, :]).astype(jnp.bfloat16)
            given = cotangent[block, :]
            grad[block, :] = jnp.where(live(j * tall), given, jnp.zeros_like(given))

        normed_t[...] = normed[...].T
        branch[...] = jnp.zeros(branch.shape, jnp.float32)
        back[...] = jnp.zeros(back.shape, jnp.float32)

    before = (
        jnp.dot(normed[...], up[0], preferred_element_type=jnp.float32) + up_shift[0].astype(jnp.float32)
    )
    hidden_grad = product_trail(grad[...], down[0])
    half = 0.5 + 0.5 * lax.erf(before * 0.5**0.5)
    hidden = (before * half).astype(jnp.bfloat16)
    slope = half + before * (jnp.exp(-0.5 * before * before) * 0.3989422804014327)
    before_grad = hidden_grad * slope
    low_grad = before_grad.astype(jnp.bfloat16)
    up_shift_sum[...] = jnp.broadcast_to(
        jnp.sum(low_grad.astype(jnp.float32), axis=0, keepdims=True), up_shift_sum.shape
    )
    branch[...] += jnp.dot(hidden, down[0], preferred_element_type=jnp.float32)
    back[...] += product_trail(low_grad, up[0])
    grad_up[...] = jnp.dot(normed_t[...], low_grad, preferred_element_type=jnp.float32).astype(
        jnp.bfloat16
    )
    grad_down[...] = jnp.dot(hidden.T, grad[...], preferred_element_type=jnp.float32).astype(
        jnp.bfloat16
    )

    @pl.when(step == pl.num_programs(0) - 1)
    def _():
        down_shift = jnp.where(pick[0] == 0, vectors[9:10, :], vectors[10:11, :])

        def fold(value):
            return jnp.sum(value.reshape(-1, 8, width), axis=0)

        def finish(j, carry):
            block = pl.ds(pl.multiple_of(j * tall, tall), tall)
            value = residual[block, :]
            kept = live(j * tall)
            output[block, :] = (
                value + jnp.where(kept, branch[block, :] + down_shift, 0.0)
            ).astype(jnp.bfloat16)
            unit, scale = unit_of(value)
            given = back[block, :]
            lifted = given * vectors[5:6, :]
            inner = jnp.mean(lifted * unit, axis=-1, keepdims=True)
            own = grad[block, :].astype(jnp.float32)
            total = own + scale * (
                lifted - jnp.mean(lifted, axis=-1, keepdims=True) - unit * inner
            )
            residual_grad[block, :] = total
            total_low = total.astype(jnp.bfloat16)
            normed[block, :] = total_low
            mixed_grad[block, :] = product_trail(total_low, out_weight[...]).astype(jnp.bfloat16)
            terms = (total_low.astype(jnp.float32), given * unit, given, own)
            return tuple(held + fold(term) for held, term in zip(carry, terms))

        zero = jnp.zeros((8, width), jnp.float32)
        sums = lax.fori_loop(0, rows // tall, finish, (zero,) * 4)
        lines = [jnp.sum(value, axis=0, keepdims=True) for value in sums]
        small[...] = jnp.concatenate(lines + [jnp.zeros((4, width), jnp.float32)], axis=0)
        grad_out[...] = jnp.dot(
            mixed[...].T, normed[...], preferred_element_type=jnp.float32
        ).astype(jnp.bfloat16)


def feed(pick, place_at, kind, vectors, up_shift, tokens, mixed, out_weight, cotangent, up, down):
    rows, width = tokens.shape
    ff = up.shape[2]
    band = 512
    low, wide = jnp.bfloat16, jnp.float32

    def whole(array):
        return pl.BlockSpec(array.shape, lambda i, pick, place_at: (0,) * array.ndim)

    fixed = [
        jax.ShapeDtypeStruct((rows, width), low),
        jax.ShapeDtypeStruct((rows, width), wide),
        jax.ShapeDtypeStruct((width, width), low),
        jax.ShapeDtypeStruct((rows, width), low),
    ]
    last = jax.ShapeDtypeStruct((8, width), wide)
    return pl.pallas_call(
        feed_kernel,
        out_shape=fixed
        + [
            jax.ShapeDtypeStruct((width, ff), low),
            jax.ShapeDtypeStruct((ff, width), low),
            last,
            jax.ShapeDtypeStruct((8, ff), wide),
        ],
        grid_spec=pltpu.PrefetchScalarGridSpec(
            num_scalar_prefetch=2,
            grid=(ff // band,),
            in_specs=[
                whole(kind),
                whole(vectors),
                pl.BlockSpec((1, 1, band), lambda i, pick, place_at: (pick[0], 0, i)),
                whole(tokens),
                whole(mixed),
                whole(out_weight),
                whole(cotangent),
                pl.BlockSpec((1, width, band), lambda i, pick, place_at: (pick[0], 0, i)),
                pl.BlockSpec((1, band, width), lambda i, pick, place_at: (pick[0], i, 0)),
            ],
            out_specs=[whole(array) for array in fixed]
            + [
                pl.BlockSpec((width, band), lambda i, pick, place_at: (0, i)),
                pl.BlockSpec((band, width), lambda i, pick, place_at: (i, 0)),
                whole(last),
                pl.BlockSpec((8, band), lambda i, pick, place_at: (0, i)),
            ],
            scratch_shapes=[
                pltpu.VMEM((rows, width), wide),
                pltpu.VMEM((rows, width), low),
                pltpu.VMEM((width, rows), low),
                pltpu.VMEM((rows, width), low),
                pltpu.VMEM((rows, width), wide),
                pltpu.VMEM((rows, width), wide),
            ],
        ),
        compiler_params=pltpu.CompilerParams(vmem_limit_bytes=62 << 20),
    )(pick, place_at, kind, vectors, up_shift, tokens, mixed, out_weight, cotangent, up, down)


MESH = pl.DeviceIdType.MESH
GATHER_ORDERS = (("z", "f", "x", "y"), ("z", "f", "y", "x"), ("y", "x", "z", "f"))
SCATTER_ORDERS = (("y", "x", "a", "z"), ("x", "y", "a", "z"), ("a", "z", "x", "y"))
STEPS = 5
EVERY = slice(None)
THIN_ROWS = 16


def coords():
    items, stream = lax.axis_index("items"), lax.axis_index("stream")
    return dict(z=items // 2, x=items % 2, y=stream // 2, c=stream % 2)


def place(at):
    return (at["z"] * 2 + at["x"], at["y"] * 2 + at["c"])


def moved(at, dim, by, depth):
    return {**at, dim: lax.rem(at[dim] + by, depth if dim == "z" else 2)}


def greet(at, depth):
    peers = [moved(at, "z", k, depth) for k in range(1, depth)]
    peers += [moved(at, d, 1, depth) for d in "xyc"]
    barrier = pltpu.get_barrier_semaphore()
    for peer in peers:
        pl.semaphore_signal(barrier, inc=1, device_id=place(peer), device_id_type=MESH)
    pl.semaphore_wait(barrier, len(peers))


def guard(cond, act):
    if cond is None:
        act()
    else:
        pl.when(cond)(act)


def remote(src, dst, sems, index, device):
    return pltpu.make_async_remote_copy(
        src_ref=src,
        dst_ref=dst,
        send_sem=sems[0].at[index],
        recv_sem=sems[1].at[index],
        device_id=place(device),
        device_id_type=MESH,
    )


def both_of(first, second):
    if first is None or second is None:
        return second if first is None else first
    return jnp.logical_and(first, second)


class Pipeline:
    def __init__(self, chunks, ahead, start, wait):
        self.chunks, self.ahead, self.start, self.wait = chunks, ahead, start, wait
        self.ticks = 0
        for chunk in chunks[:ahead]:
            start(chunk, 0)

    def tick(self, times=1):
        count = len(self.chunks)
        for t in range(self.ticks, min(self.ticks + times, count + STEPS - 1)):
            if t + self.ahead < count:
                self.start(self.chunks[t + self.ahead], 0)
            for step in range(STEPS):
                if 0 <= t - step < count:
                    self.wait(self.chunks[t - step], step)
                    if step < STEPS - 1:
                        self.start(self.chunks[t - step], step + 1)
        self.ticks += times


def spots_of(depth):
    return [(a, b, c, d) for a in range(depth) for b in range(2) for c in range(2) for d in range(2)]


def columns_over(share, width):
    column = lax.broadcasted_iota(jnp.int32, (1, width), 1).astype(jnp.float32)
    owner = jnp.floor((column + 0.5) * (1.0 / share))
    return owner, column - owner * share


def spread(thin, share, width):
    owner, lane = columns_over(share, width)
    picks = lax.broadcasted_iota(jnp.int32, (128, width), 0).astype(jnp.float32) == lane
    wide = jnp.dot(thin, picks.astype(jnp.bfloat16), preferred_element_type=jnp.float32)
    total = jnp.zeros((THIN_ROWS, width), jnp.float32)
    for device in range(thin.shape[0] // THIN_ROWS):
        part = wide[device * THIN_ROWS : (device + 1) * THIN_ROWS]
        total = total + jnp.where(owner == device, part, 0.0)
    return total


def dealt(rows, share, devices):
    width = rows.shape[1]
    owner, lane = columns_over(share, width)
    picks = lax.broadcasted_iota(jnp.int32, (128, width), 0).astype(jnp.float32) == lane
    tall = jnp.concatenate(
        [jnp.where(owner == device, rows, 0.0) for device in range(devices)], axis=0
    )
    return lax.dot_general(
        tall,
        picks.astype(jnp.float32),
        (((1,), (1,)), ((), ())),
        precision=lax.Precision.HIGHEST,
        preferred_element_type=jnp.float32,
    )


def gather_kernel(depth, chunks, entries, *refs):
    it = iter(refs)
    take = lambda count: [next(it) for _ in range(count)]
    ins = take(5)
    tokens, kind = take(2)
    thin_out, out_all, up_all, down_all = take(4)
    weight_out, normed_out, queries_out, vectors, kv_out, mixed, mixed_t_out, log_total = take(8)
    (far_normed_out,) = take(1)
    thin_all, qkv_all, kv, values_t, scaled, top, total = take(7)
    qkv_weight, normed, queries, mixed_t, far_tokens, far_normed = take(6)
    local_sem = next(it)
    sems, kv_sems = take(2), take(2)
    keep_sem = next(it)
    outs = (thin_all, qkv_all, out_all, up_all, down_all)
    rows, width = tokens.shape
    devices = depth * 8
    share = width // devices
    at = coords()
    mine = (at["z"], at["x"], at["y"], at["c"])
    slot = at["y"] * 2 + at["c"]

    def source(entry):
        k, e = entry
        return ins[k] if e is None else ins[k].at[e]

    def target(entry):
        k, e = entry
        return outs[k] if e is None else outs[k].at[e]

    local = [
        pltpu.make_async_copy(source(entry), target(entry).at[mine], local_sem.at[j])
        for j, entry in enumerate(entries)
    ]
    for copy in local:
        copy.start()
    greet(at, depth)
    for copy in local:
        copy.wait()
    lower, upper = at["y"] == 0, at["y"] == 1
    number = {piece: j for j, piece in enumerate(piece for chunk in chunks for piece in chunk)}

    z = at["z"]

    def stage(piece, step):
        entry, band, cols, order, text = piece
        dims = GATHER_ORDERS[order] + ("c",)
        dim = dims[step]
        box = (pl.ds(*band), pl.ds(*cols))
        live = upper if text and "y" in dims[:step] else None

        def held(level):
            spot = {d: EVERY if d in dims[:step] else pl.ds(at[d], 1) for d in "zxyc"}
            if level is not None:
                spot["z"] = pl.ds(level, 1)
            return target(entry).at[tuple(spot[d] for d in "zxyc") + box]

        if dim == "f":
            up_view, down_view = held(0), held(depth - 1)
            up = remote(up_view, up_view, sems, (number[piece], depth + 2), {**at, "z": z + 1})
            down = remote(down_view, down_view, sems, (number[piece], depth + 2), {**at, "z": z - 1})
            return [
                (up, both_of(live, z == depth - 2), both_of(live, z == depth - 1)),
                (down, both_of(live, z == 1), both_of(live, z == 0)),
            ]
        view = held(None)
        if dim == "z":
            found = []
            for k in range(1, depth):
                to, source_level = lax.rem(z + k, depth), lax.rem(z + depth - k, depth)
                copy = remote(view, view, sems, (number[piece], k - 1), {**at, "z": to})
                sends = both_of(live, jnp.abs(to - z) != depth - 1)
                found.append((copy, sends, both_of(live, jnp.abs(source_level - z) != depth - 1)))
            return found
        sem = {"x": depth - 1, "y": depth, "c": depth + 1}[dim]
        copy = remote(view, view, sems, (number[piece], sem), moved(at, dim, 1, depth))
        if text and dim == "y":
            return [(copy, lower, upper)]
        return [(copy, live, live)]

    def each(chunk, step, which, call):
        for piece in chunk:
            for found in stage(piece, step):
                guard(found[which], functools.partial(call, found[0]))

    beside, across = moved(at, "c", 1, depth), moved(at, "y", 1, depth)
    other = across["y"] * 2 + across["c"]
    own_slot = pl.ds(pl.multiple_of(slot * rows, rows), rows)
    other_slot = pl.ds(pl.multiple_of(other * rows, rows), rows)
    to_across = remote(tokens, far_tokens, kv_sems, 0, across)
    to_beside = remote(kv.at[own_slot], kv.at[own_slot], kv_sems, 1, beside)
    onward = remote(kv.at[other_slot], kv.at[other_slot], kv_sems, 2, beside)
    to_across.start()
    keep_kv = pltpu.make_async_copy(kv, kv_out, keep_sem.at[0])
    keep_mixed = pltpu.make_async_copy(mixed_t, mixed_t_out, keep_sem.at[1])
    keep_early = [
        pltpu.make_async_copy(src, dst, keep_sem.at[2 + j])
        for j, (src, dst) in enumerate(
            [
                (thin_all, thin_out),
                (qkv_weight, weight_out),
                (normed, normed_out),
                (far_normed, far_normed_out),
                (queries, queries_out),
            ]
        )
    ]

    def project():
        spots = spots_of(depth)
        for j, spot in enumerate(spots):
            qkv_weight[j * share : (j + 1) * share, :] = qkv_all[spot]
        thin = jnp.concatenate([thin_all[spot] for spot in spots], axis=0)
        vectors[...] = spread(thin, share, width)

        to_across.wait_recv()
        for given, made in ((tokens, normed), (far_tokens, far_normed)):

            @pl.loop(0, rows // 128)
            def _(j, given=given, made=made):
                block = pl.ds(pl.multiple_of(j * 128, 128), 128)
                value = given[block, :].astype(jnp.float32)
                centred = value - jnp.mean(value, axis=-1, keepdims=True)
                scale = lax.rsqrt(jnp.mean(centred * centred, axis=-1, keepdims=True) + NORM_EPS)
                made[block, :] = (centred * scale * vectors[0:1, :] + vectors[1:2, :]).astype(
                    jnp.bfloat16
                )

        step = width // 2
        for part in (1, 2, 0):

            @pl.loop(0, 2)
            def _(j, part=part):
                cols = pl.ds(pl.multiple_of(j * step, 128), step)
                weight_cols = qkv_weight[:, pl.ds(pl.multiple_of(part * width + j * step, 128), step)]
                value = jnp.dot(normed[...], weight_cols, preferred_element_type=jnp.float32)
                if part == 0:
                    queries[:, cols] = (value + vectors[2:3, cols]).astype(jnp.bfloat16)
                    return
                far_value = jnp.dot(far_normed[...], weight_cols, preferred_element_type=jnp.float32)
                to = pl.ds(pl.multiple_of((part - 1) * width + j * step, 128), step)
                shift = vectors[3:4, cols] if part == 2 else 0.0
                kv[own_slot, to] = (value + shift).astype(jnp.bfloat16)
                kv[other_slot, to] = (far_value + shift).astype(jnp.bfloat16)

            if part == 2:
                to_beside.start()
                onward.start()
        for copy in keep_early:
            copy.start()
        scale_queries(queries, scaled)

    def attend_first():
        to_beside.wait_recv()
        onward.wait_recv()
        keep_kv.start()
        flip_columns(kv, width, values_t)

    parts = (kind, slot, kv, values_t, scaled, mixed, mixed_t, log_total, top, total)

    def attention(qt, begin, end):
        def act():
            if qt == 0 and begin == 0:
                attend_first()
            attend_part(qt, begin, end, *parts)

        return act

    everyone = kv.shape[0] // TK
    flow = Pipeline(
        chunks,
        2,
        lambda chunk, step: each(chunk, step, 1, lambda copy: copy.start()),
        lambda chunk, step: each(chunk, step, 2, lambda copy: copy.wait_recv()),
    )
    flow.tick(5)
    project()
    flow.tick()
    attention(0, 0, everyone // 2)()
    flow.tick()
    attention(0, everyone // 2, everyone)()
    flow.tick()
    attention(1, 0, everyone // 2)()
    flow.tick()
    attention(1, everyone // 2, everyone)()
    flow.tick(STEPS + len(chunks))
    for copy in (to_beside, to_across, onward):
        copy.wait_send()
    keep_mixed.start()
    for copy in keep_early + [keep_kv, keep_mixed]:
        copy.wait()
    for chunk in chunks:
        for step in range(STEPS):
            each(chunk, step, 1, lambda copy: copy.wait_send())


def gather_all(thin, w_qkv, w_out, w_up, w_down, tokens, kind, depth):
    rows, width = tokens.shape
    share, ff_share, ff = w_qkv.shape[0], w_down.shape[1], w_up.shape[2]
    entries = [(0, None), (1, None), (2, None), (3, 0), (3, 1), (4, 0), (4, 1)]
    chunks = gather_chunks(share, width, ff_share, ff)
    n_pieces = sum(len(chunk) for chunk in chunks)
    anywhere = pl.BlockSpec(memory_space=pl.ANY)
    inside = pl.BlockSpec(memory_space=pltpu.VMEM)
    low = jnp.bfloat16
    box = (depth, 2, 2, 2)
    heads, lines = width // HEAD_DIM, -(-(width // HEAD_DIM) // 8) * 8
    return pl.pallas_call(
        functools.partial(gather_kernel, depth, chunks, entries),
        out_shape=[
            jax.ShapeDtypeStruct(box + thin.shape, low),
            jax.ShapeDtypeStruct(box + (share, width), low),
            jax.ShapeDtypeStruct((2,) + box + (share, ff), low),
            jax.ShapeDtypeStruct((2,) + box + (ff_share, width), low),
            jax.ShapeDtypeStruct((width, 3 * width), low),
            jax.ShapeDtypeStruct((rows, width), low),
            jax.ShapeDtypeStruct((rows, width), low),
            jax.ShapeDtypeStruct((THIN_ROWS, width), jnp.float32),
            jax.ShapeDtypeStruct((4 * rows, 2 * width), low),
            jax.ShapeDtypeStruct((rows, width), low),
            jax.ShapeDtypeStruct((width, rows), jnp.float32),
            jax.ShapeDtypeStruct((lines, rows), jnp.float32),
            jax.ShapeDtypeStruct((rows, width), low),
        ],
        in_specs=[inside] * 7,
        out_specs=[anywhere] * 7 + [inside, anywhere, inside, anywhere, inside, anywhere],
        scratch_shapes=[
            pltpu.VMEM(box + thin.shape, low),
            pltpu.VMEM(box + (share, 3 * width), low),
            pltpu.VMEM((4 * rows, 2 * width), low),
            pltpu.VMEM((width, 4 * rows), low),
            pltpu.VMEM((heads, PAIR, rows), low),
            pltpu.VMEM((lines, TQ), jnp.float32),
            pltpu.VMEM((lines, TQ), jnp.float32),
            pltpu.VMEM((width, 3 * width), low),
            pltpu.VMEM((rows, width), low),
            pltpu.VMEM((rows, width), low),
            pltpu.VMEM((width, rows), jnp.float32),
            pltpu.VMEM((rows, width), low),
            pltpu.VMEM((rows, width), low),
            pltpu.SemaphoreType.DMA((len(entries),)),
            pltpu.SemaphoreType.DMA((n_pieces, depth + 3)),
            pltpu.SemaphoreType.DMA((n_pieces, depth + 3)),
            pltpu.SemaphoreType.DMA((3,)),
            pltpu.SemaphoreType.DMA((3,)),
            pltpu.SemaphoreType.DMA((7,)),
        ],
        compiler_params=pltpu.CompilerParams(
            collective_id=1, has_side_effects=True, vmem_limit_bytes=62 << 20
        ),
    )(thin, w_qkv, w_out, w_up, w_down, tokens, kind)


def rows_of_kind(kind, rows):
    patch_len, members = ((PATCH_S, ITEMS_S), (PATCH_L, ITEMS_L))[kind]
    return float(min(patch_len * members, 3 * rows)), float(min(TEXT_LEN * members, rows))


def scatter_kernel(depth, kinds, chunks, cuts, *refs):
    n, n_far = len(kinds), 3
    it = iter(refs)
    take = lambda count: [next(it) for _ in range(count)]
    far = take(n_far)
    small, up_shift_sum, vectors, kind, log_total = take(5)
    queries, kv, mixed_grad, mixed_t, normed, far_normed, weight, tokens, residual_grad = take(9)
    outs = take(n)
    token_grad, kv_away = take(2)
    acc, first, second, last = take(n), take(n), take(n), take(n)
    relay, z_relay, z_first, z_second, z_last = (take(n) for _ in range(5))
    own_half = take(n_far)
    qkv_terms, thin_terms, kv_sum, far_terms, far_got, kv_mine, dq = take(7)
    sems = take(2)
    local_sem, away_sem = take(2)
    kv_sems = take(2)
    rows, width = residual_grad.shape
    devices = depth * 8
    share = width // devices
    at = coords()
    z, x, y, c = (at[d] for d in "zxyc")
    ins = far + [qkv_terms, thin_terms]
    groups = devices // 4
    lane = lax.broadcasted_iota(jnp.int32, (1, width), 1)
    marks = functools.reduce(
        jnp.logical_or, [lane == group * (width // groups) for group in range(groups)]
    )
    second_kind = jnp.sum(jnp.where(marks, vectors[11:12, :], 0.0), axis=1, keepdims=True)
    counts = [
        first_count * (groups - second_kind) + second_count * second_kind
        for first_count, second_count in zip(*(rows_of_kind(kind_of, rows) for kind_of in range(2)))
    ]
    factors = [lax.rsqrt(count) for count in counts]
    local = [
        pltpu.make_async_copy(far[k].at[EVERY, EVERY, EVERY, c], own_half[k], local_sem.at[k])
        for k in range(n_far)
    ]
    for copy in local:
        copy.start()
    greet(at, depth)
    for copy in local:
        copy.wait()
    beside, across = moved(at, "c", 1, depth), moved(at, "y", 1, depth)
    kv_beside = remote(kv_away, kv_sum, kv_sems, 0, beside)
    kv_across = remote(far_terms, far_got, kv_sems, 1, across)
    lower, upper = y == 0, y == 1
    text_device = jnp.logical_and(upper, c == 1)
    image_device = jnp.logical_or(lower, c == 0)
    beside_text = jnp.logical_and(upper, c == 0)
    beside_image = jnp.logical_or(lower, c == 1)
    number = {piece: j for j, piece in enumerate(piece for chunk in chunks for piece in chunk)}

    sources = (
        (z == 0, range(2, depth)),
        (jnp.logical_and(z > 0, z < depth - 1), range(1, depth)),
        (z == depth - 1, range(1, depth - 1)),
    )

    def boxes(piece):
        k, e, band, cols, order = piece
        cut = cuts[k] if order == 2 else (0, 0)
        return (
            (pl.ds(*band), pl.ds(*cols)),
            (pl.ds(band[0] - cut[0], band[1]), pl.ds(cols[0] - cut[1], cols[1])),
        )

    def copies_of(piece, step):
        k, e, band, cols, order = piece
        box, inner = boxes(piece)
        image, text = kinds[k] and e == 0, kinds[k] and e == 1
        dims = ("c",) + SCATTER_ORDERS[order]
        dim = dims[step]
        here = acc[k].at[e]

        def make(src, dst, sem, by=1):
            return remote(src, dst, sems, (number[piece], sem), moved(at, dim, by, depth))

        sends = recvs = None
        if dim == "c":
            if image:
                sends, recvs = image_device, beside_image
            elif text:
                sends, recvs = text_device, beside_text
            src = ins[k].at[(EVERY, EVERY, EVERY, 1 - c) + box]
            return [(make(src, here.at[(EVERY, EVERY, EVERY) + box], 0), sends, recvs)]
        if text and dim == "y":
            sends, recvs = upper, lower
        elif text and "y" not in dims[:step]:
            sends = recvs = upper
        where = (EVERY, EVERY) if order == 2 else (x, y)
        if dim == "a":
            src = here.at[(depth - 1 - z,) + where + box]
            dst = z_relay[k].at[(e, EVERY, EVERY) + inner] if order == 2 else relay[k].at[(e,) + inner]
            to = {**at, "z": jnp.where(z == 0, 1, depth - 2)}
            copy = remote(src, dst, sems, (number[piece], depth + 2), to)
            ends = jnp.logical_or(z == 0, z == depth - 1)
            middle = jnp.logical_and(z > 0, z < depth - 1)
            return [(copy, both_of(sends, ends), both_of(recvs, middle))]
        if dim == "z":
            found = []
            for by in range(1, depth):
                to, source_level = lax.rem(z + by, depth), lax.rem(z + depth - by, depth)
                src = here.at[(to,) + where + box]
                if order == 2:
                    dst = z_first[k].at[(e, by - 1, EVERY, EVERY) + inner]
                else:
                    dst = last[k].at[(e, by - 1) + inner]
                found.append(
                    (
                        make(src, dst, 2 + by, by),
                        both_of(sends, jnp.abs(to - z) != depth - 1),
                        both_of(recvs, jnp.abs(source_level - z) != depth - 1),
                    )
                )
            return found
        if order == 2 and dim == "x":
            src, dst = here.at[(z, 1 - x, EVERY) + box], z_second[k].at[(e, EVERY) + inner]
            return [(make(src, dst, 1), sends, recvs)]
        if order == 2:
            src, dst = here.at[(z, x, 1 - y) + box], z_last[k].at[(e,) + inner]
            return [(make(src, dst, 2), sends, recvs)]
        if step == 1:
            spot = (EVERY, EVERY, 1 - y) if dim == "y" else (EVERY, 1 - x, EVERY)
            dst = first[k].at[(e, EVERY, EVERY) + inner]
        else:
            spot = (EVERY, x, 1 - y) if dim == "y" else (EVERY, 1 - x, y)
            dst = second[k].at[(e, EVERY) + inner]
        return [(make(here.at[spot + box], dst, step), sends, recvs)]

    def combine(piece, step):
        k, e, band, cols, order = piece
        box, inner = boxes(piece)
        image, text = kinds[k] and e == 0, kinds[k] and e == 1
        dims = ("c",) + SCATTER_ORDERS[order]
        dim = dims[step]
        here = acc[k].at[e]

        def over(spots, value_of, keep):
            @pl.loop(0, depth)
            def _(level):
                for index, spot in enumerate(spots):
                    where = (level,) + spot + box
                    value = value_of(level, index, spot)
                    here[where] = value if keep else here[where] + value

        def wide(value):
            return value.astype(jnp.float32)

        if step == 0:
            spots = [(0, 0), (0, 1), (1, 0), (1, 1)]

            def own(level, index, spot):
                if k < n_far:
                    return own_half[k][(level,) + spot + box]
                return ins[k][(level,) + spot + (c,) + box]

            if image:
                pl.when(lower)(lambda: over(spots, own, False))
                pl.when(beside_text)(lambda: over(spots, own, True))
            elif text:
                pl.when(text_device)(lambda: over(spots, own, True))
            else:
                over(spots, own, False)
        elif dim == "a":
            dest = jnp.where(z == 1, depth - 1, 0)

            def act():
                if order == 2:
                    for spot in [(0, 0), (0, 1), (1, 0), (1, 1)]:
                        where = (dest,) + spot + box
                        here[where] = here[where] + z_relay[k][(e,) + spot + inner]
                else:
                    where = (dest, x, y) + box
                    here[where] = here[where] + relay[k][(e,) + inner]

            middle = jnp.logical_and(z > 0, z < depth - 1)
            guard(both_of(upper if text and order == 2 else None, middle), act)
        elif step == STEPS - 1:

            def finish(total):
                if kinds[k]:
                    total = total * factors[e]
                outs[k][(e,) + box] = total

            def own():
                return wide(here[(z, x, y) + box])

            if order == 2:
                got = lambda: wide(z_last[k][(e,) + inner])
                if text:
                    pl.when(lower)(lambda: finish(got()))
                    pl.when(upper)(lambda: finish(own()))
                else:
                    finish(own() + got())
            else:
                for cond, bys in sources:

                    @pl.when(cond)
                    def _(bys=bys):
                        total = own()
                        for by in bys:
                            total = total + wide(last[k][(e, by - 1) + inner])
                        finish(total)
        elif dim == "z":
            for cond, bys in sources:

                def act(bys=bys):
                    for spot in [(0, 0), (0, 1), (1, 0), (1, 1)]:
                        where = (z,) + spot + box
                        total = wide(here[where])
                        for by in bys:
                            total = total + wide(z_first[k][(e, by - 1) + spot + inner])
                        here[where] = total.astype(here.dtype)

                guard(both_of(upper if text else None, cond), act)
        elif order == 2:

            def act():
                for other in range(2):
                    where = (z, x, other) + box
                    here[where] = here[where] + z_second[k][(e, other) + inner]

            guard(upper if text else None, act)
        elif step == 1:
            spots = [(0, y), (1, y)] if dim == "y" else [(x, 0), (x, 1)]
            got = lambda level, index, spot: first[k][(e, level, index) + inner]
            if text and dim == "y":
                pl.when(lower)(lambda: over(spots, got, True))
            elif text:
                pl.when(upper)(lambda: over(spots, got, False))
            else:
                over(spots, got, False)
        else:
            got = lambda level, index, spot: second[k][(e, level) + inner]
            if text and dim == "y":
                pl.when(lower)(lambda: over([(x, y)], got, True))
            else:
                over([(x, y)], got, False)

    def start(chunk, step):
        for piece in chunk:
            for copy, sends, _ in copies_of(piece, step):
                guard(sends, copy.start)

    def wait(chunk, step):
        for piece in chunk:
            for copy, _, recvs in copies_of(piece, step):
                guard(recvs, copy.wait_recv)
            combine(piece, step)

    def halve():
        kv_beside.wait_recv()

        @pl.loop(0, rows // 64)
        def _(j):
            block = pl.ds(pl.multiple_of(j * 64, 64), 64)
            for level in range(2):
                kv_sum[level, block, :] = kv_sum[level, block, :] + kv_mine[level, block, :]

    def project_back(qkv_grad, flipped, normed_in, far_in, weight_in, tokens_in, residual_in, token_out):
        pairs = [
            (weight, weight_in),
            (normed, normed_in),
            (far_normed, far_in),
            (tokens, tokens_in),
            (residual_grad, residual_in),
        ]
        loads = [pltpu.make_async_copy(src, dst, away_sem.at[j]) for j, (src, dst) in enumerate(pairs)]
        for copy in loads:
            copy.start()
        halve()
        qkv_grad[:rows, :width] = dq[...]
        qkv_grad[:rows, width:] = kv_sum[y]
        qkv_grad[rows:, width:] = kv_sum[1 - y]
        for copy in loads:
            copy.wait()

        @pl.loop(0, rows // 128)
        def _(j):
            block = pl.ds(pl.multiple_of(j * 128, 128), 128)
            below = pl.ds(pl.multiple_of(rows + j * 128, 128), 128)
            far_terms[block, :] = product_trail(
                qkv_grad[below, width:], weight_in[:, width:]
            ).astype(jnp.bfloat16)

        kv_across.start()
        flipped[:, :rows] = normed_in[...].T
        flipped[:, rows:] = far_in[...].T

        def fold(value):
            return jnp.sum(value.reshape(-1, 8, width), axis=0)

        zero = jnp.zeros((8, width), jnp.float32)

        def gather_sums(j, carry):
            block = pl.ds(pl.multiple_of(j * 64, 64), 64)
            below = pl.ds(pl.multiple_of(rows + j * 64, 64), 64)
            own, far_part = qkv_grad[block, 2 * width :], qkv_grad[below, 2 * width :]
            return (
                carry[0] + fold(dq[block, :].astype(jnp.float32)),
                carry[1] + fold(own.astype(jnp.float32) + far_part.astype(jnp.float32)),
            )

        sum_q, sum_v = lax.fori_loop(0, rows // 64, gather_sums, (zero, zero))
        step = width // 2
        spots = spots_of(depth)
        for begin, count, depth_rows in ((0, 2, rows), (2, 4, 2 * rows)):

            @pl.loop(begin, begin + count)
            def _(j, depth_rows=depth_rows):
                cols = pl.ds(pl.multiple_of(j * step, 128), step)
                value = jnp.dot(
                    flipped[:, :depth_rows],
                    qkv_grad[:depth_rows, cols],
                    preferred_element_type=jnp.float32,
                ).astype(jnp.bfloat16)
                for index, spot in enumerate(spots):
                    qkv_terms[spot + (EVERY, cols)] = value[index * share : (index + 1) * share]

        flow.tick()
        kv_across.wait_recv()

        def back(j, carry):
            block = pl.ds(pl.multiple_of(j * 128, 128), 128)
            value = tokens_in[block, :].astype(jnp.float32)
            centred = value - jnp.mean(value, axis=-1, keepdims=True)
            scale = lax.rsqrt(jnp.mean(centred * centred, axis=-1, keepdims=True) + NORM_EPS)
            unit = centred * scale
            grad = product_trail(qkv_grad[block, :], weight_in[...]) + far_got[block, :].astype(
                jnp.float32
            )
            lifted = grad * vectors[0:1, :]
            inner = jnp.mean(lifted * unit, axis=-1, keepdims=True)
            part = scale * (lifted - jnp.mean(lifted, axis=-1, keepdims=True) - unit * inner)
            token_out[block, :] = (residual_in[block, :] + part).astype(jnp.bfloat16)
            return carry[0] + fold(grad * unit), carry[1] + fold(grad)

        sum_gain, sum_shift = lax.fori_loop(0, rows // 128, back, (zero, zero))
        store = pltpu.make_async_copy(token_out, token_grad, away_sem.at[0])
        store.start()
        lines = [jnp.sum(value, axis=0, keepdims=True) for value in (sum_gain, sum_shift, sum_q, sum_v)]
        def stack(parts):
            count = sum(part.shape[0] for part in parts)
            return jnp.concatenate(parts + [jnp.zeros((8 - count, parts[0].shape[1]), jnp.float32)])

        scales = [
            jnp.where(text_device == (e == 1), factors[e], 0.0)
            for e in range(2)
        ]
        down_part = [small[3:4, :] * scale for scale in scales]
        up_part = [up_shift_sum[0:1, :] * scale for scale in scales]
        ff = up_shift_sum.shape[1]
        head = dealt(stack(lines + [small[0:3, :]]), share, devices)
        tail = dealt(stack(down_part), share, devices) + dealt(
            stack([jnp.zeros((2, ff), jnp.float32)] + up_part), ff // devices, devices
        )
        for index, spot in enumerate(spots):
            rows_of = slice(index * 8, (index + 1) * 8)
            thin_terms[spot] = jnp.concatenate([head[rows_of], tail[rows_of]], axis=0)
        store.wait()

    def project_scope():
        low = jnp.bfloat16
        pl.run_scoped(
            project_back,
            pltpu.VMEM((2 * rows, 3 * width), low),
            pltpu.VMEM((width, 2 * rows), low),
            pltpu.VMEM((rows, width), low),
            pltpu.VMEM((rows, width), low),
            pltpu.VMEM((width, 3 * width), low),
            pltpu.VMEM((rows, width), low),
            pltpu.VMEM((rows, width), jnp.float32),
            pltpu.VMEM((rows, width), low),
        )

    group_width = width // 2
    stream = y * 2 + c

    def attention(group):
        cols = pl.ds(group * group_width, group_width)
        value_cols = pl.ds(width + group * group_width, group_width)

        def act(keys, values, q_in, g_in, mixed_in, *work):
            pairs = [
                (kv.at[:, cols], keys),
                (kv.at[:, value_cols], values),
                (queries.at[:, cols], q_in),
                (mixed_grad.at[:, cols], g_in),
                (mixed_t.at[cols, :], mixed_in),
            ]
            loads = [pltpu.make_async_copy(src, dst, away_sem.at[j]) for j, (src, dst) in enumerate(pairs)]
            for copy in loads:
                copy.start()
            for copy in loads:
                copy.wait()
            back_group(
                group, kind, stream, log_total, keys, values, q_in, g_in, mixed_in,
                dq.at[:, cols], flow.tick, *work,
            )
            dk, dv = work[-2:]
            for part, (terms, rest, begin) in enumerate(((dk, keys, cols), (dv, values, value_cols))):
                for level in range(2):
                    mine = (level * 2 + c) * rows
                    away = (level * 2 + 1 - c) * rows

                    @pl.loop(0, rows // 128)
                    def _(j, level=level, mine=mine, away=away, terms=terms, rest=rest, begin=begin):
                        to = pl.ds(pl.multiple_of(j * 128, 128), 128)
                        kept = pl.ds(pl.multiple_of(mine + j * 128, 128), 128)
                        sent = pl.ds(pl.multiple_of(away + j * 128, 128), 128)
                        kv_mine[level, to, begin] = terms[kept, :].astype(jnp.bfloat16)
                        rest[sent, :] = terms[sent, :].astype(jnp.bfloat16)

            stores = []
            for part, (rest, begin) in enumerate(((keys, cols), (values, value_cols))):
                for level in range(2):
                    sent = pl.ds(pl.multiple_of((level * 2 + 1 - c) * rows, rows), rows)
                    stores.append(
                        pltpu.make_async_copy(
                            rest.at[sent], kv_away.at[level, :, begin], away_sem.at[part * 2 + level]
                        )
                    )
            for copy in stores:
                copy.start()
            for copy in stores:
                copy.wait()
            if group == 1:
                kv_beside.start()

        def scope():
            low = jnp.bfloat16
            heads = group_width // HEAD_DIM
            everyone = 4 * rows
            pl.run_scoped(
                act,
                pltpu.VMEM((everyone, group_width), low),
                pltpu.VMEM((everyone, group_width), low),
                pltpu.VMEM((rows, group_width), low),
                pltpu.VMEM((rows, group_width), low),
                pltpu.VMEM((group_width, rows), jnp.float32),
                pltpu.VMEM((group_width, everyone), low),
                pltpu.VMEM((heads, rows, PAIR), low),
                pltpu.VMEM((heads, rows, PAIR), low),
                pltpu.VMEM((heads, PAIR, rows), low),
                pltpu.VMEM((heads, PAIR, rows), low),
                pltpu.VMEM((group_width, TQ), jnp.float32),
                pltpu.VMEM((8, rows), jnp.float32),
                pltpu.VMEM((everyone, group_width), jnp.float32),
                pltpu.VMEM((everyone, group_width), jnp.float32),
            )

        return scope

    flow = Pipeline(chunks, 2, start, wait)
    attention(0)()
    flow.tick()
    attention(1)()
    flow.tick()
    project_scope()
    flow.tick(STEPS + len(chunks))
    lane = lax.broadcasted_iota(jnp.int32, (1, 128), 1)
    outs[4][0, THIN_ROWS - 1 : THIN_ROWS, :] = jnp.where(
        lane == 0, counts[0], jnp.where(lane == 1, counts[1], 0.0)
    )
    for copy in (kv_beside, kv_across):
        copy.wait_send()
    for chunk in chunks:
        for step in range(STEPS):
            for piece in chunk:
                for copy, sends, _ in copies_of(piece, step):
                    guard(sends, copy.wait_send)


def scatter_all(
    up, down, out, small, up_shift_sum, vectors, kind, log_total,
    queries, kv, mixed_grad, mixed_t, normed, far_normed, weight, tokens, residual_grad, depth,
):
    rows, width = tokens.shape
    far = [up, down, out]
    kinds = (True, True, False, False, False)
    share, ff_share, ff = up.shape[4], down.shape[4], up.shape[5]
    chunks, cuts = scatter_chunks(share, width, ff_share, ff)
    n_pieces = sum(len(chunk) for chunk in chunks)
    anywhere, inside = pl.BlockSpec(memory_space=pl.ANY), pl.BlockSpec(memory_space=pltpu.VMEM)
    low, box = jnp.bfloat16, (depth, 2, 2, 2)
    tails = [a.shape[4:] for a in far] + [(share, 3 * width), (THIN_ROWS, 128)]
    dtypes = [low] * 4 + [jnp.float32]
    experts = [2 if kind else 1 for kind in kinds]
    scratch = [
        pltpu.VMEM((e, depth, 2, 2) + tail, dtype) for e, tail, dtype in zip(experts, tails, dtypes)
    ]
    plain, turned = [], []
    for tail, cut in zip(tails, cuts):
        plain.append((cut[0] or tail[0], cut[1] or tail[1]))
        turned.append((tail[0] - cut[0], tail[1] - cut[1]) if any(cut) else (8, 128))
    for middle in ((depth, 2), (depth,), (depth - 1,)):
        scratch += [pltpu.VMEM((e,) + middle + t, d) for e, t, d in zip(experts, plain, dtypes)]
    scratch += [pltpu.VMEM((e,) + t, d) for e, t, d in zip(experts, plain, dtypes)]
    for middle in ((2, 2), (depth - 1, 2, 2), (2,), ()):
        scratch += [pltpu.VMEM((e,) + middle + t, d) for e, t, d in zip(experts, turned, dtypes)]
    scratch += [pltpu.VMEM((depth, 2, 2) + a.shape[4:], low) for a in far]
    scratch += [
        pltpu.VMEM(box + (share, 3 * width), low),
        pltpu.VMEM(box + (THIN_ROWS, 128), jnp.float32),
        pltpu.VMEM((2, rows, 2 * width), low),
        pltpu.VMEM((rows, width), low),
        pltpu.VMEM((rows, width), low),
        pltpu.VMEM((2, rows, 2 * width), low),
        pltpu.VMEM((rows, width), low),
        pltpu.SemaphoreType.DMA((n_pieces, depth + 3)),
        pltpu.SemaphoreType.DMA((n_pieces, depth + 3)),
        pltpu.SemaphoreType.DMA((3,)),
        pltpu.SemaphoreType.DMA((5,)),
        pltpu.SemaphoreType.DMA((2,)),
        pltpu.SemaphoreType.DMA((2,)),
    ]
    return pl.pallas_call(
        functools.partial(scatter_kernel, depth, kinds, chunks, cuts),
        out_shape=[
            jax.ShapeDtypeStruct((e,) + tail, jnp.float32) for e, tail in zip(experts, tails)
        ]
        + [jax.ShapeDtypeStruct((rows, width), low), jax.ShapeDtypeStruct((2, rows, 2 * width), low)],
        in_specs=[anywhere] * 3 + [inside] * 5 + [anywhere] * 9,
        out_specs=[inside] * 5 + [anywhere] * 2,
        scratch_shapes=scratch,
        compiler_params=pltpu.CompilerParams(
            collective_id=2, has_side_effects=True, vmem_limit_bytes=61 << 20
        ),
    )(
        up, down, out, small, up_shift_sum, vectors, kind, log_total,
        queries, kv, mixed_grad, mixed_t, normed, far_normed, weight, tokens, residual_grad,
    )[:6]


def publish_kernel(count, share, ff_share, *refs):
    far, thin = refs[:count], refs[count]
    outs, smalls = refs[count + 1 : 2 * count + 1], refs[2 * count + 1 : 2 * count + 11]
    held, sems = refs[2 * count + 11 : 3 * count + 11], refs[-1]
    inward = [pltpu.make_async_copy(far[j], held[j], sems.at[0, j]) for j in range(count)]
    outward = [pltpu.make_async_copy(held[j], outs[j], sems.at[1, j]) for j in range(count)]
    for copy in inward:
        copy.start()
    for j in range(7):
        smalls[j][...] = thin[j, :share]
    smalls[7][...] = thin[10:12, :ff_share]
    smalls[8][...] = thin[8:10, :share]
    smalls[9][...] = thin[THIN_ROWS - 1, :2]
    for first, second in zip(inward, outward):
        first.wait()
        second.start()
    for copy in outward:
        copy.wait()


def publish(arrays, thin, share, ff_share):
    anywhere, inside = pl.BlockSpec(memory_space=pl.ANY), pl.BlockSpec(memory_space=pltpu.VMEM)
    count = len(arrays)
    small = [(share,)] * 7 + [(2, ff_share), (2, share), (2,)]
    return pl.pallas_call(
        functools.partial(publish_kernel, count, share, ff_share),
        out_shape=[jax.ShapeDtypeStruct(array.shape, array.dtype) for array in arrays]
        + [jax.ShapeDtypeStruct(shape, jnp.float32) for shape in small],
        in_specs=[anywhere] * count + [inside],
        out_specs=[anywhere] * count + [inside] * len(small),
        scratch_shapes=[pltpu.VMEM(array.shape, array.dtype) for array in arrays]
        + [pltpu.SemaphoreType.DMA((2, count))],
        compiler_params=pltpu.CompilerParams(vmem_limit_bytes=62 << 20),
    )(*arrays, thin)


def padded(values):
    return jnp.pad(values, ((0, 0), (0, 128 - values.shape[1])))


def body(
    near,
    tokens,
    group_kind,
    ln1_gain,
    ln1_bias,
    w_qkv,
    q_bias,
    v_bias,
    w_out,
    out_bias,
    ln2_gain,
    ln2_bias,
    w_up,
    b_up,
    w_down,
    b_down,
    cotangent,
):
    row_count, model_width = tokens.shape
    stream_size = lax.axis_size("stream")
    stream_place = lax.axis_index("stream")
    devices = lax.axis_size("items") * stream_size
    group_type = group_kind[0]
    expert_pick = jnp.where(stream_place == stream_size - 1, 1, 0).astype(jnp.int32)
    share, ff_share, ff = model_width // devices, w_down.shape[1], w_up.shape[2]
    both = ("items", "stream")
    low = jnp.bfloat16
    thin = jnp.stack([ln1_gain, ln1_bias, q_bias, v_bias, out_bias, ln2_gain, ln2_bias])
    thin = jnp.concatenate(
        [padded(thin), padded(b_up), padded(b_down), padded(group_kind.astype(low)[:, None])]
    )
    thin = jnp.pad(thin, ((0, THIN_ROWS - thin.shape[0]), (0, 0)))
    tokens_f = tokens.astype(jnp.float32)
    kind_wide = jnp.broadcast_to(group_type.astype(jnp.float32), (8, 128))
    place_at = stream_place.astype(jnp.int32)[None]
    if near:
        depth = lax.axis_size("items") // 2
        (
            thin_all,
            out_weight,
            up_all,
            down_all,
            qkv_weight,
            normed_low,
            queries,
            vectors,
            kv,
            mixed_low,
            mixed_t,
            log_total,
            far_normed,
        ) = gather_all(thin, w_qkv, w_out, w_up, w_down, tokens, kind_wide, depth)
        thin_all = thin_all.reshape(devices, THIN_ROWS, 128)
        out_weight = out_weight.reshape(model_width, model_width)
        up_all = up_all.reshape(2, model_width, ff)
        down_all = down_all.reshape(2, ff, model_width)
    else:
        thin_all = lax.all_gather(thin, both, axis=0)
        qkv_weight = lax.all_gather(w_qkv, both, axis=0, tiled=True)
        out_weight = lax.all_gather(w_out, both, axis=0, tiled=True)
        up_all = lax.all_gather(w_up, both, axis=1, tiled=True)
        down_all = lax.all_gather(w_down, both, axis=1, tiled=True)
        vectors = (
            thin_all[:, :, :share].transpose(1, 0, 2).reshape(THIN_ROWS, -1).astype(jnp.float32)
        )
        normed_low = layer_norm(tokens_f, vectors[0], vectors[1]).astype(low)
        shifts = jnp.concatenate([vectors[2], jnp.zeros_like(vectors[2]), vectors[3]])
        projected = (product(normed_low, qkv_weight) + shifts).astype(low)
        queries = projected[:, :model_width]
        kv = lax.all_gather(projected[:, model_width:], "stream", axis=0, tiled=True)
        mixed_low, mixed_t, log_total = attend(kind_wide, place_at, queries, kv)
    up_shift_all = thin_all[:, 7:9, :ff_share].transpose(1, 0, 2).reshape(2, ff)
    (
        output,
        residual_grad,
        grad_out_weight,
        mixed_grad,
        grad_up,
        grad_down,
        small,
        grad_up_shift,
    ) = feed(
        expert_pick[None],
        place_at,
        kind_wide,
        vectors,
        up_shift_all[:, None],
        tokens,
        mixed_low,
        out_weight,
        cotangent,
        up_all,
        down_all,
    )
    if near:
        box = (depth, 2, 2, 2)
        up_sum, down_sum, out_sum, qkv_sum, thin_sum, token_grad = scatter_all(
            grad_up.reshape(box + (share, ff)),
            grad_down.reshape(box + (ff_share, model_width)),
            grad_out_weight.reshape(box + (share, model_width)),
            small,
            grad_up_shift,
            vectors,
            kind_wide,
            log_total,
            queries,
            kv,
            mixed_grad,
            mixed_t,
            normed_low,
            far_normed,
            qkv_weight,
            tokens,
            residual_grad,
            depth,
        )
        thin_sum = thin_sum[0]
        (
            up_sum,
            down_sum,
            out_sum,
            qkv_sum,
            token_grad,
            *lines,
            up_shift_sum,
            down_shift_sum,
            totals,
        ) = publish(
            [up_sum, down_sum, out_sum[0], qkv_sum[0], token_grad], thin_sum, share, ff_share
        )
    else:
        kinds = vectors[11, :: stream_size * share].astype(jnp.int32)
        tally = []
        for kind in range(2):
            modality = layout(
                jnp.int32(kind), jnp.arange(stream_size * row_count, dtype=jnp.int32), row_count
            )[1]
            tally.append([jnp.sum((modality == e).astype(jnp.float32)) for e in range(2)])
        totals = jnp.stack(
            [jnp.sum(jnp.where(kinds == 0, tally[0][e], tally[1][e])) for e in range(2)]
        )
        factor = lax.rsqrt(totals)
        pick = (jnp.arange(2, dtype=jnp.int32) == expert_pick).astype(jnp.float32) * factor

        def lanes(values):
            values = values.reshape(values.shape[0], devices, -1).transpose(1, 0, 2)
            return jnp.pad(values, ((0, 0), (0, 0), (0, 128 - values.shape[2])))

        scatter = functools.partial(
            lax.psum_scatter, axis_name=both, scatter_dimension=0, tiled=True
        )
        wide = functools.partial(lax.psum_scatter, axis_name=both, scatter_dimension=1, tiled=True)
        query_grad, kv_terms = attend_back(
            kind_wide, place_at, queries, kv, mixed_grad, mixed_t, log_total
        )
        kv_grad = lax.psum_scatter(
            kv_terms.astype(jnp.float32), "stream", scatter_dimension=0, tiled=True
        )
        qkv_grad = jnp.concatenate([query_grad, kv_grad.astype(low)], axis=1)
        grad_qkv = product_lead(normed_low, qkv_grad)
        early = [
            jnp.sum(qkv_grad[:, :model_width].astype(jnp.float32), axis=0),
            jnp.sum(qkv_grad[:, 2 * model_width :].astype(jnp.float32), axis=0),
        ]
        norm_one_grad = product_trail(qkv_grad, qkv_weight)
        token_part, *grads_one = jax.vjp(layer_norm, tokens_f, vectors[0], vectors[1])[1](
            norm_one_grad
        )
        token_grad = (residual_grad + token_part).astype(low)
        up_sum = wide(pick[:, None, None] * grad_up.astype(jnp.float32)[None])
        down_sum = wide(pick[:, None, None] * grad_down.astype(jnp.float32)[None])
        out_sum, qkv_sum = scatter(grad_out_weight.astype(jnp.float32)), scatter(grad_qkv)
        thin_terms = [
            lanes(jnp.stack(grads_one + early + [small[0], small[1], small[2]])),
            jnp.zeros((devices, 1, 128), jnp.float32),
            lanes(pick[:, None] * small[3][None]),
            lanes(pick[:, None] * grad_up_shift[0][None]),
            jnp.zeros((devices, THIN_ROWS - 12, 128), jnp.float32),
        ]
        thin_sum = scatter(jnp.concatenate(thin_terms, axis=1))[0]
        lines = [thin_sum[k, :share] for k in range(7)]
        up_shift_sum, down_shift_sum = thin_sum[10:12, :ff_share], thin_sum[8:10, :share]
    return (
        output,
        token_grad,
        lines[0],
        lines[1],
        qkv_sum,
        lines[2],
        lines[3],
        out_sum,
        lines[4],
        lines[5],
        lines[6],
        up_sum,
        up_shift_sum,
        down_sum,
        down_shift_sum,
        totals,
    )


def solution(mesh):
    placed = (
        P(("items", "stream"), None),
        P("items"),
        P(("items", "stream")),
        P(("items", "stream")),
        P(("items", "stream"), None),
        P(("items", "stream")),
        P(("items", "stream")),
        P(("items", "stream"), None),
        P(("items", "stream")),
        P(("items", "stream")),
        P(("items", "stream")),
        P(None, ("items", "stream"), None),
        P(None, ("items", "stream")),
        P(None, ("items", "stream"), None),
        P(None, ("items", "stream")),
        P(("items", "stream"), None),
    )
    near = mesh.shape["items"] == 8 and mesh.shape["stream"] == 4
    return jax.shard_map(
        functools.partial(body, near),
        mesh=mesh,
        in_specs=placed,
        out_specs=(
            P(("items", "stream"), None),
            P(("items", "stream"), None),
            P(("items", "stream")),
            P(("items", "stream")),
            P(("items", "stream"), None),
            P(("items", "stream")),
            P(("items", "stream")),
            P(("items", "stream"), None),
            P(("items", "stream")),
            P(("items", "stream")),
            P(("items", "stream")),
            P(None, ("items", "stream"), None),
            P(None, ("items", "stream")),
            P(None, ("items", "stream"), None),
            P(None, ("items", "stream")),
            P(),
        ),
        check_vma=False,
    )
```

```python
import functools

import jax
import jax.numpy as jnp
from jax import lax
from jax.experimental import pallas as pl
from jax.experimental.pallas import tpu as pltpu
from jax.sharding import PartitionSpec as P

HEADS = 12
HEAD_DIM = 64
PATCH_S = 197
PATCH_L = 577
TEXT_LEN = 40
ITEMS_S = 7
ITEMS_L = 2


NORM_EPS = 1e-05
MASKED = -1000000000.0


def layer_norm(values, gain_row, shift_row):
    row_mean = jnp.mean(values, axis=-1, keepdims=True)
    centred = values - row_mean
    variance = jnp.mean(centred * centred, axis=-1, keepdims=True)
    return centred * lax.rsqrt(variance + NORM_EPS) * gain_row + shift_row


def gelu_exact(values):
    return jax.nn.gelu(values, approximate=False)


def layout(group_type, positions, row_count):
    patch_len = jnp.where(group_type == 0, PATCH_S, PATCH_L).astype(jnp.int32)
    members = jnp.where(group_type == 0, ITEMS_S, ITEMS_L).astype(jnp.int32)
    is_patch = positions < 3 * row_count
    patch_item = positions // patch_len
    text_item = jnp.maximum(positions - 3 * row_count, 0) // TEXT_LEN
    member = jnp.where(is_patch, patch_item, text_item)
    member = jnp.where(member < members, member, -1)
    modality = jnp.where(member < 0, 2, jnp.where(is_patch, 0, 1)).astype(jnp.int32)
    return (member, modality)


def product(first_op, second_op):
    return jnp.dot(first_op, second_op, preferred_element_type=jnp.float32)


def product_lead(first_op, second_op):
    return lax.dot_general(
        first_op, second_op, (((0,), (0,)), ((), ())), preferred_element_type=jnp.float32
    )


def product_trail(first_op, second_op):
    return lax.dot_general(
        first_op, second_op, (((1,), (1,)), ((), ())), preferred_element_type=jnp.float32
    )


def halves(length):
    return ((0, length // 2), (length // 2, length // 2))


def divided(length, unit, *shares):
    found, begin = [], 0
    for share in shares:
        found.append((begin, share * unit))
        begin += share * unit
    assert begin == length
    return found


def gather_chunks(share, width, ff_share, ff):
    rows = (0, share)
    near_cols = divided(3 * width, 128, 9, 9)
    out_cols = divided(width, 128, 3, 3)
    up_cols = divided(ff, 128, 8, 8, 8)
    down_rows = divided(ff_share, 16, 2, 2, 2)
    chunks = [
        [((0, None), (0, THIN_ROWS), (0, 128), 0, False)]
        + [((1, None), rows, cols, order, False) for order, cols in enumerate(near_cols)],
        [((2, None), rows, cols, order, False) for order, cols in enumerate(out_cols)],
    ]
    def up_chunk(e, parts):
        return [((3, e), rows, cols, order, e == 1) for order, cols in enumerate(parts) if cols[1]]

    def down_chunk(e, parts):
        return [((4, e), band, (0, width), order, e == 1) for order, band in enumerate(parts)]

    chunks += [up_chunk(1, up_cols), down_chunk(1, down_rows), down_chunk(0, down_rows)]
    unit, begin = 128, 0
    for shares in ((4, 4, 4), (3, 2, 3), (1, 2, 1)):
        parts = []
        for blocks in shares:
            parts.append((begin * unit, blocks * unit))
            begin += blocks
        chunks.append(up_chunk(0, parts))
    return chunks


def scatter_chunks(share, width, ff_share, ff):
    rows = (0, share)
    near_cols = divided(3 * width, 128, 7, 7, 4)
    out_cols = divided(width, 128, 2, 3, 1)
    up_cols = divided(ff, 128, 4, 14, 6)
    down_rows = divided(ff_share, 16, 1, 3, 2)
    chunks = [[(2, 0, rows, cols, order) for order, cols in enumerate(out_cols)]]
    for e in (1, 0):
        chunks.append([(0, e, rows, cols, order) for order, cols in enumerate(up_cols)])
        chunks.append(
            [(1, e, band, (0, width), order) for order, band in enumerate(down_rows)]
        )
    chunks += [[], []]
    chunks.append(
        [(3, 0, rows, cols, order) for order, cols in enumerate(near_cols)]
    )
    chunks.append([(4, 0, (0, THIN_ROWS), (0, 128), 0)])
    cuts = (
        (0, up_cols[2][0]),
        (down_rows[2][0], 0),
        (0, out_cols[2][0]),
        (0, near_cols[2][0]),
        (0, 0),
    )
    return chunks, cuts


TQ, TK = 256, 128
PAIR = 2 * HEAD_DIM


def trail(first_op, second_op):
    return lax.dot_general(
        first_op, second_op, (((1,), (1,)), ((), ())), preferred_element_type=jnp.float32
    )


def span(kind, start, length, image_rows):
    patch_len, members = ((PATCH_S, ITEMS_S), (PATCH_L, ITEMS_L))[kind]
    image = start < image_rows
    low = jnp.where(image, lax.div(start, patch_len), lax.div(start - image_rows, TEXT_LEN))
    high = jnp.where(
        image,
        lax.div(start + length - 1, patch_len),
        lax.div(start + length - 1 - image_rows, TEXT_LEN),
    )
    return low, high, members


def meets(first, second, image_rows, loose):
    found = False
    for kind in range(2):
        low_a, high_a, members = span(kind, *first, image_rows)
        low_b, high_b, _ = span(kind, *second, image_rows)
        low = jnp.maximum(low_a, low_b)
        high = jnp.minimum(jnp.minimum(high_a, high_b), members - 1)
        found = jnp.logical_or(found, low <= high)
        if loose:
            both = jnp.logical_and(high_a >= members, high_b >= members)
            found = jnp.logical_or(found, both)
    return found


def member_of(kind, position, image_rows):
    patch_len = PATCH_S + kind * float(PATCH_L - PATCH_S)
    members = ITEMS_S + kind * float(ITEMS_L - ITEMS_S)
    patch = jnp.floor((position + 0.5) / patch_len)
    text = jnp.floor((position - image_rows + 0.5) * (1.0 / TEXT_LEN))
    member = jnp.where(position < image_rows, patch, text)
    return jnp.where(member < members, member, -1.0)


def same_item(kind, stream, rows, qt, kt, image_rows):
    keys = lax.broadcasted_iota(jnp.int32, (TK, 1), 0) + kt * TK
    own = lax.broadcasted_iota(jnp.int32, (1, TQ), 1) + (stream * rows + qt * TQ)
    key_member = member_of(kind, keys.astype(jnp.float32), image_rows)
    return key_member == member_of(kind, own.astype(jnp.float32), image_rows)


def half_of(pair, which):
    lanes = lax.broadcasted_iota(jnp.int32, pair.shape, 1)
    return jnp.where((lanes < HEAD_DIM) == (which == 0), pair, jnp.zeros_like(pair))


def upper_of(pair, which):
    keep = pair[which * HEAD_DIM : (which + 1) * HEAD_DIM]
    parts = [keep, jnp.zeros_like(keep)]
    return jnp.concatenate(parts if which == 0 else parts[::-1], axis=0)


def scale_queries(q_ref, scaled):
    for pair in range(q_ref.shape[1] // PAIR):
        columns = slice(pair * PAIR, (pair + 1) * PAIR)
        value = (q_ref[:, columns] * jnp.bfloat16(HEAD_DIM ** (-0.5))).T
        for which in range(2):
            scaled[2 * pair + which] = upper_of(value, which)


def flip_columns(kv_ref, begin, flipped):
    width = flipped.shape[0]

    @pl.loop(0, flipped.shape[1] // TK)
    def _(kt):
        keys = pl.ds(pl.multiple_of(kt * TK, TK), TK)
        flipped[:, keys] = kv_ref[keys, begin : begin + width].T


def attend_part(qt, begin, end, kind_ref, stream, kv_ref, values_t, scaled, mixed_ref, mixed_t, log_total, top, total):
    width, everyone = values_t.shape
    rows = mixed_ref.shape[0]
    heads = width // HEAD_DIM
    image_rows = everyone - rows
    here = slice(qt * TQ, (qt + 1) * TQ)
    if begin == 0:
        top[...] = jnp.full(top.shape, -1e30, jnp.float32)
        total[...] = jnp.zeros(total.shape, jnp.float32)
        mixed_t[:, here] = jnp.zeros((width, TQ), jnp.float32)

    @pl.loop(begin, end)
    def _(kt):
        needed = meets((stream * rows + qt * TQ, TQ), (kt * TK, TK), image_rows, True)

        @pl.when(needed)
        def _():
            keys = pl.ds(pl.multiple_of(kt * TK, TK), TK)
            allowed = same_item(kind_ref[0:1, 0:1], stream, rows, qt, kt, image_rows)
            scores, parts, fades = [], [], []
            for head in range(heads):
                pair = slice(head // 2 * PAIR, (head // 2 + 1) * PAIR)
                raw = jnp.dot(
                    kv_ref[keys, pair], scaled[head, :, here], preferred_element_type=jnp.float32
                )
                scores.append(jnp.where(allowed, raw, MASKED))
            for head, score in enumerate(scores):
                line = slice(head, head + 1)
                old = top[line]
                new = jnp.maximum(old, jnp.max(score, axis=0, keepdims=True))
                top[line] = new
                fade = jnp.exp(old - new)
                part = jnp.exp(score - new)
                total[line] = total[line] * fade + jnp.sum(part, axis=0, keepdims=True)
                parts.append(part.astype(jnp.bfloat16))
                fades.append(fade)
            for head in range(heads):
                own = slice(head * HEAD_DIM, (head + 1) * HEAD_DIM)
                mixed_t[own, here] = mixed_t[own, here] * fades[head] + jnp.dot(
                    values_t[own, keys], parts[head], preferred_element_type=jnp.float32
                )

    if end == everyone // TK:
        for head in range(heads):
            own = slice(head * HEAD_DIM, (head + 1) * HEAD_DIM)
            mixed_t[own, here] = mixed_t[own, here] / total[head : head + 1]
        log_total[:, here] = top[...] + jnp.log(total[...])
        mixed_ref[here, :] = mixed_t[:, here].T.astype(jnp.bfloat16)


def attend_kernel(kind, place_ref, q_ref, kv_ref, mixed_ref, mixed_t, log_total, values_t, scaled, top, total):
    scale_queries(q_ref, scaled)
    flip_columns(kv_ref, q_ref.shape[1], values_t)
    for qt in range(q_ref.shape[0] // TQ):
        attend_part(
            qt, 0, kv_ref.shape[0] // TK, kind, place_ref[0], kv_ref, values_t, scaled, mixed_ref,
            mixed_t, log_total, top, total,
        )


def attend(kind, place_at, queries, kv):
    rows, width = queries.shape
    heads = width // HEAD_DIM
    inside = pl.BlockSpec(memory_space=pltpu.VMEM)
    lines = -(-heads // 8) * 8
    return pl.pallas_call(
        attend_kernel,
        out_shape=(
            jax.ShapeDtypeStruct((rows, width), jnp.bfloat16),
            jax.ShapeDtypeStruct((width, rows), jnp.float32),
            jax.ShapeDtypeStruct((lines, rows), jnp.float32),
        ),
        in_specs=[inside, pl.BlockSpec(memory_space=pltpu.SMEM)] + [inside] * 2,
        out_specs=(inside,) * 3,
        scratch_shapes=[
            pltpu.VMEM((width, kv.shape[0]), jnp.bfloat16),
            pltpu.VMEM((heads, PAIR, rows), jnp.bfloat16),
            pltpu.VMEM((lines, TQ), jnp.float32),
            pltpu.VMEM((lines, TQ), jnp.float32),
        ],
        compiler_params=pltpu.CompilerParams(vmem_limit_bytes=56 << 20),
    )(kind, place_at, queries, kv)


def back_group(
    group, kind, stream, log_total, keys_ref, values_ref, q_ref, g_ref, mixed_t, dq_ref, between,
    keys_t, scaled, grads, scaled_t, grads_t, dq_t, centre, dk, dv,
):
    everyone, width = keys_ref.shape
    rows = q_ref.shape[0]
    heads = width // HEAD_DIM
    image_rows = everyone - rows
    for pair in range(heads // 2):
        columns = slice(pair * PAIR, (pair + 1) * PAIR)
        value = q_ref[:, columns] * jnp.bfloat16(HEAD_DIM ** (-0.5))
        grad = g_ref[:, columns]
        value_t, grad_t = value.T, grad.T
        product = mixed_t[columns, :] * grad_t.astype(jnp.float32)
        for which in range(2):
            head = 2 * pair + which
            scaled[head] = half_of(value, which)
            grads[head] = half_of(grad, which)
            scaled_t[head] = upper_of(value_t, which)
            grads_t[head] = upper_of(grad_t, which)
            centre[head : head + 1] = jnp.sum(
                product[which * HEAD_DIM : (which + 1) * HEAD_DIM], axis=0, keepdims=True
            )
    flip_columns(keys_ref, 0, keys_t)

    @pl.loop(0, everyone // TK)
    def _(kt):
        keys = pl.ds(pl.multiple_of(kt * TK, TK), TK)
        dk[keys, :] = jnp.zeros((TK, width), jnp.float32)
        dv[keys, :] = jnp.zeros((TK, width), jnp.float32)

    for qt in range(rows // TQ):
        here = slice(qt * TQ, (qt + 1) * TQ)
        if qt:
            between()
        dq_t[...] = jnp.zeros(dq_t.shape, jnp.float32)

        @pl.loop(0, everyone // TK)
        def _(kt, qt=qt, here=here):
            needed = meets((stream * rows + qt * TQ, TQ), (kt * TK, TK), image_rows, False)

            @pl.when(needed)
            def _():
                keys = pl.ds(pl.multiple_of(kt * TK, TK), TK)
                allowed = same_item(kind[0:1, 0:1], stream, rows, qt, kt, image_rows)
                scores, prob_grads, probs_low, score_low = [], [], [], []
                for head in range(heads):
                    pair = slice(head // 2 * PAIR, (head // 2 + 1) * PAIR)
                    scores.append(
                        jnp.dot(
                            keys_ref[keys, pair],
                            scaled_t[head, :, here],
                            preferred_element_type=jnp.float32,
                        )
                    )
                    prob_grads.append(
                        jnp.dot(
                            values_ref[keys, pair],
                            grads_t[head, :, here],
                            preferred_element_type=jnp.float32,
                        )
                    )
                for head in range(heads):
                    line = slice(group * heads + head, group * heads + head + 1)
                    shifted = scores[head] - log_total[line, here]
                    probs = jnp.exp(jnp.where(allowed, shifted, MASKED))
                    probs_low.append(probs.astype(jnp.bfloat16))
                    inner = prob_grads[head] - centre[head : head + 1, here]
                    score_low.append((probs * inner).astype(jnp.bfloat16))
                for head in range(heads):
                    own = slice(head * HEAD_DIM, (head + 1) * HEAD_DIM)
                    dq_t[own, :] += jnp.dot(
                        keys_t[own, keys], score_low[head], preferred_element_type=jnp.float32
                    )
                for head in range(0, heads, 2):
                    columns = slice(head * HEAD_DIM, head * HEAD_DIM + PAIR)
                    for terms, left, right in ((dk, score_low, scaled), (dv, probs_low, grads)):
                        terms[keys, columns] += jnp.dot(
                            left[head], right[head, here, :], preferred_element_type=jnp.float32
                        ) + jnp.dot(
                            left[head + 1],
                            right[head + 1, here, :],
                            preferred_element_type=jnp.float32,
                        )

        dq_ref[here, :] = (dq_t[...].T * HEAD_DIM ** (-0.5)).astype(jnp.bfloat16)


def attend_back_kernel(
    kind, place_ref, q_ref, kv_ref, g_ref, mixed_t, log_total, dq_ref, dkv_ref, *work
):
    width = q_ref.shape[1]
    back_group(
        0, kind, place_ref[0], log_total, kv_ref.at[:, pl.ds(0, width)],
        kv_ref.at[:, pl.ds(width, width)], q_ref, g_ref, mixed_t, dq_ref, lambda: None,
        *work,
    )
    dk, dv = work[-2:]

    @pl.loop(0, kv_ref.shape[0] // TK)
    def _(kt):
        keys = pl.ds(pl.multiple_of(kt * TK, TK), TK)
        dkv_ref[keys, :width] = dk[keys, :].astype(jnp.bfloat16)
        dkv_ref[keys, width:] = dv[keys, :].astype(jnp.bfloat16)


def attend_back(kind, place_at, queries, kv, mixed_grad, mixed_t, log_total):
    rows, width = queries.shape
    heads = width // HEAD_DIM
    inside = pl.BlockSpec(memory_space=pltpu.VMEM)
    lines = -(-heads // 8) * 8
    everyone = kv.shape[0]
    return pl.pallas_call(
        attend_back_kernel,
        out_shape=(
            jax.ShapeDtypeStruct((rows, width), jnp.bfloat16),
            jax.ShapeDtypeStruct((everyone, 2 * width), jnp.bfloat16),
        ),
        in_specs=[inside, pl.BlockSpec(memory_space=pltpu.SMEM)] + [inside] * 5,
        out_specs=(inside,) * 2,
        scratch_shapes=[
            pltpu.VMEM((width, everyone), jnp.bfloat16),
            pltpu.VMEM((heads, rows, PAIR), jnp.bfloat16),
            pltpu.VMEM((heads, rows, PAIR), jnp.bfloat16),
            pltpu.VMEM((heads, PAIR, rows), jnp.bfloat16),
            pltpu.VMEM((heads, PAIR, rows), jnp.bfloat16),
            pltpu.VMEM((width, TQ), jnp.float32),
            pltpu.VMEM((lines, rows), jnp.float32),
            pltpu.VMEM((everyone, width), jnp.float32),
            pltpu.VMEM((everyone, width), jnp.float32),
        ],
        compiler_params=pltpu.CompilerParams(vmem_limit_bytes=58 << 20),
    )(kind, place_at, queries, kv, mixed_grad, mixed_t, log_total)

def feed_kernel(
    pick, place_ref, kind, vectors, up_shift, tokens, mixed, out_weight, cotangent, up, down,
    output, residual_grad, grad_out, mixed_grad, grad_up, grad_down, small, up_shift_sum,
    residual, normed, normed_t, grad, branch, back,
):
    step = pl.program_id(0)
    rows, width = tokens.shape
    image_rows = (lax.axis_size("stream") - 1) * rows
    tall = 128

    def blocks(act):
        @pl.loop(0, rows // tall)
        def _(j):
            act(pl.ds(pl.multiple_of(j * tall, tall), tall))

    def unit_of(value):
        centred = value - jnp.mean(value, axis=-1, keepdims=True)
        scale = lax.rsqrt(jnp.mean(centred * centred, axis=-1, keepdims=True) + NORM_EPS)
        return centred * scale, scale

    def live(j_start):
        position = lax.broadcasted_iota(jnp.int32, (tall, 1), 0) + (place_ref[0] * rows + j_start)
        return member_of(kind[0:1, 0:1], position.astype(jnp.float32), image_rows) >= 0.0

    @pl.when(step == 0)
    def _():
        @pl.loop(0, rows // tall)
        def _(j):
            block = pl.ds(pl.multiple_of(j * tall, tall), tall)
            value = (
                tokens[block, :].astype(jnp.float32)
                + jnp.dot(mixed[block, :], out_weight[...], preferred_element_type=jnp.float32)
                + vectors[4:5, :]
            )
            residual[block, :] = value
            unit, _ = unit_of(value)
            normed[block, :] = (unit * vectors[5:6, :] + vectors[6:7, :]).astype(jnp.bfloat16)
            given = cotangent[block, :]
            grad[block, :] = jnp.where(live(j * tall), given, jnp.zeros_like(given))

        normed_t[...] = normed[...].T
        branch[...] = jnp.zeros(branch.shape, jnp.float32)
        back[...] = jnp.zeros(back.shape, jnp.float32)

    before = (
        jnp.dot(normed[...], up[0], preferred_element_type=jnp.float32) + up_shift[0].astype(jnp.float32)
    )
    hidden_grad = product_trail(grad[...], down[0])
    half = 0.5 + 0.5 * lax.erf(before * 0.5**0.5)
    hidden = (before * half).astype(jnp.bfloat16)
    slope = half + before * (jnp.exp(-0.5 * before * before) * 0.3989422804014327)
    before_grad = hidden_grad * slope
    low_grad = before_grad.astype(jnp.bfloat16)
    up_shift_sum[...] = jnp.broadcast_to(
        jnp.sum(low_grad.astype(jnp.float32), axis=0, keepdims=True), up_shift_sum.shape
    )
    branch[...] += jnp.dot(hidden, down[0], preferred_element_type=jnp.float32)
    back[...] += product_trail(low_grad, up[0])
    grad_up[...] = jnp.dot(normed_t[...], low_grad, preferred_element_type=jnp.float32).astype(
        jnp.bfloat16
    )
    grad_down[...] = jnp.dot(hidden.T, grad[...], preferred_element_type=jnp.float32).astype(
        jnp.bfloat16
    )

    @pl.when(step == pl.num_programs(0) - 1)
    def _():
        down_shift = jnp.where(pick[0] == 0, vectors[9:10, :], vectors[10:11, :])

        def fold(value):
            return jnp.sum(value.reshape(-1, 8, width), axis=0)

        def finish(j, carry):
            block = pl.ds(pl.multiple_of(j * tall, tall), tall)
            value = residual[block, :]
            kept = live(j * tall)
            output[block, :] = (
                value + jnp.where(kept, branch[block, :] + down_shift, 0.0)
            ).astype(jnp.bfloat16)
            unit, scale = unit_of(value)
            given = back[block, :]
            lifted = given * vectors[5:6, :]
            inner = jnp.mean(lifted * unit, axis=-1, keepdims=True)
            own = grad[block, :].astype(jnp.float32)
            total = own + scale * (
                lifted - jnp.mean(lifted, axis=-1, keepdims=True) - unit * inner
            )
            residual_grad[block, :] = total
            total_low = total.astype(jnp.bfloat16)
            normed[block, :] = total_low
            mixed_grad[block, :] = product_trail(total_low, out_weight[...]).astype(jnp.bfloat16)
            terms = (total_low.astype(jnp.float32), given * unit, given, own)
            return tuple(held + fold(term) for held, term in zip(carry, terms))

        zero = jnp.zeros((8, width), jnp.float32)
        sums = lax.fori_loop(0, rows // tall, finish, (zero,) * 4)
        lines = [jnp.sum(value, axis=0, keepdims=True) for value in sums]
        small[...] = jnp.concatenate(lines + [jnp.zeros((4, width), jnp.float32)], axis=0)
        grad_out[...] = jnp.dot(
            mixed[...].T, normed[...], preferred_element_type=jnp.float32
        ).astype(jnp.bfloat16)


def feed(pick, place_at, kind, vectors, up_shift, tokens, mixed, out_weight, cotangent, up, down):
    rows, width = tokens.shape
    ff = up.shape[2]
    band = 512
    low, wide = jnp.bfloat16, jnp.float32

    def whole(array):
        return pl.BlockSpec(array.shape, lambda i, pick, place_at: (0,) * array.ndim)

    fixed = [
        jax.ShapeDtypeStruct((rows, width), low),
        jax.ShapeDtypeStruct((rows, width), wide),
        jax.ShapeDtypeStruct((width, width), low),
        jax.ShapeDtypeStruct((rows, width), low),
    ]
    last = jax.ShapeDtypeStruct((8, width), wide)
    return pl.pallas_call(
        feed_kernel,
        out_shape=fixed
        + [
            jax.ShapeDtypeStruct((width, ff), low),
            jax.ShapeDtypeStruct((ff, width), low),
            last,
            jax.ShapeDtypeStruct((8, ff), wide),
        ],
        grid_spec=pltpu.PrefetchScalarGridSpec(
            num_scalar_prefetch=2,
            grid=(ff // band,),
            in_specs=[
                whole(kind),
                whole(vectors),
                pl.BlockSpec((1, 1, band), lambda i, pick, place_at: (pick[0], 0, i)),
                whole(tokens),
                whole(mixed),
                whole(out_weight),
                whole(cotangent),
                pl.BlockSpec((1, width, band), lambda i, pick, place_at: (pick[0], 0, i)),
                pl.BlockSpec((1, band, width), lambda i, pick, place_at: (pick[0], i, 0)),
            ],
            out_specs=[whole(array) for array in fixed]
            + [
                pl.BlockSpec((width, band), lambda i, pick, place_at: (0, i)),
                pl.BlockSpec((band, width), lambda i, pick, place_at: (i, 0)),
                whole(last),
                pl.BlockSpec((8, band), lambda i, pick, place_at: (0, i)),
            ],
            scratch_shapes=[
                pltpu.VMEM((rows, width), wide),
                pltpu.VMEM((rows, width), low),
                pltpu.VMEM((width, rows), low),
                pltpu.VMEM((rows, width), low),
                pltpu.VMEM((rows, width), wide),
                pltpu.VMEM((rows, width), wide),
            ],
        ),
        compiler_params=pltpu.CompilerParams(vmem_limit_bytes=62 << 20),
    )(pick, place_at, kind, vectors, up_shift, tokens, mixed, out_weight, cotangent, up, down)


MESH = pl.DeviceIdType.MESH
GATHER_ORDERS = (("z", "f", "x", "y"), ("z", "f", "y", "x"), ("y", "x", "z", "f"))
SCATTER_ORDERS = (("y", "x", "a", "z"), ("x", "y", "a", "z"), ("a", "z", "x", "y"))
STEPS = 5
EVERY = slice(None)
THIN_ROWS = 16


def coords():
    items, stream = lax.axis_index("items"), lax.axis_index("stream")
    return dict(z=items // 2, x=items % 2, y=stream // 2, c=stream % 2)


def place(at):
    return (at["z"] * 2 + at["x"], at["y"] * 2 + at["c"])


def moved(at, dim, by, depth):
    return {**at, dim: lax.rem(at[dim] + by, depth if dim == "z" else 2)}


def greet(at, depth):
    peers = [moved(at, "z", k, depth) for k in range(1, depth)]
    peers += [moved(at, d, 1, depth) for d in "xyc"]
    barrier = pltpu.get_barrier_semaphore()
    for peer in peers:
        pl.semaphore_signal(barrier, inc=1, device_id=place(peer), device_id_type=MESH)
    pl.semaphore_wait(barrier, len(peers))


def guard(cond, act):
    if cond is None:
        act()
    else:
        pl.when(cond)(act)


def remote(src, dst, sems, index, device):
    return pltpu.make_async_remote_copy(
        src_ref=src,
        dst_ref=dst,
        send_sem=sems[0].at[index],
        recv_sem=sems[1].at[index],
        device_id=place(device),
        device_id_type=MESH,
    )


def both_of(first, second):
    if first is None or second is None:
        return second if first is None else first
    return jnp.logical_and(first, second)


class Pipeline:
    def __init__(self, chunks, ahead, start, wait):
        self.chunks, self.ahead, self.start, self.wait = chunks, ahead, start, wait
        self.ticks = 0
        for chunk in chunks[:ahead]:
            start(chunk, 0)

    def tick(self, times=1):
        count = len(self.chunks)
        for t in range(self.ticks, min(self.ticks + times, count + STEPS - 1)):
            if t + self.ahead < count:
                self.start(self.chunks[t + self.ahead], 0)
            for step in range(STEPS):
                if 0 <= t - step < count:
                    self.wait(self.chunks[t - step], step)
                    if step < STEPS - 1:
                        self.start(self.chunks[t - step], step + 1)
        self.ticks += times


def spots_of(depth):
    return [(a, b, c, d) for a in range(depth) for b in range(2) for c in range(2) for d in range(2)]


def columns_over(share, width):
    column = lax.broadcasted_iota(jnp.int32, (1, width), 1).astype(jnp.float32)
    owner = jnp.floor((column + 0.5) * (1.0 / share))
    return owner, column - owner * share


def spread(thin, share, width):
    owner, lane = columns_over(share, width)
    picks = lax.broadcasted_iota(jnp.int32, (128, width), 0).astype(jnp.float32) == lane
    wide = jnp.dot(thin, picks.astype(jnp.bfloat16), preferred_element_type=jnp.float32)
    total = jnp.zeros((THIN_ROWS, width), jnp.float32)
    for device in range(thin.shape[0] // THIN_ROWS):
        part = wide[device * THIN_ROWS : (device + 1) * THIN_ROWS]
        total = total + jnp.where(owner == device, part, 0.0)
    return total


def dealt(rows, share, devices):
    width = rows.shape[1]
    owner, lane = columns_over(share, width)
    picks = lax.broadcasted_iota(jnp.int32, (128, width), 0).astype(jnp.float32) == lane
    tall = jnp.concatenate(
        [jnp.where(owner == device, rows, 0.0) for device in range(devices)], axis=0
    )
    return lax.dot_general(
        tall,
        picks.astype(jnp.float32),
        (((1,), (1,)), ((), ())),
        precision=lax.Precision.HIGHEST,
        preferred_element_type=jnp.float32,
    )


def gather_kernel(depth, chunks, entries, *refs):
    it = iter(refs)
    take = lambda count: [next(it) for _ in range(count)]
    ins = take(5)
    tokens, kind = take(2)
    thin_out, out_all, up_all, down_all = take(4)
    weight_out, normed_out, queries_out, vectors, kv_out, mixed, mixed_t_out, log_total = take(8)
    (far_normed_out,) = take(1)
    thin_all, qkv_all, kv, values_t, scaled, top, total = take(7)
    qkv_weight, normed, queries, mixed_t, far_tokens, far_normed = take(6)
    local_sem = next(it)
    sems, kv_sems = take(2), take(2)
    keep_sem = next(it)
    outs = (thin_all, qkv_all, out_all, up_all, down_all)
    rows, width = tokens.shape
    devices = depth * 8
    share = width // devices
    at = coords()
    mine = (at["z"], at["x"], at["y"], at["c"])
    slot = at["y"] * 2 + at["c"]

    def source(entry):
        k, e = entry
        return ins[k] if e is None else ins[k].at[e]

    def target(entry):
        k, e = entry
        return outs[k] if e is None else outs[k].at[e]

    local = [
        pltpu.make_async_copy(source(entry), target(entry).at[mine], local_sem.at[j])
        for j, entry in enumerate(entries)
    ]
    for copy in local:
        copy.start()
    greet(at, depth)
    for copy in local:
        copy.wait()
    lower, upper = at["y"] == 0, at["y"] == 1
    number = {piece: j for j, piece in enumerate(piece for chunk in chunks for piece in chunk)}

    z = at["z"]

    def stage(piece, step):
        entry, band, cols, order, text = piece
        dims = GATHER_ORDERS[order] + ("c",)
        dim = dims[step]
        box = (pl.ds(*band), pl.ds(*cols))
        live = upper if text and "y" in dims[:step] else None

        def held(level):
            spot = {d: EVERY if d in dims[:step] else pl.ds(at[d], 1) for d in "zxyc"}
            if level is not None:
                spot["z"] = pl.ds(level, 1)
            return target(entry).at[tuple(spot[d] for d in "zxyc") + box]

        if dim == "f":
            up_view, down_view = held(0), held(depth - 1)
            up = remote(up_view, up_view, sems, (number[piece], depth + 2), {**at, "z": z + 1})
            down = remote(down_view, down_view, sems, (number[piece], depth + 2), {**at, "z": z - 1})
            return [
                (up, both_of(live, z == depth - 2), both_of(live, z == depth - 1)),
                (down, both_of(live, z == 1), both_of(live, z == 0)),
            ]
        view = held(None)
        if dim == "z":
            found = []
            for k in range(1, depth):
                to, source_level = lax.rem(z + k, depth), lax.rem(z + depth - k, depth)
                copy = remote(view, view, sems, (number[piece], k - 1), {**at, "z": to})
                sends = both_of(live, jnp.abs(to - z) != depth - 1)
                found.append((copy, sends, both_of(live, jnp.abs(source_level - z) != depth - 1)))
            return found
        sem = {"x": depth - 1, "y": depth, "c": depth + 1}[dim]
        copy = remote(view, view, sems, (number[piece], sem), moved(at, dim, 1, depth))
        if text and dim == "y":
            return [(copy, lower, upper)]
        return [(copy, live, live)]

    def each(chunk, step, which, call):
        for piece in chunk:
            for found in stage(piece, step):
                guard(found[which], functools.partial(call, found[0]))

    beside, across = moved(at, "c", 1, depth), moved(at, "y", 1, depth)
    other = across["y"] * 2 + across["c"]
    own_slot = pl.ds(pl.multiple_of(slot * rows, rows), rows)
    other_slot = pl.ds(pl.multiple_of(other * rows, rows), rows)
    to_across = remote(tokens, far_tokens, kv_sems, 0, across)
    to_beside = remote(kv.at[own_slot], kv.at[own_slot], kv_sems, 1, beside)
    onward = remote(kv.at[other_slot], kv.at[other_slot], kv_sems, 2, beside)
    to_across.start()
    keep_kv = pltpu.make_async_copy(kv, kv_out, keep_sem.at[0])
    keep_mixed = pltpu.make_async_copy(mixed_t, mixed_t_out, keep_sem.at[1])
    keep_early = [
        pltpu.make_async_copy(src, dst, keep_sem.at[2 + j])
        for j, (src, dst) in enumerate(
            [
                (thin_all, thin_out),
                (qkv_weight, weight_out),
                (normed, normed_out),
                (far_normed, far_normed_out),
                (queries, queries_out),
            ]
        )
    ]

    def project():
        spots = spots_of(depth)
        for j, spot in enumerate(spots):
            qkv_weight[j * share : (j + 1) * share, :] = qkv_all[spot]
        thin = jnp.concatenate([thin_all[spot] for spot in spots], axis=0)
        vectors[...] = spread(thin, share, width)

        to_across.wait_recv()
        for given, made in ((tokens, normed), (far_tokens, far_normed)):

            @pl.loop(0, rows // 128)
            def _(j, given=given, made=made):
                block = pl.ds(pl.multiple_of(j * 128, 128), 128)
                value = given[block, :].astype(jnp.float32)
                centred = value - jnp.mean(value, axis=-1, keepdims=True)
                scale = lax.rsqrt(jnp.mean(centred * centred, axis=-1, keepdims=True) + NORM_EPS)
                made[block, :] = (centred * scale * vectors[0:1, :] + vectors[1:2, :]).astype(
                    jnp.bfloat16
                )

        step = width // 2
        for part in (1, 2, 0):

            @pl.loop(0, 2)
            def _(j, part=part):
                cols = pl.ds(pl.multiple_of(j * step, 128), step)
                weight_cols = qkv_weight[:, pl.ds(pl.multiple_of(part * width + j * step, 128), step)]
                value = jnp.dot(normed[...], weight_cols, preferred_element_type=jnp.float32)
                if part == 0:
                    queries[:, cols] = (value + vectors[2:3, cols]).astype(jnp.bfloat16)
                    return
                far_value = jnp.dot(far_normed[...], weight_cols, preferred_element_type=jnp.float32)
                to = pl.ds(pl.multiple_of((part - 1) * width + j * step, 128), step)
                shift = vectors[3:4, cols] if part == 2 else 0.0
                kv[own_slot, to] = (value + shift).astype(jnp.bfloat16)
                kv[other_slot, to] = (far_value + shift).astype(jnp.bfloat16)

            if part == 2:
                to_beside.start()
                onward.start()
        for copy in keep_early:
            copy.start()
        scale_queries(queries, scaled)

    def attend_first():
        to_beside.wait_recv()
        onward.wait_recv()
        keep_kv.start()
        flip_columns(kv, width, values_t)

    parts = (kind, slot, kv, values_t, scaled, mixed, mixed_t, log_total, top, total)

    def attention(qt, begin, end):
        def act():
            if qt == 0 and begin == 0:
                attend_first()
            attend_part(qt, begin, end, *parts)

        return act

    everyone = kv.shape[0] // TK
    flow = Pipeline(
        chunks,
        2,
        lambda chunk, step: each(chunk, step, 1, lambda copy: copy.start()),
        lambda chunk, step: each(chunk, step, 2, lambda copy: copy.wait_recv()),
    )
    flow.tick(5)
    project()
    flow.tick()
    attention(0, 0, everyone // 2)()
    flow.tick()
    attention(0, everyone // 2, everyone)()
    flow.tick()
    attention(1, 0, everyone // 2)()
    flow.tick()
    attention(1, everyone // 2, everyone)()
    flow.tick(STEPS + len(chunks))
    for copy in (to_beside, to_across, onward):
        copy.wait_send()
    keep_mixed.start()
    for copy in keep_early + [keep_kv, keep_mixed]:
        copy.wait()
    for chunk in chunks:
        for step in range(STEPS):
            each(chunk, step, 1, lambda copy: copy.wait_send())


def gather_all(thin, w_qkv, w_out, w_up, w_down, tokens, kind, depth):
    rows, width = tokens.shape
    share, ff_share, ff = w_qkv.shape[0], w_down.shape[1], w_up.shape[2]
    entries = [(0, None), (1, None), (2, None), (3, 0), (3, 1), (4, 0), (4, 1)]
    chunks = gather_chunks(share, width, ff_share, ff)
    n_pieces = sum(len(chunk) for chunk in chunks)
    anywhere = pl.BlockSpec(memory_space=pl.ANY)
    inside = pl.BlockSpec(memory_space=pltpu.VMEM)
    low = jnp.bfloat16
    box = (depth, 2, 2, 2)
    heads, lines = width // HEAD_DIM, -(-(width // HEAD_DIM) // 8) * 8
    return pl.pallas_call(
        functools.partial(gather_kernel, depth, chunks, entries),
        out_shape=[
            jax.ShapeDtypeStruct(box + thin.shape, low),
            jax.ShapeDtypeStruct(box + (share, width), low),
            jax.ShapeDtypeStruct((2,) + box + (share, ff), low),
            jax.ShapeDtypeStruct((2,) + box + (ff_share, width), low),
            jax.ShapeDtypeStruct((width, 3 * width), low),
            jax.ShapeDtypeStruct((rows, width), low),
            jax.ShapeDtypeStruct((rows, width), low),
            jax.ShapeDtypeStruct((THIN_ROWS, width), jnp.float32),
            jax.ShapeDtypeStruct((4 * rows, 2 * width), low),
            jax.ShapeDtypeStruct((rows, width), low),
            jax.ShapeDtypeStruct((width, rows), jnp.float32),
            jax.ShapeDtypeStruct((lines, rows), jnp.float32),
            jax.ShapeDtypeStruct((rows, width), low),
        ],
        in_specs=[inside] * 7,
        out_specs=[anywhere] * 7 + [inside, anywhere, inside, anywhere, inside, anywhere],
        scratch_shapes=[
            pltpu.VMEM(box + thin.shape, low),
            pltpu.VMEM(box + (share, 3 * width), low),
            pltpu.VMEM((4 * rows, 2 * width), low),
            pltpu.VMEM((width, 4 * rows), low),
            pltpu.VMEM((heads, PAIR, rows), low),
            pltpu.VMEM((lines, TQ), jnp.float32),
            pltpu.VMEM((lines, TQ), jnp.float32),
            pltpu.VMEM((width, 3 * width), low),
            pltpu.VMEM((rows, width), low),
            pltpu.VMEM((rows, width), low),
            pltpu.VMEM((width, rows), jnp.float32),
            pltpu.VMEM((rows, width), low),
            pltpu.VMEM((rows, width), low),
            pltpu.SemaphoreType.DMA((len(entries),)),
            pltpu.SemaphoreType.DMA((n_pieces, depth + 3)),
            pltpu.SemaphoreType.DMA((n_pieces, depth + 3)),
            pltpu.SemaphoreType.DMA((3,)),
            pltpu.SemaphoreType.DMA((3,)),
            pltpu.SemaphoreType.DMA((7,)),
        ],
        compiler_params=pltpu.CompilerParams(
            collective_id=1, has_side_effects=True, vmem_limit_bytes=62 << 20
        ),
    )(thin, w_qkv, w_out, w_up, w_down, tokens, kind)


def rows_of_kind(kind, rows):
    patch_len, members = ((PATCH_S, ITEMS_S), (PATCH_L, ITEMS_L))[kind]
    return float(min(patch_len * members, 3 * rows)), float(min(TEXT_LEN * members, rows))


def scatter_kernel(depth, kinds, chunks, cuts, *refs):
    n, n_far = len(kinds), 3
    it = iter(refs)
    take = lambda count: [next(it) for _ in range(count)]
    far = take(n_far)
    small, up_shift_sum, vectors, kind, log_total = take(5)
    queries, kv, mixed_grad, mixed_t, normed, far_normed, weight, tokens, residual_grad = take(9)
    outs = take(n)
    token_grad, kv_away = take(2)
    acc, first, second, last = take(n), take(n), take(n), take(n)
    relay, z_relay, z_first, z_second, z_last = (take(n) for _ in range(5))
    own_half = take(n_far)
    qkv_terms, thin_terms, kv_sum, far_terms, far_got, kv_mine, dq = take(7)
    sems = take(2)
    local_sem, away_sem = take(2)
    kv_sems = take(2)
    rows, width = residual_grad.shape
    devices = depth * 8
    share = width // devices
    at = coords()
    z, x, y, c = (at[d] for d in "zxyc")
    ins = far + [qkv_terms, thin_terms]
    groups = devices // 4
    lane = lax.broadcasted_iota(jnp.int32, (1, width), 1)
    marks = functools.reduce(
        jnp.logical_or, [lane == group * (width // groups) for group in range(groups)]
    )
    second_kind = jnp.sum(jnp.where(marks, vectors[11:12, :], 0.0), axis=1, keepdims=True)
    counts = [
        first_count * (groups - second_kind) + second_count * second_kind
        for first_count, second_count in zip(*(rows_of_kind(kind_of, rows) for kind_of in range(2)))
    ]
    factors = [lax.rsqrt(count) for count in counts]
    local = [
        pltpu.make_async_copy(far[k].at[EVERY, EVERY, EVERY, c], own_half[k], local_sem.at[k])
        for k in range(n_far)
    ]
    for copy in local:
        copy.start()
    greet(at, depth)
    beside, across = moved(at, "c", 1, depth), moved(at, "y", 1, depth)
    kv_beside = remote(kv_away, kv_sum, kv_sems, 0, beside)
    kv_across = remote(far_terms, far_got, kv_sems, 1, across)
    lower, upper = y == 0, y == 1
    text_device = jnp.logical_and(upper, c == 1)
    image_device = jnp.logical_or(lower, c == 0)
    beside_text = jnp.logical_and(upper, c == 0)
    beside_image = jnp.logical_or(lower, c == 1)
    number = {piece: j for j, piece in enumerate(piece for chunk in chunks for piece in chunk)}

    sources = (
        (z == 0, range(2, depth)),
        (jnp.logical_and(z > 0, z < depth - 1), range(1, depth)),
        (z == depth - 1, range(1, depth - 1)),
    )

    def boxes(piece):
        k, e, band, cols, order = piece
        cut = cuts[k] if order == 2 else (0, 0)
        return (
            (pl.ds(*band), pl.ds(*cols)),
            (pl.ds(band[0] - cut[0], band[1]), pl.ds(cols[0] - cut[1], cols[1])),
        )

    def copies_of(piece, step):
        k, e, band, cols, order = piece
        box, inner = boxes(piece)
        image, text = kinds[k] and e == 0, kinds[k] and e == 1
        dims = ("c",) + SCATTER_ORDERS[order]
        dim = dims[step]
        here = acc[k].at[e]

        def make(src, dst, sem, by=1):
            return remote(src, dst, sems, (number[piece], sem), moved(at, dim, by, depth))

        sends = recvs = None
        if dim == "c":
            if image:
                sends, recvs = image_device, beside_image
            elif text:
                sends, recvs = text_device, beside_text
            src = ins[k].at[(EVERY, EVERY, EVERY, 1 - c) + box]
            return [(make(src, here.at[(EVERY, EVERY, EVERY) + box], 0), sends, recvs)]
        if text and dim == "y":
            sends, recvs = upper, lower
        elif text and "y" not in dims[:step]:
            sends = recvs = upper
        where = (EVERY, EVERY) if order == 2 else (x, y)
        if dim == "a":
            src = here.at[(depth - 1 - z,) + where + box]
            dst = z_relay[k].at[(e, EVERY, EVERY) + inner] if order == 2 else relay[k].at[(e,) + inner]
            to = {**at, "z": jnp.where(z == 0, 1, depth - 2)}
            copy = remote(src, dst, sems, (number[piece], depth + 2), to)
            ends = jnp.logical_or(z == 0, z == depth - 1)
            middle = jnp.logical_and(z > 0, z < depth - 1)
            return [(copy, both_of(sends, ends), both_of(recvs, middle))]
        if dim == "z":
            found = []
            for by in range(1, depth):
                to, source_level = lax.rem(z + by, depth), lax.rem(z + depth - by, depth)
                src = here.at[(to,) + where + box]
                if order == 2:
                    dst = z_first[k].at[(e, by - 1, EVERY, EVERY) + inner]
                else:
                    dst = last[k].at[(e, by - 1) + inner]
                found.append(
                    (
                        make(src, dst, 2 + by, by),
                        both_of(sends, jnp.abs(to - z) != depth - 1),
                        both_of(recvs, jnp.abs(source_level - z) != depth - 1),
                    )
                )
            return found
        if order == 2 and dim == "x":
            src, dst = here.at[(z, 1 - x, EVERY) + box], z_second[k].at[(e, EVERY) + inner]
            return [(make(src, dst, 1), sends, recvs)]
        if order == 2:
            src, dst = here.at[(z, x, 1 - y) + box], z_last[k].at[(e,) + inner]
            return [(make(src, dst, 2), sends, recvs)]
        if step == 1:
            spot = (EVERY, EVERY, 1 - y) if dim == "y" else (EVERY, 1 - x, EVERY)
            dst = first[k].at[(e, EVERY, EVERY) + inner]
        else:
            spot = (EVERY, x, 1 - y) if dim == "y" else (EVERY, 1 - x, y)
            dst = second[k].at[(e, EVERY) + inner]
        return [(make(here.at[spot + box], dst, step), sends, recvs)]

    def combine(piece, step):
        k, e, band, cols, order = piece
        box, inner = boxes(piece)
        image, text = kinds[k] and e == 0, kinds[k] and e == 1
        dims = ("c",) + SCATTER_ORDERS[order]
        dim = dims[step]
        here = acc[k].at[e]

        def over(spots, value_of, keep):
            @pl.loop(0, depth)
            def _(level):
                for index, spot in enumerate(spots):
                    where = (level,) + spot + box
                    value = value_of(level, index, spot)
                    here[where] = value if keep else here[where] + value

        def wide(value):
            return value.astype(jnp.float32)

        if step == 0:
            spots = [(0, 0), (0, 1), (1, 0), (1, 1)]

            def own(level, index, spot):
                if k < n_far:
                    return own_half[k][(level,) + spot + box]
                return ins[k][(level,) + spot + (c,) + box]

            if image:
                pl.when(lower)(lambda: over(spots, own, False))
                pl.when(beside_text)(lambda: over(spots, own, True))
            elif text:
                pl.when(text_device)(lambda: over(spots, own, True))
            else:
                over(spots, own, False)
        elif dim == "a":
            dest = jnp.where(z == 1, depth - 1, 0)

            def act():
                if order == 2:
                    for spot in [(0, 0), (0, 1), (1, 0), (1, 1)]:
                        where = (dest,) + spot + box
                        here[where] = here[where] + z_relay[k][(e,) + spot + inner]
                else:
                    where = (dest, x, y) + box
                    here[where] = here[where] + relay[k][(e,) + inner]

            middle = jnp.logical_and(z > 0, z < depth - 1)
            guard(both_of(upper if text and order == 2 else None, middle), act)
        elif step == STEPS - 1:

            def finish(total):
                if kinds[k]:
                    total = total * factors[e]
                outs[k][(e,) + box] = total

            def own():
                return wide(here[(z, x, y) + box])

            if order == 2:
                got = lambda: wide(z_last[k][(e,) + inner])
                if text:
                    pl.when(lower)(lambda: finish(got()))
                    pl.when(upper)(lambda: finish(own()))
                else:
                    finish(own() + got())
            else:
                for cond, bys in sources:

                    @pl.when(cond)
                    def _(bys=bys):
                        total = own()
                        for by in bys:
                            total = total + wide(last[k][(e, by - 1) + inner])
                        finish(total)
        elif dim == "z":
            for cond, bys in sources:

                def act(bys=bys):
                    for spot in [(0, 0), (0, 1), (1, 0), (1, 1)]:
                        where = (z,) + spot + box
                        total = wide(here[where])
                        for by in bys:
                            total = total + wide(z_first[k][(e, by - 1) + spot + inner])
                        here[where] = total.astype(here.dtype)

                guard(both_of(upper if text else None, cond), act)
        elif order == 2:

            def act():
                for other in range(2):
                    where = (z, x, other) + box
                    here[where] = here[where] + z_second[k][(e, other) + inner]

            guard(upper if text else None, act)
        elif step == 1:
            spots = [(0, y), (1, y)] if dim == "y" else [(x, 0), (x, 1)]
            got = lambda level, index, spot: first[k][(e, level, index) + inner]
            if text and dim == "y":
                pl.when(lower)(lambda: over(spots, got, True))
            elif text:
                pl.when(upper)(lambda: over(spots, got, False))
            else:
                over(spots, got, False)
        else:
            got = lambda level, index, spot: second[k][(e, level) + inner]
            if text and dim == "y":
                pl.when(lower)(lambda: over([(x, y)], got, True))
            else:
                over([(x, y)], got, False)

    def start(chunk, step):
        for piece in chunk:
            for copy, sends, _ in copies_of(piece, step):
                guard(sends, copy.start)

    def wait(chunk, step):
        for piece in chunk:
            for copy, _, recvs in copies_of(piece, step):
                guard(recvs, copy.wait_recv)
            combine(piece, step)

    def halve():
        kv_beside.wait_recv()

        @pl.loop(0, rows // 64)
        def _(j):
            block = pl.ds(pl.multiple_of(j * 64, 64), 64)
            for level in range(2):
                kv_sum[level, block, :] = kv_sum[level, block, :] + kv_mine[level, block, :]

    def project_back(qkv_grad, flipped, normed_in, far_in, weight_in, tokens_in, residual_in, token_out):
        pairs = [
            (weight, weight_in),
            (normed, normed_in),
            (far_normed, far_in),
            (tokens, tokens_in),
            (residual_grad, residual_in),
        ]
        loads = [pltpu.make_async_copy(src, dst, away_sem.at[j]) for j, (src, dst) in enumerate(pairs)]
        for copy in loads:
            copy.start()
        halve()
        qkv_grad[:rows, :width] = dq[...]
        qkv_grad[:rows, width:] = kv_sum[y]
        qkv_grad[rows:, width:] = kv_sum[1 - y]
        for copy in loads:
            copy.wait()

        @pl.loop(0, rows // 128)
        def _(j):
            block = pl.ds(pl.multiple_of(j * 128, 128), 128)
            below = pl.ds(pl.multiple_of(rows + j * 128, 128), 128)
            far_terms[block, :] = product_trail(
                qkv_grad[below, width:], weight_in[:, width:]
            ).astype(jnp.bfloat16)

        kv_across.start()
        flipped[:, :rows] = normed_in[...].T
        flipped[:, rows:] = far_in[...].T

        def fold(value):
            return jnp.sum(value.reshape(-1, 8, width), axis=0)

        zero = jnp.zeros((8, width), jnp.float32)

        def gather_sums(j, carry):
            block = pl.ds(pl.multiple_of(j * 64, 64), 64)
            below = pl.ds(pl.multiple_of(rows + j * 64, 64), 64)
            own, far_part = qkv_grad[block, 2 * width :], qkv_grad[below, 2 * width :]
            return (
                carry[0] + fold(dq[block, :].astype(jnp.float32)),
                carry[1] + fold(own.astype(jnp.float32) + far_part.astype(jnp.float32)),
            )

        sum_q, sum_v = lax.fori_loop(0, rows // 64, gather_sums, (zero, zero))
        step = width // 2
        spots = spots_of(depth)
        for begin, count, depth_rows in ((0, 2, rows), (2, 4, 2 * rows)):

            @pl.loop(begin, begin + count)
            def _(j, depth_rows=depth_rows):
                cols = pl.ds(pl.multiple_of(j * step, 128), step)
                value = jnp.dot(
                    flipped[:, :depth_rows],
                    qkv_grad[:depth_rows, cols],
                    preferred_element_type=jnp.float32,
                ).astype(jnp.bfloat16)
                for index, spot in enumerate(spots):
                    qkv_terms[spot + (EVERY, cols)] = value[index * share : (index + 1) * share]

        flow.tick()
        kv_across.wait_recv()

        def back(j, carry):
            block = pl.ds(pl.multiple_of(j * 128, 128), 128)
            value = tokens_in[block, :].astype(jnp.float32)
            centred = value - jnp.mean(value, axis=-1, keepdims=True)
            scale = lax.rsqrt(jnp.mean(centred * centred, axis=-1, keepdims=True) + NORM_EPS)
            unit = centred * scale
            grad = product_trail(qkv_grad[block, :], weight_in[...]) + far_got[block, :].astype(
                jnp.float32
            )
            lifted = grad * vectors[0:1, :]
            inner = jnp.mean(lifted * unit, axis=-1, keepdims=True)
            part = scale * (lifted - jnp.mean(lifted, axis=-1, keepdims=True) - unit * inner)
            token_out[block, :] = (residual_in[block, :] + part).astype(jnp.bfloat16)
            return carry[0] + fold(grad * unit), carry[1] + fold(grad)

        sum_gain, sum_shift = lax.fori_loop(0, rows // 128, back, (zero, zero))
        store = pltpu.make_async_copy(token_out, token_grad, away_sem.at[0])
        store.start()
        lines = [jnp.sum(value, axis=0, keepdims=True) for value in (sum_gain, sum_shift, sum_q, sum_v)]
        def stack(parts):
            count = sum(part.shape[0] for part in parts)
            return jnp.concatenate(parts + [jnp.zeros((8 - count, parts[0].shape[1]), jnp.float32)])

        scales = [
            jnp.where(text_device == (e == 1), factors[e], 0.0)
            for e in range(2)
        ]
        down_part = [small[3:4, :] * scale for scale in scales]
        up_part = [up_shift_sum[0:1, :] * scale for scale in scales]
        ff = up_shift_sum.shape[1]
        head = dealt(stack(lines + [small[0:3, :]]), share, devices)
        tail = dealt(stack(down_part), share, devices) + dealt(
            stack([jnp.zeros((2, ff), jnp.float32)] + up_part), ff // devices, devices
        )
        for index, spot in enumerate(spots):
            rows_of = slice(index * 8, (index + 1) * 8)
            thin_terms[spot] = jnp.concatenate([head[rows_of], tail[rows_of]], axis=0)
        store.wait()

    def project_scope():
        low = jnp.bfloat16
        pl.run_scoped(
            project_back,
            pltpu.VMEM((2 * rows, 3 * width), low),
            pltpu.VMEM((width, 2 * rows), low),
            pltpu.VMEM((rows, width), low),
            pltpu.VMEM((rows, width), low),
            pltpu.VMEM((width, 3 * width), low),
            pltpu.VMEM((rows, width), low),
            pltpu.VMEM((rows, width), jnp.float32),
            pltpu.VMEM((rows, width), low),
        )

    group_width = width // 2
    stream = y * 2 + c

    def attention(group):
        cols = pl.ds(group * group_width, group_width)
        value_cols = pl.ds(width + group * group_width, group_width)

        def act(keys, values, q_in, g_in, mixed_in, *work):
            pairs = [
                (kv.at[:, cols], keys),
                (kv.at[:, value_cols], values),
                (queries.at[:, cols], q_in),
                (mixed_grad.at[:, cols], g_in),
                (mixed_t.at[cols, :], mixed_in),
            ]
            loads = [pltpu.make_async_copy(src, dst, away_sem.at[j]) for j, (src, dst) in enumerate(pairs)]
            for copy in loads:
                copy.start()
            for copy in loads:
                copy.wait()
            back_group(
                group, kind, stream, log_total, keys, values, q_in, g_in, mixed_in,
                dq.at[:, cols], flow.tick, *work,
            )
            dk, dv = work[-2:]
            for part, (terms, rest, begin) in enumerate(((dk, keys, cols), (dv, values, value_cols))):
                for level in range(2):
                    mine = (level * 2 + c) * rows
                    away = (level * 2 + 1 - c) * rows

                    @pl.loop(0, rows // 128)
                    def _(j, level=level, mine=mine, away=away, terms=terms, rest=rest, begin=begin):
                        to = pl.ds(pl.multiple_of(j * 128, 128), 128)
                        kept = pl.ds(pl.multiple_of(mine + j * 128, 128), 128)
                        sent = pl.ds(pl.multiple_of(away + j * 128, 128), 128)
                        kv_mine[level, to, begin] = terms[kept, :].astype(jnp.bfloat16)
                        rest[sent, :] = terms[sent, :].astype(jnp.bfloat16)

            stores = []
            for part, (rest, begin) in enumerate(((keys, cols), (values, value_cols))):
                for level in range(2):
                    sent = pl.ds(pl.multiple_of((level * 2 + 1 - c) * rows, rows), rows)
                    stores.append(
                        pltpu.make_async_copy(
                            rest.at[sent], kv_away.at[level, :, begin], away_sem.at[part * 2 + level]
                        )
                    )
            for copy in stores:
                copy.start()
            for copy in stores:
                copy.wait()
            if group == 1:
                kv_beside.start()

        def scope():
            low = jnp.bfloat16
            heads = group_width // HEAD_DIM
            everyone = 4 * rows
            pl.run_scoped(
                act,
                pltpu.VMEM((everyone, group_width), low),
                pltpu.VMEM((everyone, group_width), low),
                pltpu.VMEM((rows, group_width), low),
                pltpu.VMEM((rows, group_width), low),
                pltpu.VMEM((group_width, rows), jnp.float32),
                pltpu.VMEM((group_width, everyone), low),
                pltpu.VMEM((heads, rows, PAIR), low),
                pltpu.VMEM((heads, rows, PAIR), low),
                pltpu.VMEM((heads, PAIR, rows), low),
                pltpu.VMEM((heads, PAIR, rows), low),
                pltpu.VMEM((group_width, TQ), jnp.float32),
                pltpu.VMEM((8, rows), jnp.float32),
                pltpu.VMEM((everyone, group_width), jnp.float32),
                pltpu.VMEM((everyone, group_width), jnp.float32),
            )

        return scope

    flow = Pipeline(chunks, 2, start, wait)
    for copy in local:
        copy.wait()
    flow.tick()
    attention(0)()
    flow.tick()
    attention(1)()
    flow.tick()
    project_scope()
    flow.tick(STEPS + len(chunks))
    lane = lax.broadcasted_iota(jnp.int32, (1, 128), 1)
    outs[4][0, THIN_ROWS - 1 : THIN_ROWS, :] = jnp.where(
        lane == 0, counts[0], jnp.where(lane == 1, counts[1], 0.0)
    )
    for copy in (kv_beside, kv_across):
        copy.wait_send()
    for chunk in chunks:
        for step in range(STEPS):
            for piece in chunk:
                for copy, sends, _ in copies_of(piece, step):
                    guard(sends, copy.wait_send)


def scatter_all(
    up, down, out, small, up_shift_sum, vectors, kind, log_total,
    queries, kv, mixed_grad, mixed_t, normed, far_normed, weight, tokens, residual_grad, depth,
):
    rows, width = tokens.shape
    far = [up, down, out]
    kinds = (True, True, False, False, False)
    share, ff_share, ff = up.shape[4], down.shape[4], up.shape[5]
    chunks, cuts = scatter_chunks(share, width, ff_share, ff)
    n_pieces = sum(len(chunk) for chunk in chunks)
    anywhere, inside = pl.BlockSpec(memory_space=pl.ANY), pl.BlockSpec(memory_space=pltpu.VMEM)
    low, box = jnp.bfloat16, (depth, 2, 2, 2)
    tails = [a.shape[4:] for a in far] + [(share, 3 * width), (THIN_ROWS, 128)]
    dtypes = [low] * 4 + [jnp.float32]
    experts = [2 if kind else 1 for kind in kinds]
    scratch = [
        pltpu.VMEM((e, depth, 2, 2) + tail, dtype) for e, tail, dtype in zip(experts, tails, dtypes)
    ]
    plain, turned = [], []
    for tail, cut in zip(tails, cuts):
        plain.append((cut[0] or tail[0], cut[1] or tail[1]))
        turned.append((tail[0] - cut[0], tail[1] - cut[1]) if any(cut) else (8, 128))
    for middle in ((depth, 2), (depth,), (depth - 1,)):
        scratch += [pltpu.VMEM((e,) + middle + t, d) for e, t, d in zip(experts, plain, dtypes)]
    scratch += [pltpu.VMEM((e,) + t, d) for e, t, d in zip(experts, plain, dtypes)]
    for middle in ((2, 2), (depth - 1, 2, 2), (2,), ()):
        scratch += [pltpu.VMEM((e,) + middle + t, d) for e, t, d in zip(experts, turned, dtypes)]
    scratch += [pltpu.VMEM((depth, 2, 2) + a.shape[4:], low) for a in far]
    scratch += [
        pltpu.VMEM(box + (share, 3 * width), low),
        pltpu.VMEM(box + (THIN_ROWS, 128), jnp.float32),
        pltpu.VMEM((2, rows, 2 * width), low),
        pltpu.VMEM((rows, width), low),
        pltpu.VMEM((rows, width), low),
        pltpu.VMEM((2, rows, 2 * width), low),
        pltpu.VMEM((rows, width), low),
        pltpu.SemaphoreType.DMA((n_pieces, depth + 3)),
        pltpu.SemaphoreType.DMA((n_pieces, depth + 3)),
        pltpu.SemaphoreType.DMA((3,)),
        pltpu.SemaphoreType.DMA((5,)),
        pltpu.SemaphoreType.DMA((2,)),
        pltpu.SemaphoreType.DMA((2,)),
    ]
    return pl.pallas_call(
        functools.partial(scatter_kernel, depth, kinds, chunks, cuts),
        out_shape=[
            jax.ShapeDtypeStruct((e,) + tail, jnp.float32) for e, tail in zip(experts, tails)
        ]
        + [jax.ShapeDtypeStruct((rows, width), low), jax.ShapeDtypeStruct((2, rows, 2 * width), low)],
        in_specs=[anywhere] * 3 + [inside] * 5 + [anywhere] * 9,
        out_specs=[inside] * 5 + [anywhere] * 2,
        scratch_shapes=scratch,
        compiler_params=pltpu.CompilerParams(
            collective_id=2, has_side_effects=True, vmem_limit_bytes=61 << 20
        ),
    )(
        up, down, out, small, up_shift_sum, vectors, kind, log_total,
        queries, kv, mixed_grad, mixed_t, normed, far_normed, weight, tokens, residual_grad,
    )[:6]


def publish_kernel(count, share, ff_share, *refs):
    far, thin = refs[:count], refs[count]
    outs, smalls = refs[count + 1 : 2 * count + 1], refs[2 * count + 1 : 2 * count + 11]
    held, sems = refs[2 * count + 11 : 3 * count + 11], refs[-1]
    inward = [pltpu.make_async_copy(far[j], held[j], sems.at[0, j]) for j in range(count)]
    outward = [pltpu.make_async_copy(held[j], outs[j], sems.at[1, j]) for j in range(count)]
    for copy in inward:
        copy.start()
    for j in range(7):
        smalls[j][...] = thin[j, :share]
    smalls[7][...] = thin[10:12, :ff_share]
    smalls[8][...] = thin[8:10, :share]
    smalls[9][...] = thin[THIN_ROWS - 1, :2]
    for first, second in zip(inward, outward):
        first.wait()
        second.start()
    for copy in outward:
        copy.wait()


def publish(arrays, thin, share, ff_share):
    anywhere, inside = pl.BlockSpec(memory_space=pl.ANY), pl.BlockSpec(memory_space=pltpu.VMEM)
    count = len(arrays)
    small = [(share,)] * 7 + [(2, ff_share), (2, share), (2,)]
    return pl.pallas_call(
        functools.partial(publish_kernel, count, share, ff_share),
        out_shape=[jax.ShapeDtypeStruct(array.shape, array.dtype) for array in arrays]
        + [jax.ShapeDtypeStruct(shape, jnp.float32) for shape in small],
        in_specs=[anywhere] * count + [inside],
        out_specs=[anywhere] * count + [inside] * len(small),
        scratch_shapes=[pltpu.VMEM(array.shape, array.dtype) for array in arrays]
        + [pltpu.SemaphoreType.DMA((2, count))],
        compiler_params=pltpu.CompilerParams(vmem_limit_bytes=62 << 20),
    )(*arrays, thin)


def padded(values):
    return jnp.pad(values, ((0, 0), (0, 128 - values.shape[1])))


def body(
    near,
    tokens,
    group_kind,
    ln1_gain,
    ln1_bias,
    w_qkv,
    q_bias,
    v_bias,
    w_out,
    out_bias,
    ln2_gain,
    ln2_bias,
    w_up,
    b_up,
    w_down,
    b_down,
    cotangent,
):
    row_count, model_width = tokens.shape
    stream_size = lax.axis_size("stream")
    stream_place = lax.axis_index("stream")
    devices = lax.axis_size("items") * stream_size
    group_type = group_kind[0]
    expert_pick = jnp.where(stream_place == stream_size - 1, 1, 0).astype(jnp.int32)
    share, ff_share, ff = model_width // devices, w_down.shape[1], w_up.shape[2]
    both = ("items", "stream")
    low = jnp.bfloat16
    thin = jnp.stack([ln1_gain, ln1_bias, q_bias, v_bias, out_bias, ln2_gain, ln2_bias])
    thin = jnp.concatenate(
        [padded(thin), padded(b_up), padded(b_down), padded(group_kind.astype(low)[:, None])]
    )
    thin = jnp.pad(thin, ((0, THIN_ROWS - thin.shape[0]), (0, 0)))
    tokens_f = tokens.astype(jnp.float32)
    kind_wide = jnp.broadcast_to(group_type.astype(jnp.float32), (8, 128))
    place_at = stream_place.astype(jnp.int32)[None]
    if near:
        depth = lax.axis_size("items") // 2
        (
            thin_all,
            out_weight,
            up_all,
            down_all,
            qkv_weight,
            normed_low,
            queries,
            vectors,
            kv,
            mixed_low,
            mixed_t,
            log_total,
            far_normed,
        ) = gather_all(thin, w_qkv, w_out, w_up, w_down, tokens, kind_wide, depth)
        thin_all = thin_all.reshape(devices, THIN_ROWS, 128)
        out_weight = out_weight.reshape(model_width, model_width)
        up_all = up_all.reshape(2, model_width, ff)
        down_all = down_all.reshape(2, ff, model_width)
    else:
        thin_all = lax.all_gather(thin, both, axis=0)
        qkv_weight = lax.all_gather(w_qkv, both, axis=0, tiled=True)
        out_weight = lax.all_gather(w_out, both, axis=0, tiled=True)
        up_all = lax.all_gather(w_up, both, axis=1, tiled=True)
        down_all = lax.all_gather(w_down, both, axis=1, tiled=True)
        vectors = (
            thin_all[:, :, :share].transpose(1, 0, 2).reshape(THIN_ROWS, -1).astype(jnp.float32)
        )
        normed_low = layer_norm(tokens_f, vectors[0], vectors[1]).astype(low)
        shifts = jnp.concatenate([vectors[2], jnp.zeros_like(vectors[2]), vectors[3]])
        projected = (product(normed_low, qkv_weight) + shifts).astype(low)
        queries = projected[:, :model_width]
        kv = lax.all_gather(projected[:, model_width:], "stream", axis=0, tiled=True)
        mixed_low, mixed_t, log_total = attend(kind_wide, place_at, queries, kv)
    up_shift_all = thin_all[:, 7:9, :ff_share].transpose(1, 0, 2).reshape(2, ff)
    (
        output,
        residual_grad,
        grad_out_weight,
        mixed_grad,
        grad_up,
        grad_down,
        small,
        grad_up_shift,
    ) = feed(
        expert_pick[None],
        place_at,
        kind_wide,
        vectors,
        up_shift_all[:, None],
        tokens,
        mixed_low,
        out_weight,
        cotangent,
        up_all,
        down_all,
    )
    if near:
        box = (depth, 2, 2, 2)
        up_sum, down_sum, out_sum, qkv_sum, thin_sum, token_grad = scatter_all(
            grad_up.reshape(box + (share, ff)),
            grad_down.reshape(box + (ff_share, model_width)),
            grad_out_weight.reshape(box + (share, model_width)),
            small,
            grad_up_shift,
            vectors,
            kind_wide,
            log_total,
            queries,
            kv,
            mixed_grad,
            mixed_t,
            normed_low,
            far_normed,
            qkv_weight,
            tokens,
            residual_grad,
            depth,
        )
        thin_sum = thin_sum[0]
        (
            up_sum,
            down_sum,
            out_sum,
            qkv_sum,
            token_grad,
            *lines,
            up_shift_sum,
            down_shift_sum,
            totals,
        ) = publish(
            [up_sum, down_sum, out_sum[0], qkv_sum[0], token_grad], thin_sum, share, ff_share
        )
    else:
        kinds = vectors[11, :: stream_size * share].astype(jnp.int32)
        tally = []
        for kind in range(2):
            modality = layout(
                jnp.int32(kind), jnp.arange(stream_size * row_count, dtype=jnp.int32), row_count
            )[1]
            tally.append([jnp.sum((modality == e).astype(jnp.float32)) for e in range(2)])
        totals = jnp.stack(
            [jnp.sum(jnp.where(kinds == 0, tally[0][e], tally[1][e])) for e in range(2)]
        )
        factor = lax.rsqrt(totals)
        pick = (jnp.arange(2, dtype=jnp.int32) == expert_pick).astype(jnp.float32) * factor

        def lanes(values):
            values = values.reshape(values.shape[0], devices, -1).transpose(1, 0, 2)
            return jnp.pad(values, ((0, 0), (0, 0), (0, 128 - values.shape[2])))

        scatter = functools.partial(
            lax.psum_scatter, axis_name=both, scatter_dimension=0, tiled=True
        )
        wide = functools.partial(lax.psum_scatter, axis_name=both, scatter_dimension=1, tiled=True)
        query_grad, kv_terms = attend_back(
            kind_wide, place_at, queries, kv, mixed_grad, mixed_t, log_total
        )
        kv_grad = lax.psum_scatter(
            kv_terms.astype(jnp.float32), "stream", scatter_dimension=0, tiled=True
        )
        qkv_grad = jnp.concatenate([query_grad, kv_grad.astype(low)], axis=1)
        grad_qkv = product_lead(normed_low, qkv_grad)
        early = [
            jnp.sum(qkv_grad[:, :model_width].astype(jnp.float32), axis=0),
            jnp.sum(qkv_grad[:, 2 * model_width :].astype(jnp.float32), axis=0),
        ]
        norm_one_grad = product_trail(qkv_grad, qkv_weight)
        token_part, *grads_one = jax.vjp(layer_norm, tokens_f, vectors[0], vectors[1])[1](
            norm_one_grad
        )
        token_grad = (residual_grad + token_part).astype(low)
        up_sum = wide(pick[:, None, None] * grad_up.astype(jnp.float32)[None])
        down_sum = wide(pick[:, None, None] * grad_down.astype(jnp.float32)[None])
        out_sum, qkv_sum = scatter(grad_out_weight.astype(jnp.float32)), scatter(grad_qkv)
        thin_terms = [
            lanes(jnp.stack(grads_one + early + [small[0], small[1], small[2]])),
            jnp.zeros((devices, 1, 128), jnp.float32),
            lanes(pick[:, None] * small[3][None]),
            lanes(pick[:, None] * grad_up_shift[0][None]),
            jnp.zeros((devices, THIN_ROWS - 12, 128), jnp.float32),
        ]
        thin_sum = scatter(jnp.concatenate(thin_terms, axis=1))[0]
        lines = [thin_sum[k, :share] for k in range(7)]
        up_shift_sum, down_shift_sum = thin_sum[10:12, :ff_share], thin_sum[8:10, :share]
    return (
        output,
        token_grad,
        lines[0],
        lines[1],
        qkv_sum,
        lines[2],
        lines[3],
        out_sum,
        lines[4],
        lines[5],
        lines[6],
        up_sum,
        up_shift_sum,
        down_sum,
        down_shift_sum,
        totals,
    )


def solution(mesh):
    placed = (
        P(("items", "stream"), None),
        P("items"),
        P(("items", "stream")),
        P(("items", "stream")),
        P(("items", "stream"), None),
        P(("items", "stream")),
        P(("items", "stream")),
        P(("items", "stream"), None),
        P(("items", "stream")),
        P(("items", "stream")),
        P(("items", "stream")),
        P(None, ("items", "stream"), None),
        P(None, ("items", "stream")),
        P(None, ("items", "stream"), None),
        P(None, ("items", "stream")),
        P(("items", "stream"), None),
    )
    near = mesh.shape["items"] == 8 and mesh.shape["stream"] == 4
    return jax.shard_map(
        functools.partial(body, near),
        mesh=mesh,
        in_specs=placed,
        out_specs=(
            P(("items", "stream"), None),
            P(("items", "stream"), None),
            P(("items", "stream")),
            P(("items", "stream")),
            P(("items", "stream"), None),
            P(("items", "stream")),
            P(("items", "stream")),
            P(("items", "stream"), None),
            P(("items", "stream")),
            P(("items", "stream")),
            P(("items", "stream")),
            P(None, ("items", "stream"), None),
            P(None, ("items", "stream")),
            P(None, ("items", "stream"), None),
            P(None, ("items", "stream")),
            P(),
        ),
        check_vma=False,
    )
```

```python
import functools

import jax
import jax.numpy as jnp
from jax import lax
from jax.experimental import pallas as pl
from jax.experimental.pallas import tpu as pltpu
from jax.sharding import PartitionSpec as P

HEADS = 12
HEAD_DIM = 64
PATCH_S = 197
PATCH_L = 577
TEXT_LEN = 40
ITEMS_S = 7
ITEMS_L = 2


NORM_EPS = 1e-05
MASKED = -1000000000.0


def layer_norm(values, gain_row, shift_row):
    row_mean = jnp.mean(values, axis=-1, keepdims=True)
    centred = values - row_mean
    variance = jnp.mean(centred * centred, axis=-1, keepdims=True)
    return centred * lax.rsqrt(variance + NORM_EPS) * gain_row + shift_row


def gelu_exact(values):
    return jax.nn.gelu(values, approximate=False)


def layout(group_type, positions, row_count):
    patch_len = jnp.where(group_type == 0, PATCH_S, PATCH_L).astype(jnp.int32)
    members = jnp.where(group_type == 0, ITEMS_S, ITEMS_L).astype(jnp.int32)
    is_patch = positions < 3 * row_count
    patch_item = positions // patch_len
    text_item = jnp.maximum(positions - 3 * row_count, 0) // TEXT_LEN
    member = jnp.where(is_patch, patch_item, text_item)
    member = jnp.where(member < members, member, -1)
    modality = jnp.where(member < 0, 2, jnp.where(is_patch, 0, 1)).astype(jnp.int32)
    return (member, modality)


def product(first_op, second_op):
    return jnp.dot(first_op, second_op, preferred_element_type=jnp.float32)


def product_lead(first_op, second_op):
    return lax.dot_general(
        first_op, second_op, (((0,), (0,)), ((), ())), preferred_element_type=jnp.float32
    )


def product_trail(first_op, second_op):
    return lax.dot_general(
        first_op, second_op, (((1,), (1,)), ((), ())), preferred_element_type=jnp.float32
    )


def halves(length):
    return ((0, length // 2), (length // 2, length // 2))


def divided(length, unit, *shares):
    found, begin = [], 0
    for share in shares:
        found.append((begin, share * unit))
        begin += share * unit
    assert begin == length
    return found


def gather_chunks(share, width, ff_share, ff):
    rows = (0, share)
    near_cols = divided(3 * width, 128, 9, 9)
    out_cols = divided(width, 128, 3, 3)
    up_cols = divided(ff, 128, 8, 8, 8)
    down_rows = divided(ff_share, 16, 2, 2, 2)
    chunks = [
        [((0, None), (0, THIN_ROWS), (0, 128), 0, False)]
        + [((1, None), rows, cols, order, False) for order, cols in enumerate(near_cols)],
        [((2, None), rows, cols, order, False) for order, cols in enumerate(out_cols)],
    ]
    def up_chunk(e, parts):
        return [((3, e), rows, cols, order, e == 1) for order, cols in enumerate(parts) if cols[1]]

    def down_chunk(e, parts):
        return [((4, e), band, (0, width), order, e == 1) for order, band in enumerate(parts)]

    chunks += [up_chunk(1, up_cols), down_chunk(1, down_rows), down_chunk(0, down_rows)]
    unit, begin = 128, 0
    for shares in ((4, 4, 4), (3, 2, 3), (1, 2, 1)):
        parts = []
        for blocks in shares:
            parts.append((begin * unit, blocks * unit))
            begin += blocks
        chunks.append(up_chunk(0, parts))
    return chunks


def scatter_chunks(share, width, ff_share, ff):
    rows = (0, share)
    near_cols = divided(3 * width, 128, 7, 7, 4)
    out_cols = divided(width, 128, 2, 3, 1)
    up_cols = divided(ff, 128, 6, 10, 8)
    down_rows = divided(ff_share, 16, 2, 2, 2)
    chunks = [[(2, 0, rows, cols, order) for order, cols in enumerate(out_cols)]]
    for e in (1, 0):
        chunks.append([(0, e, rows, cols, order) for order, cols in enumerate(up_cols)])
        chunks.append(
            [(1, e, band, (0, width), order) for order, band in enumerate(down_rows)]
        )
    chunks += [[], []]
    chunks.append(
        [(3, 0, rows, cols, order) for order, cols in enumerate(near_cols)]
    )
    chunks.append([(4, 0, (0, THIN_ROWS), (0, 128), 0)])
    cuts = (
        (0, up_cols[2][0]),
        (down_rows[2][0], 0),
        (0, out_cols[2][0]),
        (0, near_cols[2][0]),
        (0, 0),
    )
    return chunks, cuts


TQ, TK = 256, 128
PAIR = 2 * HEAD_DIM


def trail(first_op, second_op):
    return lax.dot_general(
        first_op, second_op, (((1,), (1,)), ((), ())), preferred_element_type=jnp.float32
    )


def span(kind, start, length, image_rows):
    patch_len, members = ((PATCH_S, ITEMS_S), (PATCH_L, ITEMS_L))[kind]
    image = start < image_rows
    low = jnp.where(image, lax.div(start, patch_len), lax.div(start - image_rows, TEXT_LEN))
    high = jnp.where(
        image,
        lax.div(start + length - 1, patch_len),
        lax.div(start + length - 1 - image_rows, TEXT_LEN),
    )
    return low, high, members


def meets(first, second, image_rows, loose):
    found = False
    for kind in range(2):
        low_a, high_a, members = span(kind, *first, image_rows)
        low_b, high_b, _ = span(kind, *second, image_rows)
        low = jnp.maximum(low_a, low_b)
        high = jnp.minimum(jnp.minimum(high_a, high_b), members - 1)
        found = jnp.logical_or(found, low <= high)
        if loose:
            both = jnp.logical_and(high_a >= members, high_b >= members)
            found = jnp.logical_or(found, both)
    return found


def member_of(kind, position, image_rows):
    patch_len = PATCH_S + kind * float(PATCH_L - PATCH_S)
    members = ITEMS_S + kind * float(ITEMS_L - ITEMS_S)
    patch = jnp.floor((position + 0.5) / patch_len)
    text = jnp.floor((position - image_rows + 0.5) * (1.0 / TEXT_LEN))
    member = jnp.where(position < image_rows, patch, text)
    return jnp.where(member < members, member, -1.0)


def same_item(kind, stream, rows, qt, kt, image_rows):
    keys = lax.broadcasted_iota(jnp.int32, (TK, 1), 0) + kt * TK
    own = lax.broadcasted_iota(jnp.int32, (1, TQ), 1) + (stream * rows + qt * TQ)
    key_member = member_of(kind, keys.astype(jnp.float32), image_rows)
    return key_member == member_of(kind, own.astype(jnp.float32), image_rows)


def half_of(pair, which):
    lanes = lax.broadcasted_iota(jnp.int32, pair.shape, 1)
    return jnp.where((lanes < HEAD_DIM) == (which == 0), pair, jnp.zeros_like(pair))


def upper_of(pair, which):
    keep = pair[which * HEAD_DIM : (which + 1) * HEAD_DIM]
    parts = [keep, jnp.zeros_like(keep)]
    return jnp.concatenate(parts if which == 0 else parts[::-1], axis=0)


def scale_queries(q_ref, scaled):
    for pair in range(q_ref.shape[1] // PAIR):
        columns = slice(pair * PAIR, (pair + 1) * PAIR)
        value = (q_ref[:, columns] * jnp.bfloat16(HEAD_DIM ** (-0.5))).T
        for which in range(2):
            scaled[2 * pair + which] = upper_of(value, which)


def flip_columns(kv_ref, begin, flipped):
    width = flipped.shape[0]

    @pl.loop(0, flipped.shape[1] // TK)
    def _(kt):
        keys = pl.ds(pl.multiple_of(kt * TK, TK), TK)
        flipped[:, keys] = kv_ref[keys, begin : begin + width].T


def attend_part(qt, begin, end, kind_ref, stream, kv_ref, values_t, scaled, mixed_ref, mixed_t, log_total, top, total):
    width, everyone = values_t.shape
    rows = mixed_ref.shape[0]
    heads = width // HEAD_DIM
    image_rows = everyone - rows
    here = slice(qt * TQ, (qt + 1) * TQ)
    if begin == 0:
        top[...] = jnp.full(top.shape, -1e30, jnp.float32)
        total[...] = jnp.zeros(total.shape, jnp.float32)
        mixed_t[:, here] = jnp.zeros((width, TQ), jnp.float32)

    @pl.loop(begin, end)
    def _(kt):
        needed = meets((stream * rows + qt * TQ, TQ), (kt * TK, TK), image_rows, True)

        @pl.when(needed)
        def _():
            keys = pl.ds(pl.multiple_of(kt * TK, TK), TK)
            allowed = same_item(kind_ref[0:1, 0:1], stream, rows, qt, kt, image_rows)
            scores, parts, fades = [], [], []
            for head in range(heads):
                pair = slice(head // 2 * PAIR, (head // 2 + 1) * PAIR)
                raw = jnp.dot(
                    kv_ref[keys, pair], scaled[head, :, here], preferred_element_type=jnp.float32
                )
                scores.append(jnp.where(allowed, raw, MASKED))
            for head, score in enumerate(scores):
                line = slice(head, head + 1)
                old = top[line]
                new = jnp.maximum(old, jnp.max(score, axis=0, keepdims=True))
                top[line] = new
                fade = jnp.exp(old - new)
                part = jnp.exp(score - new)
                total[line] = total[line] * fade + jnp.sum(part, axis=0, keepdims=True)
                parts.append(part.astype(jnp.bfloat16))
                fades.append(fade)
            for head in range(heads):
                own = slice(head * HEAD_DIM, (head + 1) * HEAD_DIM)
                mixed_t[own, here] = mixed_t[own, here] * fades[head] + jnp.dot(
                    values_t[own, keys], parts[head], preferred_element_type=jnp.float32
                )

    if end == everyone // TK:
        for head in range(heads):
            own = slice(head * HEAD_DIM, (head + 1) * HEAD_DIM)
            mixed_t[own, here] = mixed_t[own, here] / total[head : head + 1]
        log_total[:, here] = top[...] + jnp.log(total[...])
        mixed_ref[here, :] = mixed_t[:, here].T.astype(jnp.bfloat16)


def attend_kernel(kind, place_ref, q_ref, kv_ref, mixed_ref, mixed_t, log_total, values_t, scaled, top, total):
    scale_queries(q_ref, scaled)
    flip_columns(kv_ref, q_ref.shape[1], values_t)
    for qt in range(q_ref.shape[0] // TQ):
        attend_part(
            qt, 0, kv_ref.shape[0] // TK, kind, place_ref[0], kv_ref, values_t, scaled, mixed_ref,
            mixed_t, log_total, top, total,
        )


def attend(kind, place_at, queries, kv):
    rows, width = queries.shape
    heads = width // HEAD_DIM
    inside = pl.BlockSpec(memory_space=pltpu.VMEM)
    lines = -(-heads // 8) * 8
    return pl.pallas_call(
        attend_kernel,
        out_shape=(
            jax.ShapeDtypeStruct((rows, width), jnp.bfloat16),
            jax.ShapeDtypeStruct((width, rows), jnp.float32),
            jax.ShapeDtypeStruct((lines, rows), jnp.float32),
        ),
        in_specs=[inside, pl.BlockSpec(memory_space=pltpu.SMEM)] + [inside] * 2,
        out_specs=(inside,) * 3,
        scratch_shapes=[
            pltpu.VMEM((width, kv.shape[0]), jnp.bfloat16),
            pltpu.VMEM((heads, PAIR, rows), jnp.bfloat16),
            pltpu.VMEM((lines, TQ), jnp.float32),
            pltpu.VMEM((lines, TQ), jnp.float32),
        ],
        compiler_params=pltpu.CompilerParams(vmem_limit_bytes=56 << 20),
    )(kind, place_at, queries, kv)


def back_group(
    group, kind, stream, log_total, keys_ref, values_ref, q_ref, g_ref, mixed_t, dq_ref, between,
    keys_t, scaled, grads, scaled_t, grads_t, dq_t, centre, dk, dv,
):
    everyone, width = keys_ref.shape
    rows = q_ref.shape[0]
    heads = width // HEAD_DIM
    image_rows = everyone - rows
    for pair in range(heads // 2):
        columns = slice(pair * PAIR, (pair + 1) * PAIR)
        value = q_ref[:, columns] * jnp.bfloat16(HEAD_DIM ** (-0.5))
        grad = g_ref[:, columns]
        value_t, grad_t = value.T, grad.T
        product = mixed_t[columns, :] * grad_t.astype(jnp.float32)
        for which in range(2):
            head = 2 * pair + which
            scaled[head] = half_of(value, which)
            grads[head] = half_of(grad, which)
            scaled_t[head] = upper_of(value_t, which)
            grads_t[head] = upper_of(grad_t, which)
            centre[head : head + 1] = jnp.sum(
                product[which * HEAD_DIM : (which + 1) * HEAD_DIM], axis=0, keepdims=True
            )
    flip_columns(keys_ref, 0, keys_t)

    @pl.loop(0, everyone // TK)
    def _(kt):
        keys = pl.ds(pl.multiple_of(kt * TK, TK), TK)
        dk[keys, :] = jnp.zeros((TK, width), jnp.float32)
        dv[keys, :] = jnp.zeros((TK, width), jnp.float32)

    for qt in range(rows // TQ):
        here = slice(qt * TQ, (qt + 1) * TQ)
        if qt:
            between()
        dq_t[...] = jnp.zeros(dq_t.shape, jnp.float32)

        @pl.loop(0, everyone // TK)
        def _(kt, qt=qt, here=here):
            needed = meets((stream * rows + qt * TQ, TQ), (kt * TK, TK), image_rows, False)

            @pl.when(needed)
            def _():
                keys = pl.ds(pl.multiple_of(kt * TK, TK), TK)
                allowed = same_item(kind[0:1, 0:1], stream, rows, qt, kt, image_rows)
                scores, prob_grads, probs_low, score_low = [], [], [], []
                for head in range(heads):
                    pair = slice(head // 2 * PAIR, (head // 2 + 1) * PAIR)
                    scores.append(
                        jnp.dot(
                            keys_ref[keys, pair],
                            scaled_t[head, :, here],
                            preferred_element_type=jnp.float32,
                        )
                    )
                    prob_grads.append(
                        jnp.dot(
                            values_ref[keys, pair],
                            grads_t[head, :, here],
                            preferred_element_type=jnp.float32,
                        )
                    )
                for head in range(heads):
                    line = slice(group * heads + head, group * heads + head + 1)
                    shifted = scores[head] - log_total[line, here]
                    probs = jnp.exp(jnp.where(allowed, shifted, MASKED))
                    probs_low.append(probs.astype(jnp.bfloat16))
                    inner = prob_grads[head] - centre[head : head + 1, here]
                    score_low.append((probs * inner).astype(jnp.bfloat16))
                for head in range(heads):
                    own = slice(head * HEAD_DIM, (head + 1) * HEAD_DIM)
                    dq_t[own, :] += jnp.dot(
                        keys_t[own, keys], score_low[head], preferred_element_type=jnp.float32
                    )
                for head in range(0, heads, 2):
                    columns = slice(head * HEAD_DIM, head * HEAD_DIM + PAIR)
                    for terms, left, right in ((dk, score_low, scaled), (dv, probs_low, grads)):
                        terms[keys, columns] += jnp.dot(
                            left[head], right[head, here, :], preferred_element_type=jnp.float32
                        ) + jnp.dot(
                            left[head + 1],
                            right[head + 1, here, :],
                            preferred_element_type=jnp.float32,
                        )

        dq_ref[here, :] = (dq_t[...].T * HEAD_DIM ** (-0.5)).astype(jnp.bfloat16)


def attend_back_kernel(
    kind, place_ref, q_ref, kv_ref, g_ref, mixed_t, log_total, dq_ref, dkv_ref, *work
):
    width = q_ref.shape[1]
    back_group(
        0, kind, place_ref[0], log_total, kv_ref.at[:, pl.ds(0, width)],
        kv_ref.at[:, pl.ds(width, width)], q_ref, g_ref, mixed_t, dq_ref, lambda: None,
        *work,
    )
    dk, dv = work[-2:]

    @pl.loop(0, kv_ref.shape[0] // TK)
    def _(kt):
        keys = pl.ds(pl.multiple_of(kt * TK, TK), TK)
        dkv_ref[keys, :width] = dk[keys, :].astype(jnp.bfloat16)
        dkv_ref[keys, width:] = dv[keys, :].astype(jnp.bfloat16)


def attend_back(kind, place_at, queries, kv, mixed_grad, mixed_t, log_total):
    rows, width = queries.shape
    heads = width // HEAD_DIM
    inside = pl.BlockSpec(memory_space=pltpu.VMEM)
    lines = -(-heads // 8) * 8
    everyone = kv.shape[0]
    return pl.pallas_call(
        attend_back_kernel,
        out_shape=(
            jax.ShapeDtypeStruct((rows, width), jnp.bfloat16),
            jax.ShapeDtypeStruct((everyone, 2 * width), jnp.bfloat16),
        ),
        in_specs=[inside, pl.BlockSpec(memory_space=pltpu.SMEM)] + [inside] * 5,
        out_specs=(inside,) * 2,
        scratch_shapes=[
            pltpu.VMEM((width, everyone), jnp.bfloat16),
            pltpu.VMEM((heads, rows, PAIR), jnp.bfloat16),
            pltpu.VMEM((heads, rows, PAIR), jnp.bfloat16),
            pltpu.VMEM((heads, PAIR, rows), jnp.bfloat16),
            pltpu.VMEM((heads, PAIR, rows), jnp.bfloat16),
            pltpu.VMEM((width, TQ), jnp.float32),
            pltpu.VMEM((lines, rows), jnp.float32),
            pltpu.VMEM((everyone, width), jnp.float32),
            pltpu.VMEM((everyone, width), jnp.float32),
        ],
        compiler_params=pltpu.CompilerParams(vmem_limit_bytes=58 << 20),
    )(kind, place_at, queries, kv, mixed_grad, mixed_t, log_total)

def feed_kernel(
    pick, place_ref, kind, vectors, up_shift, tokens, mixed, out_weight, cotangent, up, down,
    output, residual_grad, grad_out, mixed_grad, grad_up, grad_down, small, up_shift_sum,
    residual, normed, normed_t, grad, branch, back,
):
    step = pl.program_id(0)
    rows, width = tokens.shape
    image_rows = (lax.axis_size("stream") - 1) * rows
    tall = 128

    def blocks(act):
        @pl.loop(0, rows // tall)
        def _(j):
            act(pl.ds(pl.multiple_of(j * tall, tall), tall))

    def unit_of(value):
        centred = value - jnp.mean(value, axis=-1, keepdims=True)
        scale = lax.rsqrt(jnp.mean(centred * centred, axis=-1, keepdims=True) + NORM_EPS)
        return centred * scale, scale

    def live(j_start):
        position = lax.broadcasted_iota(jnp.int32, (tall, 1), 0) + (place_ref[0] * rows + j_start)
        return member_of(kind[0:1, 0:1], position.astype(jnp.float32), image_rows) >= 0.0

    @pl.when(step == 0)
    def _():
        @pl.loop(0, rows // tall)
        def _(j):
            block = pl.ds(pl.multiple_of(j * tall, tall), tall)
            value = (
                tokens[block, :].astype(jnp.float32)
                + jnp.dot(mixed[block, :], out_weight[...], preferred_element_type=jnp.float32)
                + vectors[4:5, :]
            )
            residual[block, :] = value
            unit, _ = unit_of(value)
            normed[block, :] = (unit * vectors[5:6, :] + vectors[6:7, :]).astype(jnp.bfloat16)
            given = cotangent[block, :]
            grad[block, :] = jnp.where(live(j * tall), given, jnp.zeros_like(given))

        normed_t[...] = normed[...].T
        branch[...] = jnp.zeros(branch.shape, jnp.float32)
        back[...] = jnp.zeros(back.shape, jnp.float32)

    before = (
        jnp.dot(normed[...], up[0], preferred_element_type=jnp.float32) + up_shift[0].astype(jnp.float32)
    )
    hidden_grad = product_trail(grad[...], down[0])
    half = 0.5 + 0.5 * lax.erf(before * 0.5**0.5)
    hidden = (before * half).astype(jnp.bfloat16)
    slope = half + before * (jnp.exp(-0.5 * before * before) * 0.3989422804014327)
    before_grad = hidden_grad * slope
    low_grad = before_grad.astype(jnp.bfloat16)
    up_shift_sum[...] = jnp.broadcast_to(
        jnp.sum(low_grad.astype(jnp.float32), axis=0, keepdims=True), up_shift_sum.shape
    )
    branch[...] += jnp.dot(hidden, down[0], preferred_element_type=jnp.float32)
    back[...] += product_trail(low_grad, up[0])
    grad_up[...] = jnp.dot(normed_t[...], low_grad, preferred_element_type=jnp.float32).astype(
        jnp.bfloat16
    )
    grad_down[...] = jnp.dot(hidden.T, grad[...], preferred_element_type=jnp.float32).astype(
        jnp.bfloat16
    )

    @pl.when(step == pl.num_programs(0) - 1)
    def _():
        down_shift = jnp.where(pick[0] == 0, vectors[9:10, :], vectors[10:11, :])

        def fold(value):
            return jnp.sum(value.reshape(-1, 8, width), axis=0)

        def finish(j, carry):
            block = pl.ds(pl.multiple_of(j * tall, tall), tall)
            value = residual[block, :]
            kept = live(j * tall)
            output[block, :] = (
                value + jnp.where(kept, branch[block, :] + down_shift, 0.0)
            ).astype(jnp.bfloat16)
            unit, scale = unit_of(value)
            given = back[block, :]
            lifted = given * vectors[5:6, :]
            inner = jnp.mean(lifted * unit, axis=-1, keepdims=True)
            own = grad[block, :].astype(jnp.float32)
            total = own + scale * (
                lifted - jnp.mean(lifted, axis=-1, keepdims=True) - unit * inner
            )
            residual_grad[block, :] = total
            total_low = total.astype(jnp.bfloat16)
            normed[block, :] = total_low
            mixed_grad[block, :] = product_trail(total_low, out_weight[...]).astype(jnp.bfloat16)
            terms = (total_low.astype(jnp.float32), given * unit, given, own)
            return tuple(held + fold(term) for held, term in zip(carry, terms))

        zero = jnp.zeros((8, width), jnp.float32)
        sums = lax.fori_loop(0, rows // tall, finish, (zero,) * 4)
        lines = [jnp.sum(value, axis=0, keepdims=True) for value in sums]
        small[...] = jnp.concatenate(lines + [jnp.zeros((4, width), jnp.float32)], axis=0)
        grad_out[...] = jnp.dot(
            mixed[...].T, normed[...], preferred_element_type=jnp.float32
        ).astype(jnp.bfloat16)


def feed(pick, place_at, kind, vectors, up_shift, tokens, mixed, out_weight, cotangent, up, down):
    rows, width = tokens.shape
    ff = up.shape[2]
    band = 512
    low, wide = jnp.bfloat16, jnp.float32

    def whole(array):
        return pl.BlockSpec(array.shape, lambda i, pick, place_at: (0,) * array.ndim)

    fixed = [
        jax.ShapeDtypeStruct((rows, width), low),
        jax.ShapeDtypeStruct((rows, width), wide),
        jax.ShapeDtypeStruct((width, width), low),
        jax.ShapeDtypeStruct((rows, width), low),
    ]
    last = jax.ShapeDtypeStruct((8, width), wide)
    return pl.pallas_call(
        feed_kernel,
        out_shape=fixed
        + [
            jax.ShapeDtypeStruct((width, ff), low),
            jax.ShapeDtypeStruct((ff, width), low),
            last,
            jax.ShapeDtypeStruct((8, ff), wide),
        ],
        grid_spec=pltpu.PrefetchScalarGridSpec(
            num_scalar_prefetch=2,
            grid=(ff // band,),
            in_specs=[
                whole(kind),
                whole(vectors),
                pl.BlockSpec((1, 1, band), lambda i, pick, place_at: (pick[0], 0, i)),
                whole(tokens),
                whole(mixed),
                whole(out_weight),
                whole(cotangent),
                pl.BlockSpec((1, width, band), lambda i, pick, place_at: (pick[0], 0, i)),
                pl.BlockSpec((1, band, width), lambda i, pick, place_at: (pick[0], i, 0)),
            ],
            out_specs=[whole(array) for array in fixed]
            + [
                pl.BlockSpec((width, band), lambda i, pick, place_at: (0, i)),
                pl.BlockSpec((band, width), lambda i, pick, place_at: (i, 0)),
                whole(last),
                pl.BlockSpec((8, band), lambda i, pick, place_at: (0, i)),
            ],
            scratch_shapes=[
                pltpu.VMEM((rows, width), wide),
                pltpu.VMEM((rows, width), low),
                pltpu.VMEM((width, rows), low),
                pltpu.VMEM((rows, width), low),
                pltpu.VMEM((rows, width), wide),
                pltpu.VMEM((rows, width), wide),
            ],
        ),
        compiler_params=pltpu.CompilerParams(vmem_limit_bytes=62 << 20),
    )(pick, place_at, kind, vectors, up_shift, tokens, mixed, out_weight, cotangent, up, down)


MESH = pl.DeviceIdType.MESH
GATHER_ORDERS = (("z", "f", "x", "y"), ("z", "f", "y", "x"), ("y", "x", "z", "f"))
SCATTER_ORDERS = (("y", "x", "a", "z"), ("x", "y", "a", "z"), ("a", "z", "x", "y"))
STEPS = 5
EVERY = slice(None)
THIN_ROWS = 16


def coords():
    items, stream = lax.axis_index("items"), lax.axis_index("stream")
    return dict(z=items // 2, x=items % 2, y=stream // 2, c=stream % 2)


def place(at):
    return (at["z"] * 2 + at["x"], at["y"] * 2 + at["c"])


def moved(at, dim, by, depth):
    return {**at, dim: lax.rem(at[dim] + by, depth if dim == "z" else 2)}


def greet(at, depth):
    peers = [moved(at, "z", k, depth) for k in range(1, depth)]
    peers += [moved(at, d, 1, depth) for d in "xyc"]
    barrier = pltpu.get_barrier_semaphore()
    for peer in peers:
        pl.semaphore_signal(barrier, inc=1, device_id=place(peer), device_id_type=MESH)
    pl.semaphore_wait(barrier, len(peers))


def guard(cond, act):
    if cond is None:
        act()
    else:
        pl.when(cond)(act)


def remote(src, dst, sems, index, device):
    return pltpu.make_async_remote_copy(
        src_ref=src,
        dst_ref=dst,
        send_sem=sems[0].at[index],
        recv_sem=sems[1].at[index],
        device_id=place(device),
        device_id_type=MESH,
    )


def both_of(first, second):
    if first is None or second is None:
        return second if first is None else first
    return jnp.logical_and(first, second)


class Pipeline:
    def __init__(self, chunks, ahead, start, wait):
        self.chunks, self.ahead, self.start, self.wait = chunks, ahead, start, wait
        self.ticks = 0
        for chunk in chunks[:ahead]:
            start(chunk, 0)

    def tick(self, times=1):
        count = len(self.chunks)
        for t in range(self.ticks, min(self.ticks + times, count + STEPS - 1)):
            if t + self.ahead < count:
                self.start(self.chunks[t + self.ahead], 0)
            for step in range(STEPS):
                if 0 <= t - step < count:
                    self.wait(self.chunks[t - step], step)
                    if step < STEPS - 1:
                        self.start(self.chunks[t - step], step + 1)
        self.ticks += times


def spots_of(depth):
    return [(a, b, c, d) for a in range(depth) for b in range(2) for c in range(2) for d in range(2)]


def columns_over(share, width):
    column = lax.broadcasted_iota(jnp.int32, (1, width), 1).astype(jnp.float32)
    owner = jnp.floor((column + 0.5) * (1.0 / share))
    return owner, column - owner * share


def spread(thin, share, width):
    owner, lane = columns_over(share, width)
    picks = lax.broadcasted_iota(jnp.int32, (128, width), 0).astype(jnp.float32) == lane
    wide = jnp.dot(thin, picks.astype(jnp.bfloat16), preferred_element_type=jnp.float32)
    total = jnp.zeros((THIN_ROWS, width), jnp.float32)
    for device in range(thin.shape[0] // THIN_ROWS):
        part = wide[device * THIN_ROWS : (device + 1) * THIN_ROWS]
        total = total + jnp.where(owner == device, part, 0.0)
    return total


def dealt(rows, share, devices):
    width = rows.shape[1]
    owner, lane = columns_over(share, width)
    picks = lax.broadcasted_iota(jnp.int32, (128, width), 0).astype(jnp.float32) == lane
    tall = jnp.concatenate(
        [jnp.where(owner == device, rows, 0.0) for device in range(devices)], axis=0
    )
    return lax.dot_general(
        tall,
        picks.astype(jnp.float32),
        (((1,), (1,)), ((), ())),
        precision=lax.Precision.HIGHEST,
        preferred_element_type=jnp.float32,
    )


def gather_kernel(depth, chunks, entries, *refs):
    it = iter(refs)
    take = lambda count: [next(it) for _ in range(count)]
    ins = take(5)
    tokens, kind = take(2)
    thin_out, out_all, up_all, down_all = take(4)
    weight_out, normed_out, queries_out, vectors, kv_out, mixed, mixed_t_out, log_total = take(8)
    (far_normed_out,) = take(1)
    thin_all, qkv_all, kv, values_t, scaled, top, total = take(7)
    qkv_weight, normed, queries, mixed_t, far_tokens, far_normed = take(6)
    local_sem = next(it)
    sems, kv_sems = take(2), take(2)
    keep_sem = next(it)
    outs = (thin_all, qkv_all, out_all, up_all, down_all)
    rows, width = tokens.shape
    devices = depth * 8
    share = width // devices
    at = coords()
    mine = (at["z"], at["x"], at["y"], at["c"])
    slot = at["y"] * 2 + at["c"]

    def source(entry):
        k, e = entry
        return ins[k] if e is None else ins[k].at[e]

    def target(entry):
        k, e = entry
        return outs[k] if e is None else outs[k].at[e]

    local = [
        pltpu.make_async_copy(source(entry), target(entry).at[mine], local_sem.at[j])
        for j, entry in enumerate(entries)
    ]
    for copy in local:
        copy.start()
    greet(at, depth)
    for copy in local:
        copy.wait()
    lower, upper = at["y"] == 0, at["y"] == 1
    number = {piece: j for j, piece in enumerate(piece for chunk in chunks for piece in chunk)}

    z = at["z"]

    def stage(piece, step):
        entry, band, cols, order, text = piece
        dims = GATHER_ORDERS[order] + ("c",)
        dim = dims[step]
        box = (pl.ds(*band), pl.ds(*cols))
        live = upper if text and "y" in dims[:step] else None

        def held(level):
            spot = {d: EVERY if d in dims[:step] else pl.ds(at[d], 1) for d in "zxyc"}
            if level is not None:
                spot["z"] = pl.ds(level, 1)
            return target(entry).at[tuple(spot[d] for d in "zxyc") + box]

        if dim == "f":
            up_view, down_view = held(0), held(depth - 1)
            up = remote(up_view, up_view, sems, (number[piece], depth + 2), {**at, "z": z + 1})
            down = remote(down_view, down_view, sems, (number[piece], depth + 2), {**at, "z": z - 1})
            return [
                (up, both_of(live, z == depth - 2), both_of(live, z == depth - 1)),
                (down, both_of(live, z == 1), both_of(live, z == 0)),
            ]
        view = held(None)
        if dim == "z":
            found = []
            for k in range(1, depth):
                to, source_level = lax.rem(z + k, depth), lax.rem(z + depth - k, depth)
                copy = remote(view, view, sems, (number[piece], k - 1), {**at, "z": to})
                sends = both_of(live, jnp.abs(to - z) != depth - 1)
                found.append((copy, sends, both_of(live, jnp.abs(source_level - z) != depth - 1)))
            return found
        sem = {"x": depth - 1, "y": depth, "c": depth + 1}[dim]
        copy = remote(view, view, sems, (number[piece], sem), moved(at, dim, 1, depth))
        if text and dim == "y":
            return [(copy, lower, upper)]
        return [(copy, live, live)]

    def each(chunk, step, which, call):
        for piece in chunk:
            for found in stage(piece, step):
                guard(found[which], functools.partial(call, found[0]))

    beside, across = moved(at, "c", 1, depth), moved(at, "y", 1, depth)
    other = across["y"] * 2 + across["c"]
    own_slot = pl.ds(pl.multiple_of(slot * rows, rows), rows)
    other_slot = pl.ds(pl.multiple_of(other * rows, rows), rows)
    to_across = remote(tokens, far_tokens, kv_sems, 0, across)
    to_beside = remote(kv.at[own_slot], kv.at[own_slot], kv_sems, 1, beside)
    onward = remote(kv.at[other_slot], kv.at[other_slot], kv_sems, 2, beside)
    to_across.start()
    keep_kv = pltpu.make_async_copy(kv, kv_out, keep_sem.at[0])
    keep_mixed = pltpu.make_async_copy(mixed_t, mixed_t_out, keep_sem.at[1])
    keep_early = [
        pltpu.make_async_copy(src, dst, keep_sem.at[2 + j])
        for j, (src, dst) in enumerate(
            [
                (thin_all, thin_out),
                (qkv_weight, weight_out),
                (normed, normed_out),
                (far_normed, far_normed_out),
                (queries, queries_out),
            ]
        )
    ]

    def project():
        spots = spots_of(depth)
        for j, spot in enumerate(spots):
            qkv_weight[j * share : (j + 1) * share, :] = qkv_all[spot]
        thin = jnp.concatenate([thin_all[spot] for spot in spots], axis=0)
        vectors[...] = spread(thin, share, width)

        to_across.wait_recv()
        for given, made in ((tokens, normed), (far_tokens, far_normed)):

            @pl.loop(0, rows // 128)
            def _(j, given=given, made=made):
                block = pl.ds(pl.multiple_of(j * 128, 128), 128)
                value = given[block, :].astype(jnp.float32)
                centred = value - jnp.mean(value, axis=-1, keepdims=True)
                scale = lax.rsqrt(jnp.mean(centred * centred, axis=-1, keepdims=True) + NORM_EPS)
                made[block, :] = (centred * scale * vectors[0:1, :] + vectors[1:2, :]).astype(
                    jnp.bfloat16
                )

        step = width // 2
        for part in (1, 2, 0):

            @pl.loop(0, 2)
            def _(j, part=part):
                cols = pl.ds(pl.multiple_of(j * step, 128), step)
                weight_cols = qkv_weight[:, pl.ds(pl.multiple_of(part * width + j * step, 128), step)]
                value = jnp.dot(normed[...], weight_cols, preferred_element_type=jnp.float32)
                if part == 0:
                    queries[:, cols] = (value + vectors[2:3, cols]).astype(jnp.bfloat16)
                    return
                far_value = jnp.dot(far_normed[...], weight_cols, preferred_element_type=jnp.float32)
                to = pl.ds(pl.multiple_of((part - 1) * width + j * step, 128), step)
                shift = vectors[3:4, cols] if part == 2 else 0.0
                kv[own_slot, to] = (value + shift).astype(jnp.bfloat16)
                kv[other_slot, to] = (far_value + shift).astype(jnp.bfloat16)

            if part == 2:
                to_beside.start()
                onward.start()
        for copy in keep_early:
            copy.start()
        scale_queries(queries, scaled)

    def attend_first():
        to_beside.wait_recv()
        onward.wait_recv()
        keep_kv.start()
        flip_columns(kv, width, values_t)

    parts = (kind, slot, kv, values_t, scaled, mixed, mixed_t, log_total, top, total)

    def attention(qt, begin, end):
        def act():
            if qt == 0 and begin == 0:
                attend_first()
            attend_part(qt, begin, end, *parts)

        return act

    everyone = kv.shape[0] // TK
    flow = Pipeline(
        chunks,
        2,
        lambda chunk, step: each(chunk, step, 1, lambda copy: copy.start()),
        lambda chunk, step: each(chunk, step, 2, lambda copy: copy.wait_recv()),
    )
    flow.tick(5)
    project()
    flow.tick()
    attention(0, 0, everyone // 2)()
    flow.tick()
    attention(0, everyone // 2, everyone)()
    flow.tick()
    attention(1, 0, everyone // 2)()
    flow.tick()
    attention(1, everyone // 2, everyone)()
    flow.tick(STEPS + len(chunks))
    for copy in (to_beside, to_across, onward):
        copy.wait_send()
    keep_mixed.start()
    for copy in keep_early + [keep_kv, keep_mixed]:
        copy.wait()
    for chunk in chunks:
        for step in range(STEPS):
            each(chunk, step, 1, lambda copy: copy.wait_send())


def gather_all(thin, w_qkv, w_out, w_up, w_down, tokens, kind, depth):
    rows, width = tokens.shape
    share, ff_share, ff = w_qkv.shape[0], w_down.shape[1], w_up.shape[2]
    entries = [(0, None), (1, None), (2, None), (3, 0), (3, 1), (4, 0), (4, 1)]
    chunks = gather_chunks(share, width, ff_share, ff)
    n_pieces = sum(len(chunk) for chunk in chunks)
    anywhere = pl.BlockSpec(memory_space=pl.ANY)
    inside = pl.BlockSpec(memory_space=pltpu.VMEM)
    low = jnp.bfloat16
    box = (depth, 2, 2, 2)
    heads, lines = width // HEAD_DIM, -(-(width // HEAD_DIM) // 8) * 8
    return pl.pallas_call(
        functools.partial(gather_kernel, depth, chunks, entries),
        out_shape=[
            jax.ShapeDtypeStruct(box + thin.shape, low),
            jax.ShapeDtypeStruct(box + (share, width), low),
            jax.ShapeDtypeStruct((2,) + box + (share, ff), low),
            jax.ShapeDtypeStruct((2,) + box + (ff_share, width), low),
            jax.ShapeDtypeStruct((width, 3 * width), low),
            jax.ShapeDtypeStruct((rows, width), low),
            jax.ShapeDtypeStruct((rows, width), low),
            jax.ShapeDtypeStruct((THIN_ROWS, width), jnp.float32),
            jax.ShapeDtypeStruct((4 * rows, 2 * width), low),
            jax.ShapeDtypeStruct((rows, width), low),
            jax.ShapeDtypeStruct((width, rows), jnp.float32),
            jax.ShapeDtypeStruct((lines, rows), jnp.float32),
            jax.ShapeDtypeStruct((rows, width), low),
        ],
        in_specs=[inside] * 7,
        out_specs=[anywhere] * 7 + [inside, anywhere, inside, anywhere, inside, anywhere],
        scratch_shapes=[
            pltpu.VMEM(box + thin.shape, low),
            pltpu.VMEM(box + (share, 3 * width), low),
            pltpu.VMEM((4 * rows, 2 * width), low),
            pltpu.VMEM((width, 4 * rows), low),
            pltpu.VMEM((heads, PAIR, rows), low),
            pltpu.VMEM((lines, TQ), jnp.float32),
            pltpu.VMEM((lines, TQ), jnp.float32),
            pltpu.VMEM((width, 3 * width), low),
            pltpu.VMEM((rows, width), low),
            pltpu.VMEM((rows, width), low),
            pltpu.VMEM((width, rows), jnp.float32),
            pltpu.VMEM((rows, width), low),
            pltpu.VMEM((rows, width), low),
            pltpu.SemaphoreType.DMA((len(entries),)),
            pltpu.SemaphoreType.DMA((n_pieces, depth + 3)),
            pltpu.SemaphoreType.DMA((n_pieces, depth + 3)),
            pltpu.SemaphoreType.DMA((3,)),
            pltpu.SemaphoreType.DMA((3,)),
            pltpu.SemaphoreType.DMA((7,)),
        ],
        compiler_params=pltpu.CompilerParams(
            collective_id=1, has_side_effects=True, vmem_limit_bytes=62 << 20
        ),
    )(thin, w_qkv, w_out, w_up, w_down, tokens, kind)


def rows_of_kind(kind, rows):
    patch_len, members = ((PATCH_S, ITEMS_S), (PATCH_L, ITEMS_L))[kind]
    return float(min(patch_len * members, 3 * rows)), float(min(TEXT_LEN * members, rows))


def scatter_kernel(depth, kinds, chunks, cuts, *refs):
    n, n_far = len(kinds), 3
    it = iter(refs)
    take = lambda count: [next(it) for _ in range(count)]
    far = take(n_far)
    small, up_shift_sum, vectors, kind, log_total = take(5)
    queries, kv, mixed_grad, mixed_t, normed, far_normed, weight, tokens, residual_grad = take(9)
    outs = take(n)
    token_grad, kv_away = take(2)
    acc, first, second, last = take(n), take(n), take(n), take(n)
    relay, z_relay, z_first, z_second, z_last = (take(n) for _ in range(5))
    own_half = take(n_far)
    qkv_terms, thin_terms, kv_sum, far_terms, far_got, kv_mine, dq = take(7)
    sems = take(2)
    local_sem, away_sem = take(2)
    kv_sems = take(2)
    rows, width = residual_grad.shape
    devices = depth * 8
    share = width // devices
    at = coords()
    z, x, y, c = (at[d] for d in "zxyc")
    ins = far + [qkv_terms, thin_terms]
    groups = devices // 4
    lane = lax.broadcasted_iota(jnp.int32, (1, width), 1)
    marks = functools.reduce(
        jnp.logical_or, [lane == group * (width // groups) for group in range(groups)]
    )
    second_kind = jnp.sum(jnp.where(marks, vectors[11:12, :], 0.0), axis=1, keepdims=True)
    counts = [
        first_count * (groups - second_kind) + second_count * second_kind
        for first_count, second_count in zip(*(rows_of_kind(kind_of, rows) for kind_of in range(2)))
    ]
    factors = [lax.rsqrt(count) for count in counts]
    local = [
        pltpu.make_async_copy(far[k].at[EVERY, EVERY, EVERY, c], own_half[k], local_sem.at[k])
        for k in range(n_far)
    ]
    for copy in local:
        copy.start()
    greet(at, depth)
    beside, across = moved(at, "c", 1, depth), moved(at, "y", 1, depth)
    kv_beside = remote(kv_away, kv_sum, kv_sems, 0, beside)
    kv_across = remote(far_terms, far_got, kv_sems, 1, across)
    lower, upper = y == 0, y == 1
    text_device = jnp.logical_and(upper, c == 1)
    image_device = jnp.logical_or(lower, c == 0)
    beside_text = jnp.logical_and(upper, c == 0)
    beside_image = jnp.logical_or(lower, c == 1)
    number = {piece: j for j, piece in enumerate(piece for chunk in chunks for piece in chunk)}

    sources = (
        (z == 0, range(2, depth)),
        (jnp.logical_and(z > 0, z < depth - 1), range(1, depth)),
        (z == depth - 1, range(1, depth - 1)),
    )

    def boxes(piece):
        k, e, band, cols, order = piece
        cut = cuts[k] if order == 2 else (0, 0)
        return (
            (pl.ds(*band), pl.ds(*cols)),
            (pl.ds(band[0] - cut[0], band[1]), pl.ds(cols[0] - cut[1], cols[1])),
        )

    def copies_of(piece, step):
        k, e, band, cols, order = piece
        box, inner = boxes(piece)
        image, text = kinds[k] and e == 0, kinds[k] and e == 1
        dims = ("c",) + SCATTER_ORDERS[order]
        dim = dims[step]
        here = acc[k].at[e]

        def make(src, dst, sem, by=1):
            return remote(src, dst, sems, (number[piece], sem), moved(at, dim, by, depth))

        sends = recvs = None
        if dim == "c":
            if image:
                sends, recvs = image_device, beside_image
            elif text:
                sends, recvs = text_device, beside_text
            src = ins[k].at[(EVERY, EVERY, EVERY, 1 - c) + box]
            return [(make(src, here.at[(EVERY, EVERY, EVERY) + box], 0), sends, recvs)]
        if text and dim == "y":
            sends, recvs = upper, lower
        elif text and "y" not in dims[:step]:
            sends = recvs = upper
        where = (EVERY, EVERY) if order == 2 else (x, y)
        if dim == "a":
            src = here.at[(depth - 1 - z,) + where + box]
            dst = z_relay[k].at[(e, EVERY, EVERY) + inner] if order == 2 else relay[k].at[(e,) + inner]
            to = {**at, "z": jnp.where(z == 0, 1, depth - 2)}
            copy = remote(src, dst, sems, (number[piece], depth + 2), to)
            ends = jnp.logical_or(z == 0, z == depth - 1)
            middle = jnp.logical_and(z > 0, z < depth - 1)
            return [(copy, both_of(sends, ends), both_of(recvs, middle))]
        if dim == "z":
            found = []
            for by in range(1, depth):
                to, source_level = lax.rem(z + by, depth), lax.rem(z + depth - by, depth)
                src = here.at[(to,) + where + box]
                if order == 2:
                    dst = z_first[k].at[(e, by - 1, EVERY, EVERY) + inner]
                else:
                    dst = last[k].at[(e, by - 1) + inner]
                found.append(
                    (
                        make(src, dst, 2 + by, by),
                        both_of(sends, jnp.abs(to - z) != depth - 1),
                        both_of(recvs, jnp.abs(source_level - z) != depth - 1),
                    )
                )
            return found
        if order == 2 and dim == "x":
            src, dst = here.at[(z, 1 - x, EVERY) + box], z_second[k].at[(e, EVERY) + inner]
            return [(make(src, dst, 1), sends, recvs)]
        if order == 2:
            src, dst = here.at[(z, x, 1 - y) + box], z_last[k].at[(e,) + inner]
            return [(make(src, dst, 2), sends, recvs)]
        if step == 1:
            spot = (EVERY, EVERY, 1 - y) if dim == "y" else (EVERY, 1 - x, EVERY)
            dst = first[k].at[(e, EVERY, EVERY) + inner]
        else:
            spot = (EVERY, x, 1 - y) if dim == "y" else (EVERY, 1 - x, y)
            dst = second[k].at[(e, EVERY) + inner]
        return [(make(here.at[spot + box], dst, step), sends, recvs)]

    def combine(piece, step):
        k, e, band, cols, order = piece
        box, inner = boxes(piece)
        image, text = kinds[k] and e == 0, kinds[k] and e == 1
        dims = ("c",) + SCATTER_ORDERS[order]
        dim = dims[step]
        here = acc[k].at[e]

        def over(spots, value_of, keep):
            @pl.loop(0, depth)
            def _(level):
                for index, spot in enumerate(spots):
                    where = (level,) + spot + box
                    value = value_of(level, index, spot)
                    here[where] = value if keep else here[where] + value

        def wide(value):
            return value.astype(jnp.float32)

        if step == 0:
            spots = [(0, 0), (0, 1), (1, 0), (1, 1)]

            def own(level, index, spot):
                if k < n_far:
                    return own_half[k][(level,) + spot + box]
                return ins[k][(level,) + spot + (c,) + box]

            if image:
                pl.when(lower)(lambda: over(spots, own, False))
                pl.when(beside_text)(lambda: over(spots, own, True))
            elif text:
                pl.when(text_device)(lambda: over(spots, own, True))
            else:
                over(spots, own, False)
        elif dim == "a":
            dest = jnp.where(z == 1, depth - 1, 0)

            def act():
                if order == 2:
                    for spot in [(0, 0), (0, 1), (1, 0), (1, 1)]:
                        where = (dest,) + spot + box
                        here[where] = here[where] + z_relay[k][(e,) + spot + inner]
                else:
                    where = (dest, x, y) + box
                    here[where] = here[where] + relay[k][(e,) + inner]

            middle = jnp.logical_and(z > 0, z < depth - 1)
            guard(both_of(upper if text and order == 2 else None, middle), act)
        elif step == STEPS - 1:

            def finish(total):
                if kinds[k]:
                    total = total * factors[e]
                outs[k][(e,) + box] = total

            def own():
                return wide(here[(z, x, y) + box])

            if order == 2:
                got = lambda: wide(z_last[k][(e,) + inner])
                if text:
                    pl.when(lower)(lambda: finish(got()))
                    pl.when(upper)(lambda: finish(own()))
                else:
                    finish(own() + got())
            else:
                for cond, bys in sources:

                    @pl.when(cond)
                    def _(bys=bys):
                        total = own()
                        for by in bys:
                            total = total + wide(last[k][(e, by - 1) + inner])
                        finish(total)
        elif dim == "z":
            for cond, bys in sources:

                def act(bys=bys):
                    for spot in [(0, 0), (0, 1), (1, 0), (1, 1)]:
                        where = (z,) + spot + box
                        total = wide(here[where])
                        for by in bys:
                            total = total + wide(z_first[k][(e, by - 1) + spot + inner])
                        here[where] = total.astype(here.dtype)

                guard(both_of(upper if text else None, cond), act)
        elif order == 2:

            def act():
                for other in range(2):
                    where = (z, x, other) + box
                    here[where] = here[where] + z_second[k][(e, other) + inner]

            guard(upper if text else None, act)
        elif step == 1:
            spots = [(0, y), (1, y)] if dim == "y" else [(x, 0), (x, 1)]
            got = lambda level, index, spot: first[k][(e, level, index) + inner]
            if text and dim == "y":
                pl.when(lower)(lambda: over(spots, got, True))
            elif text:
                pl.when(upper)(lambda: over(spots, got, False))
            else:
                over(spots, got, False)
        else:
            got = lambda level, index, spot: second[k][(e, level) + inner]
            if text and dim == "y":
                pl.when(lower)(lambda: over([(x, y)], got, True))
            else:
                over([(x, y)], got, False)

    def start(chunk, step):
        for piece in chunk:
            for copy, sends, _ in copies_of(piece, step):
                guard(sends, copy.start)

    def wait(chunk, step):
        for piece in chunk:
            for copy, _, recvs in copies_of(piece, step):
                guard(recvs, copy.wait_recv)
            combine(piece, step)

    def halve():
        kv_beside.wait_recv()

        @pl.loop(0, rows // 64)
        def _(j):
            block = pl.ds(pl.multiple_of(j * 64, 64), 64)
            for level in range(2):
                kv_sum[level, block, :] = kv_sum[level, block, :] + kv_mine[level, block, :]

    def project_back(qkv_grad, flipped, normed_in, far_in, weight_in, tokens_in, residual_in, token_out):
        pairs = [
            (weight, weight_in),
            (normed, normed_in),
            (far_normed, far_in),
            (tokens, tokens_in),
            (residual_grad, residual_in),
        ]
        loads = [pltpu.make_async_copy(src, dst, away_sem.at[j]) for j, (src, dst) in enumerate(pairs)]
        for copy in loads:
            copy.start()
        halve()
        qkv_grad[:rows, :width] = dq[...]
        qkv_grad[:rows, width:] = kv_sum[y]
        qkv_grad[rows:, width:] = kv_sum[1 - y]
        for copy in loads:
            copy.wait()

        @pl.loop(0, rows // 128)
        def _(j):
            block = pl.ds(pl.multiple_of(j * 128, 128), 128)
            below = pl.ds(pl.multiple_of(rows + j * 128, 128), 128)
            far_terms[block, :] = product_trail(
                qkv_grad[below, width:], weight_in[:, width:]
            ).astype(jnp.bfloat16)

        kv_across.start()
        flipped[:, :rows] = normed_in[...].T
        flipped[:, rows:] = far_in[...].T

        def fold(value):
            return jnp.sum(value.reshape(-1, 8, width), axis=0)

        zero = jnp.zeros((8, width), jnp.float32)

        def gather_sums(j, carry):
            block = pl.ds(pl.multiple_of(j * 64, 64), 64)
            below = pl.ds(pl.multiple_of(rows + j * 64, 64), 64)
            own, far_part = qkv_grad[block, 2 * width :], qkv_grad[below, 2 * width :]
            return (
                carry[0] + fold(dq[block, :].astype(jnp.float32)),
                carry[1] + fold(own.astype(jnp.float32) + far_part.astype(jnp.float32)),
            )

        sum_q, sum_v = lax.fori_loop(0, rows // 64, gather_sums, (zero, zero))
        step = width // 2
        spots = spots_of(depth)
        for begin, count, depth_rows in ((0, 2, rows), (2, 4, 2 * rows)):

            @pl.loop(begin, begin + count)
            def _(j, depth_rows=depth_rows):
                cols = pl.ds(pl.multiple_of(j * step, 128), step)
                value = jnp.dot(
                    flipped[:, :depth_rows],
                    qkv_grad[:depth_rows, cols],
                    preferred_element_type=jnp.float32,
                ).astype(jnp.bfloat16)
                for index, spot in enumerate(spots):
                    qkv_terms[spot + (EVERY, cols)] = value[index * share : (index + 1) * share]

        flow.tick()
        kv_across.wait_recv()

        def back(j, carry):
            block = pl.ds(pl.multiple_of(j * 128, 128), 128)
            value = tokens_in[block, :].astype(jnp.float32)
            centred = value - jnp.mean(value, axis=-1, keepdims=True)
            scale = lax.rsqrt(jnp.mean(centred * centred, axis=-1, keepdims=True) + NORM_EPS)
            unit = centred * scale
            grad = product_trail(qkv_grad[block, :], weight_in[...]) + far_got[block, :].astype(
                jnp.float32
            )
            lifted = grad * vectors[0:1, :]
            inner = jnp.mean(lifted * unit, axis=-1, keepdims=True)
            part = scale * (lifted - jnp.mean(lifted, axis=-1, keepdims=True) - unit * inner)
            token_out[block, :] = (residual_in[block, :] + part).astype(jnp.bfloat16)
            return carry[0] + fold(grad * unit), carry[1] + fold(grad)

        sum_gain, sum_shift = lax.fori_loop(0, rows // 128, back, (zero, zero))
        store = pltpu.make_async_copy(token_out, token_grad, away_sem.at[0])
        store.start()
        lines = [jnp.sum(value, axis=0, keepdims=True) for value in (sum_gain, sum_shift, sum_q, sum_v)]
        def stack(parts):
            count = sum(part.shape[0] for part in parts)
            return jnp.concatenate(parts + [jnp.zeros((8 - count, parts[0].shape[1]), jnp.float32)])

        scales = [
            jnp.where(text_device == (e == 1), factors[e], 0.0)
            for e in range(2)
        ]
        down_part = [small[3:4, :] * scale for scale in scales]
        up_part = [up_shift_sum[0:1, :] * scale for scale in scales]
        ff = up_shift_sum.shape[1]
        head = dealt(stack(lines + [small[0:3, :]]), share, devices)
        tail = dealt(stack(down_part), share, devices) + dealt(
            stack([jnp.zeros((2, ff), jnp.float32)] + up_part), ff // devices, devices
        )
        for index, spot in enumerate(spots):
            rows_of = slice(index * 8, (index + 1) * 8)
            thin_terms[spot] = jnp.concatenate([head[rows_of], tail[rows_of]], axis=0)
        store.wait()

    def project_scope():
        low = jnp.bfloat16
        pl.run_scoped(
            project_back,
            pltpu.VMEM((2 * rows, 3 * width), low),
            pltpu.VMEM((width, 2 * rows), low),
            pltpu.VMEM((rows, width), low),
            pltpu.VMEM((rows, width), low),
            pltpu.VMEM((width, 3 * width), low),
            pltpu.VMEM((rows, width), low),
            pltpu.VMEM((rows, width), jnp.float32),
            pltpu.VMEM((rows, width), low),
        )

    group_width = width // 2
    stream = y * 2 + c

    def attention(group):
        cols = pl.ds(group * group_width, group_width)
        value_cols = pl.ds(width + group * group_width, group_width)

        def act(keys, values, q_in, g_in, mixed_in, *work):
            pairs = [
                (kv.at[:, cols], keys),
                (kv.at[:, value_cols], values),
                (queries.at[:, cols], q_in),
                (mixed_grad.at[:, cols], g_in),
                (mixed_t.at[cols, :], mixed_in),
            ]
            loads = [pltpu.make_async_copy(src, dst, away_sem.at[j]) for j, (src, dst) in enumerate(pairs)]
            for copy in loads:
                copy.start()
            for copy in loads:
                copy.wait()
            back_group(
                group, kind, stream, log_total, keys, values, q_in, g_in, mixed_in,
                dq.at[:, cols], flow.tick, *work,
            )
            dk, dv = work[-2:]
            for part, (terms, rest, begin) in enumerate(((dk, keys, cols), (dv, values, value_cols))):
                for level in range(2):
                    mine = (level * 2 + c) * rows
                    away = (level * 2 + 1 - c) * rows

                    @pl.loop(0, rows // 128)
                    def _(j, level=level, mine=mine, away=away, terms=terms, rest=rest, begin=begin):
                        to = pl.ds(pl.multiple_of(j * 128, 128), 128)
                        kept = pl.ds(pl.multiple_of(mine + j * 128, 128), 128)
                        sent = pl.ds(pl.multiple_of(away + j * 128, 128), 128)
                        kv_mine[level, to, begin] = terms[kept, :].astype(jnp.bfloat16)
                        rest[sent, :] = terms[sent, :].astype(jnp.bfloat16)

            stores = []
            for part, (rest, begin) in enumerate(((keys, cols), (values, value_cols))):
                for level in range(2):
                    sent = pl.ds(pl.multiple_of((level * 2 + 1 - c) * rows, rows), rows)
                    stores.append(
                        pltpu.make_async_copy(
                            rest.at[sent], kv_away.at[level, :, begin], away_sem.at[part * 2 + level]
                        )
                    )
            for copy in stores:
                copy.start()
            for copy in stores:
                copy.wait()
            if group == 1:
                kv_beside.start()

        def scope():
            low = jnp.bfloat16
            heads = group_width // HEAD_DIM
            everyone = 4 * rows
            pl.run_scoped(
                act,
                pltpu.VMEM((everyone, group_width), low),
                pltpu.VMEM((everyone, group_width), low),
                pltpu.VMEM((rows, group_width), low),
                pltpu.VMEM((rows, group_width), low),
                pltpu.VMEM((group_width, rows), jnp.float32),
                pltpu.VMEM((group_width, everyone), low),
                pltpu.VMEM((heads, rows, PAIR), low),
                pltpu.VMEM((heads, rows, PAIR), low),
                pltpu.VMEM((heads, PAIR, rows), low),
                pltpu.VMEM((heads, PAIR, rows), low),
                pltpu.VMEM((group_width, TQ), jnp.float32),
                pltpu.VMEM((8, rows), jnp.float32),
                pltpu.VMEM((everyone, group_width), jnp.float32),
                pltpu.VMEM((everyone, group_width), jnp.float32),
            )

        return scope

    flow = Pipeline(chunks, 2, start, wait)
    for copy in local:
        copy.wait()
    flow.tick()
    attention(0)()
    flow.tick()
    attention(1)()
    flow.tick()
    project_scope()
    flow.tick(STEPS + len(chunks))
    lane = lax.broadcasted_iota(jnp.int32, (1, 128), 1)
    outs[4][0, THIN_ROWS - 1 : THIN_ROWS, :] = jnp.where(
        lane == 0, counts[0], jnp.where(lane == 1, counts[1], 0.0)
    )
    for copy in (kv_beside, kv_across):
        copy.wait_send()
    for chunk in chunks:
        for step in range(STEPS):
            for piece in chunk:
                for copy, sends, _ in copies_of(piece, step):
                    guard(sends, copy.wait_send)


def scatter_all(
    up, down, out, small, up_shift_sum, vectors, kind, log_total,
    queries, kv, mixed_grad, mixed_t, normed, far_normed, weight, tokens, residual_grad, depth,
):
    rows, width = tokens.shape
    far = [up, down, out]
    kinds = (True, True, False, False, False)
    share, ff_share, ff = up.shape[4], down.shape[4], up.shape[5]
    chunks, cuts = scatter_chunks(share, width, ff_share, ff)
    n_pieces = sum(len(chunk) for chunk in chunks)
    anywhere, inside = pl.BlockSpec(memory_space=pl.ANY), pl.BlockSpec(memory_space=pltpu.VMEM)
    low, box = jnp.bfloat16, (depth, 2, 2, 2)
    tails = [a.shape[4:] for a in far] + [(share, 3 * width), (THIN_ROWS, 128)]
    dtypes = [low] * 4 + [jnp.float32]
    experts = [2 if kind else 1 for kind in kinds]
    scratch = [
        pltpu.VMEM((e, depth, 2, 2) + tail, dtype) for e, tail, dtype in zip(experts, tails, dtypes)
    ]
    plain, turned = [], []
    for tail, cut in zip(tails, cuts):
        plain.append((cut[0] or tail[0], cut[1] or tail[1]))
        turned.append((tail[0] - cut[0], tail[1] - cut[1]) if any(cut) else (8, 128))
    for middle in ((depth, 2), (depth,), (depth - 1,)):
        scratch += [pltpu.VMEM((e,) + middle + t, d) for e, t, d in zip(experts, plain, dtypes)]
    scratch += [pltpu.VMEM((e,) + t, d) for e, t, d in zip(experts, plain, dtypes)]
    for middle in ((2, 2), (depth - 1, 2, 2), (2,), ()):
        scratch += [pltpu.VMEM((e,) + middle + t, d) for e, t, d in zip(experts, turned, dtypes)]
    scratch += [pltpu.VMEM((depth, 2, 2) + a.shape[4:], low) for a in far]
    scratch += [
        pltpu.VMEM(box + (share, 3 * width), low),
        pltpu.VMEM(box + (THIN_ROWS, 128), jnp.float32),
        pltpu.VMEM((2, rows, 2 * width), low),
        pltpu.VMEM((rows, width), low),
        pltpu.VMEM((rows, width), low),
        pltpu.VMEM((2, rows, 2 * width), low),
        pltpu.VMEM((rows, width), low),
        pltpu.SemaphoreType.DMA((n_pieces, depth + 3)),
        pltpu.SemaphoreType.DMA((n_pieces, depth + 3)),
        pltpu.SemaphoreType.DMA((3,)),
        pltpu.SemaphoreType.DMA((5,)),
        pltpu.SemaphoreType.DMA((2,)),
        pltpu.SemaphoreType.DMA((2,)),
    ]
    return pl.pallas_call(
        functools.partial(scatter_kernel, depth, kinds, chunks, cuts),
        out_shape=[
            jax.ShapeDtypeStruct((e,) + tail, jnp.float32) for e, tail in zip(experts, tails)
        ]
        + [jax.ShapeDtypeStruct((rows, width), low), jax.ShapeDtypeStruct((2, rows, 2 * width), low)],
        in_specs=[anywhere] * 3 + [inside] * 5 + [anywhere] * 9,
        out_specs=[inside] * 5 + [anywhere] * 2,
        scratch_shapes=scratch,
        compiler_params=pltpu.CompilerParams(
            collective_id=2, has_side_effects=True, vmem_limit_bytes=61 << 20
        ),
    )(
        up, down, out, small, up_shift_sum, vectors, kind, log_total,
        queries, kv, mixed_grad, mixed_t, normed, far_normed, weight, tokens, residual_grad,
    )[:6]


def publish_kernel(count, share, ff_share, *refs):
    far, thin = refs[:count], refs[count]
    outs, smalls = refs[count + 1 : 2 * count + 1], refs[2 * count + 1 : 2 * count + 11]
    held, sems = refs[2 * count + 11 : 3 * count + 11], refs[-1]
    inward = [pltpu.make_async_copy(far[j], held[j], sems.at[0, j]) for j in range(count)]
    outward = [pltpu.make_async_copy(held[j], outs[j], sems.at[1, j]) for j in range(count)]
    for copy in inward:
        copy.start()
    for j in range(7):
        smalls[j][...] = thin[j, :share]
    smalls[7][...] = thin[10:12, :ff_share]
    smalls[8][...] = thin[8:10, :share]
    smalls[9][...] = thin[THIN_ROWS - 1, :2]
    for first, second in zip(inward, outward):
        first.wait()
        second.start()
    for copy in outward:
        copy.wait()


def publish(arrays, thin, share, ff_share):
    anywhere, inside = pl.BlockSpec(memory_space=pl.ANY), pl.BlockSpec(memory_space=pltpu.VMEM)
    count = len(arrays)
    small = [(share,)] * 7 + [(2, ff_share), (2, share), (2,)]
    return pl.pallas_call(
        functools.partial(publish_kernel, count, share, ff_share),
        out_shape=[jax.ShapeDtypeStruct(array.shape, array.dtype) for array in arrays]
        + [jax.ShapeDtypeStruct(shape, jnp.float32) for shape in small],
        in_specs=[anywhere] * count + [inside],
        out_specs=[anywhere] * count + [inside] * len(small),
        scratch_shapes=[pltpu.VMEM(array.shape, array.dtype) for array in arrays]
        + [pltpu.SemaphoreType.DMA((2, count))],
        compiler_params=pltpu.CompilerParams(vmem_limit_bytes=62 << 20),
    )(*arrays, thin)


def padded(values):
    return jnp.pad(values, ((0, 0), (0, 128 - values.shape[1])))


def body(
    near,
    tokens,
    group_kind,
    ln1_gain,
    ln1_bias,
    w_qkv,
    q_bias,
    v_bias,
    w_out,
    out_bias,
    ln2_gain,
    ln2_bias,
    w_up,
    b_up,
    w_down,
    b_down,
    cotangent,
):
    row_count, model_width = tokens.shape
    stream_size = lax.axis_size("stream")
    stream_place = lax.axis_index("stream")
    devices = lax.axis_size("items") * stream_size
    group_type = group_kind[0]
    expert_pick = jnp.where(stream_place == stream_size - 1, 1, 0).astype(jnp.int32)
    share, ff_share, ff = model_width // devices, w_down.shape[1], w_up.shape[2]
    both = ("items", "stream")
    low = jnp.bfloat16
    thin = jnp.stack([ln1_gain, ln1_bias, q_bias, v_bias, out_bias, ln2_gain, ln2_bias])
    thin = jnp.concatenate(
        [padded(thin), padded(b_up), padded(b_down), padded(group_kind.astype(low)[:, None])]
    )
    thin = jnp.pad(thin, ((0, THIN_ROWS - thin.shape[0]), (0, 0)))
    tokens_f = tokens.astype(jnp.float32)
    kind_wide = jnp.broadcast_to(group_type.astype(jnp.float32), (8, 128))
    place_at = stream_place.astype(jnp.int32)[None]
    if near:
        depth = lax.axis_size("items") // 2
        (
            thin_all,
            out_weight,
            up_all,
            down_all,
            qkv_weight,
            normed_low,
            queries,
            vectors,
            kv,
            mixed_low,
            mixed_t,
            log_total,
            far_normed,
        ) = gather_all(thin, w_qkv, w_out, w_up, w_down, tokens, kind_wide, depth)
        thin_all = thin_all.reshape(devices, THIN_ROWS, 128)
        out_weight = out_weight.reshape(model_width, model_width)
        up_all = up_all.reshape(2, model_width, ff)
        down_all = down_all.reshape(2, ff, model_width)
    else:
        thin_all = lax.all_gather(thin, both, axis=0)
        qkv_weight = lax.all_gather(w_qkv, both, axis=0, tiled=True)
        out_weight = lax.all_gather(w_out, both, axis=0, tiled=True)
        up_all = lax.all_gather(w_up, both, axis=1, tiled=True)
        down_all = lax.all_gather(w_down, both, axis=1, tiled=True)
        vectors = (
            thin_all[:, :, :share].transpose(1, 0, 2).reshape(THIN_ROWS, -1).astype(jnp.float32)
        )
        normed_low = layer_norm(tokens_f, vectors[0], vectors[1]).astype(low)
        shifts = jnp.concatenate([vectors[2], jnp.zeros_like(vectors[2]), vectors[3]])
        projected = (product(normed_low, qkv_weight) + shifts).astype(low)
        queries = projected[:, :model_width]
        kv = lax.all_gather(projected[:, model_width:], "stream", axis=0, tiled=True)
        mixed_low, mixed_t, log_total = attend(kind_wide, place_at, queries, kv)
    up_shift_all = thin_all[:, 7:9, :ff_share].transpose(1, 0, 2).reshape(2, ff)
    (
        output,
        residual_grad,
        grad_out_weight,
        mixed_grad,
        grad_up,
        grad_down,
        small,
        grad_up_shift,
    ) = feed(
        expert_pick[None],
        place_at,
        kind_wide,
        vectors,
        up_shift_all[:, None],
        tokens,
        mixed_low,
        out_weight,
        cotangent,
        up_all,
        down_all,
    )
    if near:
        box = (depth, 2, 2, 2)
        up_sum, down_sum, out_sum, qkv_sum, thin_sum, token_grad = scatter_all(
            grad_up.reshape(box + (share, ff)),
            grad_down.reshape(box + (ff_share, model_width)),
            grad_out_weight.reshape(box + (share, model_width)),
            small,
            grad_up_shift,
            vectors,
            kind_wide,
            log_total,
            queries,
            kv,
            mixed_grad,
            mixed_t,
            normed_low,
            far_normed,
            qkv_weight,
            tokens,
            residual_grad,
            depth,
        )
        thin_sum = thin_sum[0]
        (
            up_sum,
            down_sum,
            out_sum,
            qkv_sum,
            token_grad,
            *lines,
            up_shift_sum,
            down_shift_sum,
            totals,
        ) = publish(
            [up_sum, down_sum, out_sum[0], qkv_sum[0], token_grad], thin_sum, share, ff_share
        )
    else:
        kinds = vectors[11, :: stream_size * share].astype(jnp.int32)
        tally = []
        for kind in range(2):
            modality = layout(
                jnp.int32(kind), jnp.arange(stream_size * row_count, dtype=jnp.int32), row_count
            )[1]
            tally.append([jnp.sum((modality == e).astype(jnp.float32)) for e in range(2)])
        totals = jnp.stack(
            [jnp.sum(jnp.where(kinds == 0, tally[0][e], tally[1][e])) for e in range(2)]
        )
        factor = lax.rsqrt(totals)
        pick = (jnp.arange(2, dtype=jnp.int32) == expert_pick).astype(jnp.float32) * factor

        def lanes(values):
            values = values.reshape(values.shape[0], devices, -1).transpose(1, 0, 2)
            return jnp.pad(values, ((0, 0), (0, 0), (0, 128 - values.shape[2])))

        scatter = functools.partial(
            lax.psum_scatter, axis_name=both, scatter_dimension=0, tiled=True
        )
        wide = functools.partial(lax.psum_scatter, axis_name=both, scatter_dimension=1, tiled=True)
        query_grad, kv_terms = attend_back(
            kind_wide, place_at, queries, kv, mixed_grad, mixed_t, log_total
        )
        kv_grad = lax.psum_scatter(
            kv_terms.astype(jnp.float32), "stream", scatter_dimension=0, tiled=True
        )
        qkv_grad = jnp.concatenate([query_grad, kv_grad.astype(low)], axis=1)
        grad_qkv = product_lead(normed_low, qkv_grad)
        early = [
            jnp.sum(qkv_grad[:, :model_width].astype(jnp.float32), axis=0),
            jnp.sum(qkv_grad[:, 2 * model_width :].astype(jnp.float32), axis=0),
        ]
        norm_one_grad = product_trail(qkv_grad, qkv_weight)
        token_part, *grads_one = jax.vjp(layer_norm, tokens_f, vectors[0], vectors[1])[1](
            norm_one_grad
        )
        token_grad = (residual_grad + token_part).astype(low)
        up_sum = wide(pick[:, None, None] * grad_up.astype(jnp.float32)[None])
        down_sum = wide(pick[:, None, None] * grad_down.astype(jnp.float32)[None])
        out_sum, qkv_sum = scatter(grad_out_weight.astype(jnp.float32)), scatter(grad_qkv)
        thin_terms = [
            lanes(jnp.stack(grads_one + early + [small[0], small[1], small[2]])),
            jnp.zeros((devices, 1, 128), jnp.float32),
            lanes(pick[:, None] * small[3][None]),
            lanes(pick[:, None] * grad_up_shift[0][None]),
            jnp.zeros((devices, THIN_ROWS - 12, 128), jnp.float32),
        ]
        thin_sum = scatter(jnp.concatenate(thin_terms, axis=1))[0]
        lines = [thin_sum[k, :share] for k in range(7)]
        up_shift_sum, down_shift_sum = thin_sum[10:12, :ff_share], thin_sum[8:10, :share]
    return (
        output,
        token_grad,
        lines[0],
        lines[1],
        qkv_sum,
        lines[2],
        lines[3],
        out_sum,
        lines[4],
        lines[5],
        lines[6],
        up_sum,
        up_shift_sum,
        down_sum,
        down_shift_sum,
        totals,
    )


def solution(mesh):
    placed = (
        P(("items", "stream"), None),
        P("items"),
        P(("items", "stream")),
        P(("items", "stream")),
        P(("items", "stream"), None),
        P(("items", "stream")),
        P(("items", "stream")),
        P(("items", "stream"), None),
        P(("items", "stream")),
        P(("items", "stream")),
        P(("items", "stream")),
        P(None, ("items", "stream"), None),
        P(None, ("items", "stream")),
        P(None, ("items", "stream"), None),
        P(None, ("items", "stream")),
        P(("items", "stream"), None),
    )
    near = mesh.shape["items"] == 8 and mesh.shape["stream"] == 4
    return jax.shard_map(
        functools.partial(body, near),
        mesh=mesh,
        in_specs=placed,
        out_specs=(
            P(("items", "stream"), None),
            P(("items", "stream"), None),
            P(("items", "stream")),
            P(("items", "stream")),
            P(("items", "stream"), None),
            P(("items", "stream")),
            P(("items", "stream")),
            P(("items", "stream"), None),
            P(("items", "stream")),
            P(("items", "stream")),
            P(("items", "stream")),
            P(None, ("items", "stream"), None),
            P(None, ("items", "stream")),
            P(None, ("items", "stream"), None),
            P(None, ("items", "stream")),
            P(),
        ),
        check_vma=False,
    )
```
